32 devices in a mesh: rep: 4 (over z), fsdp: 8 (over y, x, core).
Axes of the slice: x: 2, y: 2, z: 4, core: 2. Of those that a mesh axis runs over, the one named last changes fastest.
Arguments:
- tokens: bfloat16 [4, 2048, 12288], P('rep', 'fsdp'), may hold values from -8 to 8, as said below
- cotangent: bfloat16 [4, 2048, 1024], P('rep', 'fsdp'), may hold values from -1 to 1, as said below
- weights: float32 [4, 12288, 1024], P('rep', 'fsdp'), may hold values from -0.0546875 to 0.0546875
- first_moment: float32 [4, 12288, 1024], P('rep', 'fsdp'), may hold values from -0.00390625 to 0.00390625
- second_moment: float32 [4, 12288, 1024], P('rep', 'fsdp'), may hold values from 3.973643e-08 to 7.947286e-07
- anchor: float32 [12288, 1024], P(('fsdp', 'rep')), may hold values from -0.0546875 to 0.0546875
- momentum: float32 [12288, 1024], P(('fsdp', 'rep')), may hold values from -0.15625 to 0.15625
- due_fragment: int32 [1], replicated, may hold values from 0 to 7
- step_count: int32 [1], replicated, may hold values from 1 to 100000
Outputs:
- weights_out: float32 [4, 12288, 1024], P('rep', 'fsdp')
- first_out: float32 [4, 12288, 1024], P('rep', 'fsdp')
- second_out: float32 [4, 12288, 1024], P('rep', 'fsdp')
- anchor_out: float32 [12288, 1024], P(('fsdp', 'rep'))
- momentum_out: float32 [12288, 1024], P(('fsdp', 'rep'))
- plan_out: float32 [1], replicated
The draws below stay inside these ranges and needn't reach their ends.
Inputs may be any that keep to these rules, and one draw needn't show every extreme that they name: `tokens`: activations of order one. `cotangent`: each replica's entries carry a scale of its own.
All inputs are finite; a program needn't handle non-finite values.
Results may differ from the reference program's by a relative error of at most 0.0009.
Values may be sent and summed in bfloat16 or wider, within the bound.
No kernel may reach another device: no remote copies, remote signals or barrier semaphores. Data moves between devices by JAX's collectives and lax.ppermute only.
A program may use at most 192 MiB of HBM per device.

```python
import math
import jax
import jax.numpy as jnp
from jax import lax

D = 12288
HEAD = 128
TOK_DEV = 256
WARMUP = 2000
STEPS_TOTAL = 100000
FRAG_COLS = 128
KVW = 512
FRAGS = 8
TOKENS = 2048
N_REP = 4
N_FSDP = 8


def feature_scales(key, slope):
    position = jnp.arange(D, dtype=jnp.float32) / D
    rough = jnp.exp(jax.random.uniform(key, (D,), jnp.float32, jnp.log(0.7), jnp.log(1.4)))
    return jnp.sqrt(1.0 + slope * position) * rough


def replica_scales(key, low, high):
    order = jax.random.permutation(key, N_REP).astype(jnp.float32)
    return jnp.exp(jnp.log(low) + (jnp.log(high) - jnp.log(low)) * order / (N_REP - 1))


def feature_offsets(magnitude_key, sign_key):
    magnitude = jax.random.uniform(magnitude_key, (D,), jnp.float32, 0.6, 1.2)
    signed = jnp.where(jax.random.bernoulli(sign_key, 0.5, (D,)), 1.0, -1.0)
    return magnitude * signed


def draw_tokens(key, part):
    key = jax.random.fold_in(key, 11)
    scale_key, value_key, magnitude_key, sign_key = jax.random.split(key, 4)
    shifted = feature_offsets(magnitude_key, sign_key)
    scales = feature_scales(scale_key, 2.0)
    values = jnp.clip(jax.random.normal(value_key, (N_REP, TOKENS, D), jnp.float32), -5.0, 5.0)
    return jnp.clip((values + shifted[None, None, :]) * scales[None, None, :], -8.0, 8.0).astype(jnp.bfloat16)


def draw_cotangent(key, part):
    key = jax.random.fold_in(key, 23)
    scale_key, value_key, direction_key = jax.random.split(key, 3)
    total = float(TOKENS * D * 2 * KVW) ** 0.5
    share = 16.0
    scales = replica_scales(scale_key, 0.4, 3.0) / total
    values = jnp.clip(jax.random.normal(value_key, (N_REP, TOKENS, 2 * KVW), jnp.float32), -6.0, 6.0)
    common = jnp.clip(jax.random.normal(direction_key, (N_REP, 1, 2 * KVW), jnp.float32), -5.0, 5.0) * (share / TOKENS) ** 0.5
    return ((values + common) * scales[:, None, None]).astype(jnp.bfloat16)


def steps_of(stream_key, shape, cuts, low, high):
    gain = 1.0
    for dim, shards_of in cuts:
        heights = jax.random.uniform(jax.random.fold_in(jax.random.fold_in(stream_key, 6), dim), (shards_of,), jnp.float32, low / len(cuts), high / len(cuts))
        gain = gain * jnp.repeat(jnp.exp(heights), shape[dim] // shards_of).reshape((-1,) + (1,) * (len(shape) - 1 - dim))
    return gain


def scatter_about(rng, shape, spread, most, shards=(), held_as=jnp.bfloat16):
    level = steps_of(rng, shape, shards, -0.22, 0.18) if shards else 1.0
    entries = jax.random.normal(rng, shape, jnp.float32) * spread * level
    return jnp.minimum(jnp.maximum(entries, -most), most).astype(held_as)


def setup_inputs(seed: int = 0) -> dict:
    key_list = jax.random.split(jax.random.key(seed), 10)
    tokens = draw_tokens(jax.random.fold_in(key_list[9], 71), 0)
    cotangent = draw_cotangent(jax.random.fold_in(key_list[9], 71), 0)
    weights = scatter_about(key_list[2], (N_REP, D, 2 * KVW), D ** -0.5, 0.0546875, ((0, 4), (1, 8)), jnp.float32)
    first_moment = scatter_about(key_list[3], (N_REP, D, 2 * KVW), ((2 * D * KVW) ** -0.5), 0.00390625, ((0, 4), (1, 8)), jnp.float32)
    second_moment = jnp.clip(jnp.exp(math.log(7.94728578057402e-07) - 2.9957322 * jax.random.uniform(key_list[4], (N_REP, D, 2 * KVW), jnp.float32) ** steps_of(key_list[4], (N_REP, D, 2 * KVW), ((0, 4), (1, 8)), -0.2, 0.2)), 3.973643103449831e-08, 7.94728578057402e-07)
    anchor = scatter_about(key_list[5], (D, 2 * KVW), D ** -0.5, 0.0546875, ((0, 32),), jnp.float32)
    momentum = scatter_about(key_list[6], (D, 2 * KVW), 0.01, 0.15625, ((0, 32),), jnp.float32)
    due_fragment = jax.random.randint(key_list[7], (1,), 0, FRAGS).astype(jnp.int32)
    step_count = jax.random.randint(key_list[8], (1,), 1, STEPS_TOTAL + 1).astype(jnp.int32)
    return dict(tokens=tokens, cotangent=cotangent, weights=weights, first_moment=first_moment, second_moment=second_moment, anchor=anchor, momentum=momentum, due_fragment=due_fragment, step_count=step_count)


BETA_ONE = 0.9
BETA_TWO = 0.95
ADAM_EPS = 1e-08
DECAY = 0.1
PEAK_RATE = 0.0003
CLIP_NORM = 1.0
OUTER_MU = 0.9
OUTER_RATE = 0.7
MIX_LOCAL = 0.5

def key_backward(raw_keys, incoming):
    count = raw_keys.shape[0]
    heads = raw_keys.reshape(count, -1, HEAD)
    inverse = lax.rsqrt(lax.optimization_barrier(jnp.mean(heads * heads, axis=2, keepdims=True)) + 1e-06)
    normed = heads * inverse
    upper = incoming.astype(jnp.float32).reshape(heads.shape)
    back = inverse * (upper - normed * lax.optimization_barrier(jnp.mean(upper * normed, axis=2, keepdims=True)))
    return back.reshape(count, -1).astype(jnp.bfloat16)

def replica_gradient(packed):
    inputs, incoming, params = packed
    key_weights = params[:, :KVW].astype(jnp.bfloat16)
    raw_keys = jnp.dot(inputs.astype(jnp.float32), key_weights.astype(jnp.float32), precision=lax.Precision.HIGHEST)
    back = key_backward(raw_keys, incoming[:, :KVW])
    upstream = jnp.concatenate([back, incoming[:, KVW:]], axis=1)
    blocks_in = inputs.reshape(N_FSDP, TOK_DEV, D)
    blocks_up = upstream.reshape(N_FSDP, TOK_DEV, 2 * KVW)

    def add_block(total, pair):
        partial_sum = jnp.dot(pair[0].astype(jnp.float32).T, pair[1].astype(jnp.float32), precision=lax.Precision.HIGHEST)
        partial_sum = lax.optimization_barrier(partial_sum.astype(jnp.bfloat16))
        return (total + partial_sum.astype(jnp.float32), None)
    gradient, _ = lax.scan(add_block, jnp.zeros((D, 2 * KVW), jnp.float32), (blocks_in, blocks_up))
    return gradient

def reference(tokens, cotangent, weights, first_moment, second_moment, anchor, momentum, due_fragment, step_count):
    gradient = lax.map(replica_gradient, (tokens, cotangent, weights))
    square = lax.optimization_barrier(jnp.sum(gradient * gradient, axis=(1, 2)))
    factor = jnp.minimum(1.0, CLIP_NORM / (jnp.sqrt(square) + 1e-06))
    clipped = gradient * factor[:, None, None]
    steps_now = step_count[0].astype(jnp.float32)
    plan = jnp.minimum(1.0, steps_now / WARMUP) * (0.55 + 0.45 * jnp.cos(jnp.pi * steps_now / STEPS_TOTAL))
    rate = PEAK_RATE * plan
    first_out = BETA_ONE * first_moment + (1.0 - BETA_ONE) * clipped
    second_out = BETA_TWO * second_moment + (1.0 - BETA_TWO) * clipped * clipped
    correct_one = 1.0 - jnp.power(BETA_ONE, steps_now)
    correct_two = 1.0 - jnp.power(BETA_TWO, steps_now)
    inner = weights - rate * (first_out / correct_one / (jnp.sqrt(second_out / correct_two) + ADAM_EPS) + DECAY * weights)
    offset = (due_fragment[0] * FRAG_COLS).astype(jnp.int32)
    own_cols = lax.dynamic_slice_in_dim(inner, offset, FRAG_COLS, 2)
    mean_inner = lax.optimization_barrier(jnp.sum(own_cols, axis=0)) / N_REP
    anchor_cols = lax.dynamic_slice_in_dim(anchor, offset, FRAG_COLS, 1)
    moment_cols = lax.dynamic_slice_in_dim(momentum, offset, FRAG_COLS, 1)
    pseudo = anchor_cols - mean_inner
    new_moment = OUTER_MU * moment_cols + pseudo
    new_anchor = anchor_cols - OUTER_RATE * (OUTER_MU * new_moment + pseudo)
    mixed = MIX_LOCAL * own_cols + (1.0 - MIX_LOCAL) * new_anchor[None]
    weights_out = lax.dynamic_update_slice_in_dim(inner, mixed, offset, 2)
    anchor_out = lax.dynamic_update_slice_in_dim(anchor, new_anchor, offset, 1)
    momentum_out = lax.dynamic_update_slice_in_dim(momentum, new_moment, offset, 1)
    plan_out = jnp.reshape(plan, (1,)).astype(jnp.float32)
    return (weights_out, first_out, second_out, anchor_out, momentum_out, plan_out)
```

```python
import jax
import jax.numpy as jnp
from jax import lax
from jax.sharding import PartitionSpec as P

HEAD = 128
WARMUP = 2000
STEPS_TOTAL = 100000
FRAG_COLS = 128


BETA_ONE = 0.9
BETA_TWO = 0.95
ADAM_EPS = 1e-08
DECAY = 0.1
PEAK_RATE = 0.0003
CLIP_NORM = 1.0
OUTER_MU = 0.9
OUTER_RATE = 0.7
MIX_LOCAL = 0.5


def key_backward(raw_keys, incoming):
    count = raw_keys.shape[0]
    heads = raw_keys.reshape(count, -1, HEAD)
    inverse = lax.rsqrt(jnp.mean(heads * heads, axis=2, keepdims=True) + 1e-06)
    normed = heads * inverse
    upper = incoming.astype(jnp.float32).reshape(heads.shape)
    back = inverse * (upper - normed * jnp.mean(upper * normed, axis=2, keepdims=True))
    return back.reshape(count, -1).astype(jnp.bfloat16)


def swap(block, axis, offset):
    count = lax.axis_size(axis)
    return lax.ppermute(block, axis, [(i, i ^ offset) for i in range(count)])


def gather_pairs(block, axis):
    count = lax.axis_size(axis)
    blocks = [block] + [swap(block, axis, k) for k in range(2, count, 2)]
    out = []
    for held in blocks:
        out += [held, swap(held, axis, 1)]
    return out


def body(
    tokens,
    cotangent,
    weights,
    first_moment,
    second_moment,
    anchor,
    momentum,
    due_fragment,
    step_count,
):
    inputs = tokens[0]
    incoming = cotangent[0]
    params = weights[0]
    kv_width = incoming.shape[1] // 2
    rows = params.shape[0]
    replicas = lax.axis_size("rep")
    shards = lax.axis_size("fsdp")
    me = lax.axis_index("fsdp")
    my_rep = lax.axis_index("rep")
    offset = due_fragment[0] * FRAG_COLS
    part = anchor.shape[0]

    old_cols = lax.dynamic_slice_in_dim(params, offset, FRAG_COLS, 1)
    anchor_cols = lax.dynamic_slice_in_dim(anchor, offset, FRAG_COLS, 1)
    moment_cols = lax.dynamic_slice_in_dim(momentum, offset, FRAG_COLS, 1)

    def rep_piece(cols, k):
        return lax.dynamic_slice_in_dim(cols, (my_rep ^ k) * part, part, 0)

    def rep_scatter(cols, wire):
        total = rep_piece(cols, 0)
        for k in range(1, replicas):
            total = total + swap(rep_piece(cols, k).astype(wire), "rep", k).astype(jnp.float32)
        return total

    def rep_gather(piece):
        pieces = [piece] + [swap(piece, "rep", k) for k in range(1, replicas)]
        out = jnp.zeros((part * replicas,) + piece.shape[1:], piece.dtype)
        for k in range(replicas):
            out = lax.dynamic_update_slice_in_dim(out, pieces[k], (my_rep ^ k) * part, 0)
        return out

    old_sum = rep_scatter(old_cols, jnp.float32)

    def token_piece(k):
        return lax.dynamic_slice_in_dim(inputs, (me ^ k) * rows, rows, 1)

    order = [k for k in range(2, shards) if k % 2 == 0] + [k for k in range(2, shards) if k % 2 == 1] + [1]
    key_weights = params[:, :kv_width].astype(jnp.bfloat16)
    columns = {0: token_piece(0)}
    for k in order:
        columns[k] = swap(token_piece(k), "fsdp", k)
    raw_keys = jnp.dot(columns[0], key_weights, preferred_element_type=jnp.float32)
    for k in order:
        partial_keys = jnp.dot(columns[k], key_weights, preferred_element_type=jnp.float32)
        raw_keys = raw_keys + swap(partial_keys.astype(jnp.bfloat16), "fsdp", k).astype(jnp.float32)
    key_back = key_backward(raw_keys, incoming[:, :kv_width])
    all_columns = jnp.concatenate([columns[k] for k in range(shards)], axis=0)
    values = jnp.concatenate(gather_pairs(incoming[:, kv_width:], "fsdp"), axis=0)
    keys = jnp.concatenate(gather_pairs(key_back, "fsdp"), axis=0)
    dims = (((0,), (0,)), ((), ()))
    grad_values = lax.dot_general(all_columns, values, dims, preferred_element_type=jnp.float32)
    grad_keys = lax.dot_general(all_columns, keys, dims, preferred_element_type=jnp.float32)
    own_square = jnp.sum(grad_values * grad_values) + jnp.sum(grad_keys * grad_keys)
    own_square = jnp.full((8, 128), own_square, jnp.float32)
    square = own_square
    for k in range(1, shards):
        square = square + swap(own_square, "fsdp", k)
    square = square[0, 0]
    gradient = jnp.concatenate([grad_keys, grad_values], axis=1)
    factor = jnp.minimum(1.0, CLIP_NORM / (jnp.sqrt(square) + 1e-06))
    steps_now = step_count[0].astype(jnp.float32)
    plan = jnp.minimum(1.0, steps_now / WARMUP) * (
        0.55 + 0.45 * jnp.cos(jnp.pi * steps_now / STEPS_TOTAL)
    )
    rate = PEAK_RATE * plan
    correct_one = 1.0 - jnp.power(BETA_ONE, steps_now)
    correct_two = 1.0 - jnp.power(BETA_TWO, steps_now)

    def adam(old, first, second, grad):
        clipped = grad * factor
        first_new = BETA_ONE * first + (1.0 - BETA_ONE) * clipped
        second_new = BETA_TWO * second + (1.0 - BETA_TWO) * clipped * clipped
        update = rate * (
            first_new / correct_one / (jnp.sqrt(second_new / correct_two) + ADAM_EPS) + DECAY * old
        )
        return update, first_new, second_new

    frag = [lax.dynamic_slice_in_dim(a, offset, FRAG_COLS, 1) for a in (params, first_moment[0], second_moment[0], gradient)]
    frag_update, _, _ = adam(*frag)
    own_cols = old_cols - frag_update
    update_sum = rep_scatter(frag_update, jnp.bfloat16)
    mean_inner = (old_sum - update_sum) / replicas
    pseudo = anchor_cols - mean_inner
    new_moment = OUTER_MU * moment_cols + pseudo
    new_anchor = anchor_cols - OUTER_RATE * (OUTER_MU * new_moment + pseudo)
    fresh = rep_gather(new_anchor)
    update, first_out, second_out = adam(params, first_moment[0], second_moment[0], gradient)
    inner = params - update
    mixed = MIX_LOCAL * own_cols + (1.0 - MIX_LOCAL) * fresh
    weights_out = lax.dynamic_update_slice_in_dim(inner, mixed, offset, 1)
    anchor_out = lax.dynamic_update_slice_in_dim(anchor, new_anchor, offset, 1)
    momentum_out = lax.dynamic_update_slice_in_dim(momentum, new_moment, offset, 1)
    plan_out = jnp.reshape(plan, (1,))
    return (
        weights_out[None],
        first_out[None],
        second_out[None],
        anchor_out,
        momentum_out,
        plan_out,
    )


def solution(mesh):
    return jax.shard_map(
        body,
        mesh=mesh,
        in_specs=(
            P("rep", "fsdp", None),
            P("rep", "fsdp", None),
            P("rep", "fsdp", None),
            P("rep", "fsdp", None),
            P("rep", "fsdp", None),
            P(("fsdp", "rep"), None),
            P(("fsdp", "rep"), None),
            P(),
            P(),
        ),
        out_specs=(
            P("rep", "fsdp", None),
            P("rep", "fsdp", None),
            P("rep", "fsdp", None),
            P(("fsdp", "rep"), None),
            P(("fsdp", "rep"), None),
            P(),
        ),
        check_vma=False,
    )
```

```python
import functools

import jax
import jax.numpy as jnp
from jax import lax
from jax.experimental import pallas as pl
from jax.experimental.pallas import tpu as pltpu
from jax.sharding import Mesh, PartitionSpec as P

HEAD = 128
WARMUP = 2000
STEPS_TOTAL = 100000
FRAG_COLS = 128


BETA_ONE = 0.9
BETA_TWO = 0.95
ADAM_EPS = 1e-08
DECAY = 0.1
PEAK_RATE = 0.0003
CLIP_NORM = 1.0
OUTER_MU = 0.9
OUTER_RATE = 0.7
MIX_LOCAL = 0.5

MIB = 1 << 20
ANY = pl.BlockSpec(memory_space=pl.ANY)
BLOCKS = ("chip", "core")


def params_of(limit):
    return pltpu.CompilerParams(vmem_limit_bytes=limit * MIB)


def cost(flops, moved):
    return pl.CostEstimate(flops=int(flops), bytes_accessed=int(moved), transcendentals=0)


def pack_kernel(first, count, rows, tok_ref, out_ref, sems):
    def copy(s):
        return pltpu.make_async_copy(
            tok_ref.at[pl.ds(first, count), pl.ds(s * rows, rows)], out_ref.at[s], sems.at[s]
        )

    shards = out_ref.shape[0]
    for s in range(shards):
        copy(s).start()
    for s in range(shards):
        copy(s).wait()


def pack(tokens, first, count, rows):
    shards = tokens.shape[1] // rows
    return pl.pallas_call(
        functools.partial(pack_kernel, first, count, rows),
        out_shape=jax.ShapeDtypeStruct((shards, count, rows), tokens.dtype),
        in_specs=[ANY],
        out_specs=ANY,
        scratch_shapes=[pltpu.SemaphoreType.DMA((shards,))],
        cost_estimate=cost(0, 4 * shards * count * rows),
        name="pack",
    )(tokens)


def transpose_kernel(core_ref, x_ref, out_ref):
    out_ref[...] = x_ref[0, 0].T


def transpose_tokens(blocks, core):
    chips, cores, count, rows = blocks.shape
    return pl.pallas_call(
        transpose_kernel,
        out_shape=jax.ShapeDtypeStruct((rows, chips * cores * count), blocks.dtype),
        grid_spec=pltpu.PrefetchScalarGridSpec(
            num_scalar_prefetch=1,
            grid=(cores, chips),
            in_specs=[pl.BlockSpec((1, 1, count, rows), lambda o, c, core: (c, (core[0] + o) % 2, 0, 0))],
            out_specs=pl.BlockSpec((rows, count), lambda o, c, core: (0, o * chips + c)),
        ),
        compiler_params=params_of(16),
        cost_estimate=cost(0, 4 * blocks.size),
        name="transpose_tokens",
    )(core, blocks)


def key_kernel(part_ref, cot_ref, out_ref):
    raw = jnp.sum(part_ref[...].astype(jnp.float32), axis=0)
    for h in range(raw.shape[1] // HEAD):
        cols = slice(h * HEAD, (h + 1) * HEAD)
        head = raw[:, cols]
        inverse = lax.rsqrt(jnp.mean(head * head, axis=1, keepdims=True) + 1e-06)
        normed = head * inverse
        upper = cot_ref[:, cols].astype(jnp.float32)
        back = inverse * (upper - normed * jnp.mean(upper * normed, axis=1, keepdims=True))
        back = back.astype(out_ref.dtype)
        for c in range(out_ref.shape[0]):
            out_ref[c, :, cols] = back


def key_backward(parts, incoming):
    return pl.pallas_call(
        key_kernel,
        out_shape=jax.ShapeDtypeStruct(parts.shape, jnp.bfloat16),
        compiler_params=params_of(16),
        cost_estimate=cost(20 * parts.size, 4 * parts.size),
        name="key_backward",
    )(parts, incoming)


def grad_kernel(halves, has_base, last, *refs):
    refs = list(refs)
    terms = [(refs.pop(0), refs.pop(0), refs.pop(0)) for _ in range(halves)]
    base = refs.pop(0) if has_base else None
    square_in = refs.pop(0) if last and has_base else None
    out_ref = refs.pop(0)
    total = None
    for x_ref, same_ref, other_ref in terms:
        depth = same_ref.shape[0]
        for ref, at in ((same_ref, 0), (other_ref, depth)):
            term = jnp.dot(x_ref[:, at:at + depth], ref[...], preferred_element_type=jnp.float32)
            total = term if total is None else total + term
    if base is not None:
        total = total + base[...]
    out_ref[...] = total
    if last:
        sq_ref = refs.pop(0)

        @pl.when(pl.program_id(0) == 0)
        def _():
            sq_ref[...] = square_in[...] if square_in is not None else jnp.zeros_like(sq_ref)

        rows, width = total.shape
        squares = (total * total).reshape(rows // 8, 8, width).sum(axis=0)
        folded = squares[:, :HEAD]
        for h in range(1, width // HEAD):
            folded = folded + squares[:, h * HEAD:(h + 1) * HEAD]
        sq_ref[...] += folded


def gradient(terms, base=None, square=None, last=True):
    rows = terms[0][0].shape[0]
    width = terms[0][1].shape[1]
    step = 256 if rows % 256 == 0 else rows
    row_block = lambda cols: pl.BlockSpec((step, cols), lambda i: (i, 0))
    whole = lambda a: pl.BlockSpec(a.shape, lambda i: (0, 0))
    args, specs = [], []
    for x, same, other in terms:
        args += [x, same, other]
        specs += [row_block(x.shape[1]), whole(same), whole(other)]
    if base is not None:
        args.append(base)
        specs.append(row_block(width))
        if last:
            args.append(square)
            specs.append(whole(square))
    shapes = [jax.ShapeDtypeStruct((rows, width), jnp.float32)]
    outs = [row_block(width)]
    if last:
        shapes.append(jax.ShapeDtypeStruct((8, HEAD), jnp.float32))
        outs.append(pl.BlockSpec((8, HEAD), lambda i: (0, 0)))
    depth = sum(x.shape[1] for x, _, _ in terms)
    return pl.pallas_call(
        functools.partial(grad_kernel, len(terms), base is not None, last),
        out_shape=shapes,
        grid=(rows // step,),
        in_specs=specs,
        out_specs=outs,
        compiler_params=params_of(24),
        cost_estimate=cost(2 * rows * width * depth, 2 * rows * depth + 4 * rows * width),
        name="gradient",
    )(*args)


def adam(old, first, second, grad, scalars):
    factor, rate, inv_one, inv_two = (scalars[i] for i in range(4))
    clipped = grad * factor
    first_new = BETA_ONE * first + (1.0 - BETA_ONE) * clipped
    second_new = BETA_TWO * second + (1.0 - BETA_TWO) * clipped * clipped
    update = rate * (
        first_new * inv_one / (jnp.sqrt(second_new * inv_two) + ADAM_EPS) + DECAY * old
    )
    return update, first_new, second_new


def adam_kernel(sc_ref, w_ref, m_ref, v_ref, gk_ref, gv_ref, w_out, m_out, v_out):
    width = gk_ref.shape[1]
    for g_ref, cols in ((gk_ref, slice(0, width)), (gv_ref, slice(width, 2 * width))):
        old = w_ref[:, cols]
        update, first_new, second_new = adam(old, m_ref[:, cols], v_ref[:, cols], g_ref[...], sc_ref)
        w_out[:, cols] = old - update
        m_out[:, cols] = first_new
        v_out[:, cols] = second_new


def adam_all(scalars, w, m, v, gk, gv):
    rows, width = w.shape
    step = 128
    full = pl.BlockSpec((step, width), lambda i: (i, 0))
    half = pl.BlockSpec((step, width // 2), lambda i: (i, 0))
    return pl.pallas_call(
        adam_kernel,
        out_shape=[jax.ShapeDtypeStruct(w.shape, jnp.float32)] * 3,
        grid=(rows // step,),
        in_specs=[pl.BlockSpec(memory_space=pltpu.SMEM), full, full, full, half, half],
        out_specs=[full] * 3,
        compiler_params=params_of(16),
        cost_estimate=cost(20 * w.size, 28 * w.size),
        name="adam_all",
    )(scalars, w, m, v, gk, gv)


def frag_kernel(frag_ref, sc_ref, w_ref, m_ref, v_ref, gk_ref, gv_ref, out_ref):
    count = gk_ref.shape[1]
    grad = jnp.where(frag_ref[0] < frag_ref[1], gk_ref[...], gv_ref[...])
    update, _, _ = adam(w_ref[...], m_ref[...], v_ref[...], grad, sc_ref)
    del count
    out_ref[...] = update.astype(out_ref.dtype)


def adam_frag(frag, scalars, w, m, v, gk, gv):
    rows = w.shape[0]
    heads = gk.shape[1] // FRAG_COLS
    block = lambda at: pl.BlockSpec((rows, FRAG_COLS), at)
    due = block(lambda i, f: (0, f[0]))
    return pl.pallas_call(
        frag_kernel,
        out_shape=jax.ShapeDtypeStruct((rows, FRAG_COLS), jnp.bfloat16),
        grid_spec=pltpu.PrefetchScalarGridSpec(
            num_scalar_prefetch=1,
            grid=(1,),
            in_specs=[
                pl.BlockSpec(memory_space=pltpu.SMEM),
                due,
                due,
                due,
                block(lambda i, f: (0, jnp.minimum(f[0], heads - 1))),
                block(lambda i, f: (0, jnp.maximum(f[0] - heads, 0))),
            ],
            out_specs=block(lambda i, f: (0, 0)),
        ),
        compiler_params=params_of(16),
        cost_estimate=cost(20 * rows * FRAG_COLS, 22 * rows * FRAG_COLS),
        name="adam_frag",
    )(frag, scalars, w, m, v, gk, gv)


def columns_kernel(frag_ref, *refs):
    half = len(refs) // 2
    for src, dst in zip(refs[:half], refs[half:]):
        dst[...] = src[...]


def due_columns(frag, *arrays):
    specs = [pl.BlockSpec((a.shape[0], FRAG_COLS), lambda i, f: (0, f[0])) for a in arrays]
    outs = [pl.BlockSpec((a.shape[0], FRAG_COLS), lambda i, f: (0, 0)) for a in arrays]
    return pl.pallas_call(
        columns_kernel,
        out_shape=[jax.ShapeDtypeStruct((a.shape[0], FRAG_COLS), a.dtype) for a in arrays],
        grid_spec=pltpu.PrefetchScalarGridSpec(
            num_scalar_prefetch=1, grid=(1,), in_specs=specs, out_specs=outs
        ),
        compiler_params=params_of(16),
        cost_estimate=cost(0, sum(8 * a.shape[0] * FRAG_COLS for a in arrays)),
        name="due_columns",
    )(frag, *arrays)


def duplicate_kernel(*refs):
    half = (len(refs) - 1) // 2
    copies = [
        pltpu.make_async_copy(refs[i], refs[half + i], refs[-1].at[i]) for i in range(half)
    ]
    for copy in copies:
        copy.start()
    for copy in copies:
        copy.wait()


def duplicate(*arrays):
    return pl.pallas_call(
        duplicate_kernel,
        out_shape=[jax.ShapeDtypeStruct(a.shape, a.dtype) for a in arrays],
        in_specs=[ANY] * len(arrays),
        out_specs=[ANY] * len(arrays),
        scratch_shapes=[pltpu.SemaphoreType.DMA((len(arrays),))],
        cost_estimate=cost(0, sum(8 * a.size for a in arrays)),
        name="duplicate",
    )(*arrays)


def outer_kernel(
    share, frag_ref, w_ref, base_ref, sum_ref, a_ref, p_ref, m_ref, own_ref, w_out, a_out, m_out
):
    fresh = base_ref[...] - share * (1.0 + OUTER_MU) * OUTER_RATE * sum_ref[...].astype(jnp.float32)
    w_out[...] = MIX_LOCAL * w_ref[...] + (1.0 - MIX_LOCAL) * fresh
    pseudo = p_ref[...] + share * own_ref[...]
    new_moment = OUTER_MU * m_ref[...] + pseudo
    m_out[...] = new_moment
    a_out[...] = a_ref[...] - OUTER_RATE * (OUTER_MU * new_moment + pseudo)


def outer_step(frag, weights, base, update_sum, anchor, pseudo, momentum, own_sum, replicas):
    rows, part = weights.shape[0], anchor.shape[0]
    due = lambda count: pl.BlockSpec((count, FRAG_COLS), lambda i, f: (0, f[0]))
    plain = lambda count: pl.BlockSpec((count, FRAG_COLS), lambda i, f: (0, 0))
    return pl.pallas_call(
        functools.partial(outer_kernel, 1.0 / replicas),
        out_shape=[jax.ShapeDtypeStruct(a.shape, a.dtype) for a in (weights, anchor, momentum)],
        grid_spec=pltpu.PrefetchScalarGridSpec(
            num_scalar_prefetch=1,
            grid=(1,),
            in_specs=[due(rows), plain(rows), plain(rows), due(part), plain(part), due(part), plain(part)],
            out_specs=[due(rows), due(part), due(part)],
        ),
        input_output_aliases={1: 0, 4: 1, 6: 2},
        compiler_params=params_of(16),
        cost_estimate=cost(10 * rows * FRAG_COLS, 20 * rows * FRAG_COLS),
        name="outer_step",
    )(frag, weights, base, update_sum, anchor, pseudo, momentum, own_sum)


def exchange(blocks, axis):
    return lax.all_to_all(blocks, axis, split_axis=0, concat_axis=0, tiled=True)


def across(block):
    return lax.ppermute(block, "core", [(0, 1), (1, 0)])


def copies_of(block, count):
    return jnp.broadcast_to(block[None], (count,) + block.shape)


def body(
    tokens,
    cotangent,
    weights,
    first_moment,
    second_moment,
    anchor,
    momentum,
    due_fragment,
    step_count,
):
    inputs, incoming, params = tokens[0], cotangent[0], weights[0]
    tok_rows = inputs.shape[0]
    kv_width = incoming.shape[1] // 2
    rows = params.shape[0]
    part = anchor.shape[0]
    replicas = lax.axis_size("rep")
    chips = lax.axis_size("chip")
    core = lax.axis_index("core")
    core_one = jnp.reshape(core, (1,)).astype(jnp.int32)
    frag = jnp.stack([due_fragment[0], jnp.int32(kv_width // FRAG_COLS)])
    th = tok_rows // 2

    arrived = []
    for h in range(2):
        sent = pack(inputs, h * th, th, rows)
        arrived.append(exchange(sent, BLOCKS))

    key_weights = params[:, :kv_width].astype(jnp.bfloat16)
    flipped, keys = [], []
    for h in range(2):
        x = arrived[h]
        partial_keys = jnp.dot(
            x.reshape(-1, rows), key_weights, preferred_element_type=jnp.float32
        ).astype(jnp.bfloat16)
        partial_keys = partial_keys.reshape(chips, 2, th, kv_width)
        mine = lax.dynamic_index_in_dim(partial_keys, core, 1, keepdims=False)
        theirs = across(lax.dynamic_index_in_dim(partial_keys, 1 - core, 1, keepdims=False))
        summed = (mine.astype(jnp.float32) + theirs.astype(jnp.float32)).astype(jnp.bfloat16)
        parts = exchange(summed, "chip")
        back = key_backward(parts, incoming[h * th:(h + 1) * th, :kv_width])
        same = exchange(back, "chip")
        other = across(same)
        keys.append((same.reshape(-1, kv_width), other.reshape(-1, kv_width)))
        flipped.append(transpose_tokens(x.reshape(chips, 2, th, rows), core_one))

    values = incoming[:, kv_width:].reshape(2, th, kv_width)
    v_same = exchange(copies_of(values, chips), "chip")
    v_other = across(v_same)
    v_same = jnp.swapaxes(v_same, 0, 1).reshape(2, -1, kv_width)
    v_other = jnp.swapaxes(v_other, 0, 1).reshape(2, -1, kv_width)
    grad_values, square = gradient([(flipped[h], v_same[h], v_other[h]) for h in range(2)])
    grad_first = gradient([(flipped[0],) + keys[0]], last=False)[0]
    grad_keys, square = gradient([(flipped[1],) + keys[1]], grad_first, square)

    (old_cols,) = due_columns(frag, params)
    anchor_cols, moment_cols = due_columns(frag, anchor, momentum)
    old_sum = jnp.sum(exchange(old_cols.reshape(replicas, part, FRAG_COLS), "rep"), axis=0)
    pseudo_old = anchor_cols - old_sum / replicas
    base = anchor_cols - OUTER_RATE * (
        OUTER_MU * (OUTER_MU * moment_cols + pseudo_old) + pseudo_old
    )
    base = exchange(copies_of(base, replicas), "rep").reshape(rows, FRAG_COLS)
    anchor_copy, momentum_copy = duplicate(anchor, momentum)

    shards = 2 * chips
    square = jnp.sum(exchange(copies_of(square, shards), BLOCKS))
    factor = jnp.minimum(1.0, CLIP_NORM / (jnp.sqrt(square) + 1e-06))
    steps_now = step_count[0].astype(jnp.float32)
    plan = jnp.minimum(1.0, steps_now / WARMUP) * (
        0.55 + 0.45 * jnp.cos(jnp.pi * steps_now / STEPS_TOTAL)
    )
    rate = PEAK_RATE * plan
    inv_one = 1.0 / (1.0 - jnp.power(BETA_ONE, steps_now))
    inv_two = 1.0 / (1.0 - jnp.power(BETA_TWO, steps_now))
    scalars = jnp.stack([factor, rate, inv_one, inv_two])

    state = (params, first_moment[0], second_moment[0], grad_keys, grad_values)
    update = adam_frag(frag, scalars, *state)
    own_sum = jnp.sum(
        exchange(update.reshape(replicas, part, FRAG_COLS), "rep").astype(jnp.float32), axis=0
    )
    update_sum = exchange(copies_of(own_sum.astype(jnp.bfloat16), replicas), "rep")
    update_sum = update_sum.reshape(rows, FRAG_COLS)
    inner, first_out, second_out = adam_all(scalars, *state)
    weights_out, anchor_out, momentum_out = outer_step(
        frag, inner, base, update_sum, anchor_copy, pseudo_old, momentum_copy, own_sum, replicas
    )
    plan_out = jnp.reshape(plan, (1,))
    return (
        weights_out[None],
        first_out[None],
        second_out[None],
        anchor_out,
        momentum_out,
        plan_out,
    )


def solution(mesh):
    replicas, shards = mesh.shape["rep"], mesh.shape["fsdp"]
    fine = Mesh(mesh.devices.reshape(replicas, shards // 2, 2), ("rep",) + BLOCKS)
    tokens_spec = P("rep", BLOCKS, None)
    outer_spec = P(BLOCKS + ("rep",), None)
    return jax.shard_map(
        body,
        mesh=fine,
        in_specs=(tokens_spec,) * 5 + (outer_spec,) * 2 + (P(), P()),
        out_specs=(tokens_spec,) * 3 + (outer_spec,) * 2 + (P(),),
        check_vma=False,
    )
```

```python
import functools

import jax
import jax.numpy as jnp
from jax import lax
from jax.experimental import pallas as pl
from jax.experimental.pallas import tpu as pltpu
from jax.sharding import PartitionSpec as P

HEAD = 128
WARMUP = 2000
STEPS_TOTAL = 100000
FRAG_COLS = 128


BETA_ONE = 0.9
BETA_TWO = 0.95
ADAM_EPS = 1e-08
DECAY = 0.1
PEAK_RATE = 0.0003
CLIP_NORM = 1.0
OUTER_MU = 0.9
OUTER_RATE = 0.7
MIX_LOCAL = 0.5

MIB = 1 << 20


def in_hbm(*arrays):
    return [pltpu.with_memory_space_constraint(a, pltpu.HBM) for a in arrays]


def params_of(limit):
    return pltpu.CompilerParams(vmem_limit_bytes=limit * MIB)


def cost(flops, moved):
    return pl.CostEstimate(flops=int(flops), bytes_accessed=int(moved), transcendentals=0)


def copy_kernel(src_ref, out_ref):
    out_ref[...] = src_ref[...].reshape(out_ref.shape)


def pack(tokens, first, count, rows):
    shards = tokens.shape[1] // rows
    return pl.pallas_call(
        copy_kernel,
        out_shape=jax.ShapeDtypeStruct((shards, count, rows), tokens.dtype),
        grid=(shards,),
        in_specs=[pl.BlockSpec((count, rows), lambda s: (first // count, s))],
        out_specs=pl.BlockSpec((1, count, rows), lambda s: (s, 0, 0)),
        compiler_params=params_of(8),
        cost_estimate=cost(0, 4 * shards * count * rows),
        name="pack",
    )(*in_hbm(tokens))


def transpose_kernel(me_ref, x_ref, out_ref):
    out_ref[...] = x_ref[0].T


def transpose_tokens(blocks, me):
    shards, count, rows = blocks.shape
    return pl.pallas_call(
        transpose_kernel,
        out_shape=jax.ShapeDtypeStruct((rows, shards * count), blocks.dtype),
        grid_spec=pltpu.PrefetchScalarGridSpec(
            num_scalar_prefetch=1,
            grid=(shards,),
            in_specs=[pl.BlockSpec((1, count, rows), lambda j, me: (me[0] ^ j, 0, 0))],
            out_specs=pl.BlockSpec((rows, count), lambda j, me: (0, j)),
        ),
        compiler_params=params_of(8),
        cost_estimate=cost(0, 4 * blocks.size),
        name="transpose_tokens",
    )(me, blocks)


def partial_kernel(me_ref, x_ref, w_ref, out_ref):
    out_ref[0] = jnp.dot(x_ref[0], w_ref[...], preferred_element_type=jnp.float32).astype(out_ref.dtype)


def partial_keys(blocks, key_weights, me, parity):
    shards, count, rows = blocks.shape
    width = key_weights.shape[1]
    return pl.pallas_call(
        partial_kernel,
        out_shape=jax.ShapeDtypeStruct((shards // 2, count, width), jnp.bfloat16),
        grid_spec=pltpu.PrefetchScalarGridSpec(
            num_scalar_prefetch=1,
            grid=(shards // 2,),
            in_specs=[
                pl.BlockSpec((1, count, rows), lambda m, me: (me[0] ^ (2 * m + parity), 0, 0)),
                pl.BlockSpec((rows, width), lambda m, me: (0, 0)),
            ],
            out_specs=pl.BlockSpec((1, count, width), lambda m, me: (m, 0, 0)),
        ),
        compiler_params=params_of(8),
        cost_estimate=cost(shards * count * rows * width, shards * count * rows),
        name="partial_keys",
    )(me, blocks, key_weights)


def key_kernel(*refs):
    *part_refs, cot_ref, out_ref = refs
    raw = sum(ref[...].astype(jnp.float32) for ref in part_refs)
    for h in range(raw.shape[1] // HEAD):
        cols = slice(h * HEAD, (h + 1) * HEAD)
        head = raw[:, cols]
        inverse = lax.rsqrt(jnp.mean(head * head, axis=1, keepdims=True) + 1e-06)
        normed = head * inverse
        upper = cot_ref[:, cols].astype(jnp.float32)
        back = inverse * (upper - normed * jnp.mean(upper * normed, axis=1, keepdims=True))
        out_ref[:, cols] = back.astype(out_ref.dtype)


def key_backward(parts, incoming):
    shape = parts[0].shape
    return pl.pallas_call(
        key_kernel,
        out_shape=jax.ShapeDtypeStruct(shape, jnp.bfloat16),
        compiler_params=params_of(8),
        cost_estimate=cost(60 * shape[0] * shape[1], 12 * shape[0] * shape[1]),
        name="key_backward",
    )(*parts, incoming)


def grad_kernel(counts, has_base, last, *refs):
    refs = list(refs)
    terms = []
    for count in counts:
        terms.append((refs.pop(0), refs[:count]))
        del refs[:count]
    base = refs.pop(0) if has_base else None
    square_in = refs.pop(0) if last and has_base else None
    out_ref = refs.pop(0)
    sq_ref = refs.pop(0) if last else None
    joined = refs

    @pl.when(pl.program_id(0) == 0)
    def _():
        for (_, blocks), held in zip(terms, joined):
            depth = blocks[0].shape[0]
            for j, block in enumerate(blocks):
                held[j * depth:(j + 1) * depth, :] = block[...]
        if last:
            sq_ref[...] = square_in[...] if has_base else jnp.zeros_like(sq_ref)

    total = base[...] if has_base else None
    for (x_ref, _), held in zip(terms, joined):
        term = jnp.dot(x_ref[...], held[...], preferred_element_type=jnp.float32)
        total = term if total is None else total + term
    out_ref[...] = total
    if last:
        rows, width = total.shape
        squares = (total * total).reshape(rows // 8, 8, width).sum(axis=0)
        folded = squares[:, :HEAD]
        for h in range(1, width // HEAD):
            folded = folded + squares[:, h * HEAD:(h + 1) * HEAD]
        sq_ref[...] += folded


def gradient(terms, base=None, square=None, last=True):
    rows = terms[0][0].shape[0]
    width = terms[0][1][0].shape[1]
    step = 256
    row_block = lambda cols: pl.BlockSpec((step, cols), lambda i: (i, 0))
    whole = lambda a: pl.BlockSpec(a.shape, lambda i: (0, 0))
    args, specs = [], []
    for x, blocks in terms:
        args += [x, *blocks]
        specs += [row_block(x.shape[1])] + [whole(b) for b in blocks]
    if base is not None:
        args.append(base)
        specs.append(row_block(width))
        if last:
            args.append(square)
            specs.append(whole(square))
    if last:
        shapes = [pltpu.HBM((rows, width), jnp.float32), jax.ShapeDtypeStruct((8, HEAD), jnp.float32)]
        outs = [row_block(width), pl.BlockSpec((8, HEAD), lambda i: (0, 0))]
    else:
        shapes = [jax.ShapeDtypeStruct((rows, width), jnp.float32)]
        outs = [row_block(width)]
    depth = sum(x.shape[1] for x, _ in terms)
    return pl.pallas_call(
        functools.partial(grad_kernel, [len(b) for _, b in terms], base is not None, last),
        out_shape=shapes,
        grid=(rows // step,),
        in_specs=specs,
        out_specs=outs,
        scratch_shapes=[pltpu.VMEM((x.shape[1], width), jnp.bfloat16) for x, _ in terms],
        compiler_params=params_of(20),
        cost_estimate=cost(2 * rows * width * depth, 2 * rows * depth + 4 * rows * width),
        name="gradient",
    )(*args)


def adam(old, first, second, grad, scalars):
    factor, rate, inv_one, inv_two = (scalars[i] for i in range(4))
    clipped = grad * factor
    first_new = BETA_ONE * first + (1.0 - BETA_ONE) * clipped
    second_new = BETA_TWO * second + (1.0 - BETA_TWO) * clipped * clipped
    update = rate * (
        first_new * inv_one / (jnp.sqrt(second_new * inv_two) + ADAM_EPS) + DECAY * old
    )
    return update, first_new, second_new


def adam_kernel(sc_ref, w_ref, m_ref, v_ref, gk_ref, gv_ref, w_out, m_out, v_out):
    width = gk_ref.shape[1]
    for g_ref, cols in ((gk_ref, slice(0, width)), (gv_ref, slice(width, 2 * width))):
        old = w_ref[:, cols]
        update, first_new, second_new = adam(old, m_ref[:, cols], v_ref[:, cols], g_ref[...], sc_ref)
        w_out[:, cols] = old - update
        m_out[:, cols] = first_new
        v_out[:, cols] = second_new


def adam_all(scalars, *state):
    rows, width = state[0].shape
    step = 128
    full = pl.BlockSpec((step, width), lambda i: (i, 0))
    half = pl.BlockSpec((step, width // 2), lambda i: (i, 0))
    return pl.pallas_call(
        adam_kernel,
        out_shape=[pltpu.HBM((rows, width), jnp.float32)] * 3,
        grid=(rows // step,),
        in_specs=[pl.BlockSpec(memory_space=pltpu.SMEM), full, full, full, half, half],
        out_specs=[full] * 3,
        compiler_params=params_of(16),
        cost_estimate=cost(20 * rows * width, 28 * rows * width),
        name="adam_all",
    )(scalars, *in_hbm(*state))


def frag_kernel(place_ref, sc_ref, w_ref, m_ref, v_ref, gk_ref, gv_ref, out_ref):
    heads = place_ref[2]
    grad = jnp.where(place_ref[0] < heads, gk_ref[...], gv_ref[...])
    update, _, _ = adam(w_ref[...], m_ref[...], v_ref[...], grad, sc_ref)
    out_ref[0] = update.astype(out_ref.dtype)


def adam_frag(place, scalars, part, *state):
    rows = state[0].shape[0]
    block = lambda at: pl.BlockSpec((part, FRAG_COLS), at)
    due = block(lambda j, p: (p[1] ^ j, p[0]))
    return pl.pallas_call(
        frag_kernel,
        out_shape=jax.ShapeDtypeStruct((rows // part, part, FRAG_COLS), jnp.bfloat16),
        grid_spec=pltpu.PrefetchScalarGridSpec(
            num_scalar_prefetch=1,
            grid=(rows // part,),
            in_specs=[
                pl.BlockSpec(memory_space=pltpu.SMEM),
                due,
                due,
                due,
                block(lambda j, p: (p[1] ^ j, jnp.minimum(p[0], p[2] - 1))),
                block(lambda j, p: (p[1] ^ j, jnp.maximum(p[0] - p[2], 0))),
            ],
            out_specs=pl.BlockSpec((1, part, FRAG_COLS), lambda j, p: (j, 0, 0)),
        ),
        compiler_params=params_of(8),
        cost_estimate=cost(20 * rows * FRAG_COLS, 22 * rows * FRAG_COLS),
        name="adam_frag",
    )(place, scalars, *in_hbm(*state))


def pick_kernel(place_ref, src_ref, out_ref):
    out_ref[...] = src_ref[...].reshape(out_ref.shape)


def due_columns(place, array, part):
    blocks = array.shape[0] // part
    at = (lambda j, p: (p[1] ^ j, p[0])) if blocks > 1 else (lambda j, p: (0, p[0]))
    return pl.pallas_call(
        pick_kernel,
        out_shape=jax.ShapeDtypeStruct((blocks, part, FRAG_COLS), array.dtype),
        grid_spec=pltpu.PrefetchScalarGridSpec(
            num_scalar_prefetch=1,
            grid=(blocks,),
            in_specs=[pl.BlockSpec((part, FRAG_COLS), at)],
            out_specs=pl.BlockSpec((1, part, FRAG_COLS), lambda j, p: (j, 0, 0)),
        ),
        compiler_params=params_of(8),
        cost_estimate=cost(0, 8 * blocks * part * FRAG_COLS),
        name="due_columns",
    )(place, *in_hbm(array))


def duplicate(array):
    rows, width = array.shape
    step = rows // 4 if rows % 32 == 0 else rows
    block = pl.BlockSpec((step, width), lambda i: (i, 0))
    return pl.pallas_call(
        copy_kernel,
        out_shape=pltpu.HBM((rows, width), array.dtype),
        grid=(rows // step,),
        in_specs=[block],
        out_specs=block,
        compiler_params=params_of(8),
        cost_estimate=cost(0, 8 * array.size),
        name="duplicate",
    )(*in_hbm(array))


def outer_kernel(share, place_ref, w_ref, base_ref, sum_ref, a_ref, p_ref, m_ref, own_ref, w_out, a_out, m_out):
    fresh = base_ref[0] - share * (1.0 + OUTER_MU) * OUTER_RATE * sum_ref[0].astype(jnp.float32)
    w_out[...] = MIX_LOCAL * w_ref[...] + (1.0 - MIX_LOCAL) * fresh

    @pl.when(pl.program_id(0) == 0)
    def _():
        pseudo = p_ref[...] + share * own_ref[...]
        new_moment = OUTER_MU * m_ref[...] + pseudo
        m_out[...] = new_moment
        a_out[...] = a_ref[...] - OUTER_RATE * (OUTER_MU * new_moment + pseudo)


def outer_step(place, weights, base, update_sum, anchor, pseudo, momentum, own_sum, replicas):
    part = anchor.shape[0]
    mixed = pl.BlockSpec((part, FRAG_COLS), lambda j, p: (p[1] ^ j, p[0]))
    pieces = pl.BlockSpec((1, part, FRAG_COLS), lambda j, p: (j, 0, 0))
    due = pl.BlockSpec((part, FRAG_COLS), lambda j, p: (0, p[0]))
    plain = pl.BlockSpec((part, FRAG_COLS), lambda j, p: (0, 0))
    return pl.pallas_call(
        functools.partial(outer_kernel, 1.0 / replicas),
        out_shape=[pltpu.HBM(a.shape, a.dtype) for a in (weights, anchor, momentum)],
        grid_spec=pltpu.PrefetchScalarGridSpec(
            num_scalar_prefetch=1,
            grid=(replicas,),
            in_specs=[mixed, pieces, pieces, due, plain, due, plain],
            out_specs=[mixed, due, due],
        ),
        input_output_aliases={1: 0, 4: 1, 6: 2},
        compiler_params=params_of(8),
        cost_estimate=cost(10 * replicas * part * FRAG_COLS, 20 * replicas * part * FRAG_COLS),
        name="outer_step",
    )(
        place, *in_hbm(weights), base, update_sum, *in_hbm(anchor), pseudo, *in_hbm(momentum), own_sum
    )


def swap(block, axis, offset):
    count = lax.axis_size(axis)
    return lax.ppermute(block, axis, [(i, i ^ offset) for i in range(count)])


def gather_pairs(block):
    blocks = [block] + [swap(block, "fsdp", k) for k in range(2, lax.axis_size("fsdp"), 2)]
    out = []
    for held in blocks:
        out += [held, swap(held, "fsdp", 1)]
    return out


def after(value, *others):
    return lax.optimization_barrier((value,) + others)[0]


def body(
    tokens,
    cotangent,
    weights,
    first_moment,
    second_moment,
    anchor,
    momentum,
    due_fragment,
    step_count,
):
    inputs, incoming, params = tokens[0], cotangent[0], weights[0]
    tok_rows = inputs.shape[0]
    kv_width = incoming.shape[1] // 2
    rows = params.shape[0]
    part = anchor.shape[0]
    replicas = lax.axis_size("rep")
    shards = lax.axis_size("fsdp")
    me = jnp.reshape(lax.axis_index("fsdp"), (1,)).astype(jnp.int32)
    place = jnp.stack(
        [due_fragment[0], lax.axis_index("rep").astype(jnp.int32), jnp.int32(kv_width // FRAG_COLS)]
    )
    th = tok_rows // 2

    packed = [pack(inputs, h * th, th, rows) for h in range(2)]
    arrived = [lax.all_to_all(sent, "fsdp", 0, 0, tiled=True) for sent in packed]
    arrived[0] = after(arrived[0], packed[1])

    def rep_sum(pieces):
        total = pieces[0].astype(jnp.float32)
        for k in range(1, replicas):
            total = total + swap(pieces[k], "rep", k).astype(jnp.float32)
        return total

    def rep_pieces(piece):
        return jnp.stack([piece] + [swap(piece, "rep", k) for k in range(1, replicas)])

    old_sum = rep_sum(due_columns(place, params, part))
    anchor_cols = due_columns(place, anchor, part)[0]
    moment_cols = due_columns(place, momentum, part)[0]
    pseudo_old = anchor_cols - old_sum / replicas
    base = rep_pieces(
        anchor_cols - OUTER_RATE * (OUTER_MU * (OUTER_MU * moment_cols + pseudo_old) + pseudo_old)
    )
    anchor_copy, momentum_copy = duplicate(anchor), duplicate(momentum)
    arrived[1] = after(arrived[1], base, anchor_copy, momentum_copy)

    key_weights = params[:, :kv_width].astype(jnp.bfloat16)
    flipped, keys = [], []
    for h in range(2):
        x = arrived[h]
        theirs = swap(partial_keys(x, key_weights, me, 1), "fsdp", 1)
        mine = partial_keys(x, key_weights, me, 0)
        parts = []
        for m in range(shards // 2):
            both = mine[m].astype(jnp.float32) + theirs[m].astype(jnp.float32)
            both = both.astype(jnp.bfloat16)
            parts.append(swap(both, "fsdp", 2 * m) if m else both)
        keys.append(gather_pairs(key_backward(parts, incoming[h * th:(h + 1) * th, :kv_width])))
        flipped.append(transpose_tokens(x, me))

    values = gather_pairs(after(incoming[:, kv_width:], arrived[0]))
    terms = [(flipped[h], [v[h * th:(h + 1) * th] for v in values]) for h in range(2)]
    grad_values, square = gradient(terms)
    grad_first = gradient([(flipped[0], keys[0])], last=False)[0]
    grad_keys, square = gradient([(flipped[1], keys[1])], grad_first, square)

    k = 1
    while k < shards:
        square = square + swap(square, "fsdp", k)
        k *= 2
    square = jnp.sum(square)
    factor = jnp.minimum(1.0, CLIP_NORM / (jnp.sqrt(square) + 1e-06))
    steps_now = step_count[0].astype(jnp.float32)
    plan = jnp.minimum(1.0, steps_now / WARMUP) * (
        0.55 + 0.45 * jnp.cos(jnp.pi * steps_now / STEPS_TOTAL)
    )
    rate = PEAK_RATE * plan
    inv_one = 1.0 / (1.0 - jnp.power(BETA_ONE, steps_now))
    inv_two = 1.0 / (1.0 - jnp.power(BETA_TWO, steps_now))
    scalars = jnp.stack([factor, rate, inv_one, inv_two])

    state = (params, first_moment[0], second_moment[0], grad_keys, grad_values)
    own_sum = rep_sum(adam_frag(place, scalars, part, *state))
    update_sum = rep_pieces(own_sum.astype(jnp.bfloat16))
    inner, first_out, second_out = adam_all(scalars, *state)
    weights_out, anchor_out, momentum_out = outer_step(
        place, inner, base, update_sum, anchor_copy, pseudo_old, momentum_copy, own_sum, replicas
    )
    plan_out = jnp.reshape(plan, (1,))
    return (
        weights_out[None],
        first_out[None],
        second_out[None],
        anchor_out,
        momentum_out,
        plan_out,
    )


def solution(mesh):
    tokens_spec = P("rep", "fsdp", None)
    outer_spec = P(("fsdp", "rep"), None)
    return jax.shard_map(
        body,
        mesh=mesh,
        in_specs=(tokens_spec,) * 5 + (outer_spec,) * 2 + (P(), P()),
        out_specs=(tokens_spec,) * 3 + (outer_spec,) * 2 + (P(),),
        check_vma=False,
    )
```

```python
import functools

import jax
import jax.numpy as jnp
from jax import lax
from jax.experimental import pallas as pl
from jax.experimental.pallas import tpu as pltpu
from jax.sharding import PartitionSpec as P

HEAD = 128
WARMUP = 2000
STEPS_TOTAL = 100000
FRAG_COLS = 128


BETA_ONE = 0.9
BETA_TWO = 0.95
ADAM_EPS = 1e-08
DECAY = 0.1
PEAK_RATE = 0.0003
CLIP_NORM = 1.0
OUTER_MU = 0.9
OUTER_RATE = 0.7
MIX_LOCAL = 0.5

MIB = 1 << 20


def in_hbm(*arrays):
    return [pltpu.with_memory_space_constraint(a, pltpu.HBM) for a in arrays]


def params_of(limit):
    return pltpu.CompilerParams(vmem_limit_bytes=limit * MIB)


def cost(flops, moved):
    return pl.CostEstimate(flops=int(flops), bytes_accessed=int(moved), transcendentals=0)


def copy_kernel(src_ref, out_ref):
    out_ref[...] = src_ref[...].reshape(out_ref.shape)


def pack_kernel(me_ref, src_ref, out_ref):
    out_ref[...] = src_ref[...]


def pack(tokens, me, offset, half, count, rows):
    return pl.pallas_call(
        pack_kernel,
        out_shape=jax.ShapeDtypeStruct((count, rows), tokens.dtype),
        grid_spec=pltpu.PrefetchScalarGridSpec(
            num_scalar_prefetch=1,
            grid=(1,),
            in_specs=[pl.BlockSpec((count, rows), lambda i, me: (half, me[0] ^ offset))],
            out_specs=pl.BlockSpec((count, rows), lambda i, me: (0, 0)),
        ),
        compiler_params=params_of(4),
        cost_estimate=cost(0, 4 * count * rows),
        name="pack",
    )(me, *in_hbm(tokens))


def transpose_kernel(*refs):
    *x_refs, out_ref = refs
    count = x_refs[0].shape[0]
    for j, ref in enumerate(x_refs):
        out_ref[:, j * count:(j + 1) * count] = ref[...].T


def transpose_tokens(blocks):
    count, rows = blocks[0].shape
    step = 256
    return pl.pallas_call(
        transpose_kernel,
        out_shape=jax.ShapeDtypeStruct((rows, len(blocks) * count), blocks[0].dtype),
        grid=(rows // step,),
        in_specs=[pl.BlockSpec((count, step), lambda i: (0, i))] * len(blocks),
        out_specs=pl.BlockSpec((step, len(blocks) * count), lambda i: (i, 0)),
        compiler_params=params_of(8),
        cost_estimate=cost(0, 4 * len(blocks) * count * rows),
        name="transpose_tokens",
    )(*blocks)


def cast_kernel(src_ref, out_ref):
    out_ref[...] = src_ref[...].astype(out_ref.dtype)


def cast_left(array, width):
    rows = array.shape[0]
    block = pl.BlockSpec((256, width), lambda i: (i, 0))
    return pl.pallas_call(
        cast_kernel,
        out_shape=jax.ShapeDtypeStruct((rows, width), jnp.bfloat16),
        grid=(rows // 256,),
        in_specs=[block],
        out_specs=block,
        compiler_params=params_of(8),
        cost_estimate=cost(0, 6 * rows * width),
        name="cast_left",
    )(*in_hbm(array))


def partial_kernel(*refs):
    *x_refs, w_ref, out_ref = refs
    for m, ref in enumerate(x_refs):
        out_ref[m] = jnp.dot(ref[...], w_ref[...], preferred_element_type=jnp.float32).astype(out_ref.dtype)


def partial_keys(blocks, key_weights):
    count, rows = blocks[0].shape
    width = key_weights.shape[1]
    return pl.pallas_call(
        partial_kernel,
        out_shape=jax.ShapeDtypeStruct((len(blocks), count, width), jnp.bfloat16),
        compiler_params=params_of(12),
        cost_estimate=cost(2 * len(blocks) * count * rows * width, 2 * len(blocks) * count * rows),
        name="partial_keys",
    )(*blocks, key_weights)


def summed_kernel(*refs):
    half = (len(refs) - 2) // 2
    x_refs, (w_ref, add_ref), out_refs = refs[:half], refs[half:half + 2], refs[half + 2:]
    for m, ref in enumerate(x_refs):
        total = jnp.dot(ref[...], w_ref[...], preferred_element_type=jnp.float32)
        out_refs[m][...] = (total + add_ref[m].astype(jnp.float32)).astype(out_refs[m].dtype)


def summed_keys(blocks, key_weights, others):
    count, rows = blocks[0].shape
    width = key_weights.shape[1]
    return pl.pallas_call(
        summed_kernel,
        out_shape=[jax.ShapeDtypeStruct((count, width), jnp.bfloat16)] * len(blocks),
        compiler_params=params_of(12),
        cost_estimate=cost(2 * len(blocks) * count * rows * width, 2 * len(blocks) * count * rows),
        name="summed_keys",
    )(*blocks, key_weights, others)


def key_kernel(*refs):
    *part_refs, cot_ref, out_ref = refs
    raw = sum(ref[...].astype(jnp.float32) for ref in part_refs)
    for h in range(raw.shape[1] // HEAD):
        cols = slice(h * HEAD, (h + 1) * HEAD)
        head = raw[:, cols]
        inverse = lax.rsqrt(jnp.mean(head * head, axis=1, keepdims=True) + 1e-06)
        normed = head * inverse
        upper = cot_ref[:, cols].astype(jnp.float32)
        back = inverse * (upper - normed * jnp.mean(upper * normed, axis=1, keepdims=True))
        out_ref[:, cols] = back.astype(out_ref.dtype)


def key_backward(parts, incoming, half):
    block = pl.BlockSpec(parts[0].shape, lambda i: (0, 0))
    cot = pl.BlockSpec(parts[0].shape, lambda i: (half, 0))
    size = parts[0].size
    return pl.pallas_call(
        key_kernel,
        out_shape=jax.ShapeDtypeStruct(parts[0].shape, jnp.bfloat16),
        grid=(1,),
        in_specs=[block] * len(parts) + [cot],
        out_specs=block,
        compiler_params=params_of(8),
        cost_estimate=cost(60 * size, 12 * size),
        name="key_backward",
    )(*parts, incoming)


def grad_kernel(counts, has_base, last, *refs):
    refs = list(refs)
    place_ref = refs.pop(0)
    terms = []
    for count in counts:
        terms.append((refs.pop(0), refs[:count]))
        del refs[:count]
    base = refs.pop(0) if has_base else None
    square_in, due_in = (refs.pop(0), refs.pop(0)) if last and has_base else (None, None)
    out_ref = refs.pop(0)
    sq_ref, due_ref = (refs.pop(0), refs.pop(0)) if last else (None, None)
    joined = refs

    @pl.when(pl.program_id(0) == 0)
    def _():
        for (_, blocks), held in zip(terms, joined):
            depth = blocks[0].shape[0]
            for j, block in enumerate(blocks):
                held[j * depth:(j + 1) * depth, :] = block[...]
        if last:
            sq_ref[...] = square_in[...] if has_base else jnp.zeros_like(sq_ref)

    total = base[...] if has_base else None
    for (x_ref, _), held in zip(terms, joined):
        term = jnp.dot(x_ref[...], held[...], preferred_element_type=jnp.float32)
        total = term if total is None else total + term
    out_ref[...] = total
    if last:
        rows, width = total.shape
        squares = (total * total).reshape(rows // 8, 8, width).sum(axis=0)
        folded = squares[:, :HEAD]
        for h in range(1, width // HEAD):
            folded = folded + squares[:, h * HEAD:(h + 1) * HEAD]
        sq_ref[...] += folded
        heads = width // FRAG_COLS
        mine = place_ref[0] - (0 if has_base else heads)
        mine = jnp.minimum(jnp.maximum(mine, 0), heads - 1) * FRAG_COLS
        column = out_ref[:, pl.ds(pl.multiple_of(mine, FRAG_COLS), FRAG_COLS)]
        if has_base:
            column = jnp.where(place_ref[0] < heads, column, due_in[...])
        due_ref[...] = column


def gradient(place, terms, base=None, square=None, due=None, last=True):
    rows = terms[0][0].shape[0]
    width = terms[0][1][0].shape[1]
    step = 256
    row_block = lambda cols: pl.BlockSpec((step, cols), lambda i, p: (i, 0))
    fixed = pl.BlockSpec((8, HEAD), lambda i, p: (0, 0))
    args, specs, scratch = [], [], []
    for x, blocks, at in terms:
        args += [x, *blocks]
        depth = x.shape[1] // len(blocks)
        specs += [row_block(x.shape[1])]
        specs += [pl.BlockSpec((depth, width), lambda i, p, at=at: (at, 0))] * len(blocks)
        scratch.append(pltpu.VMEM((x.shape[1], width), jnp.bfloat16))
    if base is not None:
        args.append(base)
        specs.append(row_block(width))
        if last:
            args += [square, due]
            specs += [fixed, row_block(FRAG_COLS)]
    if last:
        shapes = [
            pltpu.HBM((rows, width), jnp.float32),
            jax.ShapeDtypeStruct((8, HEAD), jnp.float32),
            jax.ShapeDtypeStruct((rows, FRAG_COLS), jnp.float32),
        ]
        outs = [row_block(width), fixed, row_block(FRAG_COLS)]
    else:
        shapes = [jax.ShapeDtypeStruct((rows, width), jnp.float32)]
        outs = [row_block(width)]
    depth = sum(x.shape[1] for x, _, _ in terms)
    return pl.pallas_call(
        functools.partial(grad_kernel, [len(b) for _, b, _ in terms], base is not None, last),
        out_shape=shapes,
        grid_spec=pltpu.PrefetchScalarGridSpec(
            num_scalar_prefetch=1,
            grid=(rows // step,),
            in_specs=specs,
            out_specs=outs,
            scratch_shapes=scratch,
        ),
        compiler_params=params_of(20),
        cost_estimate=cost(2 * rows * width * depth, 2 * rows * depth + 4 * rows * width),
        name="gradient",
    )(place, *args)


def adam(old, first, second, grad, scalars):
    factor, rate, inv_one, inv_two = (scalars[i] for i in range(4))
    clipped = grad * factor
    first_new = BETA_ONE * first + (1.0 - BETA_ONE) * clipped
    second_new = BETA_TWO * second + (1.0 - BETA_TWO) * clipped * clipped
    update = rate * (
        first_new * inv_one / (jnp.sqrt(second_new * inv_two) + ADAM_EPS) + DECAY * old
    )
    return update, first_new, second_new


def adam_kernel(extra, sc_ref, w_ref, m_ref, v_ref, gk_ref, gv_ref, *refs):
    w_out, m_out, v_out, *done = refs[extra:]
    width = gk_ref.shape[1]
    for g_ref, cols in ((gk_ref, slice(0, width)), (gv_ref, slice(width, 2 * width))):
        old = w_ref[:, cols]
        update, first_new, second_new = adam(old, m_ref[:, cols], v_ref[:, cols], g_ref[...], sc_ref)
        w_out[:, cols] = old - update
        m_out[:, cols] = first_new
        v_out[:, cols] = second_new
    for ref in done:
        ref[...] = jnp.zeros_like(ref)


def adam_rows(scalars, state, first, last, into=()):
    rows, width = state[0].shape
    step = 256
    full = pl.BlockSpec((step, width), lambda i: (i + first, 0))
    half = pl.BlockSpec((step, width // 2), lambda i: (i + first, 0))
    shapes = [pltpu.HBM((rows, width), jnp.float32)] * 3
    outs = [full] * 3
    if not into:
        shapes.append(jax.ShapeDtypeStruct((8, HEAD), jnp.float32))
        outs.append(pl.BlockSpec((8, HEAD), lambda i: (0, 0)))
    count = (last - first) * step
    return pl.pallas_call(
        functools.partial(adam_kernel, len(into)),
        out_shape=shapes,
        grid=(last - first,),
        in_specs=[pl.BlockSpec(memory_space=pltpu.SMEM), full, full, full, half, half]
        + [pl.BlockSpec(memory_space=pl.ANY)] * len(into),
        out_specs=outs,
        input_output_aliases={6 + i: i for i in range(len(into))},
        compiler_params=params_of(24),
        cost_estimate=cost(20 * count * width, 28 * count * width),
        name="adam_rows",
    )(scalars, *in_hbm(*state), *in_hbm(*into))


def frag_kernel(place_ref, sc_ref, w_ref, m_ref, v_ref, g_ref, inner_ref, *out_refs):
    blocks, part, _ = w_ref.shape
    for j in range(blocks):
        at = pl.multiple_of((place_ref[1] ^ j) * part, 8)
        old = w_ref[j]
        update, _, _ = adam(old, m_ref[j], v_ref[j], g_ref[pl.ds(at, part), :], sc_ref)
        inner_ref[j] = old - update
        out_refs[j][...] = update.astype(out_refs[j].dtype)


def adam_frag(place, scalars, old, first, second, grad):
    blocks, part, width = old.shape
    smem = pl.BlockSpec(memory_space=pltpu.SMEM)
    vmem = pl.BlockSpec(memory_space=pltpu.VMEM)
    return pl.pallas_call(
        frag_kernel,
        out_shape=[jax.ShapeDtypeStruct(old.shape, jnp.float32)]
        + [jax.ShapeDtypeStruct((part, width), jnp.bfloat16)] * blocks,
        in_specs=[smem, smem] + [vmem] * 4,
        out_specs=[vmem] * (1 + blocks),
        compiler_params=params_of(12),
        cost_estimate=cost(20 * old.size, 22 * old.size),
        name="adam_frag",
    )(place, scalars, old, first, second, grad)


def pick_kernel(place_ref, *refs):
    half = len(refs) // 2
    for src_ref, out_ref in zip(refs[:half], refs[half:]):
        out_ref[...] = src_ref[...].reshape(out_ref.shape)


def due_columns(place, part, *arrays):
    blocks = arrays[0].shape[0] // part
    at = (lambda j, p: (p[1] ^ j, p[0])) if blocks > 1 else (lambda j, p: (0, p[0]))
    return pl.pallas_call(
        pick_kernel,
        out_shape=[jax.ShapeDtypeStruct((blocks, part, FRAG_COLS), a.dtype) for a in arrays],
        grid_spec=pltpu.PrefetchScalarGridSpec(
            num_scalar_prefetch=1,
            grid=(blocks,),
            in_specs=[pl.BlockSpec((part, FRAG_COLS), at)] * len(arrays),
            out_specs=[pl.BlockSpec((1, part, FRAG_COLS), lambda j, p: (j, 0, 0))] * len(arrays),
        ),
        compiler_params=params_of(8),
        cost_estimate=cost(0, 8 * blocks * part * FRAG_COLS * len(arrays)),
        name="due_columns",
    )(place, *in_hbm(*arrays))


def duplicate(array):
    rows, width = array.shape
    step = rows // 4 if rows % 32 == 0 else rows
    block = pl.BlockSpec((step, width), lambda i: (i, 0))
    return pl.pallas_call(
        copy_kernel,
        out_shape=pltpu.HBM((rows, width), array.dtype),
        grid=(rows // step,),
        in_specs=[block],
        out_specs=block,
        compiler_params=params_of(8),
        cost_estimate=cost(0, 8 * array.size),
        name="duplicate",
    )(*in_hbm(array))


def outer_kernel(replicas, place_ref, *refs):
    share = 1.0 / replicas
    base_refs, sum_refs = refs[3:3 + replicas], refs[3 + replicas:3 + 2 * replicas]
    inner_ref, a_ref, p_ref, m_ref, own_ref, w_out, a_out, m_out = refs[3 + 2 * replicas:]
    scale = share * (1.0 + OUTER_MU) * OUTER_RATE
    for j in range(replicas):

        @pl.when(pl.program_id(0) == j)
        def _():
            fresh = base_refs[j][...] - scale * sum_refs[j][...].astype(jnp.float32)
            w_out[...] = MIX_LOCAL * inner_ref[0] + (1.0 - MIX_LOCAL) * fresh

    @pl.when(pl.program_id(0) == 0)
    def _():
        pseudo = p_ref[...] + share * own_ref[...]
        new_moment = OUTER_MU * m_ref[...] + pseudo
        m_out[...] = new_moment
        a_out[...] = a_ref[...] - OUTER_RATE * (OUTER_MU * new_moment + pseudo)


def outer_step(place, outputs, base, sums, inner, anchor, pseudo, momentum, own_sum):
    replicas, part = inner.shape[0], inner.shape[1]
    mixed = pl.BlockSpec((part, FRAG_COLS), lambda j, p: (p[1] ^ j, p[0]))
    pieces = pl.BlockSpec((1, part, FRAG_COLS), lambda j, p: (j, 0, 0))
    due = pl.BlockSpec((part, FRAG_COLS), lambda j, p: (0, p[0]))
    plain = pl.BlockSpec((part, FRAG_COLS), lambda j, p: (0, 0))
    whole = pl.BlockSpec(memory_space=pl.ANY)
    return pl.pallas_call(
        functools.partial(outer_kernel, replicas),
        out_shape=[pltpu.HBM(a.shape, a.dtype) for a in outputs],
        grid_spec=pltpu.PrefetchScalarGridSpec(
            num_scalar_prefetch=1,
            grid=(replicas,),
            in_specs=[whole] * 3 + [plain] * (2 * replicas) + [pieces] + [plain] * 4,
            out_specs=[mixed, due, due],
        ),
        input_output_aliases={1: 0, 2: 1, 3: 2},
        compiler_params=params_of(12),
        cost_estimate=cost(10 * replicas * part * FRAG_COLS, 20 * replicas * part * FRAG_COLS),
        name="outer_step",
    )(place, *in_hbm(*outputs), *base, *sums, inner, anchor, pseudo, momentum, own_sum)


def swap(block, axis, offset):
    count = lax.axis_size(axis)
    return lax.ppermute(block, axis, [(i, i ^ offset) for i in range(count)])


def after(value, *others):
    return lax.optimization_barrier((value,) + others)[0]


class Line:
    def __init__(self, axis, window):
        self.axis, self.window, self.ended = axis, window, []

    def swap(self, block, offset):
        if len(self.ended) >= self.window:
            block = after(block, self.ended[-self.window])
        self.ended.append(swap(block, self.axis, offset))
        return self.ended[-1]


def body(
    tokens,
    cotangent,
    weights,
    first_moment,
    second_moment,
    anchor,
    momentum,
    due_fragment,
    step_count,
):
    inputs, incoming, params = tokens[0], cotangent[0], weights[0]
    tok_rows = inputs.shape[0]
    kv_width = incoming.shape[1] // 2
    rows = params.shape[0]
    part = anchor.shape[0]
    replicas = lax.axis_size("rep")
    shards = lax.axis_size("fsdp")
    me = jnp.reshape(lax.axis_index("fsdp"), (1,)).astype(jnp.int32)
    place = jnp.stack([due_fragment[0], lax.axis_index("rep").astype(jnp.int32)])
    th = tok_rows // 2
    chips = range(2, shards, 2)
    order = sorted(range(2, shards), key=lambda k: (-bin(k >> 1).count("1"), k & 1, k)) + [1]

    line = Line("fsdp", 3)
    blocks = [[None] * shards, [None] * shards]

    def send_tokens(half, offsets):
        for k in offsets:
            blocks[half][k] = line.swap(pack(inputs, me, k, half, th, rows), k)

    send_tokens(0, order)
    early = blocks[0][order[0]]

    rep_line = Line("rep", 1)
    place_early = after(place, early)
    old, old_first, old_second = due_columns(place_early, part, params, first_moment[0], second_moment[0])
    anchor_cols, moment_cols = (c[0] for c in due_columns(place_early, part, anchor, momentum))
    old_sum = old[0]
    for k in range(1, replicas):
        old_sum = old_sum + rep_line.swap(old[k], k)
    pseudo_old = anchor_cols - old_sum / replicas
    base = anchor_cols - OUTER_RATE * (OUTER_MU * (OUTER_MU * moment_cols + pseudo_old) + pseudo_old)
    base = [base] + [rep_line.swap(base, k) for k in range(1, replicas)]
    anchor_copy, momentum_copy = duplicate(anchor), duplicate(momentum)

    key_weights = cast_left(after(params, early), kv_width)

    def sum_keys(half):
        x = blocks[half]
        x[0] = pack(inputs, me, 0, half, th, rows)
        theirs = swap(partial_keys(x[1::2], key_weights), "fsdp", 1)
        return summed_keys(x[0::2], key_weights, theirs)

    def scatter_keys(half, parts):
        parts = [parts[0]] + [line.swap(parts[k // 2], k) for k in chips]
        return key_backward(parts, incoming, half)

    def gather(block):
        out = []
        for held in [block] + [line.swap(block, k) for k in chips]:
            out += [held, swap(held, "fsdp", 1)]
        return out

    cut = (len(order) + 1) // 2
    send_tokens(1, order[:cut])
    back = scatter_keys(0, sum_keys(0))
    send_tokens(1, order[cut:])
    keys = [gather(back)]
    flipped = [transpose_tokens(blocks[0])]
    values = gather(incoming[:, kv_width:])
    (grad_first,) = gradient(place, [(flipped[0], keys[0], 0)], last=False)
    blocks[1][1] = after(blocks[1][1], base[-1], anchor_copy, momentum_copy, grad_first, old_second)
    back = scatter_keys(1, sum_keys(1))
    keys.append(gather(back))
    flipped.append(transpose_tokens(blocks[1]))
    grad_values, square, due = gradient(place, [(flipped[h], values, h) for h in range(2)])
    grad_keys, square, due = gradient(place, [(flipped[1], keys[1], 0)], grad_first, square, due)

    square = square + swap(square, "fsdp", 1)
    square = sum([swap(square, "fsdp", k) for k in chips], square)
    square = jnp.sum(square)
    factor = jnp.minimum(1.0, CLIP_NORM / (jnp.sqrt(square) + 1e-06))
    steps_now = step_count[0].astype(jnp.float32)
    plan = jnp.minimum(1.0, steps_now / WARMUP) * (
        0.55 + 0.45 * jnp.cos(jnp.pi * steps_now / STEPS_TOTAL)
    )
    rate = PEAK_RATE * plan
    inv_one = 1.0 / (1.0 - jnp.power(BETA_ONE, steps_now))
    inv_two = 1.0 / (1.0 - jnp.power(BETA_TWO, steps_now))
    scalars = jnp.stack([factor, rate, inv_one, inv_two])

    state = (params, first_moment[0], second_moment[0], grad_keys, grad_values)
    inner, *update = adam_frag(place, scalars, old, old_first, old_second, due)
    steps = rows // 256
    *results, ticket = adam_rows(scalars, state, 0, steps // 2)
    own_sum = update[0].astype(jnp.float32)
    for k in range(1, replicas):
        own_sum = own_sum + swap(update[k], "rep", k).astype(jnp.float32)
    own_sum = after(own_sum, ticket)
    sums = [own_sum.astype(jnp.bfloat16)]
    sums += [swap(sums[0], "rep", k) for k in range(1, replicas)]
    results = adam_rows(scalars, state, steps // 2, steps, results)
    weights_out, anchor_out, momentum_out = outer_step(
        place,
        (results[0], anchor_copy, momentum_copy),
        base,
        sums,
        inner,
        anchor_cols,
        pseudo_old,
        moment_cols,
        own_sum,
    )
    plan_out = jnp.reshape(plan, (1,))
    return (
        weights_out[None],
        results[1][None],
        results[2][None],
        anchor_out,
        momentum_out,
        plan_out,
    )


def solution(mesh):
    tokens_spec = P("rep", "fsdp", None)
    outer_spec = P(("fsdp", "rep"), None)
    return jax.shard_map(
        body,
        mesh=mesh,
        in_specs=(tokens_spec,) * 5 + (outer_spec,) * 2 + (P(), P()),
        out_specs=(tokens_spec,) * 3 + (outer_spec,) * 2 + (P(),),
        check_vma=False,
    )
```

```python
import functools

import jax
import jax.numpy as jnp
from jax import lax
from jax.experimental import pallas as pl
from jax.experimental.pallas import tpu as pltpu
from jax.sharding import PartitionSpec as P

HEAD = 128
WARMUP = 2000
STEPS_TOTAL = 100000
FRAG_COLS = 128


BETA_ONE = 0.9
BETA_TWO = 0.95
ADAM_EPS = 1e-08
DECAY = 0.1
PEAK_RATE = 0.0003
CLIP_NORM = 1.0
OUTER_MU = 0.9
OUTER_RATE = 0.7
MIX_LOCAL = 0.5

MIB = 1 << 20


def in_hbm(*arrays):
    return [pltpu.with_memory_space_constraint(a, pltpu.HBM) for a in arrays]


def params_of(limit):
    return pltpu.CompilerParams(vmem_limit_bytes=limit * MIB)


def cost(flops, moved):
    return pl.CostEstimate(flops=int(flops), bytes_accessed=int(moved), transcendentals=0)


def copy_kernel(src_ref, out_ref):
    out_ref[...] = src_ref[...].reshape(out_ref.shape)


def pack_kernel(me_ref, src_ref, out_ref):
    out_ref[...] = src_ref[...]


def pack(tokens, me, offset, rows):
    count = tokens.shape[0]
    return pl.pallas_call(
        pack_kernel,
        out_shape=jax.ShapeDtypeStruct((count, rows), tokens.dtype),
        grid_spec=pltpu.PrefetchScalarGridSpec(
            num_scalar_prefetch=1,
            grid=(1,),
            in_specs=[pl.BlockSpec((count, rows), lambda i, me: (0, me[0] ^ offset))],
            out_specs=pl.BlockSpec((count, rows), lambda i, me: (0, 0)),
        ),
        compiler_params=params_of(4),
        cost_estimate=cost(0, 4 * count * rows),
        name="pack",
    )(me, *in_hbm(tokens))


def transpose_kernel(*refs):
    *x_refs, out_ref = refs
    count = x_refs[0].shape[0]
    for j, ref in enumerate(x_refs):
        out_ref[:, j * count:(j + 1) * count] = ref[...].T


def transpose_tokens(blocks):
    count, rows = blocks[0].shape
    step = 256
    return pl.pallas_call(
        transpose_kernel,
        out_shape=jax.ShapeDtypeStruct((rows, len(blocks) * count), blocks[0].dtype),
        grid=(rows // step,),
        in_specs=[pl.BlockSpec((count, step), lambda i: (0, i))] * len(blocks),
        out_specs=pl.BlockSpec((step, len(blocks) * count), lambda i: (i, 0)),
        compiler_params=params_of(8),
        cost_estimate=cost(0, 4 * len(blocks) * count * rows),
        name="transpose_tokens",
    )(*blocks)


def cast_kernel(src_ref, out_ref):
    out_ref[...] = src_ref[...].astype(out_ref.dtype)


def cast_left(array, width):
    rows = array.shape[0]
    block = pl.BlockSpec((256, width), lambda i: (i, 0))
    return pl.pallas_call(
        cast_kernel,
        out_shape=jax.ShapeDtypeStruct((rows, width), jnp.bfloat16),
        grid=(rows // 256,),
        in_specs=[block],
        out_specs=block,
        compiler_params=params_of(8),
        cost_estimate=cost(0, 6 * rows * width),
        name="cast_left",
    )(*in_hbm(array))


def partial_kernel(x_ref, w_ref, *refs):
    *add_refs, out_ref = refs
    total = jnp.dot(x_ref[...], w_ref[...], preferred_element_type=jnp.float32)
    for ref in add_refs:
        total = total + ref[...].astype(jnp.float32)
    out_ref[...] = total.astype(out_ref.dtype)


def partial_keys(block, key_weights, *others):
    count, rows = block.shape
    width = key_weights.shape[1]
    return pl.pallas_call(
        partial_kernel,
        out_shape=jax.ShapeDtypeStruct((count, width), jnp.bfloat16),
        compiler_params=params_of(8),
        cost_estimate=cost(2 * count * rows * width, 2 * count * rows),
        name="partial_keys",
    )(block, key_weights, *others)


def key_kernel(*refs):
    *part_refs, cot_ref, out_ref = refs
    raw = sum(ref[...].astype(jnp.float32) for ref in part_refs)
    for h in range(raw.shape[1] // HEAD):
        cols = slice(h * HEAD, (h + 1) * HEAD)
        head = raw[:, cols]
        inverse = lax.rsqrt(jnp.mean(head * head, axis=1, keepdims=True) + 1e-06)
        normed = head * inverse
        upper = cot_ref[:, cols].astype(jnp.float32)
        back = inverse * (upper - normed * jnp.mean(upper * normed, axis=1, keepdims=True))
        out_ref[:, cols] = back.astype(out_ref.dtype)


def key_backward(parts, incoming):
    block = pl.BlockSpec(parts[0].shape, lambda i: (0, 0))
    cot = pl.BlockSpec(parts[0].shape, lambda i: (0, 0))
    size = parts[0].size
    return pl.pallas_call(
        key_kernel,
        out_shape=jax.ShapeDtypeStruct(parts[0].shape, jnp.bfloat16),
        grid=(1,),
        in_specs=[block] * len(parts) + [cot],
        out_specs=block,
        compiler_params=params_of(8),
        cost_estimate=cost(60 * size, 12 * size),
        name="key_backward",
    )(*parts, incoming)


def grad_kernel(counts, has_base, last, *refs):
    refs = list(refs)
    place_ref = refs.pop(0)
    terms = []
    for count in counts:
        terms.append((refs.pop(0), refs[:count]))
        del refs[:count]
    base = refs.pop(0) if has_base else None
    square_in, due_in = (refs.pop(0), refs.pop(0)) if last and has_base else (None, None)
    out_ref = refs.pop(0)
    sq_ref, due_ref = (refs.pop(0), refs.pop(0)) if last else (None, None)
    joined = refs

    @pl.when(pl.program_id(0) == 0)
    def _():
        for (_, blocks), held in zip(terms, joined):
            depth = blocks[0].shape[0]
            for j, block in enumerate(blocks):
                held[j * depth:(j + 1) * depth, :] = block[...]
        if last:
            sq_ref[...] = square_in[...] if has_base else jnp.zeros_like(sq_ref)

    total = base[...] if has_base else None
    for (x_ref, _), held in zip(terms, joined):
        term = jnp.dot(x_ref[...], held[...], preferred_element_type=jnp.float32)
        total = term if total is None else total + term
    out_ref[...] = total
    if last:
        rows, width = total.shape
        squares = (total * total).reshape(rows // 8, 8, width).sum(axis=0)
        folded = squares[:, :HEAD]
        for h in range(1, width // HEAD):
            folded = folded + squares[:, h * HEAD:(h + 1) * HEAD]
        sq_ref[...] += folded
        heads = width // FRAG_COLS
        mine = place_ref[0] - (0 if has_base else heads)
        mine = jnp.minimum(jnp.maximum(mine, 0), heads - 1) * FRAG_COLS
        column = out_ref[:, pl.ds(pl.multiple_of(mine, FRAG_COLS), FRAG_COLS)]
        if has_base:
            column = jnp.where(place_ref[0] < heads, column, due_in[...])
        due_ref[...] = column


def gradient(place, terms, base=None, square=None, due=None, last=True):
    rows = terms[0][0].shape[0]
    width = terms[0][1][0].shape[1]
    step = 256
    row_block = lambda cols: pl.BlockSpec((step, cols), lambda i, p: (i, 0))
    fixed = pl.BlockSpec((8, HEAD), lambda i, p: (0, 0))
    args, specs, scratch = [], [], []
    for x, blocks in terms:
        args += [x, *blocks]
        specs += [row_block(x.shape[1])]
        specs += [pl.BlockSpec(b.shape, lambda i, p: (0, 0)) for b in blocks]
        scratch.append(pltpu.VMEM((x.shape[1], width), jnp.bfloat16))
    if base is not None:
        args.append(base)
        specs.append(row_block(width))
        if last:
            args += [square, due]
            specs += [fixed, row_block(FRAG_COLS)]
    if last:
        shapes = [
            pltpu.HBM((rows, width), jnp.float32),
            jax.ShapeDtypeStruct((8, HEAD), jnp.float32),
            jax.ShapeDtypeStruct((rows, FRAG_COLS), jnp.float32),
        ]
        outs = [row_block(width), fixed, row_block(FRAG_COLS)]
    else:
        shapes = [jax.ShapeDtypeStruct((rows, width), jnp.float32)]
        outs = [row_block(width)]
    depth = sum(x.shape[1] for x, _ in terms)
    return pl.pallas_call(
        functools.partial(grad_kernel, [len(b) for _, b in terms], base is not None, last),
        out_shape=shapes,
        grid_spec=pltpu.PrefetchScalarGridSpec(
            num_scalar_prefetch=1,
            grid=(rows // step,),
            in_specs=specs,
            out_specs=outs,
            scratch_shapes=scratch,
        ),
        compiler_params=params_of(20),
        cost_estimate=cost(2 * rows * width * depth, 2 * rows * depth + 4 * rows * width),
        name="gradient",
    )(place, *args)


def clip_factor(square_refs):
    square = jnp.sum(sum(ref[...] for ref in square_refs), keepdims=True)
    return jnp.minimum(1.0, CLIP_NORM / (jnp.sqrt(square) + 1e-06))


def adam(old, first, second, grad, factor, scalars):
    rate, inv_one, inv_two = (scalars[i] for i in range(3))
    clipped = grad * factor
    first_new = BETA_ONE * first + (1.0 - BETA_ONE) * clipped
    second_new = BETA_TWO * second + (1.0 - BETA_TWO) * clipped * clipped
    update = rate * (
        first_new * inv_one / (jnp.sqrt(second_new * inv_two) + ADAM_EPS) + DECAY * old
    )
    return update, first_new, second_new


def adam_kernel(squares, extra, sc_ref, w_ref, m_ref, v_ref, gk_ref, gv_ref, *refs):
    factor = clip_factor(refs[:squares])
    w_out, m_out, v_out, *done = refs[squares + extra:]
    width = gk_ref.shape[1]
    for g_ref, cols in ((gk_ref, slice(0, width)), (gv_ref, slice(width, 2 * width))):
        old = w_ref[:, cols]
        update, first_new, second_new = adam(
            old, m_ref[:, cols], v_ref[:, cols], g_ref[...], factor, sc_ref
        )
        w_out[:, cols] = old - update
        m_out[:, cols] = first_new
        v_out[:, cols] = second_new
    for ref in done:
        ref[...] = jnp.zeros_like(ref)


def adam_rows(scalars, squares, state, first, last, into=()):
    rows, width = state[0].shape
    step = 256
    full = pl.BlockSpec((step, width), lambda i: (i + first, 0))
    half = pl.BlockSpec((step, width // 2), lambda i: (i + first, 0))
    shapes = [pltpu.HBM((rows, width), jnp.float32)] * 3
    outs = [full] * 3
    if not into:
        shapes.append(jax.ShapeDtypeStruct((8, HEAD), jnp.float32))
        outs.append(pl.BlockSpec((8, HEAD), lambda i: (0, 0)))
    count = (last - first) * step
    return pl.pallas_call(
        functools.partial(adam_kernel, len(squares), len(into)),
        out_shape=shapes,
        grid=(last - first,),
        in_specs=[pl.BlockSpec(memory_space=pltpu.SMEM), full, full, full, half, half]
        + [pl.BlockSpec((8, HEAD), lambda i: (0, 0))] * len(squares)
        + [pl.BlockSpec(memory_space=pl.ANY)] * len(into),
        out_specs=outs,
        input_output_aliases={6 + len(squares) + i: i for i in range(len(into))},
        compiler_params=params_of(24),
        cost_estimate=cost(20 * count * width, 28 * count * width),
        name="adam_rows",
    )(scalars, *in_hbm(*state), *squares, *in_hbm(*into))


def frag_kernel(squares, place_ref, sc_ref, w_ref, m_ref, v_ref, g_ref, *refs):
    blocks, part, _ = w_ref.shape
    factor = clip_factor(refs[:squares])
    inner_ref, *out_refs = refs[squares:]
    for j in range(blocks):
        at = pl.multiple_of((place_ref[1] ^ j) * part, 8)
        old = w_ref[j]
        update, _, _ = adam(old, m_ref[j], v_ref[j], g_ref[pl.ds(at, part), :], factor, sc_ref)
        inner_ref[j] = old - update
        out_refs[j][...] = update.astype(out_refs[j].dtype)


def adam_frag(place, scalars, squares, old, first, second, grad):
    blocks, part, width = old.shape
    smem = pl.BlockSpec(memory_space=pltpu.SMEM)
    vmem = pl.BlockSpec(memory_space=pltpu.VMEM)
    return pl.pallas_call(
        functools.partial(frag_kernel, len(squares)),
        out_shape=[jax.ShapeDtypeStruct(old.shape, jnp.float32)]
        + [jax.ShapeDtypeStruct((part, width), jnp.bfloat16)] * blocks,
        in_specs=[smem, smem] + [vmem] * (4 + len(squares)),
        out_specs=[vmem] * (1 + blocks),
        compiler_params=params_of(12),
        cost_estimate=cost(20 * old.size, 22 * old.size),
        name="adam_frag",
    )(place, scalars, old, first, second, grad, *squares)


def pick_kernel(place_ref, *refs):
    half = len(refs) // 2
    for src_ref, out_ref in zip(refs[:half], refs[half:]):
        out_ref[...] = src_ref[...].reshape(out_ref.shape)


def due_columns(place, part, *arrays):
    blocks = arrays[0].shape[0] // part
    at = (lambda j, p: (p[1] ^ j, p[0])) if blocks > 1 else (lambda j, p: (0, p[0]))
    return pl.pallas_call(
        pick_kernel,
        out_shape=[jax.ShapeDtypeStruct((blocks, part, FRAG_COLS), a.dtype) for a in arrays],
        grid_spec=pltpu.PrefetchScalarGridSpec(
            num_scalar_prefetch=1,
            grid=(blocks,),
            in_specs=[pl.BlockSpec((part, FRAG_COLS), at)] * len(arrays),
            out_specs=[pl.BlockSpec((1, part, FRAG_COLS), lambda j, p: (j, 0, 0))] * len(arrays),
        ),
        compiler_params=params_of(8),
        cost_estimate=cost(0, 8 * blocks * part * FRAG_COLS * len(arrays)),
        name="due_columns",
    )(place, *in_hbm(*arrays))


def duplicate(array):
    rows, width = array.shape
    step = rows // 4 if rows % 32 == 0 else rows
    block = pl.BlockSpec((step, width), lambda i: (i, 0))
    return pl.pallas_call(
        copy_kernel,
        out_shape=pltpu.HBM((rows, width), array.dtype),
        grid=(rows // step,),
        in_specs=[block],
        out_specs=block,
        compiler_params=params_of(8),
        cost_estimate=cost(0, 8 * array.size),
        name="duplicate",
    )(*in_hbm(array))


def outer_kernel(replicas, place_ref, *refs):
    share = 1.0 / replicas
    base_refs, sum_refs = refs[3:3 + replicas], refs[3 + replicas:3 + 2 * replicas]
    inner_ref, a_ref, p_ref, m_ref, own_ref, _, w_out, a_out, m_out = refs[3 + 2 * replicas:]
    scale = share * (1.0 + OUTER_MU) * OUTER_RATE
    for j in range(replicas):

        @pl.when(pl.program_id(0) == j)
        def _():
            fresh = base_refs[j][...] - scale * sum_refs[j][...].astype(jnp.float32)
            w_out[...] = MIX_LOCAL * inner_ref[0] + (1.0 - MIX_LOCAL) * fresh

    @pl.when(pl.program_id(0) == 0)
    def _():
        pseudo = p_ref[...] + share * own_ref[...]
        new_moment = OUTER_MU * m_ref[...] + pseudo
        m_out[...] = new_moment
        a_out[...] = a_ref[...] - OUTER_RATE * (OUTER_MU * new_moment + pseudo)


def outer_step(place, outputs, base, sums, inner, anchor, pseudo, momentum, own_sum, ticket):
    replicas, part = inner.shape[0], inner.shape[1]
    mixed = pl.BlockSpec((part, FRAG_COLS), lambda j, p: (p[1] ^ j, p[0]))
    pieces = pl.BlockSpec((1, part, FRAG_COLS), lambda j, p: (j, 0, 0))
    due = pl.BlockSpec((part, FRAG_COLS), lambda j, p: (0, p[0]))
    plain = pl.BlockSpec((part, FRAG_COLS), lambda j, p: (0, 0))
    whole = pl.BlockSpec(memory_space=pl.ANY)
    return pl.pallas_call(
        functools.partial(outer_kernel, replicas),
        out_shape=[pltpu.HBM(a.shape, a.dtype) for a in outputs],
        grid_spec=pltpu.PrefetchScalarGridSpec(
            num_scalar_prefetch=1,
            grid=(replicas,),
            in_specs=[whole] * 3 + [plain] * (2 * replicas) + [pieces] + [plain] * 4 + [whole],
            out_specs=[mixed, due, due],
        ),
        input_output_aliases={1: 0, 2: 1, 3: 2},
        compiler_params=params_of(12),
        cost_estimate=cost(10 * replicas * part * FRAG_COLS, 20 * replicas * part * FRAG_COLS),
        name="outer_step",
    )(place, *in_hbm(*outputs), *base, *sums, inner, anchor, pseudo, momentum, own_sum, ticket)


def swap(block, axis, offset):
    count = lax.axis_size(axis)
    return lax.ppermute(block, axis, [(i, i ^ offset) for i in range(count)])


def after(value, *others):
    return lax.optimization_barrier((value,) + others)[0]


def by_device(pieces, me):
    count = pieces.shape[0]
    return jnp.stack([lax.dynamic_index_in_dim(pieces, me ^ k, 0, keepdims=False) for k in range(count)])


class Line:
    def __init__(self, axis, window):
        self.axis, self.window, self.ended = axis, window, []

    def swap(self, block, offset):
        if len(self.ended) >= self.window:
            block = after(block, self.ended[-self.window])
        self.ended.append(swap(block, self.axis, offset))
        return self.ended[-1]


def body(
    tokens,
    cotangent,
    weights,
    first_moment,
    second_moment,
    anchor,
    momentum,
    due_fragment,
    step_count,
):
    inputs, incoming, params = tokens[0], cotangent[0], weights[0]
    kv_width = incoming.shape[1] // 2
    rows = params.shape[0]
    part = anchor.shape[0]
    replicas = lax.axis_size("rep")
    shards = lax.axis_size("fsdp")
    me = jnp.reshape(lax.axis_index("fsdp"), (1,)).astype(jnp.int32)
    my_rep = lax.axis_index("rep").astype(jnp.int32)
    place = jnp.stack([due_fragment[0], my_rep])
    chips = range(2, shards, 2)
    far = sorted(chips, key=lambda k: (-bin(k).count("1"), k))

    line = Line("fsdp", 4)
    values = {0: incoming[:, kv_width:]}
    for k in chips:
        values[k] = line.swap(values[0], k)

    groups = [[k] for k in far if bin(k).count("1") > 1]
    groups += [[k for k in far if bin(k).count("1") == 1]]
    blocks = {0: pack(inputs, me, 0, rows)}
    for group in groups:
        for odd in range(2):
            for k in group:
                blocks[k + odd] = line.swap(pack(inputs, me, k + odd, rows), k + odd)
    early = blocks[far[0]]
    blocks[1] = swap(pack(inputs, after(me, early), 1, rows), "fsdp", 1)
    value_list = [values[k] for k in range(0, shards, 2)]
    crossed = swap(after(jnp.stack(value_list), early), "fsdp", 1)
    value_list = [v for m in range(shards // 2) for v in (value_list[m], crossed[m])]

    def to_all(pieces):
        return lax.all_to_all(pieces, "rep", 0, 0, tiled=True)

    place_early = after(place, early)
    steps_now = step_count[0].astype(jnp.float32)
    plan = jnp.minimum(1.0, steps_now / WARMUP) * (
        0.55 + 0.45 * jnp.cos(jnp.pi * steps_now / STEPS_TOTAL)
    )
    rate = PEAK_RATE * plan
    inv_one = 1.0 / (1.0 - jnp.power(BETA_ONE, steps_now))
    inv_two = 1.0 / (1.0 - jnp.power(BETA_TWO, steps_now))
    scalars = jnp.stack([rate, inv_one, inv_two])
    old, old_first, old_second = due_columns(place_early, part, params, first_moment[0], second_moment[0])
    anchor_cols, moment_cols = (c[0] for c in due_columns(place_early, part, anchor, momentum))
    old_sum = jnp.sum(to_all(by_device(old, my_rep)), axis=0)
    pseudo_old = anchor_cols - old_sum / replicas
    base = anchor_cols - OUTER_RATE * (OUTER_MU * (OUTER_MU * moment_cols + pseudo_old) + pseudo_old)
    base = to_all(jnp.broadcast_to(base[None], (replicas,) + base.shape))
    base = by_device(base, my_rep)
    base = [base[j] for j in range(replicas)]
    anchor_copy, momentum_copy = duplicate(anchor), duplicate(momentum)
    key_weights = cast_left(after(params, early), kv_width)

    last = far[-1]
    blocks[last + 1] = after(
        blocks[last + 1], base[-1], anchor_copy, momentum_copy, old_second, scalars, value_list[-1]
    )
    parts = []
    for k in far + [0]:
        theirs = swap(partial_keys(blocks[k + 1], key_weights), "fsdp", 1)
        part_k = partial_keys(blocks[k], key_weights, theirs)
        parts.append(line.swap(part_k, k) if k else part_k)
    back = key_backward(parts, incoming)
    keys = []
    for held in [back] + [line.swap(back, k) for k in chips]:
        keys += [held, swap(held, "fsdp", 1)]

    cut = shards // 2
    flipped = [
        transpose_tokens([blocks[k] for k in range(cut)]),
        transpose_tokens([blocks[k] for k in range(cut, shards)]),
    ]
    grad_values, square, due = gradient(
        place, [(flipped[0], value_list[:cut]), (flipped[1], value_list[cut:])]
    )
    (grad_first,) = gradient(place, [(flipped[0], keys[:cut])], last=False)
    grad_keys, square, due = gradient(place, [(flipped[1], keys[cut:])], grad_first, square, due)

    square = square + swap(square, "fsdp", 1)
    squares = [square] + [swap(square, "fsdp", k) for k in chips]

    state = (params, first_moment[0], second_moment[0], grad_keys, grad_values)
    inner, *update = adam_frag(place, scalars, squares, old, old_first, old_second, due)
    steps = rows // 256
    *results, ticket = adam_rows(scalars, squares, state, 0, steps // 2)
    own_sum = update[0].astype(jnp.float32)
    for k in range(1, replicas):
        own_sum = own_sum + swap(update[k], "rep", k).astype(jnp.float32)
    own_sum, ticket = lax.optimization_barrier((own_sum, ticket))
    sums = [own_sum.astype(jnp.bfloat16)]
    sums += [swap(sums[0], "rep", k) for k in range(1, replicas)]
    results = adam_rows(scalars, squares, state, steps // 2, steps, results)
    weights_out, anchor_out, momentum_out = outer_step(
        place,
        (results[0], anchor_copy, momentum_copy),
        base,
        sums,
        inner,
        anchor_cols,
        pseudo_old,
        moment_cols,
        own_sum,
        ticket,
    )
    plan_out = jnp.reshape(plan, (1,))
    return (
        weights_out[None],
        results[1][None],
        results[2][None],
        anchor_out,
        momentum_out,
        plan_out,
    )


def solution(mesh):
    tokens_spec = P("rep", "fsdp", None)
    outer_spec = P(("fsdp", "rep"), None)
    return jax.shard_map(
        body,
        mesh=mesh,
        in_specs=(tokens_spec,) * 5 + (outer_spec,) * 2 + (P(), P()),
        out_specs=(tokens_spec,) * 3 + (outer_spec,) * 2 + (P(),),
        check_vma=False,
    )
```

```python
import functools

import jax
import jax.numpy as jnp
from jax import lax
from jax.experimental import pallas as pl
from jax.experimental.pallas import tpu as pltpu
from jax.sharding import PartitionSpec as P

HEAD = 128
WARMUP = 2000
STEPS_TOTAL = 100000
FRAG_COLS = 128


BETA_ONE = 0.9
BETA_TWO = 0.95
ADAM_EPS = 1e-08
DECAY = 0.1
PEAK_RATE = 0.0003
CLIP_NORM = 1.0
OUTER_MU = 0.9
OUTER_RATE = 0.7
MIX_LOCAL = 0.5

MIB = 1 << 20


def in_hbm(*arrays):
    return [pltpu.with_memory_space_constraint(a, pltpu.HBM) for a in arrays]


def params_of(limit):
    return pltpu.CompilerParams(vmem_limit_bytes=limit * MIB)


def cost(flops, moved):
    return pl.CostEstimate(flops=int(flops), bytes_accessed=int(moved), transcendentals=0)


def copy_kernel(src_ref, out_ref):
    out_ref[...] = src_ref[...].reshape(out_ref.shape)


def pack_kernel(me_ref, src_ref, out_ref):
    out_ref[...] = src_ref[...]


def pack(tokens, me, offset, rows):
    count = tokens.shape[0]
    return pl.pallas_call(
        pack_kernel,
        out_shape=jax.ShapeDtypeStruct((count, rows), tokens.dtype),
        grid_spec=pltpu.PrefetchScalarGridSpec(
            num_scalar_prefetch=1,
            grid=(1,),
            in_specs=[pl.BlockSpec((count, rows), lambda i, me: (0, me[0] ^ offset))],
            out_specs=pl.BlockSpec((count, rows), lambda i, me: (0, 0)),
        ),
        compiler_params=params_of(4),
        cost_estimate=cost(0, 4 * count * rows),
        name="pack",
    )(me, *in_hbm(tokens))


def transpose_kernel(*refs):
    *x_refs, out_ref = refs
    count = x_refs[0].shape[0]
    for j, ref in enumerate(x_refs):
        out_ref[:, j * count:(j + 1) * count] = ref[...].T


def transpose_tokens(blocks):
    count, rows = blocks[0].shape
    step = 256
    return pl.pallas_call(
        transpose_kernel,
        out_shape=jax.ShapeDtypeStruct((rows, len(blocks) * count), blocks[0].dtype),
        grid=(rows // step,),
        in_specs=[pl.BlockSpec((count, step), lambda i: (0, i))] * len(blocks),
        out_specs=pl.BlockSpec((step, len(blocks) * count), lambda i: (i, 0)),
        compiler_params=params_of(8),
        cost_estimate=cost(0, 4 * len(blocks) * count * rows),
        name="transpose_tokens",
    )(*blocks)


def cast_kernel(src_ref, out_ref):
    out_ref[...] = src_ref[...].astype(out_ref.dtype)


def cast_left(array, width):
    rows = array.shape[0]
    block = pl.BlockSpec((256, width), lambda i: (i, 0))
    return pl.pallas_call(
        cast_kernel,
        out_shape=jax.ShapeDtypeStruct((rows, width), jnp.bfloat16),
        grid=(rows // 256,),
        in_specs=[block],
        out_specs=block,
        compiler_params=params_of(8),
        cost_estimate=cost(0, 6 * rows * width),
        name="cast_left",
    )(*in_hbm(array))


def partial_kernel(x_ref, w_ref, *refs):
    *add_refs, out_ref = refs
    total = jnp.dot(x_ref[...], w_ref[...], preferred_element_type=jnp.float32)
    for ref in add_refs:
        total = total + ref[...].astype(jnp.float32)
    out_ref[...] = total.astype(out_ref.dtype)


def partial_keys(block, key_weights, *others):
    count, rows = block.shape
    width = key_weights.shape[1]
    return pl.pallas_call(
        partial_kernel,
        out_shape=jax.ShapeDtypeStruct((count, width), jnp.bfloat16),
        compiler_params=params_of(8),
        cost_estimate=cost(2 * count * rows * width, 2 * count * rows),
        name="partial_keys",
    )(block, key_weights, *others)


def key_kernel(*refs):
    *part_refs, cot_ref, out_ref = refs
    raw = sum(ref[...].astype(jnp.float32) for ref in part_refs)
    for h in range(raw.shape[1] // HEAD):
        cols = slice(h * HEAD, (h + 1) * HEAD)
        head = raw[:, cols]
        inverse = lax.rsqrt(jnp.mean(head * head, axis=1, keepdims=True) + 1e-06)
        normed = head * inverse
        upper = cot_ref[:, cols].astype(jnp.float32)
        back = inverse * (upper - normed * jnp.mean(upper * normed, axis=1, keepdims=True))
        out_ref[:, cols] = back.astype(out_ref.dtype)


def key_backward(parts, incoming):
    block = pl.BlockSpec(parts[0].shape, lambda i: (0, 0))
    cot = pl.BlockSpec(parts[0].shape, lambda i: (0, 0))
    size = parts[0].size
    return pl.pallas_call(
        key_kernel,
        out_shape=jax.ShapeDtypeStruct(parts[0].shape, jnp.bfloat16),
        grid=(1,),
        in_specs=[block] * len(parts) + [cot],
        out_specs=block,
        compiler_params=params_of(8),
        cost_estimate=cost(60 * size, 12 * size),
        name="key_backward",
    )(*parts, incoming)


def grad_kernel(counts, has_base, has_more, last, *refs):
    refs = list(refs)
    place_ref = refs.pop(0)
    terms = []
    for count in counts:
        terms.append((refs.pop(0), refs[:count]))
        del refs[:count]
    base = refs.pop(0) if has_base else None
    square_in, due_in = (refs.pop(0), refs.pop(0)) if has_more else (None, None)
    out_ref = refs.pop(0)
    sq_ref, due_ref = (refs.pop(0), refs.pop(0)) if last else (None, None)
    joined = refs

    @pl.when(pl.program_id(0) == 0)
    def _():
        for (_, blocks), held in zip(terms, joined):
            depth = blocks[0].shape[0]
            for j, block in enumerate(blocks):
                held[j * depth:(j + 1) * depth, :] = block[...]
        if last:
            sq_ref[...] = square_in[...] if has_more else jnp.zeros_like(sq_ref)

    total = base[...] if has_base else None
    for (x_ref, _), held in zip(terms, joined):
        term = jnp.dot(x_ref[...], held[...], preferred_element_type=jnp.float32)
        total = term if total is None else total + term
    out_ref[...] = total
    if last:
        rows, width = total.shape
        squares = (total * total).reshape(rows // 8, 8, width).sum(axis=0)
        folded = squares[:, :HEAD]
        for h in range(1, width // HEAD):
            folded = folded + squares[:, h * HEAD:(h + 1) * HEAD]
        sq_ref[...] += folded
        heads = width // FRAG_COLS
        mine = place_ref[0] - (0 if has_more else heads)
        mine = jnp.minimum(jnp.maximum(mine, 0), heads - 1) * FRAG_COLS
        column = out_ref[:, pl.ds(pl.multiple_of(mine, FRAG_COLS), FRAG_COLS)]
        if has_more:
            column = jnp.where(place_ref[0] < heads, column, due_in[...])
        due_ref[...] = column


def gradient(place, terms, base=None, square=None, due=None, last=True):
    rows = terms[0][0].shape[0]
    width = terms[0][1][0].shape[1]
    step = 256
    row_block = lambda cols: pl.BlockSpec((step, cols), lambda i, p: (i, 0))
    fixed = pl.BlockSpec((8, HEAD), lambda i, p: (0, 0))
    args, specs, scratch = [], [], []
    for x, blocks in terms:
        args += [x, *blocks]
        specs += [row_block(x.shape[1])]
        specs += [pl.BlockSpec(b.shape, lambda i, p: (0, 0)) for b in blocks]
        scratch.append(pltpu.VMEM((x.shape[1], width), jnp.bfloat16))
    if base is not None:
        args.append(base)
        specs.append(row_block(width))
    if square is not None:
        args += [square, due]
        specs += [fixed, row_block(FRAG_COLS)]
    if last:
        shapes = [
            pltpu.HBM((rows, width), jnp.float32),
            jax.ShapeDtypeStruct((8, HEAD), jnp.float32),
            jax.ShapeDtypeStruct((rows, FRAG_COLS), jnp.float32),
        ]
        outs = [row_block(width), fixed, row_block(FRAG_COLS)]
    else:
        shapes = [jax.ShapeDtypeStruct((rows, width), jnp.float32)]
        outs = [row_block(width)]
    depth = sum(x.shape[1] for x, _ in terms)
    return pl.pallas_call(
        functools.partial(grad_kernel, [len(b) for _, b in terms], base is not None, square is not None, last),
        out_shape=shapes,
        grid_spec=pltpu.PrefetchScalarGridSpec(
            num_scalar_prefetch=1,
            grid=(rows // step,),
            in_specs=specs,
            out_specs=outs,
            scratch_shapes=scratch,
        ),
        compiler_params=params_of(20),
        cost_estimate=cost(2 * rows * width * depth, 2 * rows * depth + 4 * rows * width),
        name="gradient",
    )(place, *args)


def clip_factor(square_refs):
    square = jnp.sum(sum(ref[...] for ref in square_refs), keepdims=True)
    return jnp.minimum(1.0, CLIP_NORM / (jnp.sqrt(square) + 1e-06))


def adam(old, first, second, grad, factor, scalars):
    rate, inv_one, inv_two = (scalars[i] for i in range(3))
    clipped = grad * factor
    first_new = BETA_ONE * first + (1.0 - BETA_ONE) * clipped
    second_new = BETA_TWO * second + (1.0 - BETA_TWO) * clipped * clipped
    update = rate * (
        first_new * inv_one / (jnp.sqrt(second_new * inv_two) + ADAM_EPS) + DECAY * old
    )
    return update, first_new, second_new


def adam_kernel(squares, extra, sc_ref, w_ref, m_ref, v_ref, gk_ref, gv_ref, *refs):
    factor = clip_factor(refs[:squares])
    w_out, m_out, v_out, *done = refs[squares + extra:]
    width = gk_ref.shape[1]
    for g_ref, cols in ((gk_ref, slice(0, width)), (gv_ref, slice(width, 2 * width))):
        old = w_ref[:, cols]
        update, first_new, second_new = adam(
            old, m_ref[:, cols], v_ref[:, cols], g_ref[...], factor, sc_ref
        )
        w_out[:, cols] = old - update
        m_out[:, cols] = first_new
        v_out[:, cols] = second_new
    for ref in done:
        ref[...] = jnp.zeros_like(ref)


def adam_rows(scalars, squares, state, first, last, into=()):
    rows, width = state[0].shape
    step = 256
    full = pl.BlockSpec((step, width), lambda i: (i + first, 0))
    half = pl.BlockSpec((step, width // 2), lambda i: (i + first, 0))
    shapes = [pltpu.HBM((rows, width), jnp.float32)] * 3
    outs = [full] * 3
    if not into:
        shapes.append(jax.ShapeDtypeStruct((8, HEAD), jnp.float32))
        outs.append(pl.BlockSpec((8, HEAD), lambda i: (0, 0)))
    count = (last - first) * step
    return pl.pallas_call(
        functools.partial(adam_kernel, len(squares), len(into)),
        out_shape=shapes,
        grid=(last - first,),
        in_specs=[pl.BlockSpec(memory_space=pltpu.SMEM), full, full, full, half, half]
        + [pl.BlockSpec((8, HEAD), lambda i: (0, 0))] * len(squares)
        + [pl.BlockSpec(memory_space=pl.ANY)] * len(into),
        out_specs=outs,
        input_output_aliases={6 + len(squares) + i: i for i in range(len(into))},
        compiler_params=params_of(24),
        cost_estimate=cost(20 * count * width, 28 * count * width),
        name="adam_rows",
    )(scalars, *in_hbm(*state), *squares, *in_hbm(*into))


def frag_kernel(squares, place_ref, sc_ref, w_ref, m_ref, v_ref, g_ref, *refs):
    blocks, part, _ = w_ref.shape
    factor = clip_factor(refs[:squares])
    inner_ref, *out_refs = refs[squares:]
    for j in range(blocks):
        at = pl.multiple_of((place_ref[1] ^ j) * part, 8)
        old = w_ref[j]
        update, _, _ = adam(old, m_ref[j], v_ref[j], g_ref[pl.ds(at, part), :], factor, sc_ref)
        inner_ref[j] = old - update
        out_refs[j][...] = update.astype(out_refs[j].dtype)


def adam_frag(place, scalars, squares, old, first, second, grad):
    blocks, part, width = old.shape
    smem = pl.BlockSpec(memory_space=pltpu.SMEM)
    vmem = pl.BlockSpec(memory_space=pltpu.VMEM)
    return pl.pallas_call(
        functools.partial(frag_kernel, len(squares)),
        out_shape=[jax.ShapeDtypeStruct(old.shape, jnp.float32)]
        + [jax.ShapeDtypeStruct((part, width), jnp.bfloat16)] * blocks,
        in_specs=[smem, smem] + [vmem] * (4 + len(squares)),
        out_specs=[vmem] * (1 + blocks),
        compiler_params=params_of(12),
        cost_estimate=cost(20 * old.size, 22 * old.size),
        name="adam_frag",
    )(place, scalars, old, first, second, grad, *squares)


def pick_kernel(place_ref, *refs):
    half = len(refs) // 2
    for src_ref, out_ref in zip(refs[:half], refs[half:]):
        out_ref[...] = src_ref[...].reshape(out_ref.shape)


def due_columns(place, part, *arrays):
    blocks = arrays[0].shape[0] // part
    at = (lambda j, p: (p[1] ^ j, p[0])) if blocks > 1 else (lambda j, p: (0, p[0]))
    return pl.pallas_call(
        pick_kernel,
        out_shape=[pltpu.HBM((blocks, part, FRAG_COLS), a.dtype) for a in arrays],
        grid_spec=pltpu.PrefetchScalarGridSpec(
            num_scalar_prefetch=1,
            grid=(blocks,),
            in_specs=[pl.BlockSpec((part, FRAG_COLS), at)] * len(arrays),
            out_specs=[pl.BlockSpec((1, part, FRAG_COLS), lambda j, p: (j, 0, 0))] * len(arrays),
        ),
        compiler_params=params_of(8),
        cost_estimate=cost(0, 8 * blocks * part * FRAG_COLS * len(arrays)),
        name="due_columns",
    )(place, *in_hbm(*arrays))


def duplicate(array):
    rows, width = array.shape
    step = rows // 4 if rows % 32 == 0 else rows
    block = pl.BlockSpec((step, width), lambda i: (i, 0))
    return pl.pallas_call(
        copy_kernel,
        out_shape=pltpu.HBM((rows, width), array.dtype),
        grid=(rows // step,),
        in_specs=[block],
        out_specs=block,
        compiler_params=params_of(8),
        cost_estimate=cost(0, 8 * array.size),
        name="duplicate",
    )(*in_hbm(array))


def outer_kernel(replicas, place_ref, *refs):
    share = 1.0 / replicas
    base_refs, sum_refs = refs[3:3 + replicas], refs[3 + replicas:3 + 2 * replicas]
    inner_ref, a_ref, p_ref, m_ref, own_ref, _, w_out, a_out, m_out = refs[3 + 2 * replicas:]
    scale = share * (1.0 + OUTER_MU) * OUTER_RATE
    for j in range(replicas):

        @pl.when(pl.program_id(0) == j)
        def _():
            fresh = base_refs[j][...] - scale * sum_refs[j][...].astype(jnp.float32)
            w_out[...] = MIX_LOCAL * inner_ref[0] + (1.0 - MIX_LOCAL) * fresh

    @pl.when(pl.program_id(0) == 0)
    def _():
        pseudo = p_ref[...] + share * own_ref[...]
        new_moment = OUTER_MU * m_ref[...] + pseudo
        m_out[...] = new_moment
        a_out[...] = a_ref[...] - OUTER_RATE * (OUTER_MU * new_moment + pseudo)


def outer_step(place, outputs, base, sums, inner, anchor, pseudo, momentum, own_sum, ticket):
    replicas, part = inner.shape[0], inner.shape[1]
    mixed = pl.BlockSpec((part, FRAG_COLS), lambda j, p: (p[1] ^ j, p[0]))
    pieces = pl.BlockSpec((1, part, FRAG_COLS), lambda j, p: (j, 0, 0))
    due = pl.BlockSpec((part, FRAG_COLS), lambda j, p: (0, p[0]))
    plain = pl.BlockSpec((part, FRAG_COLS), lambda j, p: (0, 0))
    whole = pl.BlockSpec(memory_space=pl.ANY)
    return pl.pallas_call(
        functools.partial(outer_kernel, replicas),
        out_shape=[pltpu.HBM(a.shape, a.dtype) for a in outputs],
        grid_spec=pltpu.PrefetchScalarGridSpec(
            num_scalar_prefetch=1,
            grid=(replicas,),
            in_specs=[whole] * 3 + [plain] * (2 * replicas) + [pieces] + [plain] * 4 + [whole],
            out_specs=[mixed, due, due],
        ),
        input_output_aliases={1: 0, 2: 1, 3: 2},
        compiler_params=params_of(12),
        cost_estimate=cost(10 * replicas * part * FRAG_COLS, 20 * replicas * part * FRAG_COLS),
        name="outer_step",
    )(place, *in_hbm(*outputs), *base, *sums, inner, anchor, pseudo, momentum, own_sum, ticket)


def swap(block, axis, offset):
    count = lax.axis_size(axis)
    return lax.ppermute(block, axis, [(i, i ^ offset) for i in range(count)])


def after(value, *others):
    return lax.optimization_barrier((value,) + others)[0]


def by_device(pieces, me):
    count = pieces.shape[0]
    return jnp.stack([lax.dynamic_index_in_dim(pieces, me ^ k, 0, keepdims=False) for k in range(count)])


class Line:
    def __init__(self, axis, window):
        self.axis, self.window, self.ended = axis, window, []

    def swap(self, block, offset):
        if len(self.ended) >= self.window:
            block = after(block, self.ended[-self.window])
        self.ended.append(swap(block, self.axis, offset))
        return self.ended[-1]


def body(
    tokens,
    cotangent,
    weights,
    first_moment,
    second_moment,
    anchor,
    momentum,
    due_fragment,
    step_count,
):
    inputs, incoming, params = tokens[0], cotangent[0], weights[0]
    kv_width = incoming.shape[1] // 2
    rows = params.shape[0]
    part = anchor.shape[0]
    replicas = lax.axis_size("rep")
    shards = lax.axis_size("fsdp")
    me = jnp.reshape(lax.axis_index("fsdp"), (1,)).astype(jnp.int32)
    my_rep = lax.axis_index("rep").astype(jnp.int32)
    place = jnp.stack([due_fragment[0], my_rep])
    chips = range(2, shards, 2)
    far = sorted(chips, key=lambda k: (-bin(k).count("1"), k))

    line = Line("fsdp", 4)
    values = {0: incoming[:, kv_width:]}
    for k in chips:
        values[k] = line.swap(values[0], k)

    groups = [[k] for k in far if bin(k).count("1") > 1]
    groups += [[k for k in far if bin(k).count("1") == 1]]
    blocks, packed = {0: pack(inputs, me, 0, rows)}, {}
    for group in groups:
        for odd in range(2):
            for k in group:
                packed[k + odd] = pack(inputs, me, k + odd, rows)
                blocks[k + odd] = line.swap(packed[k + odd], k + odd)
    early = packed[far[0] + 1]
    blocks[1] = swap(pack(inputs, after(me, early), 1, rows), "fsdp", 1)
    crossed = swap(jnp.stack([values[k] for k in range(0, shards, 2)]), "fsdp", 1)
    for k in range(0, shards, 2):
        values[k + 1] = crossed[k // 2]

    def to_all(pieces):
        return lax.all_to_all(pieces, "rep", 0, 0, tiled=True)

    place_early = after(place, early)
    steps_now = step_count[0].astype(jnp.float32)
    plan = jnp.minimum(1.0, steps_now / WARMUP) * (
        0.55 + 0.45 * jnp.cos(jnp.pi * steps_now / STEPS_TOTAL)
    )
    rate = PEAK_RATE * plan
    inv_one = 1.0 / (1.0 - jnp.power(BETA_ONE, steps_now))
    inv_two = 1.0 / (1.0 - jnp.power(BETA_TWO, steps_now))
    scalars = jnp.stack([rate, inv_one, inv_two])
    old, old_first, old_second = due_columns(place_early, part, params, first_moment[0], second_moment[0])
    anchor_cols, moment_cols = (c[0] for c in due_columns(place_early, part, anchor, momentum))
    old_sum = jnp.sum(to_all(by_device(old, my_rep)), axis=0)
    pseudo_old = anchor_cols - old_sum / replicas
    base = anchor_cols - OUTER_RATE * (OUTER_MU * (OUTER_MU * moment_cols + pseudo_old) + pseudo_old)
    base = to_all(jnp.broadcast_to(base[None], (replicas,) + base.shape))
    base = by_device(base, my_rep)
    base = [base[j] for j in range(replicas)]
    anchor_copy, momentum_copy = duplicate(anchor), duplicate(momentum)
    key_weights = cast_left(after(params, early), kv_width)

    spread = [0, 1] + [k + odd for k in far for odd in range(2)]
    near, rest = spread[:shards // 2], spread[shards // 2:]
    flipped = transpose_tokens([blocks[k] for k in near])
    (values_first,) = gradient(place, [(flipped, [values[k] for k in near])], last=False)

    last = far[-1]
    blocks[last + 1] = after(
        blocks[last + 1], base[-1], anchor_copy, momentum_copy, old_second, scalars, values_first
    )
    parts = []
    for k in far + [0]:
        theirs = swap(partial_keys(blocks[k + 1], key_weights), "fsdp", 1)
        part_k = partial_keys(blocks[k], key_weights, theirs)
        parts.append(line.swap(part_k, k) if k else part_k)
    flipped_rest = transpose_tokens([blocks[k] for k in rest])
    parts[-1] = after(parts[-1], flipped_rest)
    back = key_backward(parts, incoming)
    keys = {0: back}
    for k in far:
        keys[k] = line.swap(back, k)
    for k in range(0, shards, 2):
        keys[k + 1] = swap(keys[k], "fsdp", 1)

    grad_values, square, due = gradient(
        place, [(flipped_rest, [values[k] for k in rest])], values_first
    )
    (grad_first,) = gradient(place, [(flipped, [keys[k] for k in near])], last=False)
    grad_keys, square, due = gradient(
        place, [(flipped_rest, [keys[k] for k in rest])], grad_first, square, due
    )

    square = square + swap(square, "fsdp", 1)
    squares = [square] + [swap(square, "fsdp", k) for k in chips]

    state = (params, first_moment[0], second_moment[0], grad_keys, grad_values)
    inner, *update = adam_frag(place, scalars, squares, old, old_first, old_second, due)
    steps = rows // 256
    *results, ticket = adam_rows(scalars, squares, state, 0, steps // 2)
    own_sum = update[0].astype(jnp.float32)
    for k in range(1, replicas):
        own_sum = own_sum + swap(update[k], "rep", k).astype(jnp.float32)
    own_sum, ticket = lax.optimization_barrier((own_sum, ticket))
    sums = [own_sum.astype(jnp.bfloat16)]
    sums += [swap(sums[0], "rep", k) for k in range(1, replicas)]
    results = adam_rows(scalars, squares, state, steps // 2, steps, results)
    weights_out, anchor_out, momentum_out = outer_step(
        place,
        (results[0], anchor_copy, momentum_copy),
        base,
        sums,
        inner,
        anchor_cols,
        pseudo_old,
        moment_cols,
        own_sum,
        ticket,
    )
    plan_out = jnp.reshape(plan, (1,))
    return (
        weights_out[None],
        results[1][None],
        results[2][None],
        anchor_out,
        momentum_out,
        plan_out,
    )


def solution(mesh):
    tokens_spec = P("rep", "fsdp", None)
    outer_spec = P(("fsdp", "rep"), None)
    return jax.shard_map(
        body,
        mesh=mesh,
        in_specs=(tokens_spec,) * 5 + (outer_spec,) * 2 + (P(), P()),
        out_specs=(tokens_spec,) * 3 + (outer_spec,) * 2 + (P(),),
        check_vma=False,
    )
```

```python
import functools

import jax
import jax.numpy as jnp
from jax import lax
from jax.experimental import pallas as pl
from jax.experimental.pallas import tpu as pltpu
from jax.sharding import PartitionSpec as P

HEAD = 128
WARMUP = 2000
STEPS_TOTAL = 100000
FRAG_COLS = 128


BETA_ONE = 0.9
BETA_TWO = 0.95
ADAM_EPS = 1e-08
DECAY = 0.1
PEAK_RATE = 0.0003
CLIP_NORM = 1.0
OUTER_MU = 0.9
OUTER_RATE = 0.7
MIX_LOCAL = 0.5

MIB = 1 << 20


def in_hbm(*arrays):
    return [pltpu.with_memory_space_constraint(a, pltpu.HBM) for a in arrays]


def params_of(limit):
    return pltpu.CompilerParams(vmem_limit_bytes=limit * MIB)


def cost(flops, moved):
    return pl.CostEstimate(flops=int(flops), bytes_accessed=int(moved), transcendentals=0)


def pack_kernel(first, src_ref, out_ref, held, in_sems, out_sems):
    shards, count, rows = out_ref.shape

    def fetch(s):
        block = src_ref.at[pl.ds(first, count), pl.ds(s * rows, rows)]
        return pltpu.make_async_copy(block, held.at[s], in_sems.at[s])

    def store(s):
        return pltpu.make_async_copy(held.at[s], out_ref.at[s], out_sems.at[s])

    for s in range(shards):
        fetch(s).start()
    for s in range(shards):
        fetch(s).wait()
        store(s).start()
    for s in range(shards):
        store(s).wait()


def pack(tokens, first, count, rows):
    shards = tokens.shape[1] // rows
    shape = (shards, count, rows)
    return pl.pallas_call(
        functools.partial(pack_kernel, first),
        out_shape=pltpu.HBM(shape, tokens.dtype),
        in_specs=[pl.BlockSpec(memory_space=pl.ANY)],
        out_specs=pl.BlockSpec(memory_space=pl.ANY),
        scratch_shapes=[
            pltpu.VMEM(shape, tokens.dtype),
            pltpu.SemaphoreType.DMA((shards,)),
            pltpu.SemaphoreType.DMA((shards,)),
        ],
        compiler_params=params_of(12),
        cost_estimate=cost(0, 4 * shards * count * rows),
        name="pack",
    )(*in_hbm(tokens))


def transpose_kernel(me_ref, even_ref, odd_ref, out_ref):
    out_ref[...] = jnp.concatenate([even_ref[0], odd_ref[0]], axis=0).T


def transpose_tokens(blocks, me):
    shards, count, rows = blocks.shape
    block = lambda odd: pl.BlockSpec((1, count, rows), lambda m, me: (me[0] ^ (2 * m + odd), 0, 0))
    return pl.pallas_call(
        transpose_kernel,
        out_shape=jax.ShapeDtypeStruct((rows, shards * count), blocks.dtype),
        grid_spec=pltpu.PrefetchScalarGridSpec(
            num_scalar_prefetch=1,
            grid=(shards // 2,),
            in_specs=[block(0), block(1)],
            out_specs=pl.BlockSpec((rows, 2 * count), lambda m, me: (0, m)),
        ),
        compiler_params=params_of(12),
        cost_estimate=cost(0, 4 * blocks.size),
        name="transpose_tokens",
    )(me, blocks, blocks)


def cast_kernel(src_ref, out_ref):
    out_ref[...] = src_ref[...].astype(out_ref.dtype)


def cast_left(array, width):
    rows = array.shape[0]
    block = pl.BlockSpec((256, width), lambda i: (i, 0))
    return pl.pallas_call(
        cast_kernel,
        out_shape=jax.ShapeDtypeStruct((rows, width), jnp.bfloat16),
        grid=(rows // 256,),
        in_specs=[block],
        out_specs=block,
        compiler_params=params_of(8),
        cost_estimate=cost(0, 6 * rows * width),
        name="cast_left",
    )(*in_hbm(array))


def partial_kernel(me_ref, x_ref, w_ref, out_ref):
    product = jnp.dot(x_ref[0], w_ref[...], preferred_element_type=jnp.float32)
    out_ref[0] = product.astype(out_ref.dtype)


def summed_kernel(me_ref, x_ref, w_ref, add_ref, *out_refs):
    total = jnp.dot(x_ref[0], w_ref[...], preferred_element_type=jnp.float32)
    total = (total + add_ref[0].astype(jnp.float32)).astype(out_refs[0].dtype)
    for m, ref in enumerate(out_refs):

        @pl.when(pl.program_id(0) == m)
        def _():
            ref[...] = total


def partial_keys(blocks, key_weights, me, odd, others=None):
    shards, count, rows = blocks.shape
    width = key_weights.shape[1]
    chips = shards // 2
    stacked = pl.BlockSpec((1, count, width), lambda m, me: (m, 0, 0))
    specs = [
        pl.BlockSpec((1, count, rows), lambda m, me: (me[0] ^ (2 * m + odd), 0, 0)),
        pl.BlockSpec((rows, width), lambda m, me: (0, 0)),
    ]
    if others is None:
        kernel, args = partial_kernel, ()
        shapes, outs = jax.ShapeDtypeStruct((chips, count, width), jnp.bfloat16), stacked
    else:
        kernel, args = summed_kernel, (others,)
        specs.append(stacked)
        shapes = [jax.ShapeDtypeStruct((count, width), jnp.bfloat16)] * chips
        outs = [pl.BlockSpec((count, width), lambda m, me: (0, 0))] * chips
    return pl.pallas_call(
        kernel,
        out_shape=shapes,
        grid_spec=pltpu.PrefetchScalarGridSpec(
            num_scalar_prefetch=1, grid=(chips,), in_specs=specs, out_specs=outs
        ),
        compiler_params=params_of(12),
        cost_estimate=cost(2 * chips * count * rows * width, 2 * chips * count * rows),
        name="partial_keys",
    )(me, blocks, key_weights, *args)


def key_kernel(first, *refs):
    *part_refs, cot_ref, out_ref = refs
    count = out_ref.shape[0]
    raw = sum(ref[...].astype(jnp.float32) for ref in part_refs)
    for h in range(raw.shape[1] // HEAD):
        cols = slice(h * HEAD, (h + 1) * HEAD)
        head = raw[:, cols]
        inverse = lax.rsqrt(jnp.mean(head * head, axis=1, keepdims=True) + 1e-06)
        normed = head * inverse
        upper = cot_ref[first:first + count, cols].astype(jnp.float32)
        back = inverse * (upper - normed * jnp.mean(upper * normed, axis=1, keepdims=True))
        out_ref[:, cols] = back.astype(out_ref.dtype)


def key_backward(parts, incoming, first):
    count, width = parts[0].shape
    block = pl.BlockSpec((count, width), lambda i: (0, 0))
    cot = pl.BlockSpec((incoming.shape[0], width), lambda i: (0, 0))
    return pl.pallas_call(
        functools.partial(key_kernel, first),
        out_shape=jax.ShapeDtypeStruct((count, width), jnp.bfloat16),
        grid=(1,),
        in_specs=[block] * len(parts) + [cot],
        out_specs=block,
        compiler_params=params_of(8),
        cost_estimate=cost(60 * count * width, 12 * count * width),
        name="key_backward",
    )(*parts, incoming)


def grad_kernel(firsts, has_base, has_more, last, *refs):
    refs = list(refs)
    place_ref = refs.pop(0)
    terms = []
    for count, first in firsts:
        terms.append((refs.pop(0), refs[:count], first))
        del refs[:count]
    base = refs.pop(0) if has_base else None
    square_in, due_in = (refs.pop(0), refs.pop(0)) if has_more else (None, None)
    out_ref = refs.pop(0)
    sq_ref, due_ref = (refs.pop(0), refs.pop(0)) if last else (None, None)
    joined = refs

    @pl.when(pl.program_id(0) == 0)
    def _():
        for (_, blocks, first), held in zip(terms, joined):
            depth = held.shape[0] // len(blocks)
            for j, block in enumerate(blocks):
                held[j * depth:(j + 1) * depth, :] = block[first:first + depth, :]
        if last:
            sq_ref[...] = square_in[...] if has_more else jnp.zeros_like(sq_ref)

    total = base[...] if has_base else None
    for (x_ref, _, _), held in zip(terms, joined):
        term = jnp.dot(x_ref[...], held[...], preferred_element_type=jnp.float32)
        total = term if total is None else total + term
    out_ref[...] = total
    if last:
        rows, width = total.shape
        squares = (total * total).reshape(rows // 8, 8, width).sum(axis=0)
        folded = squares[:, :HEAD]
        for h in range(1, width // HEAD):
            folded = folded + squares[:, h * HEAD:(h + 1) * HEAD]
        sq_ref[...] += folded
        heads = width // FRAG_COLS
        mine = place_ref[0] - (0 if has_more else heads)
        mine = jnp.minimum(jnp.maximum(mine, 0), heads - 1) * FRAG_COLS
        column = out_ref[:, pl.ds(pl.multiple_of(mine, FRAG_COLS), FRAG_COLS)]
        if has_more:
            column = jnp.where(place_ref[0] < heads, column, due_in[...])
        due_ref[...] = column


def gradient(place, terms, base=None, square=None, due=None, last=True):
    rows = terms[0][0].shape[0]
    width = terms[0][1][0].shape[1]
    step = 256
    row_block = lambda cols: pl.BlockSpec((step, cols), lambda i, p: (i, 0))
    fixed = pl.BlockSpec((8, HEAD), lambda i, p: (0, 0))
    args, specs, scratch = [], [], []
    for x, blocks, _ in terms:
        args += [x, *blocks]
        specs += [row_block(x.shape[1])]
        specs += [pl.BlockSpec(b.shape, lambda i, p: (0, 0)) for b in blocks]
        scratch.append(pltpu.VMEM((x.shape[1], width), jnp.bfloat16))
    if base is not None:
        args.append(base)
        specs.append(row_block(width))
    if square is not None:
        args += [square, due]
        specs += [fixed, row_block(FRAG_COLS)]
    if last:
        shapes = [
            pltpu.HBM((rows, width), jnp.float32),
            jax.ShapeDtypeStruct((8, HEAD), jnp.float32),
            jax.ShapeDtypeStruct((rows, FRAG_COLS), jnp.float32),
        ]
        outs = [row_block(width), fixed, row_block(FRAG_COLS)]
    else:
        shapes = [jax.ShapeDtypeStruct((rows, width), jnp.float32)]
        outs = [row_block(width)]
    depth = sum(x.shape[1] for x, _, _ in terms)
    return pl.pallas_call(
        functools.partial(grad_kernel, [(len(b), first) for _, b, first in terms], base is not None, square is not None, last),
        out_shape=shapes,
        grid_spec=pltpu.PrefetchScalarGridSpec(
            num_scalar_prefetch=1,
            grid=(rows // step,),
            in_specs=specs,
            out_specs=outs,
            scratch_shapes=scratch,
        ),
        compiler_params=params_of(20),
        cost_estimate=cost(2 * rows * width * depth, 2 * rows * depth + 4 * rows * width),
        name="gradient",
    )(place, *args)


def clip_factor(square_refs):
    square = jnp.sum(sum(ref[...] for ref in square_refs), keepdims=True)
    return jnp.minimum(1.0, CLIP_NORM / (jnp.sqrt(square) + 1e-06))


def adam(old, first, second, grad, factor, scalars):
    rate, inv_one, inv_two = (scalars[i] for i in range(3))
    clipped = grad * factor
    first_new = BETA_ONE * first + (1.0 - BETA_ONE) * clipped
    second_new = BETA_TWO * second + (1.0 - BETA_TWO) * clipped * clipped
    update = rate * (
        first_new * inv_one / (jnp.sqrt(second_new * inv_two) + ADAM_EPS) + DECAY * old
    )
    return update, first_new, second_new


def adam_kernel(squares, extra, sc_ref, w_ref, m_ref, v_ref, gk_ref, gv_ref, *refs):
    factor = clip_factor(refs[:squares])
    w_out, m_out, v_out, *done = refs[squares + extra:]
    width = gk_ref.shape[1]
    for g_ref, cols in ((gk_ref, slice(0, width)), (gv_ref, slice(width, 2 * width))):
        old = w_ref[:, cols]
        update, first_new, second_new = adam(
            old, m_ref[:, cols], v_ref[:, cols], g_ref[...], factor, sc_ref
        )
        w_out[:, cols] = old - update
        m_out[:, cols] = first_new
        v_out[:, cols] = second_new
    for ref in done:
        ref[...] = jnp.zeros_like(ref)


def adam_rows(scalars, squares, state, first, last, into=()):
    rows, width = state[0].shape
    step = 256
    full = pl.BlockSpec((step, width), lambda i: (i + first, 0))
    half = pl.BlockSpec((step, width // 2), lambda i: (i + first, 0))
    shapes = [pltpu.HBM((rows, width), jnp.float32)] * 3
    outs = [full] * 3
    if not into:
        shapes.append(jax.ShapeDtypeStruct((8, HEAD), jnp.float32))
        outs.append(pl.BlockSpec((8, HEAD), lambda i: (0, 0)))
    count = (last - first) * step
    return pl.pallas_call(
        functools.partial(adam_kernel, len(squares), len(into)),
        out_shape=shapes,
        grid=(last - first,),
        in_specs=[pl.BlockSpec(memory_space=pltpu.SMEM), full, full, full, half, half]
        + [pl.BlockSpec((8, HEAD), lambda i: (0, 0))] * len(squares)
        + [pl.BlockSpec(memory_space=pl.ANY)] * len(into),
        out_specs=outs,
        input_output_aliases={6 + len(squares) + i: i for i in range(len(into))},
        compiler_params=params_of(24),
        cost_estimate=cost(20 * count * width, 28 * count * width),
        name="adam_rows",
    )(scalars, *in_hbm(*state), *squares, *in_hbm(*into))


def frag_kernel(squares, place_ref, sc_ref, w_ref, m_ref, v_ref, g_ref, *refs):
    blocks, part, _ = w_ref.shape
    factor = clip_factor(refs[:squares])
    inner_ref, *out_refs = refs[squares:]
    for j in range(blocks):
        at = pl.multiple_of((place_ref[1] ^ j) * part, 8)
        old = w_ref[j]
        update, _, _ = adam(old, m_ref[j], v_ref[j], g_ref[pl.ds(at, part), :], factor, sc_ref)
        inner_ref[j] = old - update
        out_refs[j][...] = update.astype(out_refs[j].dtype)


def adam_frag(place, scalars, squares, old, first, second, grad):
    blocks, part, width = old.shape
    smem = pl.BlockSpec(memory_space=pltpu.SMEM)
    vmem = pl.BlockSpec(memory_space=pltpu.VMEM)
    return pl.pallas_call(
        functools.partial(frag_kernel, len(squares)),
        out_shape=[jax.ShapeDtypeStruct(old.shape, jnp.float32)]
        + [jax.ShapeDtypeStruct((part, width), jnp.bfloat16)] * blocks,
        in_specs=[smem, smem] + [vmem] * (4 + len(squares)),
        out_specs=[vmem] * (1 + blocks),
        compiler_params=params_of(12),
        cost_estimate=cost(20 * old.size, 22 * old.size),
        name="adam_frag",
    )(place, scalars, old, first, second, grad, *squares)


def pick_kernel(place_ref, *refs):
    half = len(refs) // 2
    for src_ref, out_ref in zip(refs[:half], refs[half:]):
        out_ref[...] = src_ref[...].reshape(out_ref.shape)


def due_columns(place, part, *arrays):
    blocks = arrays[0].shape[0] // part
    at = (lambda j, p: (p[1] ^ j, p[0])) if blocks > 1 else (lambda j, p: (0, p[0]))
    return pl.pallas_call(
        pick_kernel,
        out_shape=[pltpu.HBM((blocks, part, FRAG_COLS), a.dtype) for a in arrays],
        grid_spec=pltpu.PrefetchScalarGridSpec(
            num_scalar_prefetch=1,
            grid=(blocks,),
            in_specs=[pl.BlockSpec((part, FRAG_COLS), at)] * len(arrays),
            out_specs=[pl.BlockSpec((1, part, FRAG_COLS), lambda j, p: (j, 0, 0))] * len(arrays),
        ),
        compiler_params=params_of(8),
        cost_estimate=cost(0, 8 * blocks * part * FRAG_COLS * len(arrays)),
        name="due_columns",
    )(place, *in_hbm(*arrays))


def duplicate_kernel(*refs):
    half = (len(refs) - 3) // 2
    held, in_sems, out_sems = refs[2 * half:]
    streams = held.shape[1]
    step = held.shape[2]
    places = [(a, i, pl.ds(i * step, step)) for a in range(half) for i in range(streams)]
    fetches = [
        pltpu.make_async_copy(refs[a].at[at], held.at[a, i], in_sems.at[a, i]) for a, i, at in places
    ]
    stores = [
        pltpu.make_async_copy(held.at[a, i], refs[half + a].at[at], out_sems.at[a, i])
        for a, i, at in places
    ]
    for copy in fetches:
        copy.start()
    for fetch, store in zip(fetches, stores):
        fetch.wait()
        store.start()
    for copy in stores:
        copy.wait()


def duplicate(*arrays):
    rows, width = arrays[0].shape
    streams = 4
    whole = pl.BlockSpec(memory_space=pl.ANY)
    return pl.pallas_call(
        duplicate_kernel,
        out_shape=[pltpu.HBM(a.shape, a.dtype) for a in arrays],
        in_specs=[whole] * len(arrays),
        out_specs=[whole] * len(arrays),
        scratch_shapes=[
            pltpu.VMEM((len(arrays), streams, rows // streams, width), arrays[0].dtype),
            pltpu.SemaphoreType.DMA((len(arrays), streams)),
            pltpu.SemaphoreType.DMA((len(arrays), streams)),
        ],
        compiler_params=params_of(8),
        cost_estimate=cost(0, sum(8 * a.size for a in arrays)),
        name="duplicate",
    )(*in_hbm(*arrays))


def outer_kernel(replicas, place_ref, *refs):
    share = 1.0 / replicas
    base_refs, sum_refs = refs[3:3 + replicas], refs[3 + replicas:3 + 2 * replicas]
    inner_ref, a_ref, p_ref, m_ref, own_ref, _, w_out, a_out, m_out = refs[3 + 2 * replicas:]
    scale = share * (1.0 + OUTER_MU) * OUTER_RATE
    for j in range(replicas):

        @pl.when(pl.program_id(0) == j)
        def _():
            fresh = base_refs[j][...] - scale * sum_refs[j][...].astype(jnp.float32)
            w_out[...] = MIX_LOCAL * inner_ref[0] + (1.0 - MIX_LOCAL) * fresh

    @pl.when(pl.program_id(0) == 0)
    def _():
        pseudo = p_ref[...] + share * own_ref[...]
        new_moment = OUTER_MU * m_ref[...] + pseudo
        m_out[...] = new_moment
        a_out[...] = a_ref[...] - OUTER_RATE * (OUTER_MU * new_moment + pseudo)


def outer_step(place, outputs, base, sums, inner, anchor, pseudo, momentum, own_sum, ticket):
    replicas, part = inner.shape[0], inner.shape[1]
    mixed = pl.BlockSpec((part, FRAG_COLS), lambda j, p: (p[1] ^ j, p[0]))
    pieces = pl.BlockSpec((1, part, FRAG_COLS), lambda j, p: (j, 0, 0))
    due = pl.BlockSpec((part, FRAG_COLS), lambda j, p: (0, p[0]))
    plain = pl.BlockSpec((part, FRAG_COLS), lambda j, p: (0, 0))
    whole = pl.BlockSpec(memory_space=pl.ANY)
    return pl.pallas_call(
        functools.partial(outer_kernel, replicas),
        out_shape=[pltpu.HBM(a.shape, a.dtype) for a in outputs],
        grid_spec=pltpu.PrefetchScalarGridSpec(
            num_scalar_prefetch=1,
            grid=(replicas,),
            in_specs=[whole] * 3 + [plain] * (2 * replicas) + [pieces] + [plain] * 4 + [whole],
            out_specs=[mixed, due, due],
        ),
        input_output_aliases={1: 0, 2: 1, 3: 2},
        compiler_params=params_of(12),
        cost_estimate=cost(10 * replicas * part * FRAG_COLS, 20 * replicas * part * FRAG_COLS),
        name="outer_step",
    )(place, *in_hbm(*outputs), *base, *sums, inner, anchor, pseudo, momentum, own_sum, ticket)


def swap(block, axis, offset):
    count = lax.axis_size(axis)
    return lax.ppermute(block, axis, [(i, i ^ offset) for i in range(count)])


def after(value, *others):
    return lax.optimization_barrier((value,) + others)[0]


def body(
    tokens,
    cotangent,
    weights,
    first_moment,
    second_moment,
    anchor,
    momentum,
    due_fragment,
    step_count,
):
    inputs, incoming, params = tokens[0], cotangent[0], weights[0]
    kv_width = incoming.shape[1] // 2
    rows = params.shape[0]
    part = anchor.shape[0]
    replicas = lax.axis_size("rep")
    shards = lax.axis_size("fsdp")
    me = jnp.reshape(lax.axis_index("fsdp"), (1,)).astype(jnp.int32)
    my_rep = lax.axis_index("rep").astype(jnp.int32)
    place = jnp.stack([due_fragment[0], my_rep])
    chips = range(2, shards, 2)
    count = inputs.shape[0]
    cuts = [(0, count * 3 // 4), (count * 3 // 4, count // 4)]

    def gather(block):
        held = [block] + [swap(block, "fsdp", k) for k in chips]
        return [b for h in held for b in (h, swap(h, "fsdp", 1))]

    values = gather(incoming[:, kv_width:])

    packed = [pack(inputs, first, size, rows) for first, size in cuts]
    arrived = [lax.all_to_all(p, "fsdp", 0, 0, tiled=True) for p in packed]

    steps_now = step_count[0].astype(jnp.float32)
    plan = jnp.minimum(1.0, steps_now / WARMUP) * (
        0.55 + 0.45 * jnp.cos(jnp.pi * steps_now / STEPS_TOTAL)
    )
    rate = PEAK_RATE * plan
    inv_one = 1.0 / (1.0 - jnp.power(BETA_ONE, steps_now))
    inv_two = 1.0 / (1.0 - jnp.power(BETA_TWO, steps_now))
    scalars = jnp.stack([rate, inv_one, inv_two])
    place_early = after(place, *values[2::2])
    old, old_first, old_second = due_columns(place_early, part, params, first_moment[0], second_moment[0])
    anchor_cols, moment_cols = (c[0] for c in due_columns(place_early, part, anchor, momentum))
    old_sum = sum([swap(old[k], "rep", k) for k in range(1, replicas)], old[0])
    pseudo_old = anchor_cols - old_sum / replicas
    base = anchor_cols - OUTER_RATE * (OUTER_MU * (OUTER_MU * moment_cols + pseudo_old) + pseudo_old)
    base = [base] + [swap(base, "rep", k) for k in range(1, replicas)]
    anchor_copy, momentum_copy = duplicate(anchor, momentum)
    key_weights = cast_left(params, kv_width)

    def sum_keys(x, first, *before):
        theirs = swap(partial_keys(x, key_weights, me, 1), "fsdp", 1)
        parts = list(partial_keys(x, key_weights, me, 0, theirs))
        parts = [parts[0]] + [swap(parts[k // 2], "fsdp", k) for k in chips]
        parts[0] = after(parts[0], *before)
        return gather(key_backward(parts, incoming, first))

    arrived[0] = after(
        arrived[0], packed[1], *base, anchor_copy, momentum_copy, old_second, scalars, *values
    )
    flipped = [transpose_tokens(arrived[0], me)]
    keys = [sum_keys(arrived[0], cuts[0][0], flipped[0])]
    (values_first,) = gradient(place, [(flipped[0], values, cuts[0][0])], last=False)
    arrived[1] = after(arrived[1], *keys[0], values_first)
    flipped.append(transpose_tokens(arrived[1], me))
    keys.append(sum_keys(arrived[1], cuts[1][0], flipped[1]))

    (keys_first,) = gradient(place, [(flipped[0], keys[0], 0)], last=False)
    grad_values, square, due = gradient(place, [(flipped[1], values, cuts[1][0])], values_first)
    grad_keys, square, due = gradient(place, [(flipped[1], keys[1], 0)], keys_first, square, due)

    square = square + swap(square, "fsdp", 1)
    squares = [square] + [swap(square, "fsdp", k) for k in chips]

    state = (params, first_moment[0], second_moment[0], grad_keys, grad_values)
    inner, *update = adam_frag(place, scalars, squares, old, old_first, old_second, due)
    steps = rows // 256
    *results, ticket = adam_rows(scalars, squares, state, 0, steps // 2)
    own_sum = update[0].astype(jnp.float32)
    for k in range(1, replicas):
        own_sum = own_sum + swap(update[k], "rep", k).astype(jnp.float32)
    own_sum, ticket = lax.optimization_barrier((own_sum, ticket))
    sums = [own_sum.astype(jnp.bfloat16)]
    sums += [swap(sums[0], "rep", k) for k in range(1, replicas)]
    results = adam_rows(scalars, squares, state, steps // 2, steps, results)
    weights_out, anchor_out, momentum_out = outer_step(
        place,
        (results[0], anchor_copy, momentum_copy),
        base,
        sums,
        inner,
        anchor_cols,
        pseudo_old,
        moment_cols,
        own_sum,
        ticket,
    )
    plan_out = jnp.reshape(plan, (1,))
    return (
        weights_out[None],
        results[1][None],
        results[2][None],
        anchor_out,
        momentum_out,
        plan_out,
    )


def solution(mesh):
    tokens_spec = P("rep", "fsdp", None)
    outer_spec = P(("fsdp", "rep"), None)
    return jax.shard_map(
        body,
        mesh=mesh,
        in_specs=(tokens_spec,) * 5 + (outer_spec,) * 2 + (P(), P()),
        out_specs=(tokens_spec,) * 3 + (outer_spec,) * 2 + (P(),),
        check_vma=False,
    )
```

```python
import functools

import jax
import jax.numpy as jnp
from jax import lax
from jax.experimental import pallas as pl
from jax.experimental.pallas import tpu as pltpu
from jax.sharding import PartitionSpec as P

HEAD = 128
WARMUP = 2000
STEPS_TOTAL = 100000
FRAG_COLS = 128


BETA_ONE = 0.9
BETA_TWO = 0.95
ADAM_EPS = 1e-08
DECAY = 0.1
PEAK_RATE = 0.0003
CLIP_NORM = 1.0
OUTER_MU = 0.9
OUTER_RATE = 0.7
MIX_LOCAL = 0.5

MIB = 1 << 20


def in_hbm(*arrays):
    return [pltpu.with_memory_space_constraint(a, pltpu.HBM) for a in arrays]


def params_of(limit):
    return pltpu.CompilerParams(vmem_limit_bytes=limit * MIB)


def cost(flops, moved):
    return pl.CostEstimate(flops=int(flops), bytes_accessed=int(moved), transcendentals=0)


def pack_kernel(offsets, me_ref, src_ref, *refs):
    half = len(offsets)
    out_refs, (held, in_sems, out_sems) = refs[:half], refs[half:]
    streams = in_sems.shape[1]
    count, rows = out_refs[0].shape
    step = count // streams
    fetches, stores = [], []
    for i, offset in enumerate(offsets):
        column = pl.multiple_of((me_ref[0] ^ offset) * rows, HEAD)
        for j in range(streams):
            at = pl.ds(j * step, step)
            block = src_ref.at[at, pl.ds(column, rows)]
            fetches.append(pltpu.make_async_copy(block, held.at[i, at], in_sems.at[i, j]))
            stores.append(pltpu.make_async_copy(held.at[i, at], out_refs[i].at[at], out_sems.at[i, j]))
    for copy in fetches:
        copy.start()
    for fetch, store in zip(fetches, stores):
        fetch.wait()
        store.start()
    for copy in stores:
        copy.wait()


def pack(tokens, me, rows, offsets):
    count = tokens.shape[0]
    streams = 4
    whole = pl.BlockSpec(memory_space=pl.ANY)
    outs = pl.pallas_call(
        functools.partial(pack_kernel, offsets),
        out_shape=[pltpu.HBM((count, rows), tokens.dtype)] * len(offsets),
        in_specs=[pl.BlockSpec(memory_space=pltpu.SMEM), whole],
        out_specs=[whole] * len(offsets),
        scratch_shapes=[
            pltpu.VMEM((len(offsets), count, rows), tokens.dtype),
            pltpu.SemaphoreType.DMA((len(offsets), streams)),
            pltpu.SemaphoreType.DMA((len(offsets), streams)),
        ],
        compiler_params=params_of(12),
        cost_estimate=cost(0, 4 * len(offsets) * count * rows),
        name="pack",
    )(me, *in_hbm(tokens))
    return dict(zip(offsets, outs))


def cast_kernel(src_ref, out_ref):
    out_ref[...] = src_ref[...].astype(out_ref.dtype)


def cast_left(array, width):
    rows = array.shape[0]
    block = pl.BlockSpec((256, width), lambda i: (i, 0))
    return pl.pallas_call(
        cast_kernel,
        out_shape=jax.ShapeDtypeStruct((rows, width), jnp.bfloat16),
        grid=(rows // 256,),
        in_specs=[block],
        out_specs=block,
        compiler_params=params_of(8),
        cost_estimate=cost(0, 6 * rows * width),
        name="cast_left",
    )(*in_hbm(array))


def partial_kernel(pieces, *refs):
    x_refs, w_ref, (*add_refs, out_ref, flip_ref) = refs[:pieces], refs[pieces], refs[pieces + 1:]
    x = jnp.concatenate([ref[...] for ref in x_refs], axis=1)
    total = jnp.dot(x, w_ref[...], preferred_element_type=jnp.float32)
    for ref in add_refs:
        total = total + ref[...].astype(jnp.float32)
    out_ref[...] = total.astype(out_ref.dtype)
    step = x_refs[0].shape[1]
    for i, ref in enumerate(x_refs):
        flip_ref[i * step:(i + 1) * step, :] = ref[...].T


def partial_keys(block, key_weights, *others):
    count, rows = block.shape
    width = key_weights.shape[1]
    pieces = 4 if rows % (4 * HEAD) == 0 else 2
    fixed = lambda a: pl.BlockSpec(a.shape, lambda i: (0, 0))
    return pl.pallas_call(
        functools.partial(partial_kernel, pieces),
        out_shape=[
            jax.ShapeDtypeStruct((count, width), jnp.bfloat16),
            jax.ShapeDtypeStruct((rows, count), jnp.bfloat16),
        ],
        grid=(1,),
        in_specs=[pl.BlockSpec((count, rows // pieces), lambda i, c=c: (0, c)) for c in range(pieces)]
        + [fixed(key_weights)]
        + [fixed(o) for o in others],
        out_specs=[
            pl.BlockSpec((count, width), lambda i: (0, 0)),
            pl.BlockSpec((rows, count), lambda i: (0, 0)),
        ],
        compiler_params=params_of(12),
        cost_estimate=cost(2 * count * rows * width, 4 * count * rows),
        name="partial_keys",
    )(*[block] * pieces, key_weights, *others)


def key_kernel(first, *refs):
    *part_refs, cot_ref, out_ref = refs
    count = out_ref.shape[0]
    raw = sum(ref[...].astype(jnp.float32) for ref in part_refs)
    for h in range(raw.shape[1] // HEAD):
        cols = slice(h * HEAD, (h + 1) * HEAD)
        head = raw[:, cols]
        inverse = lax.rsqrt(jnp.mean(head * head, axis=1, keepdims=True) + 1e-06)
        normed = head * inverse
        upper = cot_ref[first:first + count, cols].astype(jnp.float32)
        back = inverse * (upper - normed * jnp.mean(upper * normed, axis=1, keepdims=True))
        out_ref[:, cols] = back.astype(out_ref.dtype)


def key_backward(parts, incoming, first):
    count, width = parts[0].shape
    block = pl.BlockSpec((count, width), lambda i: (0, 0))
    cot = pl.BlockSpec((incoming.shape[0], width), lambda i: (0, 0))
    return pl.pallas_call(
        functools.partial(key_kernel, first),
        out_shape=jax.ShapeDtypeStruct((count, width), jnp.bfloat16),
        grid=(1,),
        in_specs=[block] * len(parts) + [cot],
        out_specs=block,
        compiler_params=params_of(8),
        cost_estimate=cost(60 * count * width, 12 * count * width),
        name="key_backward",
    )(*parts, incoming)


def grad_kernel(count, has_base, has_more, last, place_ref, *refs):
    refs = list(refs)
    x_refs, u_refs = refs[:count], refs[count:2 * count]
    refs = refs[2 * count:]
    base = refs.pop(0) if has_base else None
    square_in, due_in = (refs.pop(0), refs.pop(0)) if has_more else (None, None)
    out_ref = refs.pop(0)
    x = jnp.concatenate([ref[...] for ref in x_refs], axis=1)
    u = jnp.concatenate([ref[...] for ref in u_refs], axis=0)
    total = jnp.dot(x, u, preferred_element_type=jnp.float32)
    if has_base:
        total = total + base[...]
    out_ref[...] = total
    if last:
        sq_ref, due_ref = refs

        @pl.when(pl.program_id(0) == 0)
        def _():
            sq_ref[...] = square_in[...] if has_more else jnp.zeros_like(sq_ref)

        rows, width = total.shape
        squares = (total * total).reshape(rows // 8, 8, width).sum(axis=0)
        folded = squares[:, :HEAD]
        for h in range(1, width // HEAD):
            folded = folded + squares[:, h * HEAD:(h + 1) * HEAD]
        sq_ref[...] += folded
        heads = width // FRAG_COLS
        mine = place_ref[0] - (0 if has_more else heads)
        mine = jnp.minimum(jnp.maximum(mine, 0), heads - 1) * FRAG_COLS
        column = out_ref[:, pl.ds(pl.multiple_of(mine, FRAG_COLS), FRAG_COLS)]
        if has_more:
            column = jnp.where(place_ref[0] < heads, column, due_in[...])
        due_ref[...] = column


def gradient(place, flipped, upstream, base=None, square=None, due=None, last=True):
    rows, depth = flipped[0].shape
    width = upstream[0].shape[1]
    step = 256
    row_block = lambda cols: pl.BlockSpec((step, cols), lambda i, p: (i, 0))
    fixed = pl.BlockSpec((8, HEAD), lambda i, p: (0, 0))
    args = [*flipped, *upstream]
    specs = [row_block(depth)] * len(flipped)
    specs += [pl.BlockSpec((depth, width), lambda i, p: (0, 0))] * len(upstream)
    if base is not None:
        args.append(base)
        specs.append(row_block(width))
    if square is not None:
        args += [square, due]
        specs += [fixed, row_block(FRAG_COLS)]
    if last:
        shapes = [
            pltpu.HBM((rows, width), jnp.float32),
            jax.ShapeDtypeStruct((8, HEAD), jnp.float32),
            jax.ShapeDtypeStruct((rows, FRAG_COLS), jnp.float32),
        ]
        outs = [row_block(width), fixed, row_block(FRAG_COLS)]
    else:
        shapes = [jax.ShapeDtypeStruct((rows, width), jnp.float32)]
        outs = [row_block(width)]
    depth *= len(flipped)
    return pl.pallas_call(
        functools.partial(grad_kernel, len(flipped), base is not None, square is not None, last),
        out_shape=shapes,
        grid_spec=pltpu.PrefetchScalarGridSpec(
            num_scalar_prefetch=1, grid=(rows // step,), in_specs=specs, out_specs=outs
        ),
        compiler_params=params_of(20),
        cost_estimate=cost(2 * rows * width * depth, 2 * rows * depth + 4 * rows * width),
        name="gradient",
    )(place, *args)


def clip_factor(square_refs):
    square = jnp.sum(sum(ref[...] for ref in square_refs), keepdims=True)
    return jnp.minimum(1.0, CLIP_NORM / (jnp.sqrt(square) + 1e-06))


def adam(old, first, second, grad, factor, scalars):
    rate, inv_one, inv_two = (scalars[i] for i in range(3))
    clipped = grad * factor
    first_new = BETA_ONE * first + (1.0 - BETA_ONE) * clipped
    second_new = BETA_TWO * second + (1.0 - BETA_TWO) * clipped * clipped
    update = rate * (
        first_new * inv_one / (jnp.sqrt(second_new * inv_two) + ADAM_EPS) + DECAY * old
    )
    return update, first_new, second_new


def adam_kernel(squares, extra, sc_ref, w_ref, m_ref, v_ref, gk_ref, gv_ref, *refs):
    factor = clip_factor(refs[:squares])
    w_out, m_out, v_out, *done = refs[squares + extra:]
    width = gk_ref.shape[1]
    for g_ref, cols in ((gk_ref, slice(0, width)), (gv_ref, slice(width, 2 * width))):
        old = w_ref[:, cols]
        update, first_new, second_new = adam(
            old, m_ref[:, cols], v_ref[:, cols], g_ref[...], factor, sc_ref
        )
        w_out[:, cols] = old - update
        m_out[:, cols] = first_new
        v_out[:, cols] = second_new
    for ref in done:
        ref[...] = jnp.zeros_like(ref)


def adam_rows(scalars, squares, state, first, last, into=()):
    rows, width = state[0].shape
    step = 256
    full = pl.BlockSpec((step, width), lambda i: (i + first, 0))
    half = pl.BlockSpec((step, width // 2), lambda i: (i + first, 0))
    shapes = [pltpu.HBM((rows, width), jnp.float32)] * 3
    outs = [full] * 3
    if not into:
        shapes.append(jax.ShapeDtypeStruct((8, HEAD), jnp.float32))
        outs.append(pl.BlockSpec((8, HEAD), lambda i: (0, 0)))
    count = (last - first) * step
    return pl.pallas_call(
        functools.partial(adam_kernel, len(squares), len(into)),
        out_shape=shapes,
        grid=(last - first,),
        in_specs=[pl.BlockSpec(memory_space=pltpu.SMEM), full, full, full, half, half]
        + [pl.BlockSpec((8, HEAD), lambda i: (0, 0))] * len(squares)
        + [pl.BlockSpec(memory_space=pl.ANY)] * len(into),
        out_specs=outs,
        input_output_aliases={6 + len(squares) + i: i for i in range(len(into))},
        compiler_params=params_of(24),
        cost_estimate=cost(20 * count * width, 28 * count * width),
        name="adam_rows",
    )(scalars, *in_hbm(*state), *squares, *in_hbm(*into))


def frag_kernel(squares, place_ref, sc_ref, w_ref, m_ref, v_ref, g_ref, *refs):
    blocks, part, _ = w_ref.shape
    factor = clip_factor(refs[:squares])
    inner_ref, *out_refs = refs[squares:]
    for j in range(blocks):
        at = pl.multiple_of((place_ref[1] ^ j) * part, 8)
        old = w_ref[j]
        update, _, _ = adam(old, m_ref[j], v_ref[j], g_ref[pl.ds(at, part), :], factor, sc_ref)
        inner_ref[j] = old - update
        out_refs[j][...] = update.astype(out_refs[j].dtype)


def adam_frag(place, scalars, squares, old, first, second, grad):
    blocks, part, width = old.shape
    smem = pl.BlockSpec(memory_space=pltpu.SMEM)
    vmem = pl.BlockSpec(memory_space=pltpu.VMEM)
    return pl.pallas_call(
        functools.partial(frag_kernel, len(squares)),
        out_shape=[jax.ShapeDtypeStruct(old.shape, jnp.float32)]
        + [jax.ShapeDtypeStruct((part, width), jnp.bfloat16)] * blocks,
        in_specs=[smem, smem] + [vmem] * (4 + len(squares)),
        out_specs=[vmem] * (1 + blocks),
        compiler_params=params_of(12),
        cost_estimate=cost(20 * old.size, 22 * old.size),
        name="adam_frag",
    )(place, scalars, old, first, second, grad, *squares)


def pick_kernel(place_ref, *refs):
    half = len(refs) // 2
    for src_ref, out_ref in zip(refs[:half], refs[half:]):
        out_ref[...] = src_ref[...].reshape(out_ref.shape)


def due_columns(place, part, *arrays):
    blocks = arrays[0].shape[0] // part
    at = (lambda j, p: (p[1] ^ j, p[0])) if blocks > 1 else (lambda j, p: (0, p[0]))
    return pl.pallas_call(
        pick_kernel,
        out_shape=[pltpu.HBM((blocks, part, FRAG_COLS), a.dtype) for a in arrays],
        grid_spec=pltpu.PrefetchScalarGridSpec(
            num_scalar_prefetch=1,
            grid=(blocks,),
            in_specs=[pl.BlockSpec((part, FRAG_COLS), at)] * len(arrays),
            out_specs=[pl.BlockSpec((1, part, FRAG_COLS), lambda j, p: (j, 0, 0))] * len(arrays),
        ),
        compiler_params=params_of(8),
        cost_estimate=cost(0, 8 * blocks * part * FRAG_COLS * len(arrays)),
        name="due_columns",
    )(place, *in_hbm(*arrays))


def duplicate_kernel(*refs):
    half = (len(refs) - 3) // 2
    held, in_sems, out_sems = refs[2 * half:]
    streams = held.shape[1]
    step = held.shape[2]
    places = [(a, i, pl.ds(i * step, step)) for a in range(half) for i in range(streams)]
    fetches = [
        pltpu.make_async_copy(refs[a].at[at], held.at[a, i], in_sems.at[a, i]) for a, i, at in places
    ]
    stores = [
        pltpu.make_async_copy(held.at[a, i], refs[half + a].at[at], out_sems.at[a, i])
        for a, i, at in places
    ]
    for copy in fetches:
        copy.start()
    for fetch, store in zip(fetches, stores):
        fetch.wait()
        store.start()
    for copy in stores:
        copy.wait()


def duplicate(*arrays):
    rows, width = arrays[0].shape
    streams = 4
    whole = pl.BlockSpec(memory_space=pl.ANY)
    return pl.pallas_call(
        duplicate_kernel,
        out_shape=[pltpu.HBM(a.shape, a.dtype) for a in arrays],
        in_specs=[whole] * len(arrays),
        out_specs=[whole] * len(arrays),
        scratch_shapes=[
            pltpu.VMEM((len(arrays), streams, rows // streams, width), arrays[0].dtype),
            pltpu.SemaphoreType.DMA((len(arrays), streams)),
            pltpu.SemaphoreType.DMA((len(arrays), streams)),
        ],
        compiler_params=params_of(8),
        cost_estimate=cost(0, sum(8 * a.size for a in arrays)),
        name="duplicate",
    )(*in_hbm(*arrays))


def outer_kernel(replicas, place_ref, *refs):
    share = 1.0 / replicas
    base_refs, sum_refs = refs[3:3 + replicas], refs[3 + replicas:3 + 2 * replicas]
    inner_ref, a_ref, p_ref, m_ref, own_ref, _, w_out, a_out, m_out = refs[3 + 2 * replicas:]
    scale = share * (1.0 + OUTER_MU) * OUTER_RATE
    for j in range(replicas):

        @pl.when(pl.program_id(0) == j)
        def _():
            fresh = base_refs[j][...] - scale * sum_refs[j][...].astype(jnp.float32)
            w_out[...] = MIX_LOCAL * inner_ref[0] + (1.0 - MIX_LOCAL) * fresh

    @pl.when(pl.program_id(0) == 0)
    def _():
        pseudo = p_ref[...] + share * own_ref[...]
        new_moment = OUTER_MU * m_ref[...] + pseudo
        m_out[...] = new_moment
        a_out[...] = a_ref[...] - OUTER_RATE * (OUTER_MU * new_moment + pseudo)


def outer_step(place, outputs, base, sums, inner, anchor, pseudo, momentum, own_sum, ticket):
    replicas, part = inner.shape[0], inner.shape[1]
    mixed = pl.BlockSpec((part, FRAG_COLS), lambda j, p: (p[1] ^ j, p[0]))
    pieces = pl.BlockSpec((1, part, FRAG_COLS), lambda j, p: (j, 0, 0))
    due = pl.BlockSpec((part, FRAG_COLS), lambda j, p: (0, p[0]))
    plain = pl.BlockSpec((part, FRAG_COLS), lambda j, p: (0, 0))
    whole = pl.BlockSpec(memory_space=pl.ANY)
    return pl.pallas_call(
        functools.partial(outer_kernel, replicas),
        out_shape=[pltpu.HBM(a.shape, a.dtype) for a in outputs],
        grid_spec=pltpu.PrefetchScalarGridSpec(
            num_scalar_prefetch=1,
            grid=(replicas,),
            in_specs=[whole] * 3 + [plain] * (2 * replicas) + [pieces] + [plain] * 4 + [whole],
            out_specs=[mixed, due, due],
        ),
        input_output_aliases={1: 0, 2: 1, 3: 2},
        compiler_params=params_of(12),
        cost_estimate=cost(10 * replicas * part * FRAG_COLS, 20 * replicas * part * FRAG_COLS),
        name="outer_step",
    )(place, *in_hbm(*outputs), *base, *sums, inner, anchor, pseudo, momentum, own_sum, ticket)


def swap(block, axis, offset):
    count = lax.axis_size(axis)
    return lax.ppermute(block, axis, [(i, i ^ offset) for i in range(count)])


def after(value, *others):
    return lax.optimization_barrier((value,) + others)[0]


def by_device(pieces, me):
    count = pieces.shape[0]
    return jnp.stack([lax.dynamic_index_in_dim(pieces, me ^ k, 0, keepdims=False) for k in range(count)])


def body(
    tokens,
    cotangent,
    weights,
    first_moment,
    second_moment,
    anchor,
    momentum,
    due_fragment,
    step_count,
):
    inputs, incoming, params = tokens[0], cotangent[0], weights[0]
    kv_width = incoming.shape[1] // 2
    rows = params.shape[0]
    part = anchor.shape[0]
    replicas = lax.axis_size("rep")
    shards = lax.axis_size("fsdp")
    me = jnp.reshape(lax.axis_index("fsdp"), (1,)).astype(jnp.int32)
    my_rep = lax.axis_index("rep").astype(jnp.int32)
    place = jnp.stack([due_fragment[0], my_rep])
    chips = range(2, shards, 2)
    far = sorted(chips, key=lambda k: (-bin(k).count("1"), k))
    order = [k for k in far[:-2] for k in (k, k + 1)]
    order += far[-2:] + [k + 1 for k in far[-2:]]

    packed = pack(inputs, me, rows, tuple(order[:1]))
    packed |= pack(inputs, me, rows, tuple(order[1:4]))
    packed |= pack(inputs, me, rows, tuple(order[4:]))
    blocks = {k: swap(packed[k], "fsdp", k) for k in order}
    early = packed[order[-1]]
    packed |= pack(inputs, after(me, early), rows, (0, 1))
    blocks[0], blocks[1] = packed[0], swap(packed[1], "fsdp", 1)

    values = {0: incoming[:, kv_width:]}
    for i, k in enumerate(far):
        values[k] = swap(after(values[0], blocks[order[i]]), "fsdp", k)
    for k in range(0, shards, 2):
        values[k + 1] = swap(values[k], "fsdp", 1)

    def to_all(pieces):
        return lax.all_to_all(pieces, "rep", 0, 0, tiled=True)

    steps_now = step_count[0].astype(jnp.float32)
    plan = jnp.minimum(1.0, steps_now / WARMUP) * (
        0.55 + 0.45 * jnp.cos(jnp.pi * steps_now / STEPS_TOTAL)
    )
    rate = PEAK_RATE * plan
    inv_one = 1.0 / (1.0 - jnp.power(BETA_ONE, steps_now))
    inv_two = 1.0 / (1.0 - jnp.power(BETA_TWO, steps_now))
    scalars = jnp.stack([rate, inv_one, inv_two])
    place_early = after(place, early)
    old, old_first, old_second = due_columns(place_early, part, params, first_moment[0], second_moment[0])
    anchor_cols, moment_cols = (c[0] for c in due_columns(place_early, part, anchor, momentum))
    old_sum = jnp.sum(to_all(by_device(old, my_rep)), axis=0)
    pseudo_old = anchor_cols - old_sum / replicas
    base = anchor_cols - OUTER_RATE * (OUTER_MU * (OUTER_MU * moment_cols + pseudo_old) + pseudo_old)
    base = by_device(to_all(jnp.broadcast_to(base[None], (replicas,) + base.shape)), my_rep)
    base = [base[j] for j in range(replicas)]
    anchor_copy, momentum_copy = duplicate(anchor, momentum)
    key_weights = cast_left(after(params, early), kv_width)

    parts, flipped = [], {}
    for k in far + [0]:
        theirs, flipped[k + 1] = partial_keys(blocks[k + 1], key_weights)
        part_k, flipped[k] = partial_keys(blocks[k], key_weights, swap(theirs, "fsdp", 1))
        parts.append(swap(part_k, "fsdp", k) if k else part_k)
    parts[-1] = after(
        parts[-1], *base, anchor_copy, momentum_copy, old_first, old_second, scalars, *values.values()
    )
    keys = {0: key_backward(parts, incoming, 0)}
    for k in far:
        keys[k] = swap(keys[0], "fsdp", k)
    for k in range(0, shards, 2):
        keys[k + 1] = swap(keys[k], "fsdp", 1)

    spread = [0, 1] + [k + odd for k in far for odd in range(2)]
    near, rest = spread[:shards // 2], spread[shards // 2:]
    pick = lambda table, which: [table[k] for k in which]
    (values_first,) = gradient(place, pick(flipped, near), pick(values, near), last=False)
    grad_values, square, due = gradient(place, pick(flipped, rest), pick(values, rest), values_first)
    (keys_first,) = gradient(place, pick(flipped, near), pick(keys, near), last=False)
    grad_keys, square, due = gradient(
        place, pick(flipped, rest), pick(keys, rest), keys_first, square, due
    )

    square = square + swap(square, "fsdp", 1)
    squares = [square] + [swap(square, "fsdp", k) for k in chips]

    state = (params, first_moment[0], second_moment[0], grad_keys, grad_values)
    inner, *update = adam_frag(place, scalars, squares, old, old_first, old_second, due)
    steps = rows // 256
    *results, ticket = adam_rows(scalars, squares, state, 0, steps // 2)
    own_sum = update[0].astype(jnp.float32)
    for k in range(1, replicas):
        own_sum = own_sum + swap(update[k], "rep", k).astype(jnp.float32)
    own_sum, ticket = lax.optimization_barrier((own_sum, ticket))
    sums = [own_sum.astype(jnp.bfloat16)]
    sums += [swap(sums[0], "rep", k) for k in range(1, replicas)]
    results = adam_rows(scalars, squares, state, steps // 2, steps, results)
    weights_out, anchor_out, momentum_out = outer_step(
        place,
        (results[0], anchor_copy, momentum_copy),
        base,
        sums,
        inner,
        anchor_cols,
        pseudo_old,
        moment_cols,
        own_sum,
        ticket,
    )
    plan_out = jnp.reshape(plan, (1,))
    return (
        weights_out[None],
        results[1][None],
        results[2][None],
        anchor_out,
        momentum_out,
        plan_out,
    )


def solution(mesh):
    tokens_spec = P("rep", "fsdp", None)
    outer_spec = P(("fsdp", "rep"), None)
    return jax.shard_map(
        body,
        mesh=mesh,
        in_specs=(tokens_spec,) * 5 + (outer_spec,) * 2 + (P(), P()),
        out_specs=(tokens_spec,) * 3 + (outer_spec,) * 2 + (P(),),
        check_vma=False,
    )
```

```python
import functools

import jax
import jax.numpy as jnp
from jax import lax
from jax.experimental import pallas as pl
from jax.experimental.pallas import tpu as pltpu
from jax.sharding import PartitionSpec as P

HEAD = 128
WARMUP = 2000
STEPS_TOTAL = 100000
FRAG_COLS = 128


BETA_ONE = 0.9
BETA_TWO = 0.95
ADAM_EPS = 1e-08
DECAY = 0.1
PEAK_RATE = 0.0003
CLIP_NORM = 1.0
OUTER_MU = 0.9
OUTER_RATE = 0.7
MIX_LOCAL = 0.5

MIB = 1 << 20


def in_hbm(*arrays):
    return [pltpu.with_memory_space_constraint(a, pltpu.HBM) for a in arrays]


def params_of(limit):
    return pltpu.CompilerParams(vmem_limit_bytes=limit * MIB)


def cost(flops, moved):
    return pl.CostEstimate(flops=int(flops), bytes_accessed=int(moved), transcendentals=0)


def pack_kernel(offsets, me_ref, src_ref, *refs):
    half = len(offsets)
    out_refs, (held, in_sems, out_sems) = refs[:half], refs[half:]
    streams = in_sems.shape[1]
    count, rows = out_refs[0].shape
    step = count // streams
    fetches, stores = [], []
    for i, offset in enumerate(offsets):
        column = pl.multiple_of((me_ref[0] ^ offset) * rows, HEAD)
        for j in range(streams):
            at = pl.ds(j * step, step)
            block = src_ref.at[at, pl.ds(column, rows)]
            fetches.append(pltpu.make_async_copy(block, held.at[i, at], in_sems.at[i, j]))
            stores.append(pltpu.make_async_copy(held.at[i, at], out_refs[i].at[at], out_sems.at[i, j]))
    for copy in fetches:
        copy.start()
    for fetch, store in zip(fetches, stores):
        fetch.wait()
        store.start()
    for copy in stores:
        copy.wait()


def pack(tokens, me, rows, offsets):
    count = tokens.shape[0]
    streams = 4
    whole = pl.BlockSpec(memory_space=pl.ANY)
    outs = pl.pallas_call(
        functools.partial(pack_kernel, offsets),
        out_shape=[pltpu.HBM((count, rows), tokens.dtype)] * len(offsets),
        in_specs=[pl.BlockSpec(memory_space=pltpu.SMEM), whole],
        out_specs=[whole] * len(offsets),
        scratch_shapes=[
            pltpu.VMEM((len(offsets), count, rows), tokens.dtype),
            pltpu.SemaphoreType.DMA((len(offsets), streams)),
            pltpu.SemaphoreType.DMA((len(offsets), streams)),
        ],
        compiler_params=params_of(12),
        cost_estimate=cost(0, 4 * len(offsets) * count * rows),
        name="pack",
    )(me, *in_hbm(tokens))
    return dict(zip(offsets, outs))


def cast_kernel(src_ref, out_ref):
    out_ref[...] = src_ref[...].astype(out_ref.dtype)


def cast_left(array, width):
    rows = array.shape[0]
    block = pl.BlockSpec((256, width), lambda i: (i, 0))
    return pl.pallas_call(
        cast_kernel,
        out_shape=jax.ShapeDtypeStruct((rows, width), jnp.bfloat16),
        grid=(rows // 256,),
        in_specs=[block],
        out_specs=block,
        compiler_params=params_of(8),
        cost_estimate=cost(0, 6 * rows * width),
        name="cast_left",
    )(*in_hbm(array))


def partial_kernel(pieces, *refs):
    x_refs, w_ref, (*add_refs, out_ref, flip_ref) = refs[:pieces], refs[pieces], refs[pieces + 1:]
    x = jnp.concatenate([ref[...] for ref in x_refs], axis=1)
    total = jnp.dot(x, w_ref[...], preferred_element_type=jnp.float32)
    for ref in add_refs:
        total = total + ref[...].astype(jnp.float32)
    out_ref[...] = total.astype(out_ref.dtype)
    step = x_refs[0].shape[1]
    for i, ref in enumerate(x_refs):
        flip_ref[i * step:(i + 1) * step, :] = ref[...].T


def partial_keys(block, key_weights, *others):
    count, rows = block.shape
    width = key_weights.shape[1]
    pieces = 4 if rows % (4 * HEAD) == 0 else 2
    fixed = lambda a: pl.BlockSpec(a.shape, lambda i: (0, 0))
    return pl.pallas_call(
        functools.partial(partial_kernel, pieces),
        out_shape=[
            jax.ShapeDtypeStruct((count, width), jnp.bfloat16),
            jax.ShapeDtypeStruct((rows, count), jnp.bfloat16),
        ],
        grid=(1,),
        in_specs=[pl.BlockSpec((count, rows // pieces), lambda i, c=c: (0, c)) for c in range(pieces)]
        + [fixed(key_weights)]
        + [fixed(o) for o in others],
        out_specs=[
            pl.BlockSpec((count, width), lambda i: (0, 0)),
            pl.BlockSpec((rows, count), lambda i: (0, 0)),
        ],
        compiler_params=params_of(12),
        cost_estimate=cost(2 * count * rows * width, 4 * count * rows),
        name="partial_keys",
    )(*[block] * pieces, key_weights, *others)


def key_kernel(first, *refs):
    *part_refs, cot_ref, out_ref = refs
    count = out_ref.shape[0]
    raw = sum(ref[...].astype(jnp.float32) for ref in part_refs)
    for h in range(raw.shape[1] // HEAD):
        cols = slice(h * HEAD, (h + 1) * HEAD)
        head = raw[:, cols]
        inverse = lax.rsqrt(jnp.mean(head * head, axis=1, keepdims=True) + 1e-06)
        normed = head * inverse
        upper = cot_ref[first:first + count, cols].astype(jnp.float32)
        back = inverse * (upper - normed * jnp.mean(upper * normed, axis=1, keepdims=True))
        out_ref[:, cols] = back.astype(out_ref.dtype)


def key_backward(parts, incoming, first):
    count, width = parts[0].shape
    block = pl.BlockSpec((count, width), lambda i: (0, 0))
    cot = pl.BlockSpec((incoming.shape[0], width), lambda i: (0, 0))
    return pl.pallas_call(
        functools.partial(key_kernel, first),
        out_shape=jax.ShapeDtypeStruct((count, width), jnp.bfloat16),
        grid=(1,),
        in_specs=[block] * len(parts) + [cot],
        out_specs=block,
        compiler_params=params_of(8),
        cost_estimate=cost(60 * count * width, 12 * count * width),
        name="key_backward",
    )(*parts, incoming)


def grad_kernel(count, has_base, has_more, last, place_ref, *refs):
    refs = list(refs)
    x_refs, u_refs = refs[:count], refs[count:2 * count]
    refs = refs[2 * count:]
    base = refs.pop(0) if has_base else None
    square_in, due_in = (refs.pop(0), refs.pop(0)) if has_more else (None, None)
    out_ref = refs.pop(0)
    x = jnp.concatenate([ref[...] for ref in x_refs], axis=1)
    u = jnp.concatenate([ref[...] for ref in u_refs], axis=0)
    total = jnp.dot(x, u, preferred_element_type=jnp.float32)
    if has_base:
        total = total + base[...]
    out_ref[...] = total
    if last:
        sq_ref, due_ref = refs

        @pl.when(pl.program_id(0) == 0)
        def _():
            sq_ref[...] = square_in[...] if has_more else jnp.zeros_like(sq_ref)

        rows, width = total.shape
        squares = (total * total).reshape(rows // 8, 8, width).sum(axis=0)
        folded = squares[:, :HEAD]
        for h in range(1, width // HEAD):
            folded = folded + squares[:, h * HEAD:(h + 1) * HEAD]
        sq_ref[...] += folded
        heads = width // FRAG_COLS
        mine = place_ref[0] - (0 if has_more else heads)
        mine = jnp.minimum(jnp.maximum(mine, 0), heads - 1) * FRAG_COLS
        column = out_ref[:, pl.ds(pl.multiple_of(mine, FRAG_COLS), FRAG_COLS)]
        if has_more:
            column = jnp.where(place_ref[0] < heads, column, due_in[...])
        due_ref[...] = column


def gradient(place, flipped, upstream, base=None, square=None, due=None, last=True):
    rows, depth = flipped[0].shape
    width = upstream[0].shape[1]
    step = 256
    row_block = lambda cols: pl.BlockSpec((step, cols), lambda i, p: (i, 0))
    fixed = pl.BlockSpec((8, HEAD), lambda i, p: (0, 0))
    args = [*flipped, *upstream]
    specs = [row_block(depth)] * len(flipped)
    specs += [pl.BlockSpec((depth, width), lambda i, p: (0, 0))] * len(upstream)
    if base is not None:
        args.append(base)
        specs.append(row_block(width))
    if square is not None:
        args += [square, due]
        specs += [fixed, row_block(FRAG_COLS)]
    if last:
        shapes = [
            pltpu.HBM((rows, width), jnp.float32),
            jax.ShapeDtypeStruct((8, HEAD), jnp.float32),
            jax.ShapeDtypeStruct((rows, FRAG_COLS), jnp.float32),
        ]
        outs = [row_block(width), fixed, row_block(FRAG_COLS)]
    else:
        shapes = [jax.ShapeDtypeStruct((rows, width), jnp.float32)]
        outs = [row_block(width)]
    depth *= len(flipped)
    return pl.pallas_call(
        functools.partial(grad_kernel, len(flipped), base is not None, square is not None, last),
        out_shape=shapes,
        grid_spec=pltpu.PrefetchScalarGridSpec(
            num_scalar_prefetch=1, grid=(rows // step,), in_specs=specs, out_specs=outs
        ),
        compiler_params=params_of(20),
        cost_estimate=cost(2 * rows * width * depth, 2 * rows * depth + 4 * rows * width),
        name="gradient",
    )(place, *args)


def clip_factor(square_refs):
    square = jnp.sum(sum(ref[...] for ref in square_refs), keepdims=True)
    return jnp.minimum(1.0, CLIP_NORM / (jnp.sqrt(square) + 1e-06))


def adam(old, first, second, grad, factor, scalars):
    rate, inv_one, inv_two = (scalars[i] for i in range(3))
    clipped = grad * factor
    first_new = BETA_ONE * first + (1.0 - BETA_ONE) * clipped
    second_new = BETA_TWO * second + (1.0 - BETA_TWO) * clipped * clipped
    update = rate * (
        first_new * inv_one / (jnp.sqrt(second_new * inv_two) + ADAM_EPS) + DECAY * old
    )
    return update, first_new, second_new


def adam_kernel(squares, extra, sc_ref, w_ref, m_ref, v_ref, gk_ref, gv_ref, *refs):
    factor = clip_factor(refs[:squares])
    w_out, m_out, v_out, *done = refs[squares + extra:]
    width = gk_ref.shape[1]
    for g_ref, cols in ((gk_ref, slice(0, width)), (gv_ref, slice(width, 2 * width))):
        old = w_ref[:, cols]
        update, first_new, second_new = adam(
            old, m_ref[:, cols], v_ref[:, cols], g_ref[...], factor, sc_ref
        )
        w_out[:, cols] = old - update
        m_out[:, cols] = first_new
        v_out[:, cols] = second_new
    for ref in done:
        ref[...] = jnp.zeros_like(ref)


def adam_rows(scalars, squares, state, first, last, into=()):
    rows, width = state[0].shape
    step = 256
    full = pl.BlockSpec((step, width), lambda i: (i + first, 0))
    half = pl.BlockSpec((step, width // 2), lambda i: (i + first, 0))
    shapes = [pltpu.HBM((rows, width), jnp.float32)] * 3
    outs = [full] * 3
    if not into:
        shapes.append(jax.ShapeDtypeStruct((8, HEAD), jnp.float32))
        outs.append(pl.BlockSpec((8, HEAD), lambda i: (0, 0)))
    count = (last - first) * step
    return pl.pallas_call(
        functools.partial(adam_kernel, len(squares), len(into)),
        out_shape=shapes,
        grid=(last - first,),
        in_specs=[pl.BlockSpec(memory_space=pltpu.SMEM), full, full, full, half, half]
        + [pl.BlockSpec((8, HEAD), lambda i: (0, 0))] * len(squares)
        + [pl.BlockSpec(memory_space=pl.ANY)] * len(into),
        out_specs=outs,
        input_output_aliases={6 + len(squares) + i: i for i in range(len(into))},
        compiler_params=params_of(24),
        cost_estimate=cost(20 * count * width, 28 * count * width),
        name="adam_rows",
    )(scalars, *in_hbm(*state), *squares, *in_hbm(*into))


def frag_kernel(squares, place_ref, sc_ref, w_ref, m_ref, v_ref, g_ref, *refs):
    blocks, part, _ = w_ref.shape
    factor = clip_factor(refs[:squares])
    inner_ref, *out_refs = refs[squares:]
    for j in range(blocks):
        at = pl.multiple_of((place_ref[1] ^ j) * part, 8)
        old = w_ref[j]
        update, _, _ = adam(old, m_ref[j], v_ref[j], g_ref[pl.ds(at, part), :], factor, sc_ref)
        inner_ref[j] = old - update
        out_refs[j][...] = update.astype(out_refs[j].dtype)


def adam_frag(place, scalars, squares, old, first, second, grad):
    blocks, part, width = old.shape
    smem = pl.BlockSpec(memory_space=pltpu.SMEM)
    vmem = pl.BlockSpec(memory_space=pltpu.VMEM)
    return pl.pallas_call(
        functools.partial(frag_kernel, len(squares)),
        out_shape=[jax.ShapeDtypeStruct(old.shape, jnp.float32)]
        + [jax.ShapeDtypeStruct((part, width), jnp.bfloat16)] * blocks,
        in_specs=[smem, smem] + [vmem] * (4 + len(squares)),
        out_specs=[vmem] * (1 + blocks),
        compiler_params=params_of(12),
        cost_estimate=cost(20 * old.size, 22 * old.size),
        name="adam_frag",
    )(place, scalars, old, first, second, grad, *squares)


def pick_kernel(place_ref, *refs):
    half = len(refs) // 2
    for src_ref, out_ref in zip(refs[:half], refs[half:]):
        out_ref[...] = src_ref[...].reshape(out_ref.shape)


def due_columns(place, part, *arrays):
    blocks = arrays[0].shape[0] // part
    at = (lambda j, p: (p[1] ^ j, p[0])) if blocks > 1 else (lambda j, p: (0, p[0]))
    return pl.pallas_call(
        pick_kernel,
        out_shape=[pltpu.HBM((blocks, part, FRAG_COLS), a.dtype) for a in arrays],
        grid_spec=pltpu.PrefetchScalarGridSpec(
            num_scalar_prefetch=1,
            grid=(blocks,),
            in_specs=[pl.BlockSpec((part, FRAG_COLS), at)] * len(arrays),
            out_specs=[pl.BlockSpec((1, part, FRAG_COLS), lambda j, p: (j, 0, 0))] * len(arrays),
        ),
        compiler_params=params_of(8),
        cost_estimate=cost(0, 8 * blocks * part * FRAG_COLS * len(arrays)),
        name="due_columns",
    )(place, *in_hbm(*arrays))


def duplicate_kernel(*refs):
    half = (len(refs) - 3) // 2
    held, in_sems, out_sems = refs[2 * half:]
    streams = held.shape[1]
    step = held.shape[2]
    places = [(a, i, pl.ds(i * step, step)) for a in range(half) for i in range(streams)]
    fetches = [
        pltpu.make_async_copy(refs[a].at[at], held.at[a, i], in_sems.at[a, i]) for a, i, at in places
    ]
    stores = [
        pltpu.make_async_copy(held.at[a, i], refs[half + a].at[at], out_sems.at[a, i])
        for a, i, at in places
    ]
    for copy in fetches:
        copy.start()
    for fetch, store in zip(fetches, stores):
        fetch.wait()
        store.start()
    for copy in stores:
        copy.wait()


def duplicate(*arrays):
    rows, width = arrays[0].shape
    streams = 4
    whole = pl.BlockSpec(memory_space=pl.ANY)
    return pl.pallas_call(
        duplicate_kernel,
        out_shape=[pltpu.HBM(a.shape, a.dtype) for a in arrays],
        in_specs=[whole] * len(arrays),
        out_specs=[whole] * len(arrays),
        scratch_shapes=[
            pltpu.VMEM((len(arrays), streams, rows // streams, width), arrays[0].dtype),
            pltpu.SemaphoreType.DMA((len(arrays), streams)),
            pltpu.SemaphoreType.DMA((len(arrays), streams)),
        ],
        compiler_params=params_of(8),
        cost_estimate=cost(0, sum(8 * a.size for a in arrays)),
        name="duplicate",
    )(*in_hbm(*arrays))


def outer_kernel(replicas, place_ref, *refs):
    share = 1.0 / replicas
    base_refs, sum_refs = refs[3:3 + replicas], refs[3 + replicas:3 + 2 * replicas]
    inner_ref, a_ref, p_ref, m_ref, own_ref, _, w_out, a_out, m_out = refs[3 + 2 * replicas:]
    scale = share * (1.0 + OUTER_MU) * OUTER_RATE
    for j in range(replicas):

        @pl.when(pl.program_id(0) == j)
        def _():
            fresh = base_refs[j][...] - scale * sum_refs[j][...].astype(jnp.float32)
            w_out[...] = MIX_LOCAL * inner_ref[0] + (1.0 - MIX_LOCAL) * fresh

    @pl.when(pl.program_id(0) == 0)
    def _():
        pseudo = p_ref[...] + share * own_ref[...]
        new_moment = OUTER_MU * m_ref[...] + pseudo
        m_out[...] = new_moment
        a_out[...] = a_ref[...] - OUTER_RATE * (OUTER_MU * new_moment + pseudo)


def outer_step(place, outputs, base, sums, inner, anchor, pseudo, momentum, own_sum, ticket):
    replicas, part = inner.shape[0], inner.shape[1]
    mixed = pl.BlockSpec((part, FRAG_COLS), lambda j, p: (p[1] ^ j, p[0]))
    pieces = pl.BlockSpec((1, part, FRAG_COLS), lambda j, p: (j, 0, 0))
    due = pl.BlockSpec((part, FRAG_COLS), lambda j, p: (0, p[0]))
    plain = pl.BlockSpec((part, FRAG_COLS), lambda j, p: (0, 0))
    whole = pl.BlockSpec(memory_space=pl.ANY)
    return pl.pallas_call(
        functools.partial(outer_kernel, replicas),
        out_shape=[pltpu.HBM(a.shape, a.dtype) for a in outputs],
        grid_spec=pltpu.PrefetchScalarGridSpec(
            num_scalar_prefetch=1,
            grid=(replicas,),
            in_specs=[whole] * 3 + [plain] * (2 * replicas) + [pieces] + [plain] * 4 + [whole],
            out_specs=[mixed, due, due],
        ),
        input_output_aliases={1: 0, 2: 1, 3: 2},
        compiler_params=params_of(12),
        cost_estimate=cost(10 * replicas * part * FRAG_COLS, 20 * replicas * part * FRAG_COLS),
        name="outer_step",
    )(place, *in_hbm(*outputs), *base, *sums, inner, anchor, pseudo, momentum, own_sum, ticket)


def swap(block, axis, offset):
    count = lax.axis_size(axis)
    return lax.ppermute(block, axis, [(i, i ^ offset) for i in range(count)])


def after(value, *others):
    return lax.optimization_barrier((value,) + others)[0]


class Line:
    def __init__(self, axis, window):
        self.axis, self.window, self.ended = axis, window, []

    def swap(self, block, offset):
        if len(self.ended) >= self.window:
            block = after(block, self.ended[-self.window])
        self.ended.append(swap(block, self.axis, offset))
        return self.ended[-1]


def body(
    tokens,
    cotangent,
    weights,
    first_moment,
    second_moment,
    anchor,
    momentum,
    due_fragment,
    step_count,
):
    inputs, incoming, params = tokens[0], cotangent[0], weights[0]
    kv_width = incoming.shape[1] // 2
    rows = params.shape[0]
    part = anchor.shape[0]
    replicas = lax.axis_size("rep")
    shards = lax.axis_size("fsdp")
    me = jnp.reshape(lax.axis_index("fsdp"), (1,)).astype(jnp.int32)
    my_rep = lax.axis_index("rep").astype(jnp.int32)
    place = jnp.stack([due_fragment[0], my_rep])
    chips = range(2, shards, 2)
    far = sorted(chips, key=lambda k: (-bin(k).count("1"), k))
    order = [k for k in far[:-2] for k in (k, k + 1)]
    order += far[-2:] + [k + 1 for k in far[-2:]]

    line = Line("fsdp", 3)
    packed = {}
    for offsets in (order[:1], order[1:4], order[4:]):
        packed |= pack(inputs, me, rows, tuple(offsets))
    blocks = {k: line.swap(packed[k], k) for k in order}
    early = blocks[order[0]]
    packed |= pack(inputs, after(me, early), rows, (0, 1))
    blocks[0], blocks[1] = packed[0], swap(packed[1], "fsdp", 1)

    values = {0: incoming[:, kv_width:]}
    for k in reversed(far):
        values[k] = line.swap(values[0], k)
    for k in range(0, shards, 2):
        values[k + 1] = swap(values[k], "fsdp", 1)

    steps_now = step_count[0].astype(jnp.float32)
    plan = jnp.minimum(1.0, steps_now / WARMUP) * (
        0.55 + 0.45 * jnp.cos(jnp.pi * steps_now / STEPS_TOTAL)
    )
    rate = PEAK_RATE * plan
    inv_one = 1.0 / (1.0 - jnp.power(BETA_ONE, steps_now))
    inv_two = 1.0 / (1.0 - jnp.power(BETA_TWO, steps_now))
    scalars = jnp.stack([rate, inv_one, inv_two])
    place_early = after(place, early)
    (old,) = due_columns(place_early, part, params)
    old_first, old_second = due_columns(place_early, part, first_moment[0], second_moment[0])
    anchor_cols, moment_cols = (c[0] for c in due_columns(place_early, part, anchor, momentum))
    old_sum = sum([swap(old[k], "rep", k) for k in range(1, replicas)], old[0])
    pseudo_old = anchor_cols - old_sum / replicas
    base = anchor_cols - OUTER_RATE * (OUTER_MU * (OUTER_MU * moment_cols + pseudo_old) + pseudo_old)
    base = [base] + [swap(base, "rep", k) for k in range(1, replicas)]
    anchor_copy, momentum_copy = duplicate(anchor, momentum)
    key_weights = cast_left(after(params, early), kv_width)

    parts, flipped = [], {}
    for k in far + [0]:
        theirs, flipped[k + 1] = partial_keys(blocks[k + 1], key_weights)
        part_k, flipped[k] = partial_keys(blocks[k], key_weights, swap(theirs, "fsdp", 1))
        parts.append(swap(part_k, "fsdp", k) if k else part_k)
    spread = [0, 1] + [k + odd for k in far for odd in range(2)]
    near, rest = spread[:shards // 2], spread[shards // 2:]
    pick = lambda table, which: [table[k] for k in which]
    (values_first,) = gradient(place, pick(flipped, near), pick(values, near), last=False)
    parts[-1] = after(
        parts[-1], *base, anchor_copy, momentum_copy, old_first, old_second, scalars, values_first
    )
    keys = {0: key_backward(parts, incoming, 0)}
    for k in far:
        keys[k] = swap(keys[0], "fsdp", k)
    for k in range(0, shards, 2):
        keys[k + 1] = swap(keys[k], "fsdp", 1)

    grad_values, square, due = gradient(place, pick(flipped, rest), pick(values, rest), values_first)
    (keys_first,) = gradient(place, pick(flipped, near), pick(keys, near), last=False)
    grad_keys, square, due = gradient(
        place, pick(flipped, rest), pick(keys, rest), keys_first, square, due
    )

    square = square + swap(square, "fsdp", 1)
    squares = [square] + [swap(square, "fsdp", k) for k in chips]

    state = (params, first_moment[0], second_moment[0], grad_keys, grad_values)
    inner, *update = adam_frag(place, scalars, squares, old, old_first, old_second, due)
    steps = rows // 256
    *results, ticket = adam_rows(scalars, squares, state, 0, steps // 2)
    own_sum = update[0].astype(jnp.float32)
    for k in range(1, replicas):
        own_sum = own_sum + swap(update[k], "rep", k).astype(jnp.float32)
    own_sum, ticket = lax.optimization_barrier((own_sum, ticket))
    sums = [own_sum.astype(jnp.bfloat16)]
    sums += [swap(sums[0], "rep", k) for k in range(1, replicas)]
    results = adam_rows(scalars, squares, state, steps // 2, steps, results)
    weights_out, anchor_out, momentum_out = outer_step(
        place,
        (results[0], anchor_copy, momentum_copy),
        base,
        sums,
        inner,
        anchor_cols,
        pseudo_old,
        moment_cols,
        own_sum,
        ticket,
    )
    plan_out = jnp.reshape(plan, (1,))
    return (
        weights_out[None],
        results[1][None],
        results[2][None],
        anchor_out,
        momentum_out,
        plan_out,
    )


def solution(mesh):
    tokens_spec = P("rep", "fsdp", None)
    outer_spec = P(("fsdp", "rep"), None)
    return jax.shard_map(
        body,
        mesh=mesh,
        in_specs=(tokens_spec,) * 5 + (outer_spec,) * 2 + (P(), P()),
        out_specs=(tokens_spec,) * 3 + (outer_spec,) * 2 + (P(),),
        check_vma=False,
    )
```

```python
import functools

import jax
import jax.numpy as jnp
from jax import lax
from jax.experimental import pallas as pl
from jax.experimental.pallas import tpu as pltpu
from jax.sharding import PartitionSpec as P

HEAD = 128
WARMUP = 2000
STEPS_TOTAL = 100000
FRAG_COLS = 128


BETA_ONE = 0.9
BETA_TWO = 0.95
ADAM_EPS = 1e-08
DECAY = 0.1
PEAK_RATE = 0.0003
CLIP_NORM = 1.0
OUTER_MU = 0.9
OUTER_RATE = 0.7
MIX_LOCAL = 0.5

MIB = 1 << 20


def in_hbm(*arrays):
    return [pltpu.with_memory_space_constraint(a, pltpu.HBM) for a in arrays]


def params_of(limit):
    return pltpu.CompilerParams(vmem_limit_bytes=limit * MIB)


def cost(flops, moved):
    return pl.CostEstimate(flops=int(flops), bytes_accessed=int(moved), transcendentals=0)


def pack_kernel(offsets, me_ref, src_ref, *refs):
    half = len(offsets)
    out_refs, (held, in_sems, out_sems) = refs[:half], refs[half:]
    streams = in_sems.shape[1]
    count, rows = out_refs[0].shape
    step = count // streams
    fetches, stores = [], []
    for i, offset in enumerate(offsets):
        column = pl.multiple_of((me_ref[0] ^ offset) * rows, HEAD)
        for j in range(streams):
            at = pl.ds(j * step, step)
            block = src_ref.at[at, pl.ds(column, rows)]
            fetches.append(pltpu.make_async_copy(block, held.at[i, at], in_sems.at[i, j]))
            stores.append(pltpu.make_async_copy(held.at[i, at], out_refs[i].at[at], out_sems.at[i, j]))
    for copy in fetches:
        copy.start()
    for fetch, store in zip(fetches, stores):
        fetch.wait()
        store.start()
    for copy in stores:
        copy.wait()


def pack(tokens, me, rows, offsets):
    count = tokens.shape[0]
    streams = 4
    whole = pl.BlockSpec(memory_space=pl.ANY)
    outs = pl.pallas_call(
        functools.partial(pack_kernel, offsets),
        out_shape=[pltpu.HBM((count, rows), tokens.dtype)] * len(offsets),
        in_specs=[pl.BlockSpec(memory_space=pltpu.SMEM), whole],
        out_specs=[whole] * len(offsets),
        scratch_shapes=[
            pltpu.VMEM((len(offsets), count, rows), tokens.dtype),
            pltpu.SemaphoreType.DMA((len(offsets), streams)),
            pltpu.SemaphoreType.DMA((len(offsets), streams)),
        ],
        compiler_params=params_of(12),
        cost_estimate=cost(0, 4 * len(offsets) * count * rows),
        name="pack",
    )(me, *in_hbm(tokens))
    return dict(zip(offsets, outs))


def cast_kernel(src_ref, out_ref):
    out_ref[...] = src_ref[...].astype(out_ref.dtype)


def cast_left(array, width):
    rows = array.shape[0]
    block = pl.BlockSpec((256, width), lambda i: (i, 0))
    return pl.pallas_call(
        cast_kernel,
        out_shape=jax.ShapeDtypeStruct((rows, width), jnp.bfloat16),
        grid=(rows // 256,),
        in_specs=[block],
        out_specs=block,
        compiler_params=params_of(8),
        cost_estimate=cost(0, 6 * rows * width),
        name="cast_left",
    )(*in_hbm(array))


def partial_kernel(pieces, *refs):
    x_refs, w_ref, (*add_refs, out_ref, flip_ref) = refs[:pieces], refs[pieces], refs[pieces + 1:]
    x = jnp.concatenate([ref[...] for ref in x_refs], axis=1)
    total = jnp.dot(x, w_ref[...], preferred_element_type=jnp.float32)
    for ref in add_refs:
        total = total + ref[...].astype(jnp.float32)
    out_ref[...] = total.astype(out_ref.dtype)
    step = x_refs[0].shape[1]
    for i, ref in enumerate(x_refs):
        flip_ref[i * step:(i + 1) * step, :] = ref[...].T


def partial_keys(block, key_weights, *others):
    count, rows = block.shape
    width = key_weights.shape[1]
    pieces = 4 if rows % (4 * HEAD) == 0 else 2
    fixed = lambda a: pl.BlockSpec(a.shape, lambda i: (0, 0))
    return pl.pallas_call(
        functools.partial(partial_kernel, pieces),
        out_shape=[
            jax.ShapeDtypeStruct((count, width), jnp.bfloat16),
            jax.ShapeDtypeStruct((rows, count), jnp.bfloat16),
        ],
        grid=(1,),
        in_specs=[pl.BlockSpec((count, rows // pieces), lambda i, c=c: (0, c)) for c in range(pieces)]
        + [fixed(key_weights)]
        + [fixed(o) for o in others],
        out_specs=[
            pl.BlockSpec((count, width), lambda i: (0, 0)),
            pl.BlockSpec((rows, count), lambda i: (0, 0)),
        ],
        compiler_params=params_of(12),
        cost_estimate=cost(2 * count * rows * width, 4 * count * rows),
        name="partial_keys",
    )(*[block] * pieces, key_weights, *others)


def key_kernel(first, *refs):
    *part_refs, cot_ref, out_ref = refs
    count = out_ref.shape[0]
    raw = sum(ref[...].astype(jnp.float32) for ref in part_refs)
    for h in range(raw.shape[1] // HEAD):
        cols = slice(h * HEAD, (h + 1) * HEAD)
        head = raw[:, cols]
        inverse = lax.rsqrt(jnp.mean(head * head, axis=1, keepdims=True) + 1e-06)
        normed = head * inverse
        upper = cot_ref[first:first + count, cols].astype(jnp.float32)
        back = inverse * (upper - normed * jnp.mean(upper * normed, axis=1, keepdims=True))
        out_ref[:, cols] = back.astype(out_ref.dtype)


def key_backward(parts, incoming, first):
    count, width = parts[0].shape
    block = pl.BlockSpec((count, width), lambda i: (0, 0))
    cot = pl.BlockSpec((incoming.shape[0], width), lambda i: (0, 0))
    return pl.pallas_call(
        functools.partial(key_kernel, first),
        out_shape=jax.ShapeDtypeStruct((count, width), jnp.bfloat16),
        grid=(1,),
        in_specs=[block] * len(parts) + [cot],
        out_specs=block,
        compiler_params=params_of(8),
        cost_estimate=cost(60 * count * width, 12 * count * width),
        name="key_backward",
    )(*parts, incoming)


def grad_kernel(count, has_base, has_more, last, place_ref, *refs):
    refs = list(refs)
    x_refs, u_refs = refs[:count], refs[count:2 * count]
    refs = refs[2 * count:]
    base = refs.pop(0) if has_base else None
    square_in, due_in = (refs.pop(0), refs.pop(0)) if has_more else (None, None)
    out_ref = refs.pop(0)
    x = jnp.concatenate([ref[...] for ref in x_refs], axis=1)
    u = jnp.concatenate([ref[...] for ref in u_refs], axis=0)
    total = jnp.dot(x, u, preferred_element_type=jnp.float32)
    if has_base:
        total = total + base[...]
    out_ref[...] = total
    if last:
        sq_ref, due_ref = refs

        @pl.when(pl.program_id(0) == 0)
        def _():
            sq_ref[...] = square_in[...] if has_more else jnp.zeros_like(sq_ref)

        rows, width = total.shape
        squares = (total * total).reshape(rows // 8, 8, width).sum(axis=0)
        folded = squares[:, :HEAD]
        for h in range(1, width // HEAD):
            folded = folded + squares[:, h * HEAD:(h + 1) * HEAD]
        sq_ref[...] += folded
        heads = width // FRAG_COLS
        mine = place_ref[0] - (0 if has_more else heads)
        mine = jnp.minimum(jnp.maximum(mine, 0), heads - 1) * FRAG_COLS
        column = out_ref[:, pl.ds(pl.multiple_of(mine, FRAG_COLS), FRAG_COLS)]
        if has_more:
            column = jnp.where(place_ref[0] < heads, column, due_in[...])
        due_ref[...] = column


def gradient(place, flipped, upstream, base=None, square=None, due=None, last=True):
    rows, depth = flipped[0].shape
    width = upstream[0].shape[1]
    step = 256
    row_block = lambda cols: pl.BlockSpec((step, cols), lambda i, p: (i, 0))
    fixed = pl.BlockSpec((8, HEAD), lambda i, p: (0, 0))
    args = [*flipped, *upstream]
    specs = [row_block(depth)] * len(flipped)
    specs += [pl.BlockSpec((depth, width), lambda i, p: (0, 0))] * len(upstream)
    if base is not None:
        args.append(base)
        specs.append(row_block(width))
    if square is not None:
        args += [square, due]
        specs += [fixed, row_block(FRAG_COLS)]
    if last:
        shapes = [
            pltpu.HBM((rows, width), jnp.float32),
            jax.ShapeDtypeStruct((8, HEAD), jnp.float32),
            jax.ShapeDtypeStruct((rows, FRAG_COLS), jnp.float32),
        ]
        outs = [row_block(width), fixed, row_block(FRAG_COLS)]
    else:
        shapes = [jax.ShapeDtypeStruct((rows, width), jnp.float32)]
        outs = [row_block(width)]
    depth *= len(flipped)
    return pl.pallas_call(
        functools.partial(grad_kernel, len(flipped), base is not None, square is not None, last),
        out_shape=shapes,
        grid_spec=pltpu.PrefetchScalarGridSpec(
            num_scalar_prefetch=1, grid=(rows // step,), in_specs=specs, out_specs=outs
        ),
        compiler_params=params_of(20),
        cost_estimate=cost(2 * rows * width * depth, 2 * rows * depth + 4 * rows * width),
        name="gradient",
    )(place, *args)


def clip_factor(square_refs):
    square = jnp.sum(sum(ref[...] for ref in square_refs), keepdims=True)
    return jnp.minimum(1.0, CLIP_NORM / (jnp.sqrt(square) + 1e-06))


def adam(old, first, second, grad, factor, scalars):
    rate, inv_one, inv_two = (scalars[i] for i in range(3))
    clipped = grad * factor
    first_new = BETA_ONE * first + (1.0 - BETA_ONE) * clipped
    second_new = BETA_TWO * second + (1.0 - BETA_TWO) * clipped * clipped
    update = rate * (
        first_new * inv_one / (jnp.sqrt(second_new * inv_two) + ADAM_EPS) + DECAY * old
    )
    return update, first_new, second_new


def adam_kernel(squares, extra, sc_ref, w_ref, m_ref, v_ref, gk_ref, gv_ref, *refs):
    factor = clip_factor(refs[:squares])
    w_out, m_out, v_out, *done = refs[squares + extra:]
    width = gk_ref.shape[1]
    for g_ref, cols in ((gk_ref, slice(0, width)), (gv_ref, slice(width, 2 * width))):
        old = w_ref[:, cols]
        update, first_new, second_new = adam(
            old, m_ref[:, cols], v_ref[:, cols], g_ref[...], factor, sc_ref
        )
        w_out[:, cols] = old - update
        m_out[:, cols] = first_new
        v_out[:, cols] = second_new
    for ref in done:
        ref[...] = jnp.zeros_like(ref)


def adam_rows(scalars, squares, state, first, last, into=()):
    rows, width = state[0].shape
    step = 256
    full = pl.BlockSpec((step, width), lambda i: (i + first, 0))
    half = pl.BlockSpec((step, width // 2), lambda i: (i + first, 0))
    shapes = [pltpu.HBM((rows, width), jnp.float32)] * 3
    outs = [full] * 3
    if not into:
        shapes.append(jax.ShapeDtypeStruct((8, HEAD), jnp.float32))
        outs.append(pl.BlockSpec((8, HEAD), lambda i: (0, 0)))
    count = (last - first) * step
    return pl.pallas_call(
        functools.partial(adam_kernel, len(squares), len(into)),
        out_shape=shapes,
        grid=(last - first,),
        in_specs=[pl.BlockSpec(memory_space=pltpu.SMEM), full, full, full, half, half]
        + [pl.BlockSpec((8, HEAD), lambda i: (0, 0))] * len(squares)
        + [pl.BlockSpec(memory_space=pl.ANY)] * len(into),
        out_specs=outs,
        input_output_aliases={6 + len(squares) + i: i for i in range(len(into))},
        compiler_params=params_of(24),
        cost_estimate=cost(20 * count * width, 28 * count * width),
        name="adam_rows",
    )(scalars, *in_hbm(*state), *squares, *in_hbm(*into))


def frag_kernel(squares, place_ref, sc_ref, w_ref, m_ref, v_ref, g_ref, *refs):
    blocks, part, _ = w_ref.shape
    factor = clip_factor(refs[:squares])
    inner_ref, *out_refs = refs[squares:]
    for j in range(blocks):
        at = pl.multiple_of((place_ref[1] ^ j) * part, 8)
        old = w_ref[j]
        update, _, _ = adam(old, m_ref[j], v_ref[j], g_ref[pl.ds(at, part), :], factor, sc_ref)
        inner_ref[j] = old - update
        out_refs[j][...] = update.astype(out_refs[j].dtype)


def adam_frag(place, scalars, squares, old, first, second, grad):
    blocks, part, width = old.shape
    smem = pl.BlockSpec(memory_space=pltpu.SMEM)
    vmem = pl.BlockSpec(memory_space=pltpu.VMEM)
    return pl.pallas_call(
        functools.partial(frag_kernel, len(squares)),
        out_shape=[jax.ShapeDtypeStruct(old.shape, jnp.float32)]
        + [jax.ShapeDtypeStruct((part, width), jnp.bfloat16)] * blocks,
        in_specs=[smem, smem] + [vmem] * (4 + len(squares)),
        out_specs=[vmem] * (1 + blocks),
        compiler_params=params_of(12),
        cost_estimate=cost(20 * old.size, 22 * old.size),
        name="adam_frag",
    )(place, scalars, old, first, second, grad, *squares)


def pick_kernel(blocks, place_ref, *refs):
    outs = refs[len(refs) // (blocks + 1) * blocks:]
    for i, out_ref in enumerate(outs):
        for j in range(blocks):
            out_ref[j] = refs[i * blocks + j][...]


def due_columns(place, part, *arrays):
    blocks = arrays[0].shape[0] // part
    specs = []
    for j in range(blocks):
        at = (lambda i, p, j=j: (p[1] ^ j, p[0])) if blocks > 1 else (lambda i, p: (0, p[0]))
        specs.append(pl.BlockSpec((part, FRAG_COLS), at))
    shape = (blocks, part, FRAG_COLS)
    return pl.pallas_call(
        functools.partial(pick_kernel, blocks),
        out_shape=[jax.ShapeDtypeStruct(shape, a.dtype) for a in arrays],
        grid_spec=pltpu.PrefetchScalarGridSpec(
            num_scalar_prefetch=1,
            grid=(1,),
            in_specs=specs * len(arrays),
            out_specs=[pl.BlockSpec(shape, lambda i, p: (0, 0, 0))] * len(arrays),
        ),
        compiler_params=params_of(12),
        cost_estimate=cost(0, 8 * blocks * part * FRAG_COLS * len(arrays)),
        name="due_columns",
    )(place, *[a for array in in_hbm(*arrays) for a in [array] * blocks])


def duplicate_kernel(*refs):
    half = (len(refs) - 3) // 2
    held, in_sems, out_sems = refs[2 * half:]
    streams = held.shape[1]
    step = held.shape[2]
    places = [(a, i, pl.ds(i * step, step)) for a in range(half) for i in range(streams)]
    fetches = [
        pltpu.make_async_copy(refs[a].at[at], held.at[a, i], in_sems.at[a, i]) for a, i, at in places
    ]
    stores = [
        pltpu.make_async_copy(held.at[a, i], refs[half + a].at[at], out_sems.at[a, i])
        for a, i, at in places
    ]
    for copy in fetches:
        copy.start()
    for fetch, store in zip(fetches, stores):
        fetch.wait()
        store.start()
    for copy in stores:
        copy.wait()


def duplicate(*arrays):
    rows, width = arrays[0].shape
    streams = 4
    whole = pl.BlockSpec(memory_space=pl.ANY)
    return pl.pallas_call(
        duplicate_kernel,
        out_shape=[pltpu.HBM(a.shape, a.dtype) for a in arrays],
        in_specs=[whole] * len(arrays),
        out_specs=[whole] * len(arrays),
        scratch_shapes=[
            pltpu.VMEM((len(arrays), streams, rows // streams, width), arrays[0].dtype),
            pltpu.SemaphoreType.DMA((len(arrays), streams)),
            pltpu.SemaphoreType.DMA((len(arrays), streams)),
        ],
        compiler_params=params_of(8),
        cost_estimate=cost(0, sum(8 * a.size for a in arrays)),
        name="duplicate",
    )(*in_hbm(*arrays))


def outer_kernel(replicas, place_ref, *refs):
    share = 1.0 / replicas
    base_refs, sum_refs = refs[3:3 + replicas], refs[3 + replicas:3 + 2 * replicas]
    inner_ref, a_ref, p_ref, m_ref, own_ref, _, w_out, a_out, m_out = refs[3 + 2 * replicas:]
    scale = share * (1.0 + OUTER_MU) * OUTER_RATE
    for j in range(replicas):

        @pl.when(pl.program_id(0) == j)
        def _():
            fresh = base_refs[j][...] - scale * sum_refs[j][...].astype(jnp.float32)
            w_out[...] = MIX_LOCAL * inner_ref[0] + (1.0 - MIX_LOCAL) * fresh

    @pl.when(pl.program_id(0) == 0)
    def _():
        pseudo = p_ref[...] + share * own_ref[...]
        new_moment = OUTER_MU * m_ref[...] + pseudo
        m_out[...] = new_moment
        a_out[...] = a_ref[...] - OUTER_RATE * (OUTER_MU * new_moment + pseudo)


def outer_step(place, outputs, base, sums, inner, anchor, pseudo, momentum, own_sum, ticket):
    replicas, part = inner.shape[0], inner.shape[1]
    mixed = pl.BlockSpec((part, FRAG_COLS), lambda j, p: (p[1] ^ j, p[0]))
    pieces = pl.BlockSpec((1, part, FRAG_COLS), lambda j, p: (j, 0, 0))
    due = pl.BlockSpec((part, FRAG_COLS), lambda j, p: (0, p[0]))
    plain = pl.BlockSpec((part, FRAG_COLS), lambda j, p: (0, 0))
    whole = pl.BlockSpec(memory_space=pl.ANY)
    return pl.pallas_call(
        functools.partial(outer_kernel, replicas),
        out_shape=[pltpu.HBM(a.shape, a.dtype) for a in outputs],
        grid_spec=pltpu.PrefetchScalarGridSpec(
            num_scalar_prefetch=1,
            grid=(replicas,),
            in_specs=[whole] * 3 + [plain] * (2 * replicas) + [pieces] + [plain] * 4 + [whole],
            out_specs=[mixed, due, due],
        ),
        input_output_aliases={1: 0, 2: 1, 3: 2},
        compiler_params=params_of(12),
        cost_estimate=cost(10 * replicas * part * FRAG_COLS, 20 * replicas * part * FRAG_COLS),
        name="outer_step",
    )(place, *in_hbm(*outputs), *base, *sums, inner, anchor, pseudo, momentum, own_sum, ticket)


def swap(block, axis, offset):
    count = lax.axis_size(axis)
    return lax.ppermute(block, axis, [(i, i ^ offset) for i in range(count)])


def after(value, *others):
    return lax.optimization_barrier((value,) + others)[0]


def body(
    tokens,
    cotangent,
    weights,
    first_moment,
    second_moment,
    anchor,
    momentum,
    due_fragment,
    step_count,
):
    inputs, incoming, params = tokens[0], cotangent[0], weights[0]
    kv_width = incoming.shape[1] // 2
    rows = params.shape[0]
    part = anchor.shape[0]
    replicas = lax.axis_size("rep")
    shards = lax.axis_size("fsdp")
    me = jnp.reshape(lax.axis_index("fsdp"), (1,)).astype(jnp.int32)
    my_rep = lax.axis_index("rep").astype(jnp.int32)
    place = jnp.stack([due_fragment[0], my_rep])
    chips = range(2, shards, 2)
    far = sorted(chips, key=lambda k: (-bin(k).count("1"), k))
    order = [k for k in far[:-2] for k in (k, k + 1)]
    order += far[-2:] + [k + 1 for k in far[-2:]]

    (old,) = due_columns(place, part, params)
    old_sums = [old[0]] + [swap(old[k], "rep", k) for k in range(1, replicas)]

    packed = {}
    for offsets in (order[:1], order[1:4], order[4:], (0, 1)):
        packed |= pack(inputs, me, rows, tuple(offsets))
    blocks = {k: swap(packed[k], "fsdp", k) for k in order}
    blocks[0], blocks[1] = packed[0], swap(packed[1], "fsdp", 1)

    values = {0: incoming[:, kv_width:]}
    for i, k in enumerate(far):
        values[k] = swap(after(values[0], blocks[order[i]]), "fsdp", k)
    for k in range(0, shards, 2):
        values[k + 1] = swap(values[k], "fsdp", 1)

    steps_now = step_count[0].astype(jnp.float32)
    plan = jnp.minimum(1.0, steps_now / WARMUP) * (
        0.55 + 0.45 * jnp.cos(jnp.pi * steps_now / STEPS_TOTAL)
    )
    rate = PEAK_RATE * plan
    inv_one = 1.0 / (1.0 - jnp.power(BETA_ONE, steps_now))
    inv_two = 1.0 / (1.0 - jnp.power(BETA_TWO, steps_now))
    scalars = jnp.stack([rate, inv_one, inv_two])
    old_first, old_second = due_columns(place, part, first_moment[0], second_moment[0])
    anchor_cols, moment_cols = (c[0] for c in due_columns(place, part, anchor, momentum))
    pseudo_old = anchor_cols - sum(old_sums[1:], old_sums[0]) / replicas
    base = anchor_cols - OUTER_RATE * (OUTER_MU * (OUTER_MU * moment_cols + pseudo_old) + pseudo_old)
    base = [base] + [swap(base, "rep", k) for k in range(1, replicas)]
    anchor_copy, momentum_copy = duplicate(anchor, momentum)
    key_weights = cast_left(params, kv_width)

    last = far[-1]
    blocks[last + 1] = after(blocks[last + 1], *base, anchor_copy, momentum_copy, scalars)
    parts, flipped = [], {}
    for k in far + [0]:
        theirs, flipped[k + 1] = partial_keys(blocks[k + 1], key_weights)
        theirs = swap(theirs, "fsdp", 1)
        if k == last:
            theirs = after(theirs, *parts[:1])
        part_k, flipped[k] = partial_keys(blocks[k], key_weights, theirs)
        parts.append(swap(part_k, "fsdp", k) if k else part_k)
    spread = [0, 1] + [k + odd for k in far for odd in range(2)]
    near, rest = spread[:shards // 2], spread[shards // 2:]
    pick = lambda table, which: [table[k] for k in which]
    (values_first,) = gradient(place, pick(flipped, near), pick(values, near), last=False)
    parts[-1] = after(parts[-1], values_first)
    keys = {0: key_backward(parts, incoming, 0)}
    for k in far:
        keys[k] = swap(keys[0], "fsdp", k)
    for k in range(0, shards, 2):
        keys[k + 1] = swap(keys[k], "fsdp", 1)

    grad_values, square, due = gradient(
        after(place, old_first, old_second), pick(flipped, rest), pick(values, rest), values_first
    )
    (keys_first,) = gradient(place, pick(flipped, near), pick(keys, near), last=False)
    grad_keys, square, due = gradient(
        place, pick(flipped, rest), pick(keys, rest), keys_first, square, due
    )

    square = square + swap(square, "fsdp", 1)
    squares = [square] + [swap(square, "fsdp", k) for k in chips]

    state = (params, first_moment[0], second_moment[0], grad_keys, grad_values)
    inner, *update = adam_frag(place, scalars, squares, old, old_first, old_second, due)
    steps = rows // 256
    *results, ticket = adam_rows(scalars, squares, state, 0, steps // 2)
    own_sum = update[0].astype(jnp.float32)
    for k in range(1, replicas):
        own_sum = own_sum + swap(update[k], "rep", k).astype(jnp.float32)
    own_sum, ticket = lax.optimization_barrier((own_sum, ticket))
    sums = [own_sum.astype(jnp.bfloat16)]
    sums += [swap(sums[0], "rep", k) for k in range(1, replicas)]
    results = adam_rows(scalars, squares, state, steps // 2, steps, results)
    weights_out, anchor_out, momentum_out = outer_step(
        place,
        (results[0], anchor_copy, momentum_copy),
        base,
        sums,
        inner,
        anchor_cols,
        pseudo_old,
        moment_cols,
        own_sum,
        ticket,
    )
    plan_out = jnp.reshape(plan, (1,))
    return (
        weights_out[None],
        results[1][None],
        results[2][None],
        anchor_out,
        momentum_out,
        plan_out,
    )


def solution(mesh):
    tokens_spec = P("rep", "fsdp", None)
    outer_spec = P(("fsdp", "rep"), None)
    return jax.shard_map(
        body,
        mesh=mesh,
        in_specs=(tokens_spec,) * 5 + (outer_spec,) * 2 + (P(), P()),
        out_specs=(tokens_spec,) * 3 + (outer_spec,) * 2 + (P(),),
        check_vma=False,
    )
```

```python
import functools

import jax
import jax.numpy as jnp
from jax import lax
from jax.experimental import pallas as pl
from jax.experimental.pallas import tpu as pltpu
from jax.sharding import PartitionSpec as P

HEAD = 128
WARMUP = 2000
STEPS_TOTAL = 100000
FRAG_COLS = 128


BETA_ONE = 0.9
BETA_TWO = 0.95
ADAM_EPS = 1e-08
DECAY = 0.1
PEAK_RATE = 0.0003
CLIP_NORM = 1.0
OUTER_MU = 0.9
OUTER_RATE = 0.7
MIX_LOCAL = 0.5

MIB = 1 << 20


def in_hbm(*arrays):
    return [pltpu.with_memory_space_constraint(a, pltpu.HBM) for a in arrays]


def params_of(limit):
    return pltpu.CompilerParams(vmem_limit_bytes=limit * MIB)


def cost(flops, moved):
    return pl.CostEstimate(flops=int(flops), bytes_accessed=int(moved), transcendentals=0)


def pack_kernel(offsets, me_ref, src_ref, *refs):
    half = len(offsets)
    out_refs, (held, in_sems, out_sems) = refs[:half], refs[half:]
    streams = in_sems.shape[1]
    count, rows = out_refs[0].shape
    step = count // streams
    fetches, stores = [], []
    for i, offset in enumerate(offsets):
        column = pl.multiple_of((me_ref[0] ^ offset) * rows, HEAD)
        for j in range(streams):
            at = pl.ds(j * step, step)
            block = src_ref.at[at, pl.ds(column, rows)]
            fetches.append(pltpu.make_async_copy(block, held.at[i, at], in_sems.at[i, j]))
            stores.append(pltpu.make_async_copy(held.at[i, at], out_refs[i].at[at], out_sems.at[i, j]))
    for copy in fetches:
        copy.start()
    for fetch, store in zip(fetches, stores):
        fetch.wait()
        store.start()
    for copy in stores:
        copy.wait()


def pack(tokens, me, rows, offsets):
    count = tokens.shape[0]
    streams = 4
    whole = pl.BlockSpec(memory_space=pl.ANY)
    outs = pl.pallas_call(
        functools.partial(pack_kernel, offsets),
        out_shape=[pltpu.HBM((count, rows), tokens.dtype)] * len(offsets),
        in_specs=[pl.BlockSpec(memory_space=pltpu.SMEM), whole],
        out_specs=[whole] * len(offsets),
        scratch_shapes=[
            pltpu.VMEM((len(offsets), count, rows), tokens.dtype),
            pltpu.SemaphoreType.DMA((len(offsets), streams)),
            pltpu.SemaphoreType.DMA((len(offsets), streams)),
        ],
        compiler_params=params_of(12),
        cost_estimate=cost(0, 4 * len(offsets) * count * rows),
        name="pack",
    )(me, *in_hbm(tokens))
    return dict(zip(offsets, outs))


def cast_kernel(src_ref, out_ref):
    out_ref[...] = src_ref[...].astype(out_ref.dtype)


def cast_left(array, width):
    rows = array.shape[0]
    block = pl.BlockSpec((256, width), lambda i: (i, 0))
    return pl.pallas_call(
        cast_kernel,
        out_shape=jax.ShapeDtypeStruct((rows, width), jnp.bfloat16),
        grid=(rows // 256,),
        in_specs=[block],
        out_specs=block,
        compiler_params=params_of(8),
        cost_estimate=cost(0, 6 * rows * width),
        name="cast_left",
    )(*in_hbm(array))


def partial_kernel(pieces, *refs):
    x_refs, w_ref, (*add_refs, out_ref, flip_ref) = refs[:pieces], refs[pieces], refs[pieces + 1:]
    x = jnp.concatenate([ref[...] for ref in x_refs], axis=1)
    total = jnp.dot(x, w_ref[...], preferred_element_type=jnp.float32)
    for ref in add_refs:
        total = total + ref[...].astype(jnp.float32)
    out_ref[...] = total.astype(out_ref.dtype)
    step = x_refs[0].shape[1]
    for i, ref in enumerate(x_refs):
        flip_ref[i * step:(i + 1) * step, :] = ref[...].T


def partial_keys(block, key_weights, *others):
    count, rows = block.shape
    width = key_weights.shape[1]
    pieces = 4 if rows % (4 * HEAD) == 0 else 2
    fixed = lambda a: pl.BlockSpec(a.shape, lambda i: (0, 0))
    return pl.pallas_call(
        functools.partial(partial_kernel, pieces),
        out_shape=[
            jax.ShapeDtypeStruct((count, width), jnp.bfloat16),
            jax.ShapeDtypeStruct((rows, count), jnp.bfloat16),
        ],
        grid=(1,),
        in_specs=[pl.BlockSpec((count, rows // pieces), lambda i, c=c: (0, c)) for c in range(pieces)]
        + [fixed(key_weights)]
        + [fixed(o) for o in others],
        out_specs=[
            pl.BlockSpec((count, width), lambda i: (0, 0)),
            pl.BlockSpec((rows, count), lambda i: (0, 0)),
        ],
        compiler_params=params_of(12),
        cost_estimate=cost(2 * count * rows * width, 4 * count * rows),
        name="partial_keys",
    )(*[block] * pieces, key_weights, *others)


def key_kernel(first, *refs):
    *part_refs, cot_ref, out_ref = refs
    count = out_ref.shape[0]
    raw = sum(ref[...].astype(jnp.float32) for ref in part_refs)
    for h in range(raw.shape[1] // HEAD):
        cols = slice(h * HEAD, (h + 1) * HEAD)
        head = raw[:, cols]
        inverse = lax.rsqrt(jnp.mean(head * head, axis=1, keepdims=True) + 1e-06)
        normed = head * inverse
        upper = cot_ref[first:first + count, cols].astype(jnp.float32)
        back = inverse * (upper - normed * jnp.mean(upper * normed, axis=1, keepdims=True))
        out_ref[:, cols] = back.astype(out_ref.dtype)


def key_backward(parts, incoming, first):
    count, width = parts[0].shape
    block = pl.BlockSpec((count, width), lambda i: (0, 0))
    cot = pl.BlockSpec((incoming.shape[0], width), lambda i: (0, 0))
    return pl.pallas_call(
        functools.partial(key_kernel, first),
        out_shape=jax.ShapeDtypeStruct((count, width), jnp.bfloat16),
        grid=(1,),
        in_specs=[block] * len(parts) + [cot],
        out_specs=block,
        compiler_params=params_of(8),
        cost_estimate=cost(60 * count * width, 12 * count * width),
        name="key_backward",
    )(*parts, incoming)


def grad_kernel(count, has_base, has_more, last, place_ref, *refs):
    refs = list(refs)
    x_refs, u_refs = refs[:count], refs[count:2 * count]
    refs = refs[2 * count:]
    base = refs.pop(0) if has_base else None
    square_in, due_in = (refs.pop(0), refs.pop(0)) if has_more else (None, None)
    out_ref = refs.pop(0)
    x = jnp.concatenate([ref[...] for ref in x_refs], axis=1)
    u = jnp.concatenate([ref[...] for ref in u_refs], axis=0)
    total = jnp.dot(x, u, preferred_element_type=jnp.float32)
    if has_base:
        total = total + base[...]
    out_ref[...] = total
    if last:
        sq_ref, due_ref = refs

        @pl.when(pl.program_id(0) == 0)
        def _():
            sq_ref[...] = square_in[...] if has_more else jnp.zeros_like(sq_ref)

        rows, width = total.shape
        squares = (total * total).reshape(rows // 8, 8, width).sum(axis=0)
        folded = squares[:, :HEAD]
        for h in range(1, width // HEAD):
            folded = folded + squares[:, h * HEAD:(h + 1) * HEAD]
        sq_ref[...] += folded
        heads = width // FRAG_COLS
        mine = place_ref[0] - (0 if has_more else heads)
        mine = jnp.minimum(jnp.maximum(mine, 0), heads - 1) * FRAG_COLS
        column = out_ref[:, pl.ds(pl.multiple_of(mine, FRAG_COLS), FRAG_COLS)]
        if has_more:
            column = jnp.where(place_ref[0] < heads, column, due_in[...])
        due_ref[...] = column


def gradient(place, flipped, upstream, base=None, square=None, due=None, last=True):
    rows, depth = flipped[0].shape
    width = upstream[0].shape[1]
    step = 256
    row_block = lambda cols: pl.BlockSpec((step, cols), lambda i, p: (i, 0))
    fixed = pl.BlockSpec((8, HEAD), lambda i, p: (0, 0))
    args = [*flipped, *upstream]
    specs = [row_block(depth)] * len(flipped)
    specs += [pl.BlockSpec((depth, width), lambda i, p: (0, 0))] * len(upstream)
    if base is not None:
        args.append(base)
        specs.append(row_block(width))
    if square is not None:
        args += [square, due]
        specs += [fixed, row_block(FRAG_COLS)]
    if last:
        shapes = [
            pltpu.HBM((rows, width), jnp.float32),
            jax.ShapeDtypeStruct((8, HEAD), jnp.float32),
            jax.ShapeDtypeStruct((rows, FRAG_COLS), jnp.float32),
        ]
        outs = [row_block(width), fixed, row_block(FRAG_COLS)]
    else:
        shapes = [jax.ShapeDtypeStruct((rows, width), jnp.float32)]
        outs = [row_block(width)]
    depth *= len(flipped)
    return pl.pallas_call(
        functools.partial(grad_kernel, len(flipped), base is not None, square is not None, last),
        out_shape=shapes,
        grid_spec=pltpu.PrefetchScalarGridSpec(
            num_scalar_prefetch=1, grid=(rows // step,), in_specs=specs, out_specs=outs
        ),
        compiler_params=params_of(20),
        cost_estimate=cost(2 * rows * width * depth, 2 * rows * depth + 4 * rows * width),
        name="gradient",
    )(place, *args)


def clip_factor(square_refs):
    square = jnp.sum(sum(ref[...] for ref in square_refs), keepdims=True)
    return jnp.minimum(1.0, CLIP_NORM / (jnp.sqrt(square) + 1e-06))


def adam(old, first, second, grad, factor, scalars):
    rate, inv_one, inv_two = (scalars[i] for i in range(3))
    clipped = grad * factor
    first_new = BETA_ONE * first + (1.0 - BETA_ONE) * clipped
    second_new = BETA_TWO * second + (1.0 - BETA_TWO) * clipped * clipped
    update = rate * (
        first_new * inv_one / (jnp.sqrt(second_new * inv_two) + ADAM_EPS) + DECAY * old
    )
    return update, first_new, second_new


def adam_kernel(squares, extra, sc_ref, w_ref, m_ref, v_ref, gk_ref, gv_ref, *refs):
    factor = clip_factor(refs[:squares])
    w_out, m_out, v_out, *done = refs[squares + extra:]
    width = gk_ref.shape[1]
    for g_ref, cols in ((gk_ref, slice(0, width)), (gv_ref, slice(width, 2 * width))):
        old = w_ref[:, cols]
        update, first_new, second_new = adam(
            old, m_ref[:, cols], v_ref[:, cols], g_ref[...], factor, sc_ref
        )
        w_out[:, cols] = old - update
        m_out[:, cols] = first_new
        v_out[:, cols] = second_new
    for ref in done:
        ref[...] = jnp.zeros_like(ref)


def adam_rows(scalars, squares, state, first, last, into=()):
    rows, width = state[0].shape
    step = 256
    full = pl.BlockSpec((step, width), lambda i: (i + first, 0))
    half = pl.BlockSpec((step, width // 2), lambda i: (i + first, 0))
    shapes = [pltpu.HBM((rows, width), jnp.float32)] * 3
    outs = [full] * 3
    if not into:
        shapes.append(jax.ShapeDtypeStruct((8, HEAD), jnp.float32))
        outs.append(pl.BlockSpec((8, HEAD), lambda i: (0, 0)))
    count = (last - first) * step
    return pl.pallas_call(
        functools.partial(adam_kernel, len(squares), len(into)),
        out_shape=shapes,
        grid=(last - first,),
        in_specs=[pl.BlockSpec(memory_space=pltpu.SMEM), full, full, full, half, half]
        + [pl.BlockSpec((8, HEAD), lambda i: (0, 0))] * len(squares)
        + [pl.BlockSpec(memory_space=pl.ANY)] * len(into),
        out_specs=outs,
        input_output_aliases={6 + len(squares) + i: i for i in range(len(into))},
        compiler_params=params_of(24),
        cost_estimate=cost(20 * count * width, 28 * count * width),
        name="adam_rows",
    )(scalars, *in_hbm(*state), *squares, *in_hbm(*into))


def frag_kernel(squares, place_ref, sc_ref, w_ref, m_ref, v_ref, g_ref, *refs):
    blocks, part, _ = w_ref.shape
    factor = clip_factor(refs[:squares])
    inner_ref, *out_refs = refs[squares:]
    for j in range(blocks):
        at = pl.multiple_of((place_ref[1] ^ j) * part, 8)
        old = w_ref[j]
        update, _, _ = adam(old, m_ref[j], v_ref[j], g_ref[pl.ds(at, part), :], factor, sc_ref)
        inner_ref[j] = old - update
        out_refs[j][...] = update.astype(out_refs[j].dtype)


def adam_frag(place, scalars, squares, old, first, second, grad):
    blocks, part, width = old.shape
    smem = pl.BlockSpec(memory_space=pltpu.SMEM)
    vmem = pl.BlockSpec(memory_space=pltpu.VMEM)
    return pl.pallas_call(
        functools.partial(frag_kernel, len(squares)),
        out_shape=[jax.ShapeDtypeStruct(old.shape, jnp.float32)]
        + [jax.ShapeDtypeStruct((part, width), jnp.bfloat16)] * blocks,
        in_specs=[smem, smem] + [vmem] * (4 + len(squares)),
        out_specs=[vmem] * (1 + blocks),
        compiler_params=params_of(12),
        cost_estimate=cost(20 * old.size, 22 * old.size),
        name="adam_frag",
    )(place, scalars, old, first, second, grad, *squares)


def pick_kernel(blocks, place_ref, *refs):
    outs = refs[len(refs) // (blocks + 1) * blocks:]
    for i, out_ref in enumerate(outs):
        for j in range(blocks):
            out_ref[j] = refs[i * blocks + j][...]


def due_columns(place, part, *arrays):
    blocks = arrays[0].shape[0] // part
    specs = []
    for j in range(blocks):
        at = (lambda i, p, j=j: (p[1] ^ j, p[0])) if blocks > 1 else (lambda i, p: (0, p[0]))
        specs.append(pl.BlockSpec((part, FRAG_COLS), at))
    shape = (blocks, part, FRAG_COLS)
    return pl.pallas_call(
        functools.partial(pick_kernel, blocks),
        out_shape=[jax.ShapeDtypeStruct(shape, a.dtype) for a in arrays],
        grid_spec=pltpu.PrefetchScalarGridSpec(
            num_scalar_prefetch=1,
            grid=(1,),
            in_specs=specs * len(arrays),
            out_specs=[pl.BlockSpec(shape, lambda i, p: (0, 0, 0))] * len(arrays),
        ),
        compiler_params=params_of(12),
        cost_estimate=cost(0, 8 * blocks * part * FRAG_COLS * len(arrays)),
        name="due_columns",
    )(place, *[a for array in in_hbm(*arrays) for a in [array] * blocks])


def duplicate_kernel(*refs):
    half = (len(refs) - 3) // 2
    held, in_sems, out_sems = refs[2 * half:]
    streams = held.shape[1]
    step = held.shape[2]
    places = [(a, i, pl.ds(i * step, step)) for a in range(half) for i in range(streams)]
    fetches = [
        pltpu.make_async_copy(refs[a].at[at], held.at[a, i], in_sems.at[a, i]) for a, i, at in places
    ]
    stores = [
        pltpu.make_async_copy(held.at[a, i], refs[half + a].at[at], out_sems.at[a, i])
        for a, i, at in places
    ]
    for copy in fetches:
        copy.start()
    for fetch, store in zip(fetches, stores):
        fetch.wait()
        store.start()
    for copy in stores:
        copy.wait()


def duplicate(*arrays):
    rows, width = arrays[0].shape
    streams = 4
    whole = pl.BlockSpec(memory_space=pl.ANY)
    return pl.pallas_call(
        duplicate_kernel,
        out_shape=[pltpu.HBM(a.shape, a.dtype) for a in arrays],
        in_specs=[whole] * len(arrays),
        out_specs=[whole] * len(arrays),
        scratch_shapes=[
            pltpu.VMEM((len(arrays), streams, rows // streams, width), arrays[0].dtype),
            pltpu.SemaphoreType.DMA((len(arrays), streams)),
            pltpu.SemaphoreType.DMA((len(arrays), streams)),
        ],
        compiler_params=params_of(8),
        cost_estimate=cost(0, sum(8 * a.size for a in arrays)),
        name="duplicate",
    )(*in_hbm(*arrays))


def outer_kernel(replicas, place_ref, *refs):
    share = 1.0 / replicas
    base_refs, sum_refs = refs[3:3 + replicas], refs[3 + replicas:3 + 2 * replicas]
    inner_ref, a_ref, p_ref, m_ref, own_ref, _, w_out, a_out, m_out = refs[3 + 2 * replicas:]
    scale = share * (1.0 + OUTER_MU) * OUTER_RATE
    for j in range(replicas):

        @pl.when(pl.program_id(0) == j)
        def _():
            fresh = base_refs[j][...] - scale * sum_refs[j][...].astype(jnp.float32)
            w_out[...] = MIX_LOCAL * inner_ref[0] + (1.0 - MIX_LOCAL) * fresh

    @pl.when(pl.program_id(0) == 0)
    def _():
        pseudo = p_ref[...] + share * own_ref[...]
        new_moment = OUTER_MU * m_ref[...] + pseudo
        m_out[...] = new_moment
        a_out[...] = a_ref[...] - OUTER_RATE * (OUTER_MU * new_moment + pseudo)


def outer_step(place, outputs, base, sums, inner, anchor, pseudo, momentum, own_sum, ticket):
    replicas, part = inner.shape[0], inner.shape[1]
    mixed = pl.BlockSpec((part, FRAG_COLS), lambda j, p: (p[1] ^ j, p[0]))
    pieces = pl.BlockSpec((1, part, FRAG_COLS), lambda j, p: (j, 0, 0))
    due = pl.BlockSpec((part, FRAG_COLS), lambda j, p: (0, p[0]))
    plain = pl.BlockSpec((part, FRAG_COLS), lambda j, p: (0, 0))
    whole = pl.BlockSpec(memory_space=pl.ANY)
    return pl.pallas_call(
        functools.partial(outer_kernel, replicas),
        out_shape=[pltpu.HBM(a.shape, a.dtype) for a in outputs],
        grid_spec=pltpu.PrefetchScalarGridSpec(
            num_scalar_prefetch=1,
            grid=(replicas,),
            in_specs=[whole] * 3 + [plain] * (2 * replicas) + [pieces] + [plain] * 4 + [whole],
            out_specs=[mixed, due, due],
        ),
        input_output_aliases={1: 0, 2: 1, 3: 2},
        compiler_params=params_of(12),
        cost_estimate=cost(10 * replicas * part * FRAG_COLS, 20 * replicas * part * FRAG_COLS),
        name="outer_step",
    )(place, *in_hbm(*outputs), *base, *sums, inner, anchor, pseudo, momentum, own_sum, ticket)


def swap(block, axis, offset):
    count = lax.axis_size(axis)
    return lax.ppermute(block, axis, [(i, i ^ offset) for i in range(count)])


def after(value, *others):
    return lax.optimization_barrier((value,) + others)[0]


def body(
    tokens,
    cotangent,
    weights,
    first_moment,
    second_moment,
    anchor,
    momentum,
    due_fragment,
    step_count,
):
    inputs, incoming, params = tokens[0], cotangent[0], weights[0]
    kv_width = incoming.shape[1] // 2
    rows = params.shape[0]
    part = anchor.shape[0]
    replicas = lax.axis_size("rep")
    shards = lax.axis_size("fsdp")
    me = jnp.reshape(lax.axis_index("fsdp"), (1,)).astype(jnp.int32)
    my_rep = lax.axis_index("rep").astype(jnp.int32)
    place = jnp.stack([due_fragment[0], my_rep])
    chips = range(2, shards, 2)
    far = sorted(chips, key=lambda k: (-bin(k).count("1"), k))
    order = [k for k in far[:-2] for k in (k, k + 1)]
    order += far[-2:] + [k + 1 for k in far[-2:]]

    (old,) = due_columns(place, part, params)
    old_sums = [old[0]] + [swap(old[k], "rep", k) for k in range(1, replicas)]

    packed = {}
    for offsets in (order[:1], order[1:4], order[4:], (0, 1)):
        packed |= pack(inputs, me, rows, tuple(offsets))
    blocks = {k: swap(packed[k], "fsdp", k) for k in order}
    blocks[0], blocks[1] = packed[0], swap(packed[1], "fsdp", 1)

    values = {0: incoming[:, kv_width:]}
    for i, k in enumerate(far):
        values[k] = swap(after(values[0], blocks[order[i]]), "fsdp", k)
    for k in range(0, shards, 2):
        values[k + 1] = swap(values[k], "fsdp", 1)

    steps_now = step_count[0].astype(jnp.float32)
    plan = jnp.minimum(1.0, steps_now / WARMUP) * (
        0.55 + 0.45 * jnp.cos(jnp.pi * steps_now / STEPS_TOTAL)
    )
    rate = PEAK_RATE * plan
    inv_one = 1.0 / (1.0 - jnp.power(BETA_ONE, steps_now))
    inv_two = 1.0 / (1.0 - jnp.power(BETA_TWO, steps_now))
    scalars = jnp.stack([rate, inv_one, inv_two])
    old_first, old_second = due_columns(place, part, first_moment[0], second_moment[0])
    anchor_cols, moment_cols = (c[0] for c in due_columns(place, part, anchor, momentum))
    pseudo_old = anchor_cols - sum(old_sums[1:], old_sums[0]) / replicas
    base = anchor_cols - OUTER_RATE * (OUTER_MU * (OUTER_MU * moment_cols + pseudo_old) + pseudo_old)
    base = [base] + [swap(base, "rep", k) for k in range(1, replicas)]
    anchor_copy, momentum_copy = duplicate(anchor, momentum)
    key_weights = cast_left(params, kv_width)

    last = far[-1]
    blocks[last + 1] = after(blocks[last + 1], anchor_copy, momentum_copy, scalars, old_first, old_second)
    parts, flipped = [], {}
    for k in far + [0]:
        theirs, flipped[k + 1] = partial_keys(blocks[k + 1], key_weights)
        theirs = swap(theirs, "fsdp", 1)
        if k == last:
            theirs = after(theirs, *parts[:1], *base)
        part_k, flipped[k] = partial_keys(blocks[k], key_weights, theirs)
        parts.append(swap(part_k, "fsdp", k) if k else part_k)
    spread = [0, 1] + [k + odd for k in far for odd in range(2)]
    near, rest = spread[:shards // 2], spread[shards // 2:]
    pick = lambda table, which: [table[k] for k in which]
    (values_first,) = gradient(place, pick(flipped, near), pick(values, near), last=False)
    parts[-1] = after(parts[-1], values_first)
    keys = {0: key_backward(parts, incoming, 0)}
    for k in far:
        keys[k] = swap(keys[0], "fsdp", k)
    keys[1] = swap(keys[0], "fsdp", 1)

    grad_values, square, due = gradient(
        place, pick(flipped, rest), pick(values, rest), values_first
    )
    for k in near[2::2]:
        keys[k + 1] = swap(after(keys[k], square), "fsdp", 1)
    (keys_first,) = gradient(place, pick(flipped, near), pick(keys, near), last=False)
    for k in rest[::2]:
        keys[k + 1] = swap(after(keys[k], keys_first), "fsdp", 1)
    grad_keys, square, due = gradient(
        place, pick(flipped, rest), pick(keys, rest), keys_first, square, due
    )

    square = square + swap(square, "fsdp", 1)
    squares = [square] + [swap(square, "fsdp", k) for k in chips]

    state = (params, first_moment[0], second_moment[0], grad_keys, grad_values)
    inner, *update = adam_frag(place, scalars, squares, old, old_first, old_second, due)
    steps = rows // 256
    *results, ticket = adam_rows(scalars, squares, state, 0, steps // 2)
    own_sum = update[0].astype(jnp.float32)
    for k in range(1, replicas):
        own_sum = own_sum + swap(update[k], "rep", k).astype(jnp.float32)
    own_sum, ticket = lax.optimization_barrier((own_sum, ticket))
    sums = [own_sum.astype(jnp.bfloat16)]
    sums += [swap(sums[0], "rep", k) for k in range(1, replicas)]
    results = adam_rows(scalars, squares, state, steps // 2, steps, results)
    weights_out, anchor_out, momentum_out = outer_step(
        place,
        (results[0], anchor_copy, momentum_copy),
        base,
        sums,
        inner,
        anchor_cols,
        pseudo_old,
        moment_cols,
        own_sum,
        ticket,
    )
    plan_out = jnp.reshape(plan, (1,))
    return (
        weights_out[None],
        results[1][None],
        results[2][None],
        anchor_out,
        momentum_out,
        plan_out,
    )


def solution(mesh):
    tokens_spec = P("rep", "fsdp", None)
    outer_spec = P(("fsdp", "rep"), None)
    return jax.shard_map(
        body,
        mesh=mesh,
        in_specs=(tokens_spec,) * 5 + (outer_spec,) * 2 + (P(), P()),
        out_specs=(tokens_spec,) * 3 + (outer_spec,) * 2 + (P(),),
        check_vma=False,
    )
```

```python
import functools

import jax
import jax.numpy as jnp
from jax import lax
from jax.experimental import pallas as pl
from jax.experimental.pallas import tpu as pltpu
from jax.sharding import PartitionSpec as P

HEAD = 128
WARMUP = 2000
STEPS_TOTAL = 100000
FRAG_COLS = 128


BETA_ONE = 0.9
BETA_TWO = 0.95
ADAM_EPS = 1e-08
DECAY = 0.1
PEAK_RATE = 0.0003
CLIP_NORM = 1.0
OUTER_MU = 0.9
OUTER_RATE = 0.7
MIX_LOCAL = 0.5

MIB = 1 << 20


def in_hbm(*arrays):
    return [pltpu.with_memory_space_constraint(a, pltpu.HBM) for a in arrays]


def params_of(limit):
    return pltpu.CompilerParams(vmem_limit_bytes=limit * MIB)


def cost(flops, moved):
    return pl.CostEstimate(flops=int(flops), bytes_accessed=int(moved), transcendentals=0)


def pack_kernel(offsets, me_ref, src_ref, *refs):
    half = len(offsets)
    out_refs, (held, in_sems, out_sems) = refs[:half], refs[half:]
    streams = in_sems.shape[1]
    count, rows = out_refs[0].shape
    step = count // streams
    fetches, stores = [], []
    for i, offset in enumerate(offsets):
        column = pl.multiple_of((me_ref[0] ^ offset) * rows, HEAD)
        for j in range(streams):
            at = pl.ds(j * step, step)
            block = src_ref.at[at, pl.ds(column, rows)]
            fetches.append(pltpu.make_async_copy(block, held.at[i, at], in_sems.at[i, j]))
            stores.append(pltpu.make_async_copy(held.at[i, at], out_refs[i].at[at], out_sems.at[i, j]))
    for copy in fetches:
        copy.start()
    for fetch, store in zip(fetches, stores):
        fetch.wait()
        store.start()
    for copy in stores:
        copy.wait()


def pack(tokens, me, rows, offsets):
    count = tokens.shape[0]
    streams = 4
    whole = pl.BlockSpec(memory_space=pl.ANY)
    outs = pl.pallas_call(
        functools.partial(pack_kernel, offsets),
        out_shape=[pltpu.HBM((count, rows), tokens.dtype)] * len(offsets),
        in_specs=[pl.BlockSpec(memory_space=pltpu.SMEM), whole],
        out_specs=[whole] * len(offsets),
        scratch_shapes=[
            pltpu.VMEM((len(offsets), count, rows), tokens.dtype),
            pltpu.SemaphoreType.DMA((len(offsets), streams)),
            pltpu.SemaphoreType.DMA((len(offsets), streams)),
        ],
        compiler_params=params_of(12),
        cost_estimate=cost(0, 4 * len(offsets) * count * rows),
        name="pack",
    )(me, *in_hbm(tokens))
    return dict(zip(offsets, outs))


def cast_kernel(src_ref, out_ref):
    out_ref[...] = src_ref[...].astype(out_ref.dtype)


def cast_left(array, width):
    rows = array.shape[0]
    block = pl.BlockSpec((256, width), lambda i: (i, 0))
    return pl.pallas_call(
        cast_kernel,
        out_shape=jax.ShapeDtypeStruct((rows, width), jnp.bfloat16),
        grid=(rows // 256,),
        in_specs=[block],
        out_specs=block,
        compiler_params=params_of(8),
        cost_estimate=cost(0, 6 * rows * width),
        name="cast_left",
    )(*in_hbm(array))


def partial_kernel(pieces, *refs):
    x_refs, w_ref, (*add_refs, out_ref, flip_ref) = refs[:pieces], refs[pieces], refs[pieces + 1:]
    x = jnp.concatenate([ref[...] for ref in x_refs], axis=1)
    total = jnp.dot(x, w_ref[...], preferred_element_type=jnp.float32)
    for ref in add_refs:
        total = total + ref[...].astype(jnp.float32)
    out_ref[...] = total.astype(out_ref.dtype)
    step = x_refs[0].shape[1]
    for i, ref in enumerate(x_refs):
        flip_ref[i * step:(i + 1) * step, :] = ref[...].T


def partial_keys(block, key_weights, *others):
    count, rows = block.shape
    width = key_weights.shape[1]
    pieces = 4 if rows % (4 * HEAD) == 0 else 2
    fixed = lambda a: pl.BlockSpec(a.shape, lambda i: (0, 0))
    return pl.pallas_call(
        functools.partial(partial_kernel, pieces),
        out_shape=[
            jax.ShapeDtypeStruct((count, width), jnp.bfloat16),
            jax.ShapeDtypeStruct((rows, count), jnp.bfloat16),
        ],
        grid=(1,),
        in_specs=[pl.BlockSpec((count, rows // pieces), lambda i, c=c: (0, c)) for c in range(pieces)]
        + [fixed(key_weights)]
        + [fixed(o) for o in others],
        out_specs=[
            pl.BlockSpec((count, width), lambda i: (0, 0)),
            pl.BlockSpec((rows, count), lambda i: (0, 0)),
        ],
        compiler_params=params_of(12),
        cost_estimate=cost(2 * count * rows * width, 4 * count * rows),
        name="partial_keys",
    )(*[block] * pieces, key_weights, *others)


def key_kernel(first, *refs):
    *part_refs, cot_ref, out_ref = refs
    count = out_ref.shape[0]
    raw = sum(ref[...].astype(jnp.float32) for ref in part_refs)
    for h in range(raw.shape[1] // HEAD):
        cols = slice(h * HEAD, (h + 1) * HEAD)
        head = raw[:, cols]
        inverse = lax.rsqrt(jnp.mean(head * head, axis=1, keepdims=True) + 1e-06)
        normed = head * inverse
        upper = cot_ref[first:first + count, cols].astype(jnp.float32)
        back = inverse * (upper - normed * jnp.mean(upper * normed, axis=1, keepdims=True))
        out_ref[:, cols] = back.astype(out_ref.dtype)


def key_backward(parts, incoming, first):
    count, width = parts[0].shape
    block = pl.BlockSpec((count, width), lambda i: (0, 0))
    cot = pl.BlockSpec((incoming.shape[0], width), lambda i: (0, 0))
    return pl.pallas_call(
        functools.partial(key_kernel, first),
        out_shape=jax.ShapeDtypeStruct((count, width), jnp.bfloat16),
        grid=(1,),
        in_specs=[block] * len(parts) + [cot],
        out_specs=block,
        compiler_params=params_of(8),
        cost_estimate=cost(60 * count * width, 12 * count * width),
        name="key_backward",
    )(*parts, incoming)


def grad_kernel(count, has_base, has_more, last, place_ref, *refs):
    refs = list(refs)
    x_refs, u_refs = refs[:count], refs[count:2 * count]
    refs = refs[2 * count:]
    base = refs.pop(0) if has_base else None
    square_in, due_in = (refs.pop(0), refs.pop(0)) if has_more else (None, None)
    out_ref = refs.pop(0)
    x = jnp.concatenate([ref[...] for ref in x_refs], axis=1)
    u = jnp.concatenate([ref[...] for ref in u_refs], axis=0)
    total = jnp.dot(x, u, preferred_element_type=jnp.float32)
    if has_base:
        total = total + base[...]
    out_ref[...] = total
    if last:
        sq_ref, due_ref = refs

        @pl.when(pl.program_id(0) == 0)
        def _():
            sq_ref[...] = square_in[...] if has_more else jnp.zeros_like(sq_ref)

        rows, width = total.shape
        squares = (total * total).reshape(rows // 8, 8, width).sum(axis=0)
        folded = squares[:, :HEAD]
        for h in range(1, width // HEAD):
            folded = folded + squares[:, h * HEAD:(h + 1) * HEAD]
        sq_ref[...] += folded
        heads = width // FRAG_COLS
        mine = place_ref[0] - (0 if has_more else heads)
        mine = jnp.minimum(jnp.maximum(mine, 0), heads - 1) * FRAG_COLS
        column = out_ref[:, pl.ds(pl.multiple_of(mine, FRAG_COLS), FRAG_COLS)]
        if has_more:
            column = jnp.where(place_ref[0] < heads, column, due_in[...])
        due_ref[...] = column


def gradient(place, flipped, upstream, base=None, square=None, due=None, last=True):
    rows, depth = flipped[0].shape
    width = upstream[0].shape[1]
    step = 256
    row_block = lambda cols: pl.BlockSpec((step, cols), lambda i, p: (i, 0))
    fixed = pl.BlockSpec((8, HEAD), lambda i, p: (0, 0))
    args = [*flipped, *upstream]
    specs = [row_block(depth)] * len(flipped)
    specs += [pl.BlockSpec((depth, width), lambda i, p: (0, 0))] * len(upstream)
    if base is not None:
        args.append(base)
        specs.append(row_block(width))
    if square is not None:
        args += [square, due]
        specs += [fixed, row_block(FRAG_COLS)]
    if last:
        shapes = [
            pltpu.HBM((rows, width), jnp.float32),
            jax.ShapeDtypeStruct((8, HEAD), jnp.float32),
            jax.ShapeDtypeStruct((rows, FRAG_COLS), jnp.float32),
        ]
        outs = [row_block(width), fixed, row_block(FRAG_COLS)]
    else:
        shapes = [jax.ShapeDtypeStruct((rows, width), jnp.float32)]
        outs = [row_block(width)]
    depth *= len(flipped)
    return pl.pallas_call(
        functools.partial(grad_kernel, len(flipped), base is not None, square is not None, last),
        out_shape=shapes,
        grid_spec=pltpu.PrefetchScalarGridSpec(
            num_scalar_prefetch=1, grid=(rows // step,), in_specs=specs, out_specs=outs
        ),
        compiler_params=params_of(20),
        cost_estimate=cost(2 * rows * width * depth, 2 * rows * depth + 4 * rows * width),
        name="gradient",
    )(place, *args)


def clip_factor(square_refs):
    square = jnp.sum(sum(ref[...] for ref in square_refs), keepdims=True)
    return jnp.minimum(1.0, CLIP_NORM / (jnp.sqrt(square) + 1e-06))


def adam(old, first, second, grad, factor, scalars):
    rate, inv_one, inv_two = (scalars[i] for i in range(3))
    clipped = grad * factor
    first_new = BETA_ONE * first + (1.0 - BETA_ONE) * clipped
    second_new = BETA_TWO * second + (1.0 - BETA_TWO) * clipped * clipped
    update = rate * (
        first_new * inv_one / (jnp.sqrt(second_new * inv_two) + ADAM_EPS) + DECAY * old
    )
    return update, first_new, second_new


def adam_kernel(squares, extra, sc_ref, w_ref, m_ref, v_ref, gk_ref, gv_ref, *refs):
    factor = clip_factor(refs[:squares])
    w_out, m_out, v_out, *done = refs[squares + extra:]
    width = gk_ref.shape[1]
    for g_ref, cols in ((gk_ref, slice(0, width)), (gv_ref, slice(width, 2 * width))):
        old = w_ref[:, cols]
        update, first_new, second_new = adam(
            old, m_ref[:, cols], v_ref[:, cols], g_ref[...], factor, sc_ref
        )
        w_out[:, cols] = old - update
        m_out[:, cols] = first_new
        v_out[:, cols] = second_new
    for ref in done:
        ref[...] = jnp.zeros_like(ref)


def adam_rows(scalars, squares, state, first, last, into=()):
    rows, width = state[0].shape
    step = 256
    full = pl.BlockSpec((step, width), lambda i: (i + first, 0))
    half = pl.BlockSpec((step, width // 2), lambda i: (i + first, 0))
    shapes = [pltpu.HBM((rows, width), jnp.float32)] * 3
    outs = [full] * 3
    if not into:
        shapes.append(jax.ShapeDtypeStruct((8, HEAD), jnp.float32))
        outs.append(pl.BlockSpec((8, HEAD), lambda i: (0, 0)))
    count = (last - first) * step
    return pl.pallas_call(
        functools.partial(adam_kernel, len(squares), len(into)),
        out_shape=shapes,
        grid=(last - first,),
        in_specs=[pl.BlockSpec(memory_space=pltpu.SMEM), full, full, full, half, half]
        + [pl.BlockSpec((8, HEAD), lambda i: (0, 0))] * len(squares)
        + [pl.BlockSpec(memory_space=pl.ANY)] * len(into),
        out_specs=outs,
        input_output_aliases={6 + len(squares) + i: i for i in range(len(into))},
        compiler_params=params_of(24),
        cost_estimate=cost(20 * count * width, 28 * count * width),
        name="adam_rows",
    )(scalars, *state[:3], *in_hbm(*state[3:]), *squares, *in_hbm(*into))


def frag_kernel(squares, place_ref, sc_ref, w_ref, m_ref, v_ref, g_ref, *refs):
    blocks, part, _ = w_ref.shape
    factor = clip_factor(refs[:squares])
    inner_ref, *out_refs = refs[squares:]
    for j in range(blocks):
        at = pl.multiple_of((place_ref[1] ^ j) * part, 8)
        old = w_ref[j]
        update, _, _ = adam(old, m_ref[j], v_ref[j], g_ref[pl.ds(at, part), :], factor, sc_ref)
        inner_ref[j] = old - update
        out_refs[j][...] = update.astype(out_refs[j].dtype)


def adam_frag(place, scalars, squares, old, first, second, grad):
    blocks, part, width = old.shape
    smem = pl.BlockSpec(memory_space=pltpu.SMEM)
    vmem = pl.BlockSpec(memory_space=pltpu.VMEM)
    return pl.pallas_call(
        functools.partial(frag_kernel, len(squares)),
        out_shape=[jax.ShapeDtypeStruct(old.shape, jnp.float32)]
        + [jax.ShapeDtypeStruct((part, width), jnp.bfloat16)] * blocks,
        in_specs=[smem, smem] + [vmem] * (4 + len(squares)),
        out_specs=[vmem] * (1 + blocks),
        compiler_params=params_of(12),
        cost_estimate=cost(20 * old.size, 22 * old.size),
        name="adam_frag",
    )(place, scalars, old, first, second, grad, *squares)


def pick_kernel(blocks, place_ref, *refs):
    outs = refs[len(refs) // (blocks + 1) * blocks:]
    for i, out_ref in enumerate(outs):
        for j in range(blocks):
            out_ref[j] = refs[i * blocks + j][...]


def due_columns(place, part, *arrays):
    blocks = arrays[0].shape[0] // part
    specs = []
    for j in range(blocks):
        at = (lambda i, p, j=j: (p[1] ^ j, p[0])) if blocks > 1 else (lambda i, p: (0, p[0]))
        specs.append(pl.BlockSpec((part, FRAG_COLS), at))
    shape = (blocks, part, FRAG_COLS)
    return pl.pallas_call(
        functools.partial(pick_kernel, blocks),
        out_shape=[jax.ShapeDtypeStruct(shape, a.dtype) for a in arrays],
        grid_spec=pltpu.PrefetchScalarGridSpec(
            num_scalar_prefetch=1,
            grid=(1,),
            in_specs=specs * len(arrays),
            out_specs=[pl.BlockSpec(shape, lambda i, p: (0, 0, 0))] * len(arrays),
        ),
        compiler_params=params_of(12),
        cost_estimate=cost(0, 8 * blocks * part * FRAG_COLS * len(arrays)),
        name="due_columns",
    )(place, *[a for array in in_hbm(*arrays) for a in [array] * blocks])


def duplicate_kernel(*refs):
    half = (len(refs) - 3) // 2
    held, in_sems, out_sems = refs[2 * half:]
    streams = held.shape[1]
    step = held.shape[2]
    places = [(a, i, pl.ds(i * step, step)) for a in range(half) for i in range(streams)]
    fetches = [
        pltpu.make_async_copy(refs[a].at[at], held.at[a, i], in_sems.at[a, i]) for a, i, at in places
    ]
    stores = [
        pltpu.make_async_copy(held.at[a, i], refs[half + a].at[at], out_sems.at[a, i])
        for a, i, at in places
    ]
    for copy in fetches:
        copy.start()
    for fetch, store in zip(fetches, stores):
        fetch.wait()
        store.start()
    for copy in stores:
        copy.wait()


def duplicate(*arrays):
    rows, width = arrays[0].shape
    streams = 4
    whole = pl.BlockSpec(memory_space=pl.ANY)
    return pl.pallas_call(
        duplicate_kernel,
        out_shape=[pltpu.HBM(a.shape, a.dtype) for a in arrays],
        in_specs=[whole] * len(arrays),
        out_specs=[whole] * len(arrays),
        scratch_shapes=[
            pltpu.VMEM((len(arrays), streams, rows // streams, width), arrays[0].dtype),
            pltpu.SemaphoreType.DMA((len(arrays), streams)),
            pltpu.SemaphoreType.DMA((len(arrays), streams)),
        ],
        compiler_params=params_of(8),
        cost_estimate=cost(0, sum(8 * a.size for a in arrays)),
        name="duplicate",
    )(*in_hbm(*arrays))


def outer_kernel(replicas, place_ref, *refs):
    share = 1.0 / replicas
    base_refs, sum_refs = refs[3:3 + replicas], refs[3 + replicas:3 + 2 * replicas]
    inner_ref, a_ref, p_ref, m_ref, own_ref, _, w_out, a_out, m_out = refs[3 + 2 * replicas:]
    scale = share * (1.0 + OUTER_MU) * OUTER_RATE
    for j in range(replicas):

        @pl.when(pl.program_id(0) == j)
        def _():
            fresh = base_refs[j][...] - scale * sum_refs[j][...].astype(jnp.float32)
            w_out[...] = MIX_LOCAL * inner_ref[0] + (1.0 - MIX_LOCAL) * fresh

    @pl.when(pl.program_id(0) == 0)
    def _():
        pseudo = p_ref[...] + share * own_ref[...]
        new_moment = OUTER_MU * m_ref[...] + pseudo
        m_out[...] = new_moment
        a_out[...] = a_ref[...] - OUTER_RATE * (OUTER_MU * new_moment + pseudo)


def outer_step(place, outputs, base, sums, inner, anchor, pseudo, momentum, own_sum, ticket):
    replicas, part = inner.shape[0], inner.shape[1]
    mixed = pl.BlockSpec((part, FRAG_COLS), lambda j, p: (p[1] ^ j, p[0]))
    pieces = pl.BlockSpec((1, part, FRAG_COLS), lambda j, p: (j, 0, 0))
    due = pl.BlockSpec((part, FRAG_COLS), lambda j, p: (0, p[0]))
    plain = pl.BlockSpec((part, FRAG_COLS), lambda j, p: (0, 0))
    whole = pl.BlockSpec(memory_space=pl.ANY)
    return pl.pallas_call(
        functools.partial(outer_kernel, replicas),
        out_shape=[pltpu.HBM(a.shape, a.dtype) for a in outputs],
        grid_spec=pltpu.PrefetchScalarGridSpec(
            num_scalar_prefetch=1,
            grid=(replicas,),
            in_specs=[whole] * 3 + [plain] * (2 * replicas) + [pieces] + [plain] * 4 + [whole],
            out_specs=[mixed, due, due],
        ),
        input_output_aliases={1: 0, 2: 1, 3: 2},
        compiler_params=params_of(12),
        cost_estimate=cost(10 * replicas * part * FRAG_COLS, 20 * replicas * part * FRAG_COLS),
        name="outer_step",
    )(place, *in_hbm(*outputs), *base, *sums, inner, anchor, pseudo, momentum, own_sum, ticket)


def swap(block, axis, offset):
    count = lax.axis_size(axis)
    return lax.ppermute(block, axis, [(i, i ^ offset) for i in range(count)])


def after(value, *others):
    return lax.optimization_barrier((value,) + others)[0]


def body(
    tokens,
    cotangent,
    weights,
    first_moment,
    second_moment,
    anchor,
    momentum,
    due_fragment,
    step_count,
):
    inputs, incoming, params = tokens[0], cotangent[0], weights[0]
    kv_width = incoming.shape[1] // 2
    rows = params.shape[0]
    part = anchor.shape[0]
    replicas = lax.axis_size("rep")
    shards = lax.axis_size("fsdp")
    me = jnp.reshape(lax.axis_index("fsdp"), (1,)).astype(jnp.int32)
    my_rep = lax.axis_index("rep").astype(jnp.int32)
    place = jnp.stack([due_fragment[0], my_rep])
    chips = range(2, shards, 2)
    far = sorted(chips, key=lambda k: (-bin(k).count("1"), k))
    order = [k for k in far[:-2] for k in (k, k + 1)]
    order += far[-2:] + [k + 1 for k in far[-2:]]

    (old,) = due_columns(place, part, params)
    old_sums = [old[0]] + [swap(old[k], "rep", k) for k in range(1, replicas)]

    packed = {}
    for offsets in (order[:1], order[1:4], order[4:], (0, 1)):
        packed |= pack(inputs, me, rows, tuple(offsets))
    blocks = {k: swap(packed[k], "fsdp", k) for k in order}
    blocks[0], blocks[1] = packed[0], swap(packed[1], "fsdp", 1)

    values = {0: incoming[:, kv_width:]}
    for i, k in enumerate(far):
        values[k] = swap(after(values[0], blocks[order[i]]), "fsdp", k)
    for k in range(0, shards, 2):
        values[k + 1] = swap(values[k], "fsdp", 1)

    steps_now = step_count[0].astype(jnp.float32)
    plan = jnp.minimum(1.0, steps_now / WARMUP) * (
        0.55 + 0.45 * jnp.cos(jnp.pi * steps_now / STEPS_TOTAL)
    )
    rate = PEAK_RATE * plan
    inv_one = 1.0 / (1.0 - jnp.power(BETA_ONE, steps_now))
    inv_two = 1.0 / (1.0 - jnp.power(BETA_TWO, steps_now))
    scalars = jnp.stack([rate, inv_one, inv_two])
    old_first, old_second = due_columns(place, part, first_moment[0], second_moment[0])
    anchor_cols, moment_cols = (c[0] for c in due_columns(place, part, anchor, momentum))
    pseudo_old = anchor_cols - sum(old_sums[1:], old_sums[0]) / replicas
    base = anchor_cols - OUTER_RATE * (OUTER_MU * (OUTER_MU * moment_cols + pseudo_old) + pseudo_old)
    base = [base] + [swap(base, "rep", k) for k in range(1, replicas)]
    anchor_copy, momentum_copy = duplicate(anchor, momentum)
    key_weights = cast_left(params, kv_width)

    last = far[-1]
    blocks[last + 1] = after(blocks[last + 1], anchor_copy, momentum_copy, scalars, old_first, old_second)
    parts, flipped = [], {}
    for k in far + [0]:
        theirs, flipped[k + 1] = partial_keys(blocks[k + 1], key_weights)
        theirs = swap(theirs, "fsdp", 1)
        if k == last:
            theirs = after(theirs, *parts[:1], *base)
        part_k, flipped[k] = partial_keys(blocks[k], key_weights, theirs)
        parts.append(swap(part_k, "fsdp", k) if k else part_k)
    spread = [0, 1] + [k + odd for k in far for odd in range(2)]
    near, rest = spread[:shards // 2], spread[shards // 2:]
    pick = lambda table, which: [table[k] for k in which]
    (values_first,) = gradient(place, pick(flipped, near), pick(values, near), last=False)
    parts[-1] = after(parts[-1], values_first)
    keys = {0: key_backward(parts, incoming, 0)}
    for k in far:
        keys[k] = swap(keys[0], "fsdp", k)
    keys[1] = swap(keys[0], "fsdp", 1)

    grad_values, square, due = gradient(
        place, pick(flipped, rest), pick(values, rest), values_first
    )
    for k in near[2::2]:
        keys[k + 1] = swap(after(keys[k], square), "fsdp", 1)
    (keys_first,) = gradient(place, pick(flipped, near), pick(keys, near), last=False)
    for k in rest[::2]:
        keys[k + 1] = swap(after(keys[k], square), "fsdp", 1)
    grad_keys, square, due = gradient(
        place, pick(flipped, rest), pick(keys, rest), keys_first, square, due
    )

    square = square + swap(square, "fsdp", 1)
    squares = [square] + [swap(square, "fsdp", k) for k in chips]

    state = (params, first_moment[0], second_moment[0], grad_keys, grad_values)
    inner, *update = adam_frag(place, scalars, squares, old, old_first, old_second, due)
    steps = rows // 256
    *results, ticket = adam_rows(scalars, squares, state, 0, steps // 2)
    own_sum = update[0].astype(jnp.float32)
    for k in range(1, replicas):
        own_sum = own_sum + swap(update[k], "rep", k).astype(jnp.float32)
    own_sum, ticket = lax.optimization_barrier((own_sum, ticket))
    sums = [own_sum.astype(jnp.bfloat16)]
    sums += [swap(sums[0], "rep", k) for k in range(1, replicas)]
    results = adam_rows(scalars, squares, state, steps // 2, steps, results)
    weights_out, anchor_out, momentum_out = outer_step(
        place,
        (results[0], anchor_copy, momentum_copy),
        base,
        sums,
        inner,
        anchor_cols,
        pseudo_old,
        moment_cols,
        own_sum,
        ticket,
    )
    plan_out = jnp.reshape(plan, (1,))
    return (
        weights_out[None],
        results[1][None],
        results[2][None],
        anchor_out,
        momentum_out,
        plan_out,
    )


def solution(mesh):
    tokens_spec = P("rep", "fsdp", None)
    outer_spec = P(("fsdp", "rep"), None)
    return jax.shard_map(
        body,
        mesh=mesh,
        in_specs=(tokens_spec,) * 5 + (outer_spec,) * 2 + (P(), P()),
        out_specs=(tokens_spec,) * 3 + (outer_spec,) * 2 + (P(),),
        check_vma=False,
    )
```

```python
import functools

import jax
import jax.numpy as jnp
from jax import lax
from jax.experimental import pallas as pl
from jax.experimental.pallas import tpu as pltpu
from jax.sharding import PartitionSpec as P

HEAD = 128
WARMUP = 2000
STEPS_TOTAL = 100000
FRAG_COLS = 128


BETA_ONE = 0.9
BETA_TWO = 0.95
ADAM_EPS = 1e-08
DECAY = 0.1
PEAK_RATE = 0.0003
CLIP_NORM = 1.0
OUTER_MU = 0.9
OUTER_RATE = 0.7
MIX_LOCAL = 0.5

MIB = 1 << 20
ADAM_ROWS = 128


def in_hbm(*arrays):
    return [pltpu.with_memory_space_constraint(a, pltpu.HBM) for a in arrays]


def params_of(limit):
    return pltpu.CompilerParams(vmem_limit_bytes=limit * MIB)


def cost(flops, moved):
    return pl.CostEstimate(flops=int(flops), bytes_accessed=int(moved), transcendentals=0)


def pack_kernel(offsets, me_ref, src_ref, *refs):
    half = len(offsets)
    out_refs, (held, in_sems, out_sems) = refs[:half], refs[half:]
    streams = in_sems.shape[1]
    count, rows = out_refs[0].shape
    step = count // streams
    fetches, stores = [], []
    for i, offset in enumerate(offsets):
        column = pl.multiple_of((me_ref[0] ^ offset) * rows, HEAD)
        for j in range(streams):
            at = pl.ds(j * step, step)
            block = src_ref.at[at, pl.ds(column, rows)]
            fetches.append(pltpu.make_async_copy(block, held.at[i, at], in_sems.at[i, j]))
            stores.append(pltpu.make_async_copy(held.at[i, at], out_refs[i].at[at], out_sems.at[i, j]))
    for copy in fetches:
        copy.start()
    for fetch, store in zip(fetches, stores):
        fetch.wait()
        store.start()
    for copy in stores:
        copy.wait()


def pack(tokens, me, rows, offsets):
    count = tokens.shape[0]
    streams = 4
    whole = pl.BlockSpec(memory_space=pl.ANY)
    outs = pl.pallas_call(
        functools.partial(pack_kernel, offsets),
        out_shape=[pltpu.HBM((count, rows), tokens.dtype)] * len(offsets),
        in_specs=[pl.BlockSpec(memory_space=pltpu.SMEM), whole],
        out_specs=[whole] * len(offsets),
        scratch_shapes=[
            pltpu.VMEM((len(offsets), count, rows), tokens.dtype),
            pltpu.SemaphoreType.DMA((len(offsets), streams)),
            pltpu.SemaphoreType.DMA((len(offsets), streams)),
        ],
        compiler_params=params_of(12),
        cost_estimate=cost(0, 4 * len(offsets) * count * rows),
        name="pack",
    )(me, *in_hbm(tokens))
    return dict(zip(offsets, outs))


def cast_kernel(src_ref, out_ref):
    out_ref[...] = src_ref[...].astype(out_ref.dtype)


def cast_left(array, width):
    rows = array.shape[0]
    block = pl.BlockSpec((256, width), lambda i: (i, 0))
    return pl.pallas_call(
        cast_kernel,
        out_shape=jax.ShapeDtypeStruct((rows, width), jnp.bfloat16),
        grid=(rows // 256,),
        in_specs=[block],
        out_specs=block,
        compiler_params=params_of(8),
        cost_estimate=cost(0, 6 * rows * width),
        name="cast_left",
    )(*in_hbm(array))


def partial_kernel(pieces, *refs):
    x_refs, w_ref, (*add_refs, out_ref, flip_ref) = refs[:pieces], refs[pieces], refs[pieces + 1:]
    x = jnp.concatenate([ref[...] for ref in x_refs], axis=1)
    total = jnp.dot(x, w_ref[...], preferred_element_type=jnp.float32)
    for ref in add_refs:
        total = total + ref[...].astype(jnp.float32)
    out_ref[...] = total.astype(out_ref.dtype)
    step = x_refs[0].shape[1]
    for i, ref in enumerate(x_refs):
        flip_ref[i * step:(i + 1) * step, :] = ref[...].T


def partial_keys(block, key_weights, *others):
    count, rows = block.shape
    width = key_weights.shape[1]
    pieces = 4 if rows % (4 * HEAD) == 0 else 2
    fixed = lambda a: pl.BlockSpec(a.shape, lambda i: (0, 0))
    return pl.pallas_call(
        functools.partial(partial_kernel, pieces),
        out_shape=[
            jax.ShapeDtypeStruct((count, width), jnp.bfloat16),
            jax.ShapeDtypeStruct((rows, count), jnp.bfloat16),
        ],
        grid=(1,),
        in_specs=[pl.BlockSpec((count, rows // pieces), lambda i, c=c: (0, c)) for c in range(pieces)]
        + [fixed(key_weights)]
        + [fixed(o) for o in others],
        out_specs=[
            pl.BlockSpec((count, width), lambda i: (0, 0)),
            pl.BlockSpec((rows, count), lambda i: (0, 0)),
        ],
        compiler_params=params_of(12),
        cost_estimate=cost(2 * count * rows * width, 4 * count * rows),
        name="partial_keys",
    )(*[block] * pieces, key_weights, *others)


def key_kernel(first, *refs):
    *part_refs, cot_ref, out_ref = refs
    count = out_ref.shape[0]
    raw = sum(ref[...].astype(jnp.float32) for ref in part_refs)
    for h in range(raw.shape[1] // HEAD):
        cols = slice(h * HEAD, (h + 1) * HEAD)
        head = raw[:, cols]
        inverse = lax.rsqrt(jnp.mean(head * head, axis=1, keepdims=True) + 1e-06)
        normed = head * inverse
        upper = cot_ref[first:first + count, cols].astype(jnp.float32)
        back = inverse * (upper - normed * jnp.mean(upper * normed, axis=1, keepdims=True))
        out_ref[:, cols] = back.astype(out_ref.dtype)


def key_backward(parts, incoming, first):
    count, width = parts[0].shape
    block = pl.BlockSpec((count, width), lambda i: (0, 0))
    cot = pl.BlockSpec((incoming.shape[0], width), lambda i: (0, 0))
    return pl.pallas_call(
        functools.partial(key_kernel, first),
        out_shape=jax.ShapeDtypeStruct((count, width), jnp.bfloat16),
        grid=(1,),
        in_specs=[block] * len(parts) + [cot],
        out_specs=block,
        compiler_params=params_of(8),
        cost_estimate=cost(60 * count * width, 12 * count * width),
        name="key_backward",
    )(*parts, incoming)


def grad_kernel(count, has_base, has_more, last, place_ref, *refs):
    refs = list(refs)
    x_refs, u_refs = refs[:count], refs[count:2 * count]
    refs = refs[2 * count:]
    base = refs.pop(0) if has_base else None
    square_in, due_in = (refs.pop(0), refs.pop(0)) if has_more else (None, None)
    out_ref = refs.pop(0)
    x = jnp.concatenate([ref[...] for ref in x_refs], axis=1)
    u = jnp.concatenate([ref[...] for ref in u_refs], axis=0)
    total = jnp.dot(x, u, preferred_element_type=jnp.float32)
    if has_base:
        total = total + base[...]
    out_ref[...] = total
    if last:
        sq_ref, due_ref = refs

        @pl.when(pl.program_id(0) == 0)
        def _():
            sq_ref[...] = square_in[...] if has_more else jnp.zeros_like(sq_ref)

        rows, width = total.shape
        squares = (total * total).reshape(rows // 8, 8, width).sum(axis=0)
        folded = squares[:, :HEAD]
        for h in range(1, width // HEAD):
            folded = folded + squares[:, h * HEAD:(h + 1) * HEAD]
        sq_ref[...] += folded
        heads = width // FRAG_COLS
        mine = place_ref[0] - (0 if has_more else heads)
        mine = jnp.minimum(jnp.maximum(mine, 0), heads - 1) * FRAG_COLS
        column = out_ref[:, pl.ds(pl.multiple_of(mine, FRAG_COLS), FRAG_COLS)]
        if has_more:
            column = jnp.where(place_ref[0] < heads, column, due_in[...])
        due_ref[...] = column


def gradient(place, flipped, upstream, base=None, square=None, due=None, last=True):
    rows, depth = flipped[0].shape
    width = upstream[0].shape[1]
    step = 256
    row_block = lambda cols: pl.BlockSpec((step, cols), lambda i, p: (i, 0))
    fixed = pl.BlockSpec((8, HEAD), lambda i, p: (0, 0))
    args = [*flipped, *upstream]
    specs = [row_block(depth)] * len(flipped)
    specs += [pl.BlockSpec((depth, width), lambda i, p: (0, 0))] * len(upstream)
    if base is not None:
        args.append(base)
        specs.append(row_block(width))
    if square is not None:
        args += [square, due]
        specs += [fixed, row_block(FRAG_COLS)]
    if last:
        shapes = [
            jax.ShapeDtypeStruct((rows, width), jnp.float32),
            jax.ShapeDtypeStruct((8, HEAD), jnp.float32),
            jax.ShapeDtypeStruct((rows, FRAG_COLS), jnp.float32),
        ]
        outs = [row_block(width), fixed, row_block(FRAG_COLS)]
    else:
        shapes = [jax.ShapeDtypeStruct((rows, width), jnp.float32)]
        outs = [row_block(width)]
    depth *= len(flipped)
    return pl.pallas_call(
        functools.partial(grad_kernel, len(flipped), base is not None, square is not None, last),
        out_shape=shapes,
        grid_spec=pltpu.PrefetchScalarGridSpec(
            num_scalar_prefetch=1, grid=(rows // step,), in_specs=specs, out_specs=outs
        ),
        compiler_params=params_of(12),
        cost_estimate=cost(2 * rows * width * depth, 2 * rows * depth + 4 * rows * width),
        name="gradient",
    )(place, *args)


def clip_factor(square_refs):
    square = jnp.sum(sum(ref[...] for ref in square_refs), keepdims=True)
    return jnp.minimum(1.0, CLIP_NORM / (jnp.sqrt(square) + 1e-06))


def adam(old, first, second, grad, factor, scalars):
    rate, inv_one, inv_two = (scalars[i] for i in range(3))
    clipped = grad * factor
    first_new = BETA_ONE * first + (1.0 - BETA_ONE) * clipped
    second_new = BETA_TWO * second + (1.0 - BETA_TWO) * clipped * clipped
    update = rate * (
        first_new * inv_one / (jnp.sqrt(second_new * inv_two) + ADAM_EPS) + DECAY * old
    )
    return update, first_new, second_new


def adam_kernel(squares, extra, sc_ref, w_ref, m_ref, v_ref, gk_ref, gv_ref, *refs):
    factor = clip_factor(refs[:squares])
    w_out, m_out, v_out, *done = refs[squares + extra:]
    width = gk_ref.shape[1]
    for g_ref, cols in ((gk_ref, slice(0, width)), (gv_ref, slice(width, 2 * width))):
        old = w_ref[:, cols]
        update, first_new, second_new = adam(
            old, m_ref[:, cols], v_ref[:, cols], g_ref[...], factor, sc_ref
        )
        w_out[:, cols] = old - update
        m_out[:, cols] = first_new
        v_out[:, cols] = second_new
    for ref in done:
        ref[...] = jnp.zeros_like(ref)


def adam_rows(scalars, squares, state, first, last, into=()):
    rows, width = state[0].shape
    step = ADAM_ROWS
    full = pl.BlockSpec((step, width), lambda i: (i + first, 0))
    half = pl.BlockSpec((step, width // 2), lambda i: (i + first, 0))
    shapes = [pltpu.HBM((rows, width), jnp.float32)] * 3
    outs = [full] * 3
    if not into:
        shapes.append(jax.ShapeDtypeStruct((8, HEAD), jnp.float32))
        outs.append(pl.BlockSpec((8, HEAD), lambda i: (0, 0)))
    count = (last - first) * step
    return pl.pallas_call(
        functools.partial(adam_kernel, len(squares), len(into)),
        out_shape=shapes,
        grid=(last - first,),
        in_specs=[pl.BlockSpec(memory_space=pltpu.SMEM), full, full, full, half, half]
        + [pl.BlockSpec((8, HEAD), lambda i: (0, 0))] * len(squares)
        + [pl.BlockSpec(memory_space=pl.ANY)] * len(into),
        out_specs=outs,
        input_output_aliases={6 + len(squares) + i: i for i in range(len(into))},
        compiler_params=params_of(12),
        cost_estimate=cost(20 * count * width, 28 * count * width),
        name="adam_rows",
    )(scalars, *state, *squares, *in_hbm(*into))


def frag_kernel(squares, place_ref, sc_ref, w_ref, m_ref, v_ref, g_ref, *refs):
    blocks, part, _ = w_ref.shape
    factor = clip_factor(refs[:squares])
    inner_ref, *out_refs = refs[squares:]
    for j in range(blocks):
        at = pl.multiple_of((place_ref[1] ^ j) * part, 8)
        old = w_ref[j]
        update, _, _ = adam(old, m_ref[j], v_ref[j], g_ref[pl.ds(at, part), :], factor, sc_ref)
        inner_ref[j] = old - update
        out_refs[j][...] = update.astype(out_refs[j].dtype)


def adam_frag(place, scalars, squares, old, first, second, grad):
    blocks, part, width = old.shape
    smem = pl.BlockSpec(memory_space=pltpu.SMEM)
    vmem = pl.BlockSpec(memory_space=pltpu.VMEM)
    return pl.pallas_call(
        functools.partial(frag_kernel, len(squares)),
        out_shape=[jax.ShapeDtypeStruct(old.shape, jnp.float32)]
        + [jax.ShapeDtypeStruct((part, width), jnp.bfloat16)] * blocks,
        in_specs=[smem, smem] + [vmem] * (4 + len(squares)),
        out_specs=[vmem] * (1 + blocks),
        compiler_params=params_of(12),
        cost_estimate=cost(20 * old.size, 22 * old.size),
        name="adam_frag",
    )(place, scalars, old, first, second, grad, *squares)


def pick_kernel(blocks, place_ref, *refs):
    outs = refs[len(refs) // (blocks + 1) * blocks:]
    for i, out_ref in enumerate(outs):
        for j in range(blocks):
            out_ref[j] = refs[i * blocks + j][...]


def due_columns(place, part, *arrays):
    blocks = arrays[0].shape[0] // part
    specs = []
    for j in range(blocks):
        at = (lambda i, p, j=j: (p[1] ^ j, p[0])) if blocks > 1 else (lambda i, p: (0, p[0]))
        specs.append(pl.BlockSpec((part, FRAG_COLS), at))
    shape = (blocks, part, FRAG_COLS)
    return pl.pallas_call(
        functools.partial(pick_kernel, blocks),
        out_shape=[jax.ShapeDtypeStruct(shape, a.dtype) for a in arrays],
        grid_spec=pltpu.PrefetchScalarGridSpec(
            num_scalar_prefetch=1,
            grid=(1,),
            in_specs=specs * len(arrays),
            out_specs=[pl.BlockSpec(shape, lambda i, p: (0, 0, 0))] * len(arrays),
        ),
        compiler_params=params_of(12),
        cost_estimate=cost(0, 8 * blocks * part * FRAG_COLS * len(arrays)),
        name="due_columns",
    )(place, *[a for array in in_hbm(*arrays) for a in [array] * blocks])


def duplicate_kernel(*refs):
    half = (len(refs) - 3) // 2
    held, in_sems, out_sems = refs[2 * half:]
    streams = held.shape[1]
    step = held.shape[2]
    places = [(a, i, pl.ds(i * step, step)) for a in range(half) for i in range(streams)]
    fetches = [
        pltpu.make_async_copy(refs[a].at[at], held.at[a, i], in_sems.at[a, i]) for a, i, at in places
    ]
    stores = [
        pltpu.make_async_copy(held.at[a, i], refs[half + a].at[at], out_sems.at[a, i])
        for a, i, at in places
    ]
    for copy in fetches:
        copy.start()
    for fetch, store in zip(fetches, stores):
        fetch.wait()
        store.start()
    for copy in stores:
        copy.wait()


def duplicate(*arrays):
    rows, width = arrays[0].shape
    streams = 4
    whole = pl.BlockSpec(memory_space=pl.ANY)
    return pl.pallas_call(
        duplicate_kernel,
        out_shape=[pltpu.HBM(a.shape, a.dtype) for a in arrays],
        in_specs=[whole] * len(arrays),
        out_specs=[whole] * len(arrays),
        scratch_shapes=[
            pltpu.VMEM((len(arrays), streams, rows // streams, width), arrays[0].dtype),
            pltpu.SemaphoreType.DMA((len(arrays), streams)),
            pltpu.SemaphoreType.DMA((len(arrays), streams)),
        ],
        compiler_params=params_of(8),
        cost_estimate=cost(0, sum(8 * a.size for a in arrays)),
        name="duplicate",
    )(*in_hbm(*arrays))


def outer_kernel(replicas, place_ref, *refs):
    share = 1.0 / replicas
    base_refs, sum_refs = refs[3:3 + replicas], refs[3 + replicas:3 + 2 * replicas]
    inner_ref, a_ref, p_ref, m_ref, own_ref, _, w_out, a_out, m_out = refs[3 + 2 * replicas:]
    scale = share * (1.0 + OUTER_MU) * OUTER_RATE
    for j in range(replicas):

        @pl.when(pl.program_id(0) == j)
        def _():
            fresh = base_refs[j][...] - scale * sum_refs[j][...].astype(jnp.float32)
            w_out[...] = MIX_LOCAL * inner_ref[0] + (1.0 - MIX_LOCAL) * fresh

    @pl.when(pl.program_id(0) == 0)
    def _():
        pseudo = p_ref[...] + share * own_ref[...]
        new_moment = OUTER_MU * m_ref[...] + pseudo
        m_out[...] = new_moment
        a_out[...] = a_ref[...] - OUTER_RATE * (OUTER_MU * new_moment + pseudo)


def outer_step(place, outputs, base, sums, inner, anchor, pseudo, momentum, own_sum, ticket):
    replicas, part = inner.shape[0], inner.shape[1]
    mixed = pl.BlockSpec((part, FRAG_COLS), lambda j, p: (p[1] ^ j, p[0]))
    pieces = pl.BlockSpec((1, part, FRAG_COLS), lambda j, p: (j, 0, 0))
    due = pl.BlockSpec((part, FRAG_COLS), lambda j, p: (0, p[0]))
    plain = pl.BlockSpec((part, FRAG_COLS), lambda j, p: (0, 0))
    whole = pl.BlockSpec(memory_space=pl.ANY)
    return pl.pallas_call(
        functools.partial(outer_kernel, replicas),
        out_shape=[pltpu.HBM(a.shape, a.dtype) for a in outputs],
        grid_spec=pltpu.PrefetchScalarGridSpec(
            num_scalar_prefetch=1,
            grid=(replicas,),
            in_specs=[whole] * 3 + [plain] * (2 * replicas) + [pieces] + [plain] * 4 + [whole],
            out_specs=[mixed, due, due],
        ),
        input_output_aliases={1: 0, 2: 1, 3: 2},
        compiler_params=params_of(12),
        cost_estimate=cost(10 * replicas * part * FRAG_COLS, 20 * replicas * part * FRAG_COLS),
        name="outer_step",
    )(place, *in_hbm(*outputs), *base, *sums, inner, anchor, pseudo, momentum, own_sum, ticket)


def swap(block, axis, offset):
    count = lax.axis_size(axis)
    return lax.ppermute(block, axis, [(i, i ^ offset) for i in range(count)])


def after(value, *others):
    return lax.optimization_barrier((value,) + others)[0]


def body(
    tokens,
    cotangent,
    weights,
    first_moment,
    second_moment,
    anchor,
    momentum,
    due_fragment,
    step_count,
):
    inputs, incoming, params = tokens[0], cotangent[0], weights[0]
    kv_width = incoming.shape[1] // 2
    rows = params.shape[0]
    part = anchor.shape[0]
    replicas = lax.axis_size("rep")
    shards = lax.axis_size("fsdp")
    me = jnp.reshape(lax.axis_index("fsdp"), (1,)).astype(jnp.int32)
    my_rep = lax.axis_index("rep").astype(jnp.int32)
    place = jnp.stack([due_fragment[0], my_rep])
    chips = range(2, shards, 2)
    far = sorted(chips, key=lambda k: (-bin(k).count("1"), k))
    order = [k for k in far[:-2] for k in (k, k + 1)]
    order += far[-2:] + [k + 1 for k in far[-2:]]

    packed = {}
    for offsets in (order[:1], order[1:4], order[4:], (0, 1)):
        packed |= pack(inputs, me, rows, tuple(offsets))
    blocks = {k: swap(packed[k], "fsdp", k) for k in order}
    blocks[0], blocks[1] = packed[0], swap(packed[1], "fsdp", 1)

    (old,) = due_columns(after(place, blocks[order[0]]), part, params)
    old_sums = [old[0]] + [swap(old[k], "rep", k) for k in range(1, replicas)]

    values = {0: incoming[:, kv_width:]}
    for i, k in enumerate(far):
        values[k] = swap(after(values[0], blocks[order[i]]), "fsdp", k)
    for k in range(0, shards, 2):
        values[k + 1] = swap(values[k], "fsdp", 1)

    steps_now = step_count[0].astype(jnp.float32)
    plan = jnp.minimum(1.0, steps_now / WARMUP) * (
        0.55 + 0.45 * jnp.cos(jnp.pi * steps_now / STEPS_TOTAL)
    )
    rate = PEAK_RATE * plan
    inv_one = 1.0 / (1.0 - jnp.power(BETA_ONE, steps_now))
    inv_two = 1.0 / (1.0 - jnp.power(BETA_TWO, steps_now))
    scalars = jnp.stack([rate, inv_one, inv_two])
    old_first, old_second = due_columns(place, part, first_moment[0], second_moment[0])
    anchor_cols, moment_cols = (c[0] for c in due_columns(place, part, anchor, momentum))
    pseudo_old = anchor_cols - sum(old_sums[1:], old_sums[0]) / replicas
    base = anchor_cols - OUTER_RATE * (OUTER_MU * (OUTER_MU * moment_cols + pseudo_old) + pseudo_old)
    base = [base] + [swap(base, "rep", k) for k in range(1, replicas)]
    anchor_copy, momentum_copy = duplicate(anchor, momentum)
    key_weights = cast_left(params, kv_width)

    last = far[-1]
    blocks[last + 1] = after(blocks[last + 1], anchor_copy, momentum_copy, scalars, old_first, old_second)
    parts, flipped = [], {}
    for k in far + [0]:
        theirs, flipped[k + 1] = partial_keys(blocks[k + 1], key_weights)
        theirs = swap(theirs, "fsdp", 1)
        if k == last:
            theirs = after(theirs, *parts[:1], *base)
        part_k, flipped[k] = partial_keys(blocks[k], key_weights, theirs)
        parts.append(swap(part_k, "fsdp", k) if k else part_k)
    spread = [0, 1] + [k + odd for k in far for odd in range(2)]
    near, rest = spread[:shards // 2], spread[shards // 2:]
    pick = lambda table, which: [table[k] for k in which]
    (values_first,) = gradient(place, pick(flipped, near), pick(values, near), last=False)
    parts[-1] = after(parts[-1], values_first)
    keys = {0: key_backward(parts, incoming, 0)}
    for k in far:
        keys[k] = swap(keys[0], "fsdp", k)
    keys[1] = swap(keys[0], "fsdp", 1)

    grad_values, square, due = gradient(
        place, pick(flipped, rest), pick(values, rest), values_first
    )
    for k in near[2::2]:
        keys[k + 1] = swap(after(keys[k], square), "fsdp", 1)
    (keys_first,) = gradient(place, pick(flipped, near), pick(keys, near), last=False)
    for k in rest[::2]:
        keys[k + 1] = swap(after(keys[k], square), "fsdp", 1)
    grad_keys, square, due = gradient(
        place, pick(flipped, rest), pick(keys, rest), keys_first, square, due
    )

    square = square + swap(square, "fsdp", 1)
    squares = [square] + [swap(square, "fsdp", k) for k in chips]

    state = (params, first_moment[0], second_moment[0], grad_keys, grad_values)
    inner, *update = adam_frag(place, scalars, squares, old, old_first, old_second, due)
    steps = rows // ADAM_ROWS
    *results, ticket = adam_rows(scalars, squares, state, 0, steps // 2)
    own_sum = update[0].astype(jnp.float32)
    for k in range(1, replicas):
        own_sum = own_sum + swap(update[k], "rep", k).astype(jnp.float32)
    own_sum, ticket = lax.optimization_barrier((own_sum, ticket))
    sums = [own_sum.astype(jnp.bfloat16)]
    sums += [swap(sums[0], "rep", k) for k in range(1, replicas)]
    results = adam_rows(scalars, squares, state, steps // 2, steps, results)
    weights_out, anchor_out, momentum_out = outer_step(
        place,
        (results[0], anchor_copy, momentum_copy),
        base,
        sums,
        inner,
        anchor_cols,
        pseudo_old,
        moment_cols,
        own_sum,
        ticket,
    )
    plan_out = jnp.reshape(plan, (1,))
    return (
        weights_out[None],
        results[1][None],
        results[2][None],
        anchor_out,
        momentum_out,
        plan_out,
    )


def solution(mesh):
    tokens_spec = P("rep", "fsdp", None)
    outer_spec = P(("fsdp", "rep"), None)
    return jax.shard_map(
        body,
        mesh=mesh,
        in_specs=(tokens_spec,) * 5 + (outer_spec,) * 2 + (P(), P()),
        out_specs=(tokens_spec,) * 3 + (outer_spec,) * 2 + (P(),),
        check_vma=False,
    )
```

```python
import functools

import jax
import jax.numpy as jnp
from jax import lax
from jax.experimental import pallas as pl
from jax.experimental.pallas import tpu as pltpu
from jax.sharding import PartitionSpec as P

HEAD = 128
WARMUP = 2000
STEPS_TOTAL = 100000
FRAG_COLS = 128


BETA_ONE = 0.9
BETA_TWO = 0.95
ADAM_EPS = 1e-08
DECAY = 0.1
PEAK_RATE = 0.0003
CLIP_NORM = 1.0
OUTER_MU = 0.9
OUTER_RATE = 0.7
MIX_LOCAL = 0.5

MIB = 1 << 20
ADAM_ROWS = 128


def in_hbm(*arrays):
    return [pltpu.with_memory_space_constraint(a, pltpu.HBM) for a in arrays]


def params_of(limit):
    return pltpu.CompilerParams(vmem_limit_bytes=limit * MIB)


def cost(flops, moved):
    return pl.CostEstimate(flops=int(flops), bytes_accessed=int(moved), transcendentals=0)


def pack_kernel(offsets, me_ref, src_ref, *refs):
    half = len(offsets)
    out_refs, (held, in_sems, out_sems) = refs[:half], refs[half:]
    streams = in_sems.shape[1]
    count, rows = out_refs[0].shape
    step = count // streams
    fetches, stores = [], []
    for i, offset in enumerate(offsets):
        column = pl.multiple_of((me_ref[0] ^ offset) * rows, HEAD)
        for j in range(streams):
            at = pl.ds(j * step, step)
            block = src_ref.at[at, pl.ds(column, rows)]
            fetches.append(pltpu.make_async_copy(block, held.at[i, at], in_sems.at[i, j]))
            stores.append(pltpu.make_async_copy(held.at[i, at], out_refs[i].at[at], out_sems.at[i, j]))
    for copy in fetches:
        copy.start()
    for fetch, store in zip(fetches, stores):
        fetch.wait()
        store.start()
    for copy in stores:
        copy.wait()


def pack(tokens, me, rows, offsets):
    count = tokens.shape[0]
    streams = 4
    whole = pl.BlockSpec(memory_space=pl.ANY)
    outs = pl.pallas_call(
        functools.partial(pack_kernel, offsets),
        out_shape=[pltpu.HBM((count, rows), tokens.dtype)] * len(offsets),
        in_specs=[pl.BlockSpec(memory_space=pltpu.SMEM), whole],
        out_specs=[whole] * len(offsets),
        scratch_shapes=[
            pltpu.VMEM((len(offsets), count, rows), tokens.dtype),
            pltpu.SemaphoreType.DMA((len(offsets), streams)),
            pltpu.SemaphoreType.DMA((len(offsets), streams)),
        ],
        compiler_params=params_of(12),
        cost_estimate=cost(0, 4 * len(offsets) * count * rows),
        name="pack",
    )(me, *in_hbm(tokens))
    return dict(zip(offsets, outs))


def cast_kernel(src_ref, out_ref):
    out_ref[...] = src_ref[...].astype(out_ref.dtype)


def cast_left(array, width):
    rows = array.shape[0]
    block = pl.BlockSpec((256, width), lambda i: (i, 0))
    return pl.pallas_call(
        cast_kernel,
        out_shape=jax.ShapeDtypeStruct((rows, width), jnp.bfloat16),
        grid=(rows // 256,),
        in_specs=[block],
        out_specs=block,
        compiler_params=params_of(8),
        cost_estimate=cost(0, 6 * rows * width),
        name="cast_left",
    )(*in_hbm(array))


def partial_kernel(pieces, *refs):
    x_refs, w_ref, (*add_refs, out_ref, flip_ref) = refs[:pieces], refs[pieces], refs[pieces + 1:]
    x = jnp.concatenate([ref[...] for ref in x_refs], axis=1)
    total = jnp.dot(x, w_ref[...], preferred_element_type=jnp.float32)
    for ref in add_refs:
        total = total + ref[...].astype(jnp.float32)
    out_ref[...] = total.astype(out_ref.dtype)
    step = x_refs[0].shape[1]
    for i, ref in enumerate(x_refs):
        flip_ref[i * step:(i + 1) * step, :] = ref[...].T


def partial_keys(block, key_weights, *others):
    count, rows = block.shape
    width = key_weights.shape[1]
    pieces = 4 if rows % (4 * HEAD) == 0 else 2
    fixed = lambda a: pl.BlockSpec(a.shape, lambda i: (0, 0))
    return pl.pallas_call(
        functools.partial(partial_kernel, pieces),
        out_shape=[
            jax.ShapeDtypeStruct((count, width), jnp.bfloat16),
            jax.ShapeDtypeStruct((rows, count), jnp.bfloat16),
        ],
        grid=(1,),
        in_specs=[pl.BlockSpec((count, rows // pieces), lambda i, c=c: (0, c)) for c in range(pieces)]
        + [fixed(key_weights)]
        + [fixed(o) for o in others],
        out_specs=[
            pl.BlockSpec((count, width), lambda i: (0, 0)),
            pl.BlockSpec((rows, count), lambda i: (0, 0)),
        ],
        compiler_params=params_of(12),
        cost_estimate=cost(2 * count * rows * width, 4 * count * rows),
        name="partial_keys",
    )(*[block] * pieces, key_weights, *others)


def key_kernel(first, *refs):
    *part_refs, cot_ref, out_ref = refs
    count = out_ref.shape[0]
    raw = sum(ref[...].astype(jnp.float32) for ref in part_refs)
    for h in range(raw.shape[1] // HEAD):
        cols = slice(h * HEAD, (h + 1) * HEAD)
        head = raw[:, cols]
        inverse = lax.rsqrt(jnp.mean(head * head, axis=1, keepdims=True) + 1e-06)
        normed = head * inverse
        upper = cot_ref[first:first + count, cols].astype(jnp.float32)
        back = inverse * (upper - normed * jnp.mean(upper * normed, axis=1, keepdims=True))
        out_ref[:, cols] = back.astype(out_ref.dtype)


def key_backward(parts, incoming, first):
    count, width = parts[0].shape
    block = pl.BlockSpec((count, width), lambda i: (0, 0))
    cot = pl.BlockSpec((incoming.shape[0], width), lambda i: (0, 0))
    return pl.pallas_call(
        functools.partial(key_kernel, first),
        out_shape=jax.ShapeDtypeStruct((count, width), jnp.bfloat16),
        grid=(1,),
        in_specs=[block] * len(parts) + [cot],
        out_specs=block,
        compiler_params=params_of(8),
        cost_estimate=cost(60 * count * width, 12 * count * width),
        name="key_backward",
    )(*parts, incoming)


def grad_kernel(count, has_base, has_more, last, place_ref, *refs):
    refs = list(refs)
    x_refs, u_refs = refs[:count], refs[count:2 * count]
    refs = refs[2 * count:]
    base = refs.pop(0) if has_base else None
    square_in, due_in = (refs.pop(0), refs.pop(0)) if has_more else (None, None)
    out_ref = refs.pop(0)
    x = jnp.concatenate([ref[...] for ref in x_refs], axis=1)
    u = jnp.concatenate([ref[...] for ref in u_refs], axis=0)
    total = jnp.dot(x, u, preferred_element_type=jnp.float32)
    if has_base:
        total = total + base[...]
    out_ref[...] = total
    if last:
        sq_ref, due_ref = refs

        @pl.when(pl.program_id(0) == 0)
        def _():
            sq_ref[...] = square_in[...] if has_more else jnp.zeros_like(sq_ref)

        rows, width = total.shape
        squares = (total * total).reshape(rows // 8, 8, width).sum(axis=0)
        folded = squares[:, :HEAD]
        for h in range(1, width // HEAD):
            folded = folded + squares[:, h * HEAD:(h + 1) * HEAD]
        sq_ref[...] += folded
        heads = width // FRAG_COLS
        mine = place_ref[0] - (0 if has_more else heads)
        mine = jnp.minimum(jnp.maximum(mine, 0), heads - 1) * FRAG_COLS
        column = out_ref[:, pl.ds(pl.multiple_of(mine, FRAG_COLS), FRAG_COLS)]
        if has_more:
            column = jnp.where(place_ref[0] < heads, column, due_in[...])
        due_ref[...] = column


def gradient(place, flipped, upstream, base=None, square=None, due=None, last=True):
    rows, depth = flipped[0].shape
    width = upstream[0].shape[1]
    step = 256
    row_block = lambda cols: pl.BlockSpec((step, cols), lambda i, p: (i, 0))
    fixed = pl.BlockSpec((8, HEAD), lambda i, p: (0, 0))
    args = [*flipped, *upstream]
    specs = [row_block(depth)] * len(flipped)
    specs += [pl.BlockSpec((depth, width), lambda i, p: (0, 0))] * len(upstream)
    if base is not None:
        args.append(base)
        specs.append(row_block(width))
    if square is not None:
        args += [square, due]
        specs += [fixed, row_block(FRAG_COLS)]
    if last:
        shapes = [
            jax.ShapeDtypeStruct((rows, width), jnp.float32),
            jax.ShapeDtypeStruct((8, HEAD), jnp.float32),
            jax.ShapeDtypeStruct((rows, FRAG_COLS), jnp.float32),
        ]
        outs = [row_block(width), fixed, row_block(FRAG_COLS)]
    else:
        shapes = [jax.ShapeDtypeStruct((rows, width), jnp.float32)]
        outs = [row_block(width)]
    depth *= len(flipped)
    return pl.pallas_call(
        functools.partial(grad_kernel, len(flipped), base is not None, square is not None, last),
        out_shape=shapes,
        grid_spec=pltpu.PrefetchScalarGridSpec(
            num_scalar_prefetch=1, grid=(rows // step,), in_specs=specs, out_specs=outs
        ),
        compiler_params=params_of(12),
        cost_estimate=cost(2 * rows * width * depth, 2 * rows * depth + 4 * rows * width),
        name="gradient",
    )(place, *args)


def clip_factor(square_refs):
    square = jnp.sum(sum(ref[...] for ref in square_refs), keepdims=True)
    return jnp.minimum(1.0, CLIP_NORM / (jnp.sqrt(square) + 1e-06))


def adam(old, first, second, grad, factor, scalars):
    rate, inv_one, inv_two = (scalars[i] for i in range(3))
    clipped = grad * factor
    first_new = BETA_ONE * first + (1.0 - BETA_ONE) * clipped
    second_new = BETA_TWO * second + (1.0 - BETA_TWO) * clipped * clipped
    update = rate * (
        first_new * inv_one / (jnp.sqrt(second_new * inv_two) + ADAM_EPS) + DECAY * old
    )
    return update, first_new, second_new


def adam_kernel(squares, extra, sc_ref, w_ref, m_ref, v_ref, gk_ref, gv_ref, *refs):
    factor = clip_factor(refs[:squares])
    w_out, m_out, v_out, *done = refs[squares + extra:]
    width = gk_ref.shape[1]
    for g_ref, cols in ((gk_ref, slice(0, width)), (gv_ref, slice(width, 2 * width))):
        old = w_ref[:, cols]
        update, first_new, second_new = adam(
            old, m_ref[:, cols], v_ref[:, cols], g_ref[...], factor, sc_ref
        )
        w_out[:, cols] = old - update
        m_out[:, cols] = first_new
        v_out[:, cols] = second_new
    for ref in done:
        ref[...] = jnp.zeros_like(ref)


def adam_rows(scalars, squares, state, first, last, into=()):
    rows, width = state[0].shape
    step = ADAM_ROWS
    full = pl.BlockSpec((step, width), lambda i: (i + first, 0))
    half = pl.BlockSpec((step, width // 2), lambda i: (i + first, 0))
    shapes = [pltpu.HBM((rows, width), jnp.float32)] * 3
    outs = [full] * 3
    if not into:
        shapes.append(jax.ShapeDtypeStruct((8, HEAD), jnp.float32))
        outs.append(pl.BlockSpec((8, HEAD), lambda i: (0, 0)))
    count = (last - first) * step
    return pl.pallas_call(
        functools.partial(adam_kernel, len(squares), len(into)),
        out_shape=shapes,
        grid=(last - first,),
        in_specs=[pl.BlockSpec(memory_space=pltpu.SMEM), full, full, full, half, half]
        + [pl.BlockSpec((8, HEAD), lambda i: (0, 0))] * len(squares)
        + [pl.BlockSpec(memory_space=pl.ANY)] * len(into),
        out_specs=outs,
        input_output_aliases={6 + len(squares) + i: i for i in range(len(into))},
        compiler_params=params_of(12),
        cost_estimate=cost(20 * count * width, 28 * count * width),
        name="adam_rows",
    )(scalars, *state, *squares, *in_hbm(*into))


def frag_kernel(squares, place_ref, sc_ref, w_ref, m_ref, v_ref, g_ref, *refs):
    blocks, part, _ = w_ref.shape
    factor = clip_factor(refs[:squares])
    inner_ref, *out_refs = refs[squares:]
    for j in range(blocks):
        d = place_ref[1] ^ j
        at = pl.multiple_of(d * part, 8)
        old = w_ref[d]
        update, _, _ = adam(old, m_ref[d], v_ref[d], g_ref[pl.ds(at, part), :], factor, sc_ref)
        inner_ref[j] = old - update
        out_refs[j][...] = update.astype(out_refs[j].dtype)


def adam_frag(place, scalars, squares, old, first, second, grad):
    blocks, part, width = old.shape
    smem = pl.BlockSpec(memory_space=pltpu.SMEM)
    vmem = pl.BlockSpec(memory_space=pltpu.VMEM)
    return pl.pallas_call(
        functools.partial(frag_kernel, len(squares)),
        out_shape=[jax.ShapeDtypeStruct(old.shape, jnp.float32)]
        + [jax.ShapeDtypeStruct((part, width), jnp.bfloat16)] * blocks,
        in_specs=[smem, smem] + [vmem] * (4 + len(squares)),
        out_specs=[vmem] * (1 + blocks),
        compiler_params=params_of(12),
        cost_estimate=cost(20 * old.size, 22 * old.size),
        name="adam_frag",
    )(place, scalars, old, first, second, grad, *squares)


def pick_kernel(blocks, place_ref, *refs):
    outs = refs[len(refs) // (blocks + 1) * blocks:]
    for i, out_ref in enumerate(outs):
        for j in range(blocks):
            out_ref[j] = refs[i * blocks + j][...]


def due_columns(place, part, *arrays):
    blocks = arrays[0].shape[0] // part
    specs = []
    for j in range(blocks):
        specs.append(pl.BlockSpec((part, FRAG_COLS), lambda i, p, j=j: (j, p[0])))
    shape = (blocks, part, FRAG_COLS)
    return pl.pallas_call(
        functools.partial(pick_kernel, blocks),
        out_shape=[jax.ShapeDtypeStruct(shape, a.dtype) for a in arrays],
        grid_spec=pltpu.PrefetchScalarGridSpec(
            num_scalar_prefetch=1,
            grid=(1,),
            in_specs=specs * len(arrays),
            out_specs=[pl.BlockSpec(shape, lambda i, p: (0, 0, 0))] * len(arrays),
        ),
        compiler_params=params_of(12),
        cost_estimate=cost(0, 8 * blocks * part * FRAG_COLS * len(arrays)),
        name="due_columns",
    )(place, *[a for array in in_hbm(*arrays) for a in [array] * blocks])


def duplicate_kernel(*refs):
    half = (len(refs) - 3) // 2
    held, in_sems, out_sems = refs[2 * half:]
    streams = held.shape[1]
    step = held.shape[2]
    places = [(a, i, pl.ds(i * step, step)) for a in range(half) for i in range(streams)]
    fetches = [
        pltpu.make_async_copy(refs[a].at[at], held.at[a, i], in_sems.at[a, i]) for a, i, at in places
    ]
    stores = [
        pltpu.make_async_copy(held.at[a, i], refs[half + a].at[at], out_sems.at[a, i])
        for a, i, at in places
    ]
    for copy in fetches:
        copy.start()
    for fetch, store in zip(fetches, stores):
        fetch.wait()
        store.start()
    for copy in stores:
        copy.wait()


def duplicate(*arrays):
    rows, width = arrays[0].shape
    streams = 4
    whole = pl.BlockSpec(memory_space=pl.ANY)
    return pl.pallas_call(
        duplicate_kernel,
        out_shape=[pltpu.HBM(a.shape, a.dtype) for a in arrays],
        in_specs=[whole] * len(arrays),
        out_specs=[whole] * len(arrays),
        scratch_shapes=[
            pltpu.VMEM((len(arrays), streams, rows // streams, width), arrays[0].dtype),
            pltpu.SemaphoreType.DMA((len(arrays), streams)),
            pltpu.SemaphoreType.DMA((len(arrays), streams)),
        ],
        compiler_params=params_of(8),
        cost_estimate=cost(0, sum(8 * a.size for a in arrays)),
        name="duplicate",
    )(*in_hbm(*arrays))


def outer_kernel(replicas, place_ref, *refs):
    share = 1.0 / replicas
    base_ref, sum_refs = refs[3], refs[4:4 + replicas]
    inner_ref, a_ref, p_ref, m_ref, own_ref, _, w_out, a_out, m_out = refs[4 + replicas:]
    scale = share * (1.0 + OUTER_MU) * OUTER_RATE
    for j in range(replicas):

        @pl.when(pl.program_id(0) == j)
        def _():
            fresh = base_ref[0] - scale * sum_refs[j][...].astype(jnp.float32)
            w_out[...] = MIX_LOCAL * inner_ref[0] + (1.0 - MIX_LOCAL) * fresh

    @pl.when(pl.program_id(0) == 0)
    def _():
        pseudo = p_ref[...] + share * own_ref[...]
        new_moment = OUTER_MU * m_ref[...] + pseudo
        m_out[...] = new_moment
        a_out[...] = a_ref[...] - OUTER_RATE * (OUTER_MU * new_moment + pseudo)


def outer_step(place, outputs, base, sums, inner, anchor, pseudo, momentum, own_sum, ticket):
    replicas, part = inner.shape[0], inner.shape[1]
    mixed = pl.BlockSpec((part, FRAG_COLS), lambda j, p: (p[1] ^ j, p[0]))
    pieces = pl.BlockSpec((1, part, FRAG_COLS), lambda j, p: (j, 0, 0))
    placed = pl.BlockSpec((1, part, FRAG_COLS), lambda j, p: (p[1] ^ j, 0, 0))
    due = pl.BlockSpec((part, FRAG_COLS), lambda j, p: (0, p[0]))
    plain = pl.BlockSpec((part, FRAG_COLS), lambda j, p: (0, 0))
    whole = pl.BlockSpec(memory_space=pl.ANY)
    return pl.pallas_call(
        functools.partial(outer_kernel, replicas),
        out_shape=[pltpu.HBM(a.shape, a.dtype) for a in outputs],
        grid_spec=pltpu.PrefetchScalarGridSpec(
            num_scalar_prefetch=1,
            grid=(replicas,),
            in_specs=[whole] * 3 + [placed] + [plain] * replicas + [pieces] + [plain] * 4 + [whole],
            out_specs=[mixed, due, due],
        ),
        input_output_aliases={1: 0, 2: 1, 3: 2},
        compiler_params=params_of(12),
        cost_estimate=cost(10 * replicas * part * FRAG_COLS, 20 * replicas * part * FRAG_COLS),
        name="outer_step",
    )(place, *in_hbm(*outputs), base, *sums, inner, anchor, pseudo, momentum, own_sum, ticket)


def swap(block, axis, offset):
    count = lax.axis_size(axis)
    return lax.ppermute(block, axis, [(i, i ^ offset) for i in range(count)])


def after(value, *others):
    return lax.optimization_barrier((value,) + others)[0]


def body(
    tokens,
    cotangent,
    weights,
    first_moment,
    second_moment,
    anchor,
    momentum,
    due_fragment,
    step_count,
):
    inputs, incoming, params = tokens[0], cotangent[0], weights[0]
    kv_width = incoming.shape[1] // 2
    rows = params.shape[0]
    part = anchor.shape[0]
    replicas = lax.axis_size("rep")
    shards = lax.axis_size("fsdp")
    me = jnp.reshape(lax.axis_index("fsdp"), (1,)).astype(jnp.int32)
    my_rep = lax.axis_index("rep").astype(jnp.int32)
    place = jnp.stack([due_fragment[0], my_rep])
    chips = range(2, shards, 2)
    far = sorted(chips, key=lambda k: (-bin(k).count("1"), k))
    order = [k for k in far[:-2] for k in (k, k + 1)]
    order += far[-2:] + [k + 1 for k in far[-2:]]

    packed = {}
    for offsets in (order[:1], order[1:4], order[4:], (0, 1)):
        packed |= pack(inputs, me, rows, tuple(offsets))
    blocks = {k: swap(packed[k], "fsdp", k) for k in order}
    blocks[0], blocks[1] = packed[0], swap(packed[1], "fsdp", 1)

    def to_all(pieces):
        return lax.all_to_all(pieces, "rep", 0, 0, tiled=True)

    (old,) = due_columns(after(place, blocks[order[0]]), part, params)
    old_sums = to_all(old)

    values = {0: incoming[:, kv_width:]}
    for i, k in enumerate(far):
        values[k] = swap(after(values[0], blocks[order[i]]), "fsdp", k)
    for k in range(0, shards, 2):
        values[k + 1] = swap(values[k], "fsdp", 1)

    steps_now = step_count[0].astype(jnp.float32)
    plan = jnp.minimum(1.0, steps_now / WARMUP) * (
        0.55 + 0.45 * jnp.cos(jnp.pi * steps_now / STEPS_TOTAL)
    )
    rate = PEAK_RATE * plan
    inv_one = 1.0 / (1.0 - jnp.power(BETA_ONE, steps_now))
    inv_two = 1.0 / (1.0 - jnp.power(BETA_TWO, steps_now))
    scalars = jnp.stack([rate, inv_one, inv_two])
    old_first, old_second = due_columns(place, part, first_moment[0], second_moment[0])
    anchor_cols, moment_cols = (c[0] for c in due_columns(place, part, anchor, momentum))
    pseudo_old = anchor_cols - jnp.sum(old_sums, axis=0) / replicas
    base = anchor_cols - OUTER_RATE * (OUTER_MU * (OUTER_MU * moment_cols + pseudo_old) + pseudo_old)
    base = to_all(jnp.broadcast_to(base[None], (replicas,) + base.shape))
    anchor_copy, momentum_copy = duplicate(anchor, momentum)
    key_weights = cast_left(params, kv_width)

    last = far[-1]
    blocks[last + 1] = after(blocks[last + 1], anchor_copy, momentum_copy, scalars, old_first, old_second)
    parts, flipped = [], {}
    for k in far + [0]:
        theirs, flipped[k + 1] = partial_keys(blocks[k + 1], key_weights)
        theirs = swap(theirs, "fsdp", 1)
        if k == last:
            theirs = after(theirs, *parts[:1], base)
        part_k, flipped[k] = partial_keys(blocks[k], key_weights, theirs)
        parts.append(swap(part_k, "fsdp", k) if k else part_k)
    spread = [0, 1] + [k + odd for k in far for odd in range(2)]
    near, rest = spread[:shards // 2], spread[shards // 2:]
    pick = lambda table, which: [table[k] for k in which]
    (values_first,) = gradient(place, pick(flipped, near), pick(values, near), last=False)
    parts[-1] = after(parts[-1], values_first)
    keys = {0: key_backward(parts, incoming, 0)}
    for k in far:
        keys[k] = swap(keys[0], "fsdp", k)
    keys[1] = swap(keys[0], "fsdp", 1)

    grad_values, square, due = gradient(
        place, pick(flipped, rest), pick(values, rest), values_first
    )
    for k in near[2::2]:
        keys[k + 1] = swap(after(keys[k], square), "fsdp", 1)
    (keys_first,) = gradient(place, pick(flipped, near), pick(keys, near), last=False)
    for k in rest[::2]:
        keys[k + 1] = swap(after(keys[k], square), "fsdp", 1)
    grad_keys, square, due = gradient(
        place, pick(flipped, rest), pick(keys, rest), keys_first, square, due
    )

    square = square + swap(square, "fsdp", 1)
    squares = [square] + [swap(square, "fsdp", k) for k in chips]

    state = (params, first_moment[0], second_moment[0], grad_keys, grad_values)
    inner, *update = adam_frag(place, scalars, squares, old, old_first, old_second, due)
    steps = rows // ADAM_ROWS
    *results, ticket = adam_rows(scalars, squares, state, 0, steps // 2)
    own_sum = update[0].astype(jnp.float32)
    for k in range(1, replicas):
        own_sum = own_sum + swap(update[k], "rep", k).astype(jnp.float32)
    own_sum, ticket = lax.optimization_barrier((own_sum, ticket))
    sums = [own_sum.astype(jnp.bfloat16)]
    sums += [swap(sums[0], "rep", k) for k in range(1, replicas)]
    results = adam_rows(scalars, squares, state, steps // 2, steps, results)
    weights_out, anchor_out, momentum_out = outer_step(
        place,
        (results[0], anchor_copy, momentum_copy),
        base,
        sums,
        inner,
        anchor_cols,
        pseudo_old,
        moment_cols,
        own_sum,
        ticket,
    )
    plan_out = jnp.reshape(plan, (1,))
    return (
        weights_out[None],
        results[1][None],
        results[2][None],
        anchor_out,
        momentum_out,
        plan_out,
    )


def solution(mesh):
    tokens_spec = P("rep", "fsdp", None)
    outer_spec = P(("fsdp", "rep"), None)
    return jax.shard_map(
        body,
        mesh=mesh,
        in_specs=(tokens_spec,) * 5 + (outer_spec,) * 2 + (P(), P()),
        out_specs=(tokens_spec,) * 3 + (outer_spec,) * 2 + (P(),),
        check_vma=False,
    )
```

```python
import functools

import jax
import jax.numpy as jnp
from jax import lax
from jax.experimental import pallas as pl
from jax.experimental.pallas import tpu as pltpu
from jax.sharding import PartitionSpec as P

HEAD = 128
WARMUP = 2000
STEPS_TOTAL = 100000
FRAG_COLS = 128


BETA_ONE = 0.9
BETA_TWO = 0.95
ADAM_EPS = 1e-08
DECAY = 0.1
PEAK_RATE = 0.0003
CLIP_NORM = 1.0
OUTER_MU = 0.9
OUTER_RATE = 0.7
MIX_LOCAL = 0.5

MIB = 1 << 20
ADAM_ROWS = 128


def in_hbm(*arrays):
    return [pltpu.with_memory_space_constraint(a, pltpu.HBM) for a in arrays]


def params_of(limit):
    return pltpu.CompilerParams(vmem_limit_bytes=limit * MIB)


def cost(flops, moved):
    return pl.CostEstimate(flops=int(flops), bytes_accessed=int(moved), transcendentals=0)


def pack_kernel(offsets, me_ref, src_ref, *refs):
    half = len(offsets)
    out_refs, (held, in_sems, out_sems) = refs[:half], refs[half:]
    streams = in_sems.shape[1]
    count, rows = out_refs[0].shape
    step = count // streams
    fetches, stores = [], []
    for i, offset in enumerate(offsets):
        column = pl.multiple_of((me_ref[0] ^ offset) * rows, HEAD)
        for j in range(streams):
            at = pl.ds(j * step, step)
            block = src_ref.at[at, pl.ds(column, rows)]
            fetches.append(pltpu.make_async_copy(block, held.at[i, at], in_sems.at[i, j]))
            stores.append(pltpu.make_async_copy(held.at[i, at], out_refs[i].at[at], out_sems.at[i, j]))
    for copy in fetches:
        copy.start()
    for fetch, store in zip(fetches, stores):
        fetch.wait()
        store.start()
    for copy in stores:
        copy.wait()


def pack(tokens, me, rows, offsets):
    count = tokens.shape[0]
    streams = 4
    whole = pl.BlockSpec(memory_space=pl.ANY)
    outs = pl.pallas_call(
        functools.partial(pack_kernel, offsets),
        out_shape=[pltpu.HBM((count, rows), tokens.dtype)] * len(offsets),
        in_specs=[pl.BlockSpec(memory_space=pltpu.SMEM), whole],
        out_specs=[whole] * len(offsets),
        scratch_shapes=[
            pltpu.VMEM((len(offsets), count, rows), tokens.dtype),
            pltpu.SemaphoreType.DMA((len(offsets), streams)),
            pltpu.SemaphoreType.DMA((len(offsets), streams)),
        ],
        compiler_params=params_of(12),
        cost_estimate=cost(0, 4 * len(offsets) * count * rows),
        name="pack",
    )(me, *in_hbm(tokens))
    return dict(zip(offsets, outs))


def cast_kernel(src_ref, out_ref):
    out_ref[...] = src_ref[...].astype(out_ref.dtype)


def cast_left(array, width):
    rows = array.shape[0]
    block = pl.BlockSpec((256, width), lambda i: (i, 0))
    return pl.pallas_call(
        cast_kernel,
        out_shape=jax.ShapeDtypeStruct((rows, width), jnp.bfloat16),
        grid=(rows // 256,),
        in_specs=[block],
        out_specs=block,
        compiler_params=params_of(8),
        cost_estimate=cost(0, 6 * rows * width),
        name="cast_left",
    )(*in_hbm(array))


def partial_kernel(pieces, *refs):
    x_refs, w_ref, (*add_refs, out_ref, flip_ref) = refs[:pieces], refs[pieces], refs[pieces + 1:]
    x = jnp.concatenate([ref[...] for ref in x_refs], axis=1)
    total = jnp.dot(x, w_ref[...], preferred_element_type=jnp.float32)
    for ref in add_refs:
        total = total + ref[...].astype(jnp.float32)
    out_ref[...] = total.astype(out_ref.dtype)
    step = x_refs[0].shape[1]
    for i, ref in enumerate(x_refs):
        flip_ref[i * step:(i + 1) * step, :] = ref[...].T


def partial_keys(block, key_weights, *others):
    count, rows = block.shape
    width = key_weights.shape[1]
    pieces = 4 if rows % (4 * HEAD) == 0 else 2
    fixed = lambda a: pl.BlockSpec(a.shape, lambda i: (0, 0))
    return pl.pallas_call(
        functools.partial(partial_kernel, pieces),
        out_shape=[
            jax.ShapeDtypeStruct((count, width), jnp.bfloat16),
            jax.ShapeDtypeStruct((rows, count), jnp.bfloat16),
        ],
        grid=(1,),
        in_specs=[pl.BlockSpec((count, rows // pieces), lambda i, c=c: (0, c)) for c in range(pieces)]
        + [fixed(key_weights)]
        + [fixed(o) for o in others],
        out_specs=[
            pl.BlockSpec((count, width), lambda i: (0, 0)),
            pl.BlockSpec((rows, count), lambda i: (0, 0)),
        ],
        compiler_params=params_of(12),
        cost_estimate=cost(2 * count * rows * width, 4 * count * rows),
        name="partial_keys",
    )(*[block] * pieces, key_weights, *others)


def key_kernel(first, *refs):
    *part_refs, cot_ref, out_ref = refs
    count = out_ref.shape[0]
    raw = sum(ref[...].astype(jnp.float32) for ref in part_refs)
    for h in range(raw.shape[1] // HEAD):
        cols = slice(h * HEAD, (h + 1) * HEAD)
        head = raw[:, cols]
        inverse = lax.rsqrt(jnp.mean(head * head, axis=1, keepdims=True) + 1e-06)
        normed = head * inverse
        upper = cot_ref[first:first + count, cols].astype(jnp.float32)
        back = inverse * (upper - normed * jnp.mean(upper * normed, axis=1, keepdims=True))
        out_ref[:, cols] = back.astype(out_ref.dtype)


def key_backward(parts, incoming, first):
    count, width = parts[0].shape
    block = pl.BlockSpec((count, width), lambda i: (0, 0))
    cot = pl.BlockSpec((incoming.shape[0], width), lambda i: (0, 0))
    return pl.pallas_call(
        functools.partial(key_kernel, first),
        out_shape=jax.ShapeDtypeStruct((count, width), jnp.bfloat16),
        grid=(1,),
        in_specs=[block] * len(parts) + [cot],
        out_specs=block,
        compiler_params=params_of(8),
        cost_estimate=cost(60 * count * width, 12 * count * width),
        name="key_backward",
    )(*parts, incoming)


def grad_kernel(count, has_base, has_more, last, place_ref, *refs):
    refs = list(refs)
    x_refs, u_refs = refs[:count], refs[count:2 * count]
    refs = refs[2 * count:]
    base = refs.pop(0) if has_base else None
    square_in, due_in = (refs.pop(0), refs.pop(0)) if has_more else (None, None)
    out_ref = refs.pop(0)
    x = jnp.concatenate([ref[...] for ref in x_refs], axis=1)
    u = jnp.concatenate([ref[...] for ref in u_refs], axis=0)
    total = jnp.dot(x, u, preferred_element_type=jnp.float32)
    if has_base:
        total = total + base[...]
    out_ref[...] = total
    if last:
        sq_ref, due_ref = refs

        @pl.when(pl.program_id(0) == 0)
        def _():
            sq_ref[...] = square_in[...] if has_more else jnp.zeros_like(sq_ref)

        rows, width = total.shape
        squares = (total * total).reshape(rows // 8, 8, width).sum(axis=0)
        folded = squares[:, :HEAD]
        for h in range(1, width // HEAD):
            folded = folded + squares[:, h * HEAD:(h + 1) * HEAD]
        sq_ref[...] += folded
        heads = width // FRAG_COLS
        mine = place_ref[0] - (0 if has_more else heads)
        mine = jnp.minimum(jnp.maximum(mine, 0), heads - 1) * FRAG_COLS
        column = out_ref[:, pl.ds(pl.multiple_of(mine, FRAG_COLS), FRAG_COLS)]
        if has_more:
            column = jnp.where(place_ref[0] < heads, column, due_in[...])
        due_ref[...] = column


def gradient(place, flipped, upstream, base=None, square=None, due=None, last=True):
    rows, depth = flipped[0].shape
    width = upstream[0].shape[1]
    step = 256
    row_block = lambda cols: pl.BlockSpec((step, cols), lambda i, p: (i, 0))
    fixed = pl.BlockSpec((8, HEAD), lambda i, p: (0, 0))
    args = [*flipped, *upstream]
    specs = [row_block(depth)] * len(flipped)
    specs += [pl.BlockSpec((depth, width), lambda i, p: (0, 0))] * len(upstream)
    if base is not None:
        args.append(base)
        specs.append(row_block(width))
    if square is not None:
        args += [square, due]
        specs += [fixed, row_block(FRAG_COLS)]
    if last:
        shapes = [
            jax.ShapeDtypeStruct((rows, width), jnp.float32),
            jax.ShapeDtypeStruct((8, HEAD), jnp.float32),
            jax.ShapeDtypeStruct((rows, FRAG_COLS), jnp.float32),
        ]
        outs = [row_block(width), fixed, row_block(FRAG_COLS)]
    else:
        shapes = [jax.ShapeDtypeStruct((rows, width), jnp.float32)]
        outs = [row_block(width)]
    depth *= len(flipped)
    return pl.pallas_call(
        functools.partial(grad_kernel, len(flipped), base is not None, square is not None, last),
        out_shape=shapes,
        grid_spec=pltpu.PrefetchScalarGridSpec(
            num_scalar_prefetch=1, grid=(rows // step,), in_specs=specs, out_specs=outs
        ),
        compiler_params=params_of(12),
        cost_estimate=cost(2 * rows * width * depth, 2 * rows * depth + 4 * rows * width),
        name="gradient",
    )(place, *args)


def clip_factor(square_refs):
    square = jnp.sum(sum(ref[...] for ref in square_refs), keepdims=True)
    return jnp.minimum(1.0, CLIP_NORM / (jnp.sqrt(square) + 1e-06))


def adam(old, first, second, grad, factor, scalars):
    rate, inv_one, inv_two = (scalars[i] for i in range(3))
    clipped = grad * factor
    first_new = BETA_ONE * first + (1.0 - BETA_ONE) * clipped
    second_new = BETA_TWO * second + (1.0 - BETA_TWO) * clipped * clipped
    update = rate * (
        first_new * inv_one / (jnp.sqrt(second_new * inv_two) + ADAM_EPS) + DECAY * old
    )
    return update, first_new, second_new


def adam_kernel(squares, extra, sc_ref, w_ref, m_ref, v_ref, gk_ref, gv_ref, *refs):
    factor = clip_factor(refs[:squares])
    w_out, m_out, v_out, *done = refs[squares + extra:]
    width = gk_ref.shape[1]
    for g_ref, cols in ((gk_ref, slice(0, width)), (gv_ref, slice(width, 2 * width))):
        old = w_ref[:, cols]
        update, first_new, second_new = adam(
            old, m_ref[:, cols], v_ref[:, cols], g_ref[...], factor, sc_ref
        )
        w_out[:, cols] = old - update
        m_out[:, cols] = first_new
        v_out[:, cols] = second_new
    for ref in done:
        ref[...] = jnp.zeros_like(ref)


def adam_rows(scalars, squares, state, first, last, into=()):
    rows, width = state[0].shape
    step = ADAM_ROWS
    full = pl.BlockSpec((step, width), lambda i: (i + first, 0))
    half = pl.BlockSpec((step, width // 2), lambda i: (i + first, 0))
    shapes = [pltpu.HBM((rows, width), jnp.float32)] * 3
    outs = [full] * 3
    if not into:
        shapes.append(jax.ShapeDtypeStruct((8, HEAD), jnp.float32))
        outs.append(pl.BlockSpec((8, HEAD), lambda i: (0, 0)))
    count = (last - first) * step
    return pl.pallas_call(
        functools.partial(adam_kernel, len(squares), len(into)),
        out_shape=shapes,
        grid=(last - first,),
        in_specs=[pl.BlockSpec(memory_space=pltpu.SMEM), full, full, full, half, half]
        + [pl.BlockSpec((8, HEAD), lambda i: (0, 0))] * len(squares)
        + [pl.BlockSpec(memory_space=pl.ANY)] * len(into),
        out_specs=outs,
        input_output_aliases={6 + len(squares) + i: i for i in range(len(into))},
        compiler_params=params_of(12),
        cost_estimate=cost(20 * count * width, 28 * count * width),
        name="adam_rows",
    )(scalars, *state, *squares, *in_hbm(*into))


def frag_kernel(squares, place_ref, sc_ref, w_ref, m_ref, v_ref, g_ref, *refs):
    blocks, part, _ = w_ref.shape
    factor = clip_factor(refs[:squares])
    inner_ref, *out_refs = refs[squares:]
    for j in range(blocks):
        at = pl.multiple_of((place_ref[1] ^ j) * part, 8)
        old = w_ref[j]
        update, _, _ = adam(old, m_ref[j], v_ref[j], g_ref[pl.ds(at, part), :], factor, sc_ref)
        inner_ref[j] = old - update
        out_refs[j][...] = update.astype(out_refs[j].dtype)


def adam_frag(place, scalars, squares, old, first, second, grad):
    blocks, part, width = old.shape
    smem = pl.BlockSpec(memory_space=pltpu.SMEM)
    vmem = pl.BlockSpec(memory_space=pltpu.VMEM)
    return pl.pallas_call(
        functools.partial(frag_kernel, len(squares)),
        out_shape=[jax.ShapeDtypeStruct(old.shape, jnp.float32)]
        + [jax.ShapeDtypeStruct((part, width), jnp.bfloat16)] * blocks,
        in_specs=[smem, smem] + [vmem] * (4 + len(squares)),
        out_specs=[vmem] * (1 + blocks),
        compiler_params=params_of(12),
        cost_estimate=cost(20 * old.size, 22 * old.size),
        name="adam_frag",
    )(place, scalars, old, first, second, grad, *squares)


def pick_kernel(blocks, place_ref, *refs):
    outs = refs[len(refs) // (blocks + 1) * blocks:]
    for i, out_ref in enumerate(outs):
        for j in range(blocks):
            out_ref[j] = refs[i * blocks + j][...]


def due_columns(place, part, *arrays):
    blocks = arrays[0].shape[0] // part
    specs = []
    for j in range(blocks):
        at = (lambda i, p, j=j: (p[1] ^ j, p[0])) if blocks > 1 else (lambda i, p: (0, p[0]))
        specs.append(pl.BlockSpec((part, FRAG_COLS), at))
    shape = (blocks, part, FRAG_COLS)
    return pl.pallas_call(
        functools.partial(pick_kernel, blocks),
        out_shape=[jax.ShapeDtypeStruct(shape, a.dtype) for a in arrays],
        grid_spec=pltpu.PrefetchScalarGridSpec(
            num_scalar_prefetch=1,
            grid=(1,),
            in_specs=specs * len(arrays),
            out_specs=[pl.BlockSpec(shape, lambda i, p: (0, 0, 0))] * len(arrays),
        ),
        compiler_params=params_of(12),
        cost_estimate=cost(0, 8 * blocks * part * FRAG_COLS * len(arrays)),
        name="due_columns",
    )(place, *[a for array in in_hbm(*arrays) for a in [array] * blocks])


def duplicate_kernel(*refs):
    half = (len(refs) - 3) // 2
    held, in_sems, out_sems = refs[2 * half:]
    streams = held.shape[1]
    step = held.shape[2]
    places = [(a, i, pl.ds(i * step, step)) for a in range(half) for i in range(streams)]
    fetches = [
        pltpu.make_async_copy(refs[a].at[at], held.at[a, i], in_sems.at[a, i]) for a, i, at in places
    ]
    stores = [
        pltpu.make_async_copy(held.at[a, i], refs[half + a].at[at], out_sems.at[a, i])
        for a, i, at in places
    ]
    for copy in fetches:
        copy.start()
    for fetch, store in zip(fetches, stores):
        fetch.wait()
        store.start()
    for copy in stores:
        copy.wait()


def duplicate(*arrays):
    rows, width = arrays[0].shape
    streams = 4
    whole = pl.BlockSpec(memory_space=pl.ANY)
    return pl.pallas_call(
        duplicate_kernel,
        out_shape=[pltpu.HBM(a.shape, a.dtype) for a in arrays],
        in_specs=[whole] * len(arrays),
        out_specs=[whole] * len(arrays),
        scratch_shapes=[
            pltpu.VMEM((len(arrays), streams, rows // streams, width), arrays[0].dtype),
            pltpu.SemaphoreType.DMA((len(arrays), streams)),
            pltpu.SemaphoreType.DMA((len(arrays), streams)),
        ],
        compiler_params=params_of(8),
        cost_estimate=cost(0, sum(8 * a.size for a in arrays)),
        name="duplicate",
    )(*in_hbm(*arrays))


def outer_kernel(replicas, place_ref, *refs):
    share = 1.0 / replicas
    base_refs, sum_refs = refs[3:3 + replicas], refs[3 + replicas:3 + 2 * replicas]
    inner_ref, a_ref, p_ref, m_ref, own_ref, _, w_out, a_out, m_out = refs[3 + 2 * replicas:]
    scale = share * (1.0 + OUTER_MU) * OUTER_RATE
    for j in range(replicas):

        @pl.when(pl.program_id(0) == j)
        def _():
            fresh = base_refs[j][...] - scale * sum_refs[j][...].astype(jnp.float32)
            w_out[...] = MIX_LOCAL * inner_ref[0] + (1.0 - MIX_LOCAL) * fresh

    @pl.when(pl.program_id(0) == 0)
    def _():
        pseudo = p_ref[...] + share * own_ref[...]
        new_moment = OUTER_MU * m_ref[...] + pseudo
        m_out[...] = new_moment
        a_out[...] = a_ref[...] - OUTER_RATE * (OUTER_MU * new_moment + pseudo)


def outer_step(place, outputs, base, sums, inner, anchor, pseudo, momentum, own_sum, ticket):
    replicas, part = inner.shape[0], inner.shape[1]
    mixed = pl.BlockSpec((part, FRAG_COLS), lambda j, p: (p[1] ^ j, p[0]))
    pieces = pl.BlockSpec((1, part, FRAG_COLS), lambda j, p: (j, 0, 0))
    due = pl.BlockSpec((part, FRAG_COLS), lambda j, p: (0, p[0]))
    plain = pl.BlockSpec((part, FRAG_COLS), lambda j, p: (0, 0))
    whole = pl.BlockSpec(memory_space=pl.ANY)
    return pl.pallas_call(
        functools.partial(outer_kernel, replicas),
        out_shape=[pltpu.HBM(a.shape, a.dtype) for a in outputs],
        grid_spec=pltpu.PrefetchScalarGridSpec(
            num_scalar_prefetch=1,
            grid=(replicas,),
            in_specs=[whole] * 3 + [plain] * (2 * replicas) + [pieces] + [plain] * 4 + [whole],
            out_specs=[mixed, due, due],
        ),
        input_output_aliases={1: 0, 2: 1, 3: 2},
        compiler_params=params_of(12),
        cost_estimate=cost(10 * replicas * part * FRAG_COLS, 20 * replicas * part * FRAG_COLS),
        name="outer_step",
    )(place, *in_hbm(*outputs), *base, *sums, inner, anchor, pseudo, momentum, own_sum, ticket)


def swap(block, axis, offset):
    count = lax.axis_size(axis)
    return lax.ppermute(block, axis, [(i, i ^ offset) for i in range(count)])


def after(value, *others):
    return lax.optimization_barrier((value,) + others)[0]


def body(
    tokens,
    cotangent,
    weights,
    first_moment,
    second_moment,
    anchor,
    momentum,
    due_fragment,
    step_count,
):
    inputs, incoming, params = tokens[0], cotangent[0], weights[0]
    kv_width = incoming.shape[1] // 2
    rows = params.shape[0]
    part = anchor.shape[0]
    replicas = lax.axis_size("rep")
    shards = lax.axis_size("fsdp")
    me = jnp.reshape(lax.axis_index("fsdp"), (1,)).astype(jnp.int32)
    my_rep = lax.axis_index("rep").astype(jnp.int32)
    place = jnp.stack([due_fragment[0], my_rep])
    chips = range(2, shards, 2)
    far = sorted(chips, key=lambda k: (-bin(k).count("1"), k))
    order = [k for k in far[:-2] for k in (k, k + 1)]
    order += far[-2:] + [k + 1 for k in far[-2:]]

    packed = {}
    for offsets in (order[:1], order[1:4], order[4:], (0, 1)):
        packed |= pack(inputs, me, rows, tuple(offsets))
    blocks = {k: swap(packed[k], "fsdp", k) for k in order}
    blocks[0], blocks[1] = packed[0], swap(packed[1], "fsdp", 1)

    (old,) = due_columns(after(place, blocks[order[0]]), part, params)
    old_sums = [old[0]] + [swap(old[k], "rep", k) for k in range(1, replicas)]

    values = {0: incoming[:, kv_width:]}
    for i, k in enumerate(far):
        values[k] = swap(after(values[0], blocks[order[i]]), "fsdp", k)
    for k in range(0, shards, 2):
        values[k + 1] = swap(values[k], "fsdp", 1)

    steps_now = step_count[0].astype(jnp.float32)
    plan = jnp.minimum(1.0, steps_now / WARMUP) * (
        0.55 + 0.45 * jnp.cos(jnp.pi * steps_now / STEPS_TOTAL)
    )
    rate = PEAK_RATE * plan
    inv_one = 1.0 / (1.0 - jnp.power(BETA_ONE, steps_now))
    inv_two = 1.0 / (1.0 - jnp.power(BETA_TWO, steps_now))
    scalars = jnp.stack([rate, inv_one, inv_two])
    old_first, old_second = due_columns(place, part, first_moment[0], second_moment[0])
    anchor_cols, moment_cols = (c[0] for c in due_columns(place, part, anchor, momentum))
    pseudo_old = anchor_cols - sum(old_sums[1:], old_sums[0]) / replicas
    base = anchor_cols - OUTER_RATE * (OUTER_MU * (OUTER_MU * moment_cols + pseudo_old) + pseudo_old)
    base = [base] + [swap(base, "rep", k) for k in range(1, replicas)]
    anchor_copy, momentum_copy = duplicate(anchor, momentum)
    key_weights = cast_left(params, kv_width)

    last = far[-1]
    blocks[last + 1] = after(blocks[last + 1], anchor_copy, momentum_copy, scalars, old_first, old_second)
    parts, flipped = [], {}
    for k in far + [0]:
        theirs, flipped[k + 1] = partial_keys(blocks[k + 1], key_weights)
        theirs = swap(theirs, "fsdp", 1)
        if k == last:
            theirs = after(theirs, *parts[:1], pseudo_old)
        part_k, flipped[k] = partial_keys(blocks[k], key_weights, theirs)
        parts.append(swap(part_k, "fsdp", k) if k else part_k)
    spread = [0, 1] + [k + odd for k in far for odd in range(2)]
    near, rest = spread[:shards // 2], spread[shards // 2:]
    pick = lambda table, which: [table[k] for k in which]
    (values_first,) = gradient(place, pick(flipped, near), pick(values, near), last=False)
    parts[-1] = after(parts[-1], values_first)
    keys = {0: key_backward(parts, incoming, 0)}
    for k in far:
        keys[k] = swap(keys[0], "fsdp", k)
    keys[1] = swap(keys[0], "fsdp", 1)

    grad_values, square, due = gradient(
        place, pick(flipped, rest), pick(values, rest), values_first
    )
    for k in near[2::2]:
        keys[k + 1] = swap(after(keys[k], square), "fsdp", 1)
    (keys_first,) = gradient(place, pick(flipped, near), pick(keys, near), last=False)
    for k in rest[::2]:
        keys[k + 1] = swap(after(keys[k], square), "fsdp", 1)
    grad_keys, square, due = gradient(
        after(place, *base), pick(flipped, rest), pick(keys, rest), keys_first, square, due
    )

    square = square + swap(square, "fsdp", 1)
    squares = [square] + [swap(square, "fsdp", k) for k in chips]

    state = (params, first_moment[0], second_moment[0], grad_keys, grad_values)
    inner, *update = adam_frag(place, scalars, squares, old, old_first, old_second, due)
    steps = rows // ADAM_ROWS
    *results, ticket = adam_rows(scalars, squares, state, 0, steps // 2)
    own_sum = update[0].astype(jnp.float32)
    for k in range(1, replicas):
        own_sum = own_sum + swap(update[k], "rep", k).astype(jnp.float32)
    own_sum, ticket = lax.optimization_barrier((own_sum, ticket))
    sums = [own_sum.astype(jnp.bfloat16)]
    sums += [swap(sums[0], "rep", k) for k in range(1, replicas)]
    results = adam_rows(scalars, squares, state, steps // 2, steps, results)
    weights_out, anchor_out, momentum_out = outer_step(
        place,
        (results[0], anchor_copy, momentum_copy),
        base,
        sums,
        inner,
        anchor_cols,
        pseudo_old,
        moment_cols,
        own_sum,
        ticket,
    )
    plan_out = jnp.reshape(plan, (1,))
    return (
        weights_out[None],
        results[1][None],
        results[2][None],
        anchor_out,
        momentum_out,
        plan_out,
    )


def solution(mesh):
    tokens_spec = P("rep", "fsdp", None)
    outer_spec = P(("fsdp", "rep"), None)
    return jax.shard_map(
        body,
        mesh=mesh,
        in_specs=(tokens_spec,) * 5 + (outer_spec,) * 2 + (P(), P()),
        out_specs=(tokens_spec,) * 3 + (outer_spec,) * 2 + (P(),),
        check_vma=False,
    )
```

```python
import functools

import jax
import jax.numpy as jnp
from jax import lax
from jax.experimental import pallas as pl
from jax.experimental.pallas import tpu as pltpu
from jax.sharding import PartitionSpec as P

HEAD = 128
WARMUP = 2000
STEPS_TOTAL = 100000
FRAG_COLS = 128


BETA_ONE = 0.9
BETA_TWO = 0.95
ADAM_EPS = 1e-08
DECAY = 0.1
PEAK_RATE = 0.0003
CLIP_NORM = 1.0
OUTER_MU = 0.9
OUTER_RATE = 0.7
MIX_LOCAL = 0.5

MIB = 1 << 20
ADAM_ROWS = 128


def in_hbm(*arrays):
    return [pltpu.with_memory_space_constraint(a, pltpu.HBM) for a in arrays]


def params_of(limit):
    return pltpu.CompilerParams(vmem_limit_bytes=limit * MIB)


def cost(flops, moved):
    return pl.CostEstimate(flops=int(flops), bytes_accessed=int(moved), transcendentals=0)


def pack_kernel(offsets, me_ref, src_ref, *refs):
    half = len(offsets)
    out_refs, (held, in_sems, out_sems) = refs[:half], refs[half:]
    streams = in_sems.shape[1]
    count, rows = out_refs[0].shape
    step = count // streams
    fetches, stores = [], []
    for i, offset in enumerate(offsets):
        column = pl.multiple_of((me_ref[0] ^ offset) * rows, HEAD)
        for j in range(streams):
            at = pl.ds(j * step, step)
            block = src_ref.at[at, pl.ds(column, rows)]
            fetches.append(pltpu.make_async_copy(block, held.at[i, at], in_sems.at[i, j]))
            stores.append(pltpu.make_async_copy(held.at[i, at], out_refs[i].at[at], out_sems.at[i, j]))
    for copy in fetches:
        copy.start()
    for fetch, store in zip(fetches, stores):
        fetch.wait()
        store.start()
    for copy in stores:
        copy.wait()


def pack(tokens, me, rows, offsets):
    count = tokens.shape[0]
    streams = 4
    whole = pl.BlockSpec(memory_space=pl.ANY)
    outs = pl.pallas_call(
        functools.partial(pack_kernel, offsets),
        out_shape=[pltpu.HBM((count, rows), tokens.dtype)] * len(offsets),
        in_specs=[pl.BlockSpec(memory_space=pltpu.SMEM), whole],
        out_specs=[whole] * len(offsets),
        scratch_shapes=[
            pltpu.VMEM((len(offsets), count, rows), tokens.dtype),
            pltpu.SemaphoreType.DMA((len(offsets), streams)),
            pltpu.SemaphoreType.DMA((len(offsets), streams)),
        ],
        compiler_params=params_of(12),
        cost_estimate=cost(0, 4 * len(offsets) * count * rows),
        name="pack",
    )(me, *in_hbm(tokens))
    return dict(zip(offsets, outs))


def cast_kernel(src_ref, out_ref):
    out_ref[...] = src_ref[...].astype(out_ref.dtype)


def cast_left(array, width):
    rows = array.shape[0]
    block = pl.BlockSpec((256, width), lambda i: (i, 0))
    return pl.pallas_call(
        cast_kernel,
        out_shape=jax.ShapeDtypeStruct((rows, width), jnp.bfloat16),
        grid=(rows // 256,),
        in_specs=[block],
        out_specs=block,
        compiler_params=params_of(8),
        cost_estimate=cost(0, 6 * rows * width),
        name="cast_left",
    )(*in_hbm(array))


def partial_kernel(pieces, firsts, splits, *refs):
    x_refs, w_ref, refs = refs[:pieces], refs[pieces], refs[pieces + 1:]
    add_refs, out_refs, flip_ref = refs[:len(firsts)], refs[len(firsts):-1], refs[-1]
    x = jnp.concatenate([ref[...] for ref in x_refs], axis=1)
    total = jnp.dot(x, w_ref[...], preferred_element_type=jnp.float32)
    count = total.shape[0]
    for ref, first in zip(add_refs, firsts):
        last = first + ref.shape[0]
        rows = [total[:first], total[first:last] + ref[...].astype(jnp.float32), total[last:]]
        total = jnp.concatenate([r for r in rows if r.shape[0]], axis=0)
    height = count // splits
    for i, ref in enumerate(out_refs):
        ref[...] = total[i * height:(i + 1) * height].astype(ref.dtype)
    step = x_refs[0].shape[1]
    for i, ref in enumerate(x_refs):
        flip_ref[i * step:(i + 1) * step, :] = ref[...].T


def partial_keys(block, key_weights, adds=(), splits=1):
    count, rows = block.shape
    width = key_weights.shape[1]
    pieces = 4 if rows % (4 * HEAD) == 0 else 2
    fixed = lambda a: pl.BlockSpec(a.shape, lambda i: (0, 0))
    *parts, flipped = pl.pallas_call(
        functools.partial(partial_kernel, pieces, [first for _, first in adds], splits),
        out_shape=[jax.ShapeDtypeStruct((count // splits, width), jnp.bfloat16)] * splits
        + [jax.ShapeDtypeStruct((rows, count), jnp.bfloat16)],
        grid=(1,),
        in_specs=[pl.BlockSpec((count, rows // pieces), lambda i, c=c: (0, c)) for c in range(pieces)]
        + [fixed(key_weights)]
        + [fixed(a) for a, _ in adds],
        out_specs=[pl.BlockSpec((count // splits, width), lambda i: (0, 0))] * splits
        + [pl.BlockSpec((rows, count), lambda i: (0, 0))],
        compiler_params=params_of(12),
        cost_estimate=cost(2 * count * rows * width, 4 * count * rows),
        name="partial_keys",
    )(*[block] * pieces, key_weights, *[a for a, _ in adds])
    return parts if splits > 1 else parts[0], flipped


def key_kernel(first, *refs):
    *part_refs, cot_ref, out_ref = refs
    count = out_ref.shape[0]
    raw = sum(ref[...].astype(jnp.float32) for ref in part_refs)
    for h in range(raw.shape[1] // HEAD):
        cols = slice(h * HEAD, (h + 1) * HEAD)
        head = raw[:, cols]
        inverse = lax.rsqrt(jnp.mean(head * head, axis=1, keepdims=True) + 1e-06)
        normed = head * inverse
        upper = cot_ref[first:first + count, cols].astype(jnp.float32)
        back = inverse * (upper - normed * jnp.mean(upper * normed, axis=1, keepdims=True))
        out_ref[:, cols] = back.astype(out_ref.dtype)


def key_backward(parts, incoming, first):
    count, width = parts[0].shape
    block = pl.BlockSpec((count, width), lambda i: (0, 0))
    cot = pl.BlockSpec((incoming.shape[0], width), lambda i: (0, 0))
    return pl.pallas_call(
        functools.partial(key_kernel, first),
        out_shape=jax.ShapeDtypeStruct((count, width), jnp.bfloat16),
        grid=(1,),
        in_specs=[block] * len(parts) + [cot],
        out_specs=block,
        compiler_params=params_of(8),
        cost_estimate=cost(60 * count * width, 12 * count * width),
        name="key_backward",
    )(*parts, incoming)


def grad_kernel(count, has_base, has_more, last, place_ref, *refs):
    refs = list(refs)
    x_refs, u_refs = refs[:count], refs[count:2 * count]
    refs = refs[2 * count:]
    base = refs.pop(0) if has_base else None
    square_in, due_in = (refs.pop(0), refs.pop(0)) if has_more else (None, None)
    out_ref = refs.pop(0)
    x = jnp.concatenate([ref[...] for ref in x_refs], axis=1)
    u = jnp.concatenate([ref[...] for ref in u_refs], axis=0)
    total = jnp.dot(x, u, preferred_element_type=jnp.float32)
    if has_base:
        total = total + base[...]
    out_ref[...] = total
    if last:
        sq_ref, due_ref = refs

        @pl.when(pl.program_id(0) == 0)
        def _():
            sq_ref[...] = square_in[...] if has_more else jnp.zeros_like(sq_ref)

        rows, width = total.shape
        squares = (total * total).reshape(rows // 8, 8, width).sum(axis=0)
        folded = squares[:, :HEAD]
        for h in range(1, width // HEAD):
            folded = folded + squares[:, h * HEAD:(h + 1) * HEAD]
        sq_ref[...] += folded
        heads = width // FRAG_COLS
        mine = place_ref[0] - (0 if has_more else heads)
        mine = jnp.minimum(jnp.maximum(mine, 0), heads - 1) * FRAG_COLS
        column = out_ref[:, pl.ds(pl.multiple_of(mine, FRAG_COLS), FRAG_COLS)]
        if has_more:
            column = jnp.where(place_ref[0] < heads, column, due_in[...])
        due_ref[...] = column


def gradient(place, flipped, upstream, base=None, square=None, due=None, last=True):
    rows, depth = flipped[0].shape
    width = upstream[0].shape[1]
    step = 256
    row_block = lambda cols: pl.BlockSpec((step, cols), lambda i, p: (i, 0))
    fixed = pl.BlockSpec((8, HEAD), lambda i, p: (0, 0))
    args = [*flipped, *upstream]
    specs = [row_block(depth)] * len(flipped)
    specs += [pl.BlockSpec((depth, width), lambda i, p: (0, 0))] * len(upstream)
    if base is not None:
        args.append(base)
        specs.append(row_block(width))
    if square is not None:
        args += [square, due]
        specs += [fixed, row_block(FRAG_COLS)]
    if last:
        shapes = [
            jax.ShapeDtypeStruct((rows, width), jnp.float32),
            jax.ShapeDtypeStruct((8, HEAD), jnp.float32),
            jax.ShapeDtypeStruct((rows, FRAG_COLS), jnp.float32),
        ]
        outs = [row_block(width), fixed, row_block(FRAG_COLS)]
    else:
        shapes = [jax.ShapeDtypeStruct((rows, width), jnp.float32)]
        outs = [row_block(width)]
    depth *= len(flipped)
    return pl.pallas_call(
        functools.partial(grad_kernel, len(flipped), base is not None, square is not None, last),
        out_shape=shapes,
        grid_spec=pltpu.PrefetchScalarGridSpec(
            num_scalar_prefetch=1, grid=(rows // step,), in_specs=specs, out_specs=outs
        ),
        compiler_params=params_of(12),
        cost_estimate=cost(2 * rows * width * depth, 2 * rows * depth + 4 * rows * width),
        name="gradient",
    )(place, *args)


def clip_factor(square_refs):
    square = jnp.sum(sum(ref[...] for ref in square_refs), keepdims=True)
    return jnp.minimum(1.0, CLIP_NORM / (jnp.sqrt(square) + 1e-06))


def adam(old, first, second, grad, factor, scalars):
    rate, inv_one, inv_two = (scalars[i] for i in range(3))
    clipped = grad * factor
    first_new = BETA_ONE * first + (1.0 - BETA_ONE) * clipped
    second_new = BETA_TWO * second + (1.0 - BETA_TWO) * clipped * clipped
    update = rate * (
        first_new * inv_one / (jnp.sqrt(second_new * inv_two) + ADAM_EPS) + DECAY * old
    )
    return update, first_new, second_new


def adam_kernel(squares, extra, sc_ref, w_ref, m_ref, v_ref, gk_ref, gv_ref, *refs):
    factor = clip_factor(refs[:squares])
    w_out, m_out, v_out, *done = refs[squares + extra:]
    width = gk_ref.shape[1]
    for g_ref, cols in ((gk_ref, slice(0, width)), (gv_ref, slice(width, 2 * width))):
        old = w_ref[:, cols]
        update, first_new, second_new = adam(
            old, m_ref[:, cols], v_ref[:, cols], g_ref[...], factor, sc_ref
        )
        w_out[:, cols] = old - update
        m_out[:, cols] = first_new
        v_out[:, cols] = second_new
    for ref in done:
        ref[...] = jnp.zeros_like(ref)


def adam_rows(scalars, squares, state, first, last, into=()):
    rows, width = state[0].shape
    step = ADAM_ROWS
    full = pl.BlockSpec((step, width), lambda i: (i + first, 0))
    half = pl.BlockSpec((step, width // 2), lambda i: (i + first, 0))
    shapes = [pltpu.HBM((rows, width), jnp.float32)] * 3
    outs = [full] * 3
    if not into:
        shapes.append(jax.ShapeDtypeStruct((8, HEAD), jnp.float32))
        outs.append(pl.BlockSpec((8, HEAD), lambda i: (0, 0)))
    count = (last - first) * step
    return pl.pallas_call(
        functools.partial(adam_kernel, len(squares), len(into)),
        out_shape=shapes,
        grid=(last - first,),
        in_specs=[pl.BlockSpec(memory_space=pltpu.SMEM), full, full, full, half, half]
        + [pl.BlockSpec((8, HEAD), lambda i: (0, 0))] * len(squares)
        + [pl.BlockSpec(memory_space=pl.ANY)] * len(into),
        out_specs=outs,
        input_output_aliases={6 + len(squares) + i: i for i in range(len(into))},
        compiler_params=params_of(12),
        cost_estimate=cost(20 * count * width, 28 * count * width),
        name="adam_rows",
    )(scalars, *state, *squares, *in_hbm(*into))


def frag_kernel(squares, place_ref, sc_ref, w_ref, m_ref, v_ref, g_ref, *refs):
    blocks, part, _ = w_ref.shape
    factor = clip_factor(refs[:squares])
    inner_ref, *out_refs = refs[squares:]
    for j in range(blocks):
        at = pl.multiple_of((place_ref[1] ^ j) * part, 8)
        old = w_ref[j]
        update, _, _ = adam(old, m_ref[j], v_ref[j], g_ref[pl.ds(at, part), :], factor, sc_ref)
        inner_ref[j] = old - update
        out_refs[j][...] = update.astype(out_refs[j].dtype)


def adam_frag(place, scalars, squares, old, first, second, grad):
    blocks, part, width = old.shape
    smem = pl.BlockSpec(memory_space=pltpu.SMEM)
    vmem = pl.BlockSpec(memory_space=pltpu.VMEM)
    return pl.pallas_call(
        functools.partial(frag_kernel, len(squares)),
        out_shape=[jax.ShapeDtypeStruct(old.shape, jnp.float32)]
        + [jax.ShapeDtypeStruct((part, width), jnp.bfloat16)] * blocks,
        in_specs=[smem, smem] + [vmem] * (4 + len(squares)),
        out_specs=[vmem] * (1 + blocks),
        compiler_params=params_of(12),
        cost_estimate=cost(20 * old.size, 22 * old.size),
        name="adam_frag",
    )(place, scalars, old, first, second, grad, *squares)


def pick_kernel(blocks, place_ref, *refs):
    outs = refs[len(refs) // (blocks + 1) * blocks:]
    for i, out_ref in enumerate(outs):
        for j in range(blocks):
            out_ref[j] = refs[i * blocks + j][...]


def due_columns(place, part, *arrays):
    blocks = arrays[0].shape[0] // part
    specs = []
    for j in range(blocks):
        at = (lambda i, p, j=j: (p[1] ^ j, p[0])) if blocks > 1 else (lambda i, p: (0, p[0]))
        specs.append(pl.BlockSpec((part, FRAG_COLS), at))
    shape = (blocks, part, FRAG_COLS)
    return pl.pallas_call(
        functools.partial(pick_kernel, blocks),
        out_shape=[jax.ShapeDtypeStruct(shape, a.dtype) for a in arrays],
        grid_spec=pltpu.PrefetchScalarGridSpec(
            num_scalar_prefetch=1,
            grid=(1,),
            in_specs=specs * len(arrays),
            out_specs=[pl.BlockSpec(shape, lambda i, p: (0, 0, 0))] * len(arrays),
        ),
        compiler_params=params_of(12),
        cost_estimate=cost(0, 8 * blocks * part * FRAG_COLS * len(arrays)),
        name="due_columns",
    )(place, *[a for array in in_hbm(*arrays) for a in [array] * blocks])


def duplicate_kernel(*refs):
    half = (len(refs) - 3) // 2
    held, in_sems, out_sems = refs[2 * half:]
    streams = held.shape[1]
    step = held.shape[2]
    places = [(a, i, pl.ds(i * step, step)) for a in range(half) for i in range(streams)]
    fetches = [
        pltpu.make_async_copy(refs[a].at[at], held.at[a, i], in_sems.at[a, i]) for a, i, at in places
    ]
    stores = [
        pltpu.make_async_copy(held.at[a, i], refs[half + a].at[at], out_sems.at[a, i])
        for a, i, at in places
    ]
    for copy in fetches:
        copy.start()
    for fetch, store in zip(fetches, stores):
        fetch.wait()
        store.start()
    for copy in stores:
        copy.wait()


def duplicate(*arrays):
    rows, width = arrays[0].shape
    streams = 4
    whole = pl.BlockSpec(memory_space=pl.ANY)
    return pl.pallas_call(
        duplicate_kernel,
        out_shape=[pltpu.HBM(a.shape, a.dtype) for a in arrays],
        in_specs=[whole] * len(arrays),
        out_specs=[whole] * len(arrays),
        scratch_shapes=[
            pltpu.VMEM((len(arrays), streams, rows // streams, width), arrays[0].dtype),
            pltpu.SemaphoreType.DMA((len(arrays), streams)),
            pltpu.SemaphoreType.DMA((len(arrays), streams)),
        ],
        compiler_params=params_of(8),
        cost_estimate=cost(0, sum(8 * a.size for a in arrays)),
        name="duplicate",
    )(*in_hbm(*arrays))


def outer_kernel(replicas, place_ref, *refs):
    share = 1.0 / replicas
    base_refs, sum_refs = refs[3:3 + replicas], refs[3 + replicas:3 + 2 * replicas]
    inner_ref, a_ref, p_ref, m_ref, own_ref, _, w_out, a_out, m_out = refs[3 + 2 * replicas:]
    scale = share * (1.0 + OUTER_MU) * OUTER_RATE
    for j in range(replicas):

        @pl.when(pl.program_id(0) == j)
        def _():
            fresh = base_refs[j][...] - scale * sum_refs[j][...].astype(jnp.float32)
            w_out[...] = MIX_LOCAL * inner_ref[0] + (1.0 - MIX_LOCAL) * fresh

    @pl.when(pl.program_id(0) == 0)
    def _():
        pseudo = p_ref[...] + share * own_ref[...]
        new_moment = OUTER_MU * m_ref[...] + pseudo
        m_out[...] = new_moment
        a_out[...] = a_ref[...] - OUTER_RATE * (OUTER_MU * new_moment + pseudo)


def outer_step(place, outputs, base, sums, inner, anchor, pseudo, momentum, own_sum, ticket):
    replicas, part = inner.shape[0], inner.shape[1]
    mixed = pl.BlockSpec((part, FRAG_COLS), lambda j, p: (p[1] ^ j, p[0]))
    pieces = pl.BlockSpec((1, part, FRAG_COLS), lambda j, p: (j, 0, 0))
    due = pl.BlockSpec((part, FRAG_COLS), lambda j, p: (0, p[0]))
    plain = pl.BlockSpec((part, FRAG_COLS), lambda j, p: (0, 0))
    whole = pl.BlockSpec(memory_space=pl.ANY)
    return pl.pallas_call(
        functools.partial(outer_kernel, replicas),
        out_shape=[pltpu.HBM(a.shape, a.dtype) for a in outputs],
        grid_spec=pltpu.PrefetchScalarGridSpec(
            num_scalar_prefetch=1,
            grid=(replicas,),
            in_specs=[whole] * 3 + [plain] * (2 * replicas) + [pieces] + [plain] * 4 + [whole],
            out_specs=[mixed, due, due],
        ),
        input_output_aliases={1: 0, 2: 1, 3: 2},
        compiler_params=params_of(12),
        cost_estimate=cost(10 * replicas * part * FRAG_COLS, 20 * replicas * part * FRAG_COLS),
        name="outer_step",
    )(place, *in_hbm(*outputs), *base, *sums, inner, anchor, pseudo, momentum, own_sum, ticket)


def swap(block, axis, offset):
    count = lax.axis_size(axis)
    return lax.ppermute(block, axis, [(i, i ^ offset) for i in range(count)])


def after(value, *others):
    return lax.optimization_barrier((value,) + others)[0]


def body(
    tokens,
    cotangent,
    weights,
    first_moment,
    second_moment,
    anchor,
    momentum,
    due_fragment,
    step_count,
):
    inputs, incoming, params = tokens[0], cotangent[0], weights[0]
    kv_width = incoming.shape[1] // 2
    rows = params.shape[0]
    part = anchor.shape[0]
    replicas = lax.axis_size("rep")
    shards = lax.axis_size("fsdp")
    me = jnp.reshape(lax.axis_index("fsdp"), (1,)).astype(jnp.int32)
    my_rep = lax.axis_index("rep").astype(jnp.int32)
    place = jnp.stack([due_fragment[0], my_rep])
    chips = range(2, shards, 2)
    far = sorted(chips, key=lambda k: (-bin(k).count("1"), k))
    order = [k for k in far[:-2] for k in (k, k + 1)]
    order += far[-2:] + [k + 1 for k in far[-2:]]

    (old,) = due_columns(place, part, params)
    old_sums = [old[0]] + [swap(old[k], "rep", k) for k in range(1, replicas)]

    packed = {}
    for offsets in (order[:1], order[1:4], order[4:], (0, 1)):
        packed |= pack(inputs, me, rows, tuple(offsets))
    blocks = {k: swap(packed[k], "fsdp", k) for k in order}
    blocks[0], blocks[1] = packed[0], swap(packed[1], "fsdp", 1)

    relay = len(far) == 3 and far[0] == far[1] ^ far[2]
    half = inputs.shape[0] // 2
    values = {0: incoming[:, kv_width:]}
    for i, k in enumerate(far[1:] if relay else far):
        values[k] = swap(after(values[0], blocks[order[i]]), "fsdp", k)
    if relay:
        upper = swap(values[far[1]][:half], "fsdp", far[2])
        lower = swap(values[far[2]][half:], "fsdp", far[1])
        values[far[0]] = jnp.concatenate([upper, lower], axis=0)

    steps_now = step_count[0].astype(jnp.float32)
    plan = jnp.minimum(1.0, steps_now / WARMUP) * (
        0.55 + 0.45 * jnp.cos(jnp.pi * steps_now / STEPS_TOTAL)
    )
    rate = PEAK_RATE * plan
    inv_one = 1.0 / (1.0 - jnp.power(BETA_ONE, steps_now))
    inv_two = 1.0 / (1.0 - jnp.power(BETA_TWO, steps_now))
    scalars = jnp.stack([rate, inv_one, inv_two])
    old_first, old_second = due_columns(place, part, first_moment[0], second_moment[0])
    anchor_cols, moment_cols = (c[0] for c in due_columns(place, part, anchor, momentum))
    pseudo_old = anchor_cols - sum(old_sums[1:], old_sums[0]) / replicas
    base = anchor_cols - OUTER_RATE * (OUTER_MU * (OUTER_MU * moment_cols + pseudo_old) + pseudo_old)
    base = [base] + [swap(base, "rep", k) for k in range(1, replicas)]
    anchor_copy, momentum_copy = duplicate(anchor, momentum)
    key_weights = cast_left(params, kv_width)

    last = far[-1]
    blocks[last + 1] = after(blocks[last + 1], anchor_copy, momentum_copy, scalars, old_first, old_second)
    parts, flipped, relayed = [], {}, {}
    for k in far + [0]:
        theirs, flipped[k + 1] = partial_keys(blocks[k + 1], key_weights)
        theirs = swap(theirs, "fsdp", 1)
        if k == last:
            theirs = after(theirs, *base)
        adds = [(theirs, 0)] + relayed.get(k, [])
        if relay and k == far[0]:
            (upper, lower), flipped[k] = partial_keys(blocks[k], key_weights, adds, 2)
            relayed[far[2]] = [(swap(upper, "fsdp", far[1]), 0)]
            relayed[far[1]] = [(swap(lower, "fsdp", far[2]), half)]
            continue
        part_k, flipped[k] = partial_keys(blocks[k], key_weights, adds)
        if k == last:
            for j in range(0, shards, 2):
                values[j + 1] = swap(after(values[j], part_k), "fsdp", 1)
        parts.append(swap(part_k, "fsdp", k) if k else part_k)
    spread = [0, 1] + [k + odd for k in far for odd in range(2)]
    near, rest = spread[:shards // 2], spread[shards // 2:]
    pick = lambda table, which: [table[k] for k in which]
    (values_first,) = gradient(place, pick(flipped, near), pick(values, near), last=False)
    keys = {0: key_backward(parts, incoming, 0)}
    for k in far:
        keys[k] = swap(keys[0], "fsdp", k)
    keys[1] = swap(keys[0], "fsdp", 1)

    grad_values, square, due = gradient(
        place, pick(flipped, rest), pick(values, rest), values_first
    )
    for k in near[2::2]:
        keys[k + 1] = swap(after(keys[k], square), "fsdp", 1)
    (keys_first,) = gradient(place, pick(flipped, near), pick(keys, near), last=False)
    for k in rest[::2]:
        keys[k + 1] = swap(after(keys[k], square), "fsdp", 1)
    grad_keys, square, due = gradient(
        place, pick(flipped, rest), pick(keys, rest), keys_first, square, due
    )

    square = square + swap(square, "fsdp", 1)
    squares = [square] + [swap(square, "fsdp", k) for k in chips]

    state = (params, first_moment[0], second_moment[0], grad_keys, grad_values)
    inner, *update = adam_frag(place, scalars, squares, old, old_first, old_second, due)
    steps = rows // ADAM_ROWS
    *results, ticket = adam_rows(scalars, squares, state, 0, steps // 2)
    own_sum = update[0].astype(jnp.float32)
    for k in range(1, replicas):
        own_sum = own_sum + swap(update[k], "rep", k).astype(jnp.float32)
    own_sum, ticket = lax.optimization_barrier((own_sum, ticket))
    sums = [own_sum.astype(jnp.bfloat16)]
    sums += [swap(sums[0], "rep", k) for k in range(1, replicas)]
    results = adam_rows(scalars, squares, state, steps // 2, steps, results)
    weights_out, anchor_out, momentum_out = outer_step(
        place,
        (results[0], anchor_copy, momentum_copy),
        base,
        sums,
        inner,
        anchor_cols,
        pseudo_old,
        moment_cols,
        own_sum,
        ticket,
    )
    plan_out = jnp.reshape(plan, (1,))
    return (
        weights_out[None],
        results[1][None],
        results[2][None],
        anchor_out,
        momentum_out,
        plan_out,
    )


def solution(mesh):
    tokens_spec = P("rep", "fsdp", None)
    outer_spec = P(("fsdp", "rep"), None)
    return jax.shard_map(
        body,
        mesh=mesh,
        in_specs=(tokens_spec,) * 5 + (outer_spec,) * 2 + (P(), P()),
        out_specs=(tokens_spec,) * 3 + (outer_spec,) * 2 + (P(),),
        check_vma=False,
    )
```

```python
import functools

import jax
import jax.numpy as jnp
from jax import lax
from jax.experimental import pallas as pl
from jax.experimental.pallas import tpu as pltpu
from jax.sharding import PartitionSpec as P

HEAD = 128
WARMUP = 2000
STEPS_TOTAL = 100000
FRAG_COLS = 128


BETA_ONE = 0.9
BETA_TWO = 0.95
ADAM_EPS = 1e-08
DECAY = 0.1
PEAK_RATE = 0.0003
CLIP_NORM = 1.0
OUTER_MU = 0.9
OUTER_RATE = 0.7
MIX_LOCAL = 0.5

MIB = 1 << 20
ADAM_ROWS = 128


def in_hbm(*arrays):
    return [pltpu.with_memory_space_constraint(a, pltpu.HBM) for a in arrays]


def params_of(limit):
    return pltpu.CompilerParams(vmem_limit_bytes=limit * MIB)


def cost(flops, moved):
    return pl.CostEstimate(flops=int(flops), bytes_accessed=int(moved), transcendentals=0)


def pack_kernel(offsets, me_ref, src_ref, *refs):
    half = len(offsets)
    out_refs, (held, in_sems, out_sems) = refs[:half], refs[half:]
    streams = in_sems.shape[1]
    count, rows = out_refs[0].shape
    step = count // streams
    fetches, stores = [], []
    for i, offset in enumerate(offsets):
        column = pl.multiple_of((me_ref[0] ^ offset) * rows, HEAD)
        for j in range(streams):
            at = pl.ds(j * step, step)
            block = src_ref.at[at, pl.ds(column, rows)]
            fetches.append(pltpu.make_async_copy(block, held.at[i, at], in_sems.at[i, j]))
            stores.append(pltpu.make_async_copy(held.at[i, at], out_refs[i].at[at], out_sems.at[i, j]))
    for copy in fetches:
        copy.start()
    for fetch, store in zip(fetches, stores):
        fetch.wait()
        store.start()
    for copy in stores:
        copy.wait()


def pack(tokens, me, rows, offsets):
    count = tokens.shape[0]
    streams = 4
    whole = pl.BlockSpec(memory_space=pl.ANY)
    outs = pl.pallas_call(
        functools.partial(pack_kernel, offsets),
        out_shape=[pltpu.HBM((count, rows), tokens.dtype)] * len(offsets),
        in_specs=[pl.BlockSpec(memory_space=pltpu.SMEM), whole],
        out_specs=[whole] * len(offsets),
        scratch_shapes=[
            pltpu.VMEM((len(offsets), count, rows), tokens.dtype),
            pltpu.SemaphoreType.DMA((len(offsets), streams)),
            pltpu.SemaphoreType.DMA((len(offsets), streams)),
        ],
        compiler_params=params_of(12),
        cost_estimate=cost(0, 4 * len(offsets) * count * rows),
        name="pack",
    )(me, *in_hbm(tokens))
    return dict(zip(offsets, outs))


def cast_kernel(src_ref, out_ref):
    out_ref[...] = src_ref[...].astype(out_ref.dtype)


def cast_left(array, width):
    rows = array.shape[0]
    block = pl.BlockSpec((256, width), lambda i: (i, 0))
    return pl.pallas_call(
        cast_kernel,
        out_shape=jax.ShapeDtypeStruct((rows, width), jnp.bfloat16),
        grid=(rows // 256,),
        in_specs=[block],
        out_specs=block,
        compiler_params=params_of(8),
        cost_estimate=cost(0, 6 * rows * width),
        name="cast_left",
    )(*in_hbm(array))


def partial_kernel(pieces, firsts, splits, *refs):
    x_refs, w_ref, refs = refs[:pieces], refs[pieces], refs[pieces + 1:]
    add_refs, out_refs, flip_ref = refs[:len(firsts)], refs[len(firsts):-1], refs[-1]
    x = jnp.concatenate([ref[...] for ref in x_refs], axis=1)
    total = jnp.dot(x, w_ref[...], preferred_element_type=jnp.float32)
    count = total.shape[0]
    for ref, first in zip(add_refs, firsts):
        last = first + ref.shape[0]
        rows = [total[:first], total[first:last] + ref[...].astype(jnp.float32), total[last:]]
        total = jnp.concatenate([r for r in rows if r.shape[0]], axis=0)
    height = count // splits
    for i, ref in enumerate(out_refs):
        ref[...] = total[i * height:(i + 1) * height].astype(ref.dtype)
    step = x_refs[0].shape[1]
    for i, ref in enumerate(x_refs):
        flip_ref[i * step:(i + 1) * step, :] = ref[...].T


def partial_keys(block, key_weights, adds=(), splits=1):
    count, rows = block.shape
    width = key_weights.shape[1]
    pieces = 4 if rows % (4 * HEAD) == 0 else 2
    fixed = lambda a: pl.BlockSpec(a.shape, lambda i: (0, 0))
    *parts, flipped = pl.pallas_call(
        functools.partial(partial_kernel, pieces, [first for _, first in adds], splits),
        out_shape=[jax.ShapeDtypeStruct((count // splits, width), jnp.bfloat16)] * splits
        + [jax.ShapeDtypeStruct((rows, count), jnp.bfloat16)],
        grid=(1,),
        in_specs=[pl.BlockSpec((count, rows // pieces), lambda i, c=c: (0, c)) for c in range(pieces)]
        + [fixed(key_weights)]
        + [fixed(a) for a, _ in adds],
        out_specs=[pl.BlockSpec((count // splits, width), lambda i: (0, 0))] * splits
        + [pl.BlockSpec((rows, count), lambda i: (0, 0))],
        compiler_params=params_of(12),
        cost_estimate=cost(2 * count * rows * width, 4 * count * rows),
        name="partial_keys",
    )(*[block] * pieces, key_weights, *[a for a, _ in adds])
    return parts if splits > 1 else parts[0], flipped


def key_kernel(first, *refs):
    *part_refs, cot_ref, out_ref = refs
    count = out_ref.shape[0]
    raw = sum(ref[...].astype(jnp.float32) for ref in part_refs)
    for h in range(raw.shape[1] // HEAD):
        cols = slice(h * HEAD, (h + 1) * HEAD)
        head = raw[:, cols]
        inverse = lax.rsqrt(jnp.mean(head * head, axis=1, keepdims=True) + 1e-06)
        normed = head * inverse
        upper = cot_ref[first:first + count, cols].astype(jnp.float32)
        back = inverse * (upper - normed * jnp.mean(upper * normed, axis=1, keepdims=True))
        out_ref[:, cols] = back.astype(out_ref.dtype)


def key_backward(parts, incoming, first):
    count, width = parts[0].shape
    block = pl.BlockSpec((count, width), lambda i: (0, 0))
    cot = pl.BlockSpec((incoming.shape[0], width), lambda i: (0, 0))
    return pl.pallas_call(
        functools.partial(key_kernel, first),
        out_shape=jax.ShapeDtypeStruct((count, width), jnp.bfloat16),
        grid=(1,),
        in_specs=[block] * len(parts) + [cot],
        out_specs=block,
        compiler_params=params_of(8),
        cost_estimate=cost(60 * count * width, 12 * count * width),
        name="key_backward",
    )(*parts, incoming)


def grad_kernel(count, has_base, has_more, last, place_ref, *refs):
    refs = list(refs)
    x_refs, u_refs = refs[:count], refs[count:2 * count]
    refs = refs[2 * count:]
    base = refs.pop(0) if has_base else None
    square_in, due_in = (refs.pop(0), refs.pop(0)) if has_more else (None, None)
    out_ref = refs.pop(0)
    x = jnp.concatenate([ref[...] for ref in x_refs], axis=1)
    u = jnp.concatenate([ref[...] for ref in u_refs], axis=0)
    total = jnp.dot(x, u, preferred_element_type=jnp.float32)
    if has_base:
        total = total + base[...]
    out_ref[...] = total
    if last:
        sq_ref, due_ref = refs

        @pl.when(pl.program_id(0) == 0)
        def _():
            sq_ref[...] = square_in[...] if has_more else jnp.zeros_like(sq_ref)

        rows, width = total.shape
        squares = (total * total).reshape(rows // 8, 8, width).sum(axis=0)
        folded = squares[:, :HEAD]
        for h in range(1, width // HEAD):
            folded = folded + squares[:, h * HEAD:(h + 1) * HEAD]
        sq_ref[...] += folded
        heads = width // FRAG_COLS
        mine = place_ref[0] - (0 if has_more else heads)
        mine = jnp.minimum(jnp.maximum(mine, 0), heads - 1) * FRAG_COLS
        column = out_ref[:, pl.ds(pl.multiple_of(mine, FRAG_COLS), FRAG_COLS)]
        if has_more:
            column = jnp.where(place_ref[0] < heads, column, due_in[...])
        due_ref[...] = column


def gradient(place, flipped, upstream, base=None, square=None, due=None, last=True):
    rows, depth = flipped[0].shape
    width = upstream[0].shape[1]
    step = 256
    row_block = lambda cols: pl.BlockSpec((step, cols), lambda i, p: (i, 0))
    fixed = pl.BlockSpec((8, HEAD), lambda i, p: (0, 0))
    args = [*flipped, *upstream]
    specs = [row_block(depth)] * len(flipped)
    specs += [pl.BlockSpec((depth, width), lambda i, p: (0, 0))] * len(upstream)
    if base is not None:
        args.append(base)
        specs.append(row_block(width))
    if square is not None:
        args += [square, due]
        specs += [fixed, row_block(FRAG_COLS)]
    if last:
        shapes = [
            jax.ShapeDtypeStruct((rows, width), jnp.float32),
            jax.ShapeDtypeStruct((8, HEAD), jnp.float32),
            jax.ShapeDtypeStruct((rows, FRAG_COLS), jnp.float32),
        ]
        outs = [row_block(width), fixed, row_block(FRAG_COLS)]
    else:
        shapes = [jax.ShapeDtypeStruct((rows, width), jnp.float32)]
        outs = [row_block(width)]
    depth *= len(flipped)
    return pl.pallas_call(
        functools.partial(grad_kernel, len(flipped), base is not None, square is not None, last),
        out_shape=shapes,
        grid_spec=pltpu.PrefetchScalarGridSpec(
            num_scalar_prefetch=1, grid=(rows // step,), in_specs=specs, out_specs=outs
        ),
        compiler_params=params_of(12),
        cost_estimate=cost(2 * rows * width * depth, 2 * rows * depth + 4 * rows * width),
        name="gradient",
    )(place, *args)


def clip_factor(square_refs):
    square = jnp.sum(sum(ref[...] for ref in square_refs), keepdims=True)
    return jnp.minimum(1.0, CLIP_NORM / (jnp.sqrt(square) + 1e-06))


def adam(old, first, second, grad, factor, scalars):
    rate, inv_one, inv_two = (scalars[i] for i in range(3))
    clipped = grad * factor
    first_new = BETA_ONE * first + (1.0 - BETA_ONE) * clipped
    second_new = BETA_TWO * second + (1.0 - BETA_TWO) * clipped * clipped
    update = rate * (
        first_new * inv_one / (jnp.sqrt(second_new * inv_two) + ADAM_EPS) + DECAY * old
    )
    return update, first_new, second_new


def adam_kernel(squares, extra, sc_ref, w_ref, m_ref, v_ref, gk_ref, gv_ref, *refs):
    factor = clip_factor(refs[:squares])
    w_out, m_out, v_out, *done = refs[squares + extra:]
    width = gk_ref.shape[1]
    for g_ref, cols in ((gk_ref, slice(0, width)), (gv_ref, slice(width, 2 * width))):
        old = w_ref[:, cols]
        update, first_new, second_new = adam(
            old, m_ref[:, cols], v_ref[:, cols], g_ref[...], factor, sc_ref
        )
        w_out[:, cols] = old - update
        m_out[:, cols] = first_new
        v_out[:, cols] = second_new
    for ref in done:
        ref[...] = jnp.zeros_like(ref)


def adam_rows(scalars, squares, state, first, last, into=()):
    rows, width = state[0].shape
    step = ADAM_ROWS
    full = pl.BlockSpec((step, width), lambda i: (i + first, 0))
    half = pl.BlockSpec((step, width // 2), lambda i: (i + first, 0))
    shapes = [pltpu.HBM((rows, width), jnp.float32)] * 3
    outs = [full] * 3
    if not into:
        shapes.append(jax.ShapeDtypeStruct((8, HEAD), jnp.float32))
        outs.append(pl.BlockSpec((8, HEAD), lambda i: (0, 0)))
    count = (last - first) * step
    return pl.pallas_call(
        functools.partial(adam_kernel, len(squares), len(into)),
        out_shape=shapes,
        grid=(last - first,),
        in_specs=[pl.BlockSpec(memory_space=pltpu.SMEM), full, full, full, half, half]
        + [pl.BlockSpec((8, HEAD), lambda i: (0, 0))] * len(squares)
        + [pl.BlockSpec(memory_space=pl.ANY)] * len(into),
        out_specs=outs,
        input_output_aliases={6 + len(squares) + i: i for i in range(len(into))},
        compiler_params=params_of(12),
        cost_estimate=cost(20 * count * width, 28 * count * width),
        name="adam_rows",
    )(scalars, *state, *squares, *in_hbm(*into))


def frag_kernel(squares, place_ref, sc_ref, w_ref, m_ref, v_ref, g_ref, *refs):
    blocks, part, _ = w_ref.shape
    factor = clip_factor(refs[:squares])
    inner_ref, *out_refs = refs[squares:]
    for j in range(blocks):
        at = pl.multiple_of((place_ref[1] ^ j) * part, 8)
        old = w_ref[j]
        update, _, _ = adam(old, m_ref[j], v_ref[j], g_ref[pl.ds(at, part), :], factor, sc_ref)
        inner_ref[j] = old - update
        out_refs[j][...] = update.astype(out_refs[j].dtype)


def adam_frag(place, scalars, squares, old, first, second, grad):
    blocks, part, width = old.shape
    smem = pl.BlockSpec(memory_space=pltpu.SMEM)
    vmem = pl.BlockSpec(memory_space=pltpu.VMEM)
    return pl.pallas_call(
        functools.partial(frag_kernel, len(squares)),
        out_shape=[jax.ShapeDtypeStruct(old.shape, jnp.float32)]
        + [jax.ShapeDtypeStruct((part, width), jnp.bfloat16)] * blocks,
        in_specs=[smem, smem] + [vmem] * (4 + len(squares)),
        out_specs=[vmem] * (1 + blocks),
        compiler_params=params_of(12),
        cost_estimate=cost(20 * old.size, 22 * old.size),
        name="adam_frag",
    )(place, scalars, old, first, second, grad, *squares)


def pick_kernel(blocks, place_ref, *refs):
    outs = refs[len(refs) // (blocks + 1) * blocks:]
    for i, out_ref in enumerate(outs):
        for j in range(blocks):
            out_ref[j] = refs[i * blocks + j][...]


def due_columns(place, part, *arrays):
    blocks = arrays[0].shape[0] // part
    specs = []
    for j in range(blocks):
        at = (lambda i, p, j=j: (p[1] ^ j, p[0])) if blocks > 1 else (lambda i, p: (0, p[0]))
        specs.append(pl.BlockSpec((part, FRAG_COLS), at))
    shape = (blocks, part, FRAG_COLS)
    return pl.pallas_call(
        functools.partial(pick_kernel, blocks),
        out_shape=[jax.ShapeDtypeStruct(shape, a.dtype) for a in arrays],
        grid_spec=pltpu.PrefetchScalarGridSpec(
            num_scalar_prefetch=1,
            grid=(1,),
            in_specs=specs * len(arrays),
            out_specs=[pl.BlockSpec(shape, lambda i, p: (0, 0, 0))] * len(arrays),
        ),
        compiler_params=params_of(12),
        cost_estimate=cost(0, 8 * blocks * part * FRAG_COLS * len(arrays)),
        name="due_columns",
    )(place, *[a for array in in_hbm(*arrays) for a in [array] * blocks])


def duplicate_kernel(*refs):
    half = (len(refs) - 3) // 2
    held, in_sems, out_sems = refs[2 * half:]
    streams = held.shape[1]
    step = held.shape[2]
    places = [(a, i, pl.ds(i * step, step)) for a in range(half) for i in range(streams)]
    fetches = [
        pltpu.make_async_copy(refs[a].at[at], held.at[a, i], in_sems.at[a, i]) for a, i, at in places
    ]
    stores = [
        pltpu.make_async_copy(held.at[a, i], refs[half + a].at[at], out_sems.at[a, i])
        for a, i, at in places
    ]
    for copy in fetches:
        copy.start()
    for fetch, store in zip(fetches, stores):
        fetch.wait()
        store.start()
    for copy in stores:
        copy.wait()


def duplicate(*arrays):
    rows, width = arrays[0].shape
    streams = 4
    whole = pl.BlockSpec(memory_space=pl.ANY)
    return pl.pallas_call(
        duplicate_kernel,
        out_shape=[pltpu.HBM(a.shape, a.dtype) for a in arrays],
        in_specs=[whole] * len(arrays),
        out_specs=[whole] * len(arrays),
        scratch_shapes=[
            pltpu.VMEM((len(arrays), streams, rows // streams, width), arrays[0].dtype),
            pltpu.SemaphoreType.DMA((len(arrays), streams)),
            pltpu.SemaphoreType.DMA((len(arrays), streams)),
        ],
        compiler_params=params_of(8),
        cost_estimate=cost(0, sum(8 * a.size for a in arrays)),
        name="duplicate",
    )(*in_hbm(*arrays))


def outer_kernel(replicas, place_ref, *refs):
    share = 1.0 / replicas
    base_refs, sum_refs = refs[3:3 + replicas], refs[3 + replicas:3 + 2 * replicas]
    inner_ref, a_ref, p_ref, m_ref, own_ref, _, *refs = refs[3 + 2 * replicas:]
    w_out, a_out, m_out, mixed, new_a, new_m, sems = refs
    part = a_ref.shape[0]
    scale = share * (1.0 + OUTER_MU) * OUTER_RATE
    columns = pl.ds(pl.multiple_of(place_ref[0] * FRAG_COLS, FRAG_COLS), FRAG_COLS)
    copies = []
    for j in range(replicas):
        fresh = base_refs[j][...] - scale * sum_refs[j][...].astype(jnp.float32)
        mixed[j] = MIX_LOCAL * inner_ref[j] + (1.0 - MIX_LOCAL) * fresh
        rows = pl.ds(pl.multiple_of((place_ref[1] ^ j) * part, 8), part)
        copies.append(pltpu.make_async_copy(mixed.at[j], w_out.at[rows, columns], sems.at[j]))
        copies[-1].start()
    pseudo = p_ref[...] + share * own_ref[...]
    new_moment = OUTER_MU * m_ref[...] + pseudo
    new_m[...] = new_moment
    new_a[...] = a_ref[...] - OUTER_RATE * (OUTER_MU * new_moment + pseudo)
    for i, (src, dst) in enumerate(((new_a, a_out), (new_m, m_out))):
        copies.append(pltpu.make_async_copy(src, dst.at[:, columns], sems.at[replicas + i]))
        copies[-1].start()
    for copy in copies:
        copy.wait()


def outer_step(place, outputs, base, sums, inner, anchor, pseudo, momentum, own_sum, ticket):
    replicas, part = inner.shape[0], inner.shape[1]
    whole = pl.BlockSpec(memory_space=pl.ANY)
    held = pl.BlockSpec(memory_space=pltpu.VMEM)
    return pl.pallas_call(
        functools.partial(outer_kernel, replicas),
        out_shape=[pltpu.HBM(a.shape, a.dtype) for a in outputs],
        in_specs=[pl.BlockSpec(memory_space=pltpu.SMEM)]
        + [whole] * 3
        + [held] * (2 * replicas + 5)
        + [whole],
        out_specs=[whole] * 3,
        scratch_shapes=[
            pltpu.VMEM((replicas, part, FRAG_COLS), jnp.float32),
            pltpu.VMEM((part, FRAG_COLS), jnp.float32),
            pltpu.VMEM((part, FRAG_COLS), jnp.float32),
            pltpu.SemaphoreType.DMA((replicas + 2,)),
        ],
        input_output_aliases={1: 0, 2: 1, 3: 2},
        compiler_params=params_of(12),
        cost_estimate=cost(10 * replicas * part * FRAG_COLS, 20 * replicas * part * FRAG_COLS),
        name="outer_step",
    )(place, *in_hbm(*outputs), *base, *sums, inner, anchor, pseudo, momentum, own_sum, ticket)


def swap(block, axis, offset):
    count = lax.axis_size(axis)
    return lax.ppermute(block, axis, [(i, i ^ offset) for i in range(count)])


def after(value, *others):
    return lax.optimization_barrier((value,) + others)[0]


class Line:
    def __init__(self, axis):
        self.axis, self.ended = axis, []

    def swap(self, block, offset):
        self.ended = [swap(after(block, *self.ended), self.axis, offset)]
        return self.ended[0]


def body(
    tokens,
    cotangent,
    weights,
    first_moment,
    second_moment,
    anchor,
    momentum,
    due_fragment,
    step_count,
):
    inputs, incoming, params = tokens[0], cotangent[0], weights[0]
    kv_width = incoming.shape[1] // 2
    rows = params.shape[0]
    part = anchor.shape[0]
    replicas = lax.axis_size("rep")
    shards = lax.axis_size("fsdp")
    me = jnp.reshape(lax.axis_index("fsdp"), (1,)).astype(jnp.int32)
    my_rep = lax.axis_index("rep").astype(jnp.int32)
    place = jnp.stack([due_fragment[0], my_rep])
    chips = range(2, shards, 2)
    far = sorted(chips, key=lambda k: (-bin(k).count("1"), k))
    order = [k for k in far[:-2] for k in (k, k + 1)]
    order += far[-2:] + [k + 1 for k in far[-2:]]

    (old,) = due_columns(place, part, params)
    line = Line("rep")
    old_sums = [old[0]] + [line.swap(old[k], k) for k in range(1, replicas)]

    packed = {}
    for offsets in (order[:1], order[1:4], order[4:], (0, 1)):
        packed |= pack(inputs, me, rows, tuple(offsets))
    blocks = {k: swap(packed[k], "fsdp", k) for k in order}
    blocks[0], blocks[1] = packed[0], swap(packed[1], "fsdp", 1)

    relay = len(far) == 3 and far[0] == far[1] ^ far[2]
    half = inputs.shape[0] // 2
    values = {0: incoming[:, kv_width:]}
    for i, k in enumerate(far[1:] if relay else far):
        values[k] = swap(after(values[0], blocks[order[i]]), "fsdp", k)

    steps_now = step_count[0].astype(jnp.float32)
    plan = jnp.minimum(1.0, steps_now / WARMUP) * (
        0.55 + 0.45 * jnp.cos(jnp.pi * steps_now / STEPS_TOTAL)
    )
    rate = PEAK_RATE * plan
    inv_one = 1.0 / (1.0 - jnp.power(BETA_ONE, steps_now))
    inv_two = 1.0 / (1.0 - jnp.power(BETA_TWO, steps_now))
    scalars = jnp.stack([rate, inv_one, inv_two])
    old_first, old_second = due_columns(place, part, first_moment[0], second_moment[0])
    anchor_cols, moment_cols = (c[0] for c in due_columns(place, part, anchor, momentum))
    pseudo_old = anchor_cols - sum(old_sums[1:], old_sums[0]) / replicas
    base = anchor_cols - OUTER_RATE * (OUTER_MU * (OUTER_MU * moment_cols + pseudo_old) + pseudo_old)
    base = [base] + [line.swap(base, k) for k in range(1, replicas)]
    anchor_copy, momentum_copy = duplicate(anchor, momentum)
    key_weights = cast_left(params, kv_width)

    last = far[-1]
    blocks[last + 1] = after(blocks[last + 1], anchor_copy, momentum_copy, scalars, old_first, old_second)
    parts, flipped, relayed = [], {}, {}
    for k in far + [0]:
        theirs, flipped[k + 1] = partial_keys(blocks[k + 1], key_weights)
        theirs = swap(theirs, "fsdp", 1)
        if k == last:
            theirs = after(theirs, *base)
        adds = [(theirs, 0)] + relayed.get(k, [])
        if relay and k == far[0]:
            (upper, lower), flipped[k] = partial_keys(blocks[k], key_weights, adds, 2)
            relayed[far[2]] = [(swap(upper, "fsdp", far[1]), 0)]
            relayed[far[1]] = [(swap(lower, "fsdp", far[2]), half)]
            continue
        part_k, flipped[k] = partial_keys(blocks[k], key_weights, adds)
        if k == last:
            for j in [0] + [j for j in far if j in values]:
                values[j] = after(values[j], part_k)
            if relay:
                upper = swap(values[far[1]][:half], "fsdp", far[2])
                lower = swap(values[far[2]][half:], "fsdp", far[1])
                values[far[0]] = jnp.concatenate([upper, lower], axis=0)
            for j in range(0, shards, 2):
                values[j + 1] = swap(values[j], "fsdp", 1)
        parts.append(swap(part_k, "fsdp", k) if k else part_k)
    spread = [0, 1] + [k + odd for k in far for odd in range(2)]
    near, rest = spread[:shards // 2], spread[shards // 2:]
    pick = lambda table, which: [table[k] for k in which]
    (values_first,) = gradient(place, pick(flipped, near), pick(values, near), last=False)
    keys = {0: key_backward(parts, incoming, 0)}
    for k in far:
        keys[k] = swap(keys[0], "fsdp", k)
    keys[1] = swap(keys[0], "fsdp", 1)

    grad_values, square, due = gradient(
        place, pick(flipped, rest), pick(values, rest), values_first
    )
    for k in near[2::2]:
        keys[k + 1] = swap(after(keys[k], square), "fsdp", 1)
    (keys_first,) = gradient(place, pick(flipped, near), pick(keys, near), last=False)
    for k in rest[::2]:
        keys[k + 1] = swap(after(keys[k], square), "fsdp", 1)
    grad_keys, square, due = gradient(
        place, pick(flipped, rest), pick(keys, rest), keys_first, square, due
    )

    square = square + swap(square, "fsdp", 1)
    squares = [square] + [swap(square, "fsdp", k) for k in chips]

    state = (params, first_moment[0], second_moment[0], grad_keys, grad_values)
    inner, *update = adam_frag(place, scalars, squares, old, old_first, old_second, due)
    steps = rows // ADAM_ROWS
    *results, ticket = adam_rows(scalars, squares, state, 0, steps // 2)
    own_sum = update[0].astype(jnp.float32)
    for k in range(1, replicas):
        own_sum = own_sum + swap(update[k], "rep", k).astype(jnp.float32)
    own_sum, ticket = lax.optimization_barrier((own_sum, ticket))
    sums = [own_sum.astype(jnp.bfloat16)]
    sums += [swap(sums[0], "rep", k) for k in range(1, replicas)]
    results = adam_rows(scalars, squares, state, steps // 2, steps, results)
    weights_out, anchor_out, momentum_out = outer_step(
        place,
        (results[0], anchor_copy, momentum_copy),
        base,
        sums,
        inner,
        anchor_cols,
        pseudo_old,
        moment_cols,
        own_sum,
        ticket,
    )
    plan_out = jnp.reshape(plan, (1,))
    return (
        weights_out[None],
        results[1][None],
        results[2][None],
        anchor_out,
        momentum_out,
        plan_out,
    )


def solution(mesh):
    tokens_spec = P("rep", "fsdp", None)
    outer_spec = P(("fsdp", "rep"), None)
    return jax.shard_map(
        body,
        mesh=mesh,
        in_specs=(tokens_spec,) * 5 + (outer_spec,) * 2 + (P(), P()),
        out_specs=(tokens_spec,) * 3 + (outer_spec,) * 2 + (P(),),
        check_vma=False,
    )
```

```python
import functools

import jax
import jax.numpy as jnp
from jax import lax
from jax.experimental import pallas as pl
from jax.experimental.pallas import tpu as pltpu
from jax.sharding import PartitionSpec as P

HEAD = 128
WARMUP = 2000
STEPS_TOTAL = 100000
FRAG_COLS = 128


BETA_ONE = 0.9
BETA_TWO = 0.95
ADAM_EPS = 1e-08
DECAY = 0.1
PEAK_RATE = 0.0003
CLIP_NORM = 1.0
OUTER_MU = 0.9
OUTER_RATE = 0.7
MIX_LOCAL = 0.5

MIB = 1 << 20
ADAM_ROWS = 128


def in_hbm(*arrays):
    return [pltpu.with_memory_space_constraint(a, pltpu.HBM) for a in arrays]


def params_of(limit):
    return pltpu.CompilerParams(vmem_limit_bytes=limit * MIB)


def cost(flops, moved):
    return pl.CostEstimate(flops=int(flops), bytes_accessed=int(moved), transcendentals=0)


def pack_kernel(offsets, me_ref, src_ref, *refs):
    half = len(offsets)
    out_refs, (held, in_sems, out_sems) = refs[:half], refs[half:]
    streams = in_sems.shape[1]
    count, rows = out_refs[0].shape
    step = count // streams
    fetches, stores = [], []
    for i, offset in enumerate(offsets):
        column = pl.multiple_of((me_ref[0] ^ offset) * rows, HEAD)
        for j in range(streams):
            at = pl.ds(j * step, step)
            block = src_ref.at[at, pl.ds(column, rows)]
            fetches.append(pltpu.make_async_copy(block, held.at[i, at], in_sems.at[i, j]))
            stores.append(pltpu.make_async_copy(held.at[i, at], out_refs[i].at[at], out_sems.at[i, j]))
    for copy in fetches:
        copy.start()
    for fetch, store in zip(fetches, stores):
        fetch.wait()
        store.start()
    for copy in stores:
        copy.wait()


def pack(tokens, me, rows, offsets):
    count = tokens.shape[0]
    streams = 4
    whole = pl.BlockSpec(memory_space=pl.ANY)
    outs = pl.pallas_call(
        functools.partial(pack_kernel, offsets),
        out_shape=[pltpu.HBM((count, rows), tokens.dtype)] * len(offsets),
        in_specs=[pl.BlockSpec(memory_space=pltpu.SMEM), whole],
        out_specs=[whole] * len(offsets),
        scratch_shapes=[
            pltpu.VMEM((len(offsets), count, rows), tokens.dtype),
            pltpu.SemaphoreType.DMA((len(offsets), streams)),
            pltpu.SemaphoreType.DMA((len(offsets), streams)),
        ],
        compiler_params=params_of(12),
        cost_estimate=cost(0, 4 * len(offsets) * count * rows),
        name="pack",
    )(me, *in_hbm(tokens))
    return dict(zip(offsets, outs))


def cast_kernel(src_ref, out_ref):
    out_ref[...] = src_ref[...].astype(out_ref.dtype)


def cast_left(array, width):
    rows = array.shape[0]
    block = pl.BlockSpec((256, width), lambda i: (i, 0))
    return pl.pallas_call(
        cast_kernel,
        out_shape=jax.ShapeDtypeStruct((rows, width), jnp.bfloat16),
        grid=(rows // 256,),
        in_specs=[block],
        out_specs=block,
        compiler_params=params_of(8),
        cost_estimate=cost(0, 6 * rows * width),
        name="cast_left",
    )(*in_hbm(array))


def partial_kernel(pieces, firsts, splits, *refs):
    x_refs, w_ref, refs = refs[:pieces], refs[pieces], refs[pieces + 1:]
    add_refs, out_refs, flip_ref = refs[:len(firsts)], refs[len(firsts):-1], refs[-1]
    x = jnp.concatenate([ref[...] for ref in x_refs], axis=1)
    total = jnp.dot(x, w_ref[...], preferred_element_type=jnp.float32)
    count = total.shape[0]
    for ref, first in zip(add_refs, firsts):
        last = first + ref.shape[0]
        rows = [total[:first], total[first:last] + ref[...].astype(jnp.float32), total[last:]]
        total = jnp.concatenate([r for r in rows if r.shape[0]], axis=0)
    height = count // splits
    for i, ref in enumerate(out_refs):
        ref[...] = total[i * height:(i + 1) * height].astype(ref.dtype)
    step = x_refs[0].shape[1]
    for i, ref in enumerate(x_refs):
        flip_ref[i * step:(i + 1) * step, :] = ref[...].T


def partial_keys(block, key_weights, adds=(), splits=1):
    count, rows = block.shape
    width = key_weights.shape[1]
    pieces = 4 if rows % (4 * HEAD) == 0 else 2
    fixed = lambda a: pl.BlockSpec(a.shape, lambda i: (0, 0))
    *parts, flipped = pl.pallas_call(
        functools.partial(partial_kernel, pieces, [first for _, first in adds], splits),
        out_shape=[jax.ShapeDtypeStruct((count // splits, width), jnp.bfloat16)] * splits
        + [jax.ShapeDtypeStruct((rows, count), jnp.bfloat16)],
        grid=(1,),
        in_specs=[pl.BlockSpec((count, rows // pieces), lambda i, c=c: (0, c)) for c in range(pieces)]
        + [fixed(key_weights)]
        + [fixed(a) for a, _ in adds],
        out_specs=[pl.BlockSpec((count // splits, width), lambda i: (0, 0))] * splits
        + [pl.BlockSpec((rows, count), lambda i: (0, 0))],
        compiler_params=params_of(12),
        cost_estimate=cost(2 * count * rows * width, 4 * count * rows),
        name="partial_keys",
    )(*[block] * pieces, key_weights, *[a for a, _ in adds])
    return parts if splits > 1 else parts[0], flipped


def key_kernel(first, *refs):
    *part_refs, cot_ref, out_ref = refs
    count = out_ref.shape[0]
    raw = sum(ref[...].astype(jnp.float32) for ref in part_refs)
    for h in range(raw.shape[1] // HEAD):
        cols = slice(h * HEAD, (h + 1) * HEAD)
        head = raw[:, cols]
        inverse = lax.rsqrt(jnp.mean(head * head, axis=1, keepdims=True) + 1e-06)
        normed = head * inverse
        upper = cot_ref[first:first + count, cols].astype(jnp.float32)
        back = inverse * (upper - normed * jnp.mean(upper * normed, axis=1, keepdims=True))
        out_ref[:, cols] = back.astype(out_ref.dtype)


def key_backward(parts, incoming, first):
    count, width = parts[0].shape
    block = pl.BlockSpec((count, width), lambda i: (0, 0))
    cot = pl.BlockSpec((incoming.shape[0], width), lambda i: (0, 0))
    return pl.pallas_call(
        functools.partial(key_kernel, first),
        out_shape=jax.ShapeDtypeStruct((count, width), jnp.bfloat16),
        grid=(1,),
        in_specs=[block] * len(parts) + [cot],
        out_specs=block,
        compiler_params=params_of(8),
        cost_estimate=cost(60 * count * width, 12 * count * width),
        name="key_backward",
    )(*parts, incoming)


def grad_kernel(count, has_base, has_more, last, place_ref, *refs):
    refs = list(refs)
    x_refs, u_refs = refs[:count], refs[count:2 * count]
    refs = refs[2 * count:]
    base = refs.pop(0) if has_base else None
    square_in, due_in = (refs.pop(0), refs.pop(0)) if has_more else (None, None)
    out_ref = refs.pop(0)
    x = jnp.concatenate([ref[...] for ref in x_refs], axis=1)
    u = jnp.concatenate([ref[...] for ref in u_refs], axis=0)
    total = jnp.dot(x, u, preferred_element_type=jnp.float32)
    if has_base:
        total = total + base[...]
    out_ref[...] = total
    if last:
        sq_ref, due_ref = refs

        @pl.when(pl.program_id(0) == 0)
        def _():
            sq_ref[...] = square_in[...] if has_more else jnp.zeros_like(sq_ref)

        rows, width = total.shape
        squares = (total * total).reshape(rows // 8, 8, width).sum(axis=0)
        folded = squares[:, :HEAD]
        for h in range(1, width // HEAD):
            folded = folded + squares[:, h * HEAD:(h + 1) * HEAD]
        sq_ref[...] += folded
        heads = width // FRAG_COLS
        mine = place_ref[0] - (0 if has_more else heads)
        mine = jnp.minimum(jnp.maximum(mine, 0), heads - 1) * FRAG_COLS
        column = out_ref[:, pl.ds(pl.multiple_of(mine, FRAG_COLS), FRAG_COLS)]
        if has_more:
            column = jnp.where(place_ref[0] < heads, column, due_in[...])
        due_ref[...] = column


def gradient(place, flipped, upstream, base=None, square=None, due=None, last=True):
    rows, depth = flipped[0].shape
    width = upstream[0].shape[1]
    step = 256
    row_block = lambda cols: pl.BlockSpec((step, cols), lambda i, p: (i, 0))
    fixed = pl.BlockSpec((8, HEAD), lambda i, p: (0, 0))
    args = [*flipped, *upstream]
    specs = [row_block(depth)] * len(flipped)
    specs += [pl.BlockSpec((depth, width), lambda i, p: (0, 0))] * len(upstream)
    if base is not None:
        args.append(base)
        specs.append(row_block(width))
    if square is not None:
        args += [square, due]
        specs += [fixed, row_block(FRAG_COLS)]
    if last:
        shapes = [
            jax.ShapeDtypeStruct((rows, width), jnp.float32),
            jax.ShapeDtypeStruct((8, HEAD), jnp.float32),
            jax.ShapeDtypeStruct((rows, FRAG_COLS), jnp.float32),
        ]
        outs = [row_block(width), fixed, row_block(FRAG_COLS)]
    else:
        shapes = [jax.ShapeDtypeStruct((rows, width), jnp.float32)]
        outs = [row_block(width)]
    depth *= len(flipped)
    return pl.pallas_call(
        functools.partial(grad_kernel, len(flipped), base is not None, square is not None, last),
        out_shape=shapes,
        grid_spec=pltpu.PrefetchScalarGridSpec(
            num_scalar_prefetch=1, grid=(rows // step,), in_specs=specs, out_specs=outs
        ),
        compiler_params=params_of(12),
        cost_estimate=cost(2 * rows * width * depth, 2 * rows * depth + 4 * rows * width),
        name="gradient",
    )(place, *args)


def clip_factor(square_refs):
    square = jnp.sum(sum(ref[...] for ref in square_refs), keepdims=True)
    return jnp.minimum(1.0, CLIP_NORM / (jnp.sqrt(square) + 1e-06))


def adam(old, first, second, grad, factor, scalars):
    rate, inv_one, inv_two = (scalars[i] for i in range(3))
    clipped = grad * factor
    first_new = BETA_ONE * first + (1.0 - BETA_ONE) * clipped
    second_new = BETA_TWO * second + (1.0 - BETA_TWO) * clipped * clipped
    update = rate * (
        first_new * inv_one / (jnp.sqrt(second_new * inv_two) + ADAM_EPS) + DECAY * old
    )
    return update, first_new, second_new


def adam_kernel(squares, extra, sc_ref, w_ref, m_ref, v_ref, gk_ref, gv_ref, *refs):
    factor = clip_factor(refs[:squares])
    w_out, m_out, v_out, *done = refs[squares + extra:]
    width = gk_ref.shape[1]
    for g_ref, cols in ((gk_ref, slice(0, width)), (gv_ref, slice(width, 2 * width))):
        old = w_ref[:, cols]
        update, first_new, second_new = adam(
            old, m_ref[:, cols], v_ref[:, cols], g_ref[...], factor, sc_ref
        )
        w_out[:, cols] = old - update
        m_out[:, cols] = first_new
        v_out[:, cols] = second_new
    for ref in done:
        ref[...] = jnp.zeros_like(ref)


def adam_rows(scalars, squares, state, first, last, into=()):
    rows, width = state[0].shape
    step = ADAM_ROWS
    full = pl.BlockSpec((step, width), lambda i: (i + first, 0))
    half = pl.BlockSpec((step, width // 2), lambda i: (i + first, 0))
    shapes = [pltpu.HBM((rows, width), jnp.float32)] * 3
    outs = [full] * 3
    if not into:
        shapes.append(jax.ShapeDtypeStruct((8, HEAD), jnp.float32))
        outs.append(pl.BlockSpec((8, HEAD), lambda i: (0, 0)))
    count = (last - first) * step
    return pl.pallas_call(
        functools.partial(adam_kernel, len(squares), len(into)),
        out_shape=shapes,
        grid=(last - first,),
        in_specs=[pl.BlockSpec(memory_space=pltpu.SMEM), full, full, full, half, half]
        + [pl.BlockSpec((8, HEAD), lambda i: (0, 0))] * len(squares)
        + [pl.BlockSpec(memory_space=pl.ANY)] * len(into),
        out_specs=outs,
        input_output_aliases={6 + len(squares) + i: i for i in range(len(into))},
        compiler_params=params_of(12),
        cost_estimate=cost(20 * count * width, 28 * count * width),
        name="adam_rows",
    )(scalars, *state, *squares, *in_hbm(*into))


def frag_kernel(squares, place_ref, sc_ref, w_ref, m_ref, v_ref, g_ref, *refs):
    blocks, part, _ = w_ref.shape
    factor = clip_factor(refs[:squares])
    inner_ref, *out_refs = refs[squares:]
    for j in range(blocks):
        at = pl.multiple_of((place_ref[1] ^ j) * part, 8)
        old = w_ref[j]
        update, _, _ = adam(old, m_ref[j], v_ref[j], g_ref[pl.ds(at, part), :], factor, sc_ref)
        inner_ref[j] = old - update
        out_refs[j][...] = update.astype(out_refs[j].dtype)


def adam_frag(place, scalars, squares, old, first, second, grad):
    blocks, part, width = old.shape
    smem = pl.BlockSpec(memory_space=pltpu.SMEM)
    vmem = pl.BlockSpec(memory_space=pltpu.VMEM)
    return pl.pallas_call(
        functools.partial(frag_kernel, len(squares)),
        out_shape=[jax.ShapeDtypeStruct(old.shape, jnp.float32)]
        + [jax.ShapeDtypeStruct((part, width), jnp.bfloat16)] * blocks,
        in_specs=[smem, smem] + [vmem] * (4 + len(squares)),
        out_specs=[vmem] * (1 + blocks),
        compiler_params=params_of(12),
        cost_estimate=cost(20 * old.size, 22 * old.size),
        name="adam_frag",
    )(place, scalars, old, first, second, grad, *squares)


def pick_kernel(blocks, place_ref, *refs):
    outs = refs[len(refs) // (blocks + 1) * blocks:]
    for i, out_ref in enumerate(outs):
        for j in range(blocks):
            out_ref[j] = refs[i * blocks + j][...]


def due_columns(place, part, *arrays):
    blocks = arrays[0].shape[0] // part
    specs = []
    for j in range(blocks):
        at = (lambda i, p, j=j: (p[1] ^ j, p[0])) if blocks > 1 else (lambda i, p: (0, p[0]))
        specs.append(pl.BlockSpec((part, FRAG_COLS), at))
    shape = (blocks, part, FRAG_COLS)
    return pl.pallas_call(
        functools.partial(pick_kernel, blocks),
        out_shape=[jax.ShapeDtypeStruct(shape, a.dtype) for a in arrays],
        grid_spec=pltpu.PrefetchScalarGridSpec(
            num_scalar_prefetch=1,
            grid=(1,),
            in_specs=specs * len(arrays),
            out_specs=[pl.BlockSpec(shape, lambda i, p: (0, 0, 0))] * len(arrays),
        ),
        compiler_params=params_of(12),
        cost_estimate=cost(0, 8 * blocks * part * FRAG_COLS * len(arrays)),
        name="due_columns",
    )(place, *[a for array in in_hbm(*arrays) for a in [array] * blocks])


def duplicate_kernel(*refs):
    half = (len(refs) - 3) // 2
    held, in_sems, out_sems = refs[2 * half:]
    streams = held.shape[1]
    step = held.shape[2]
    places = [(a, i, pl.ds(i * step, step)) for a in range(half) for i in range(streams)]
    fetches = [
        pltpu.make_async_copy(refs[a].at[at], held.at[a, i], in_sems.at[a, i]) for a, i, at in places
    ]
    stores = [
        pltpu.make_async_copy(held.at[a, i], refs[half + a].at[at], out_sems.at[a, i])
        for a, i, at in places
    ]
    for copy in fetches:
        copy.start()
    for fetch, store in zip(fetches, stores):
        fetch.wait()
        store.start()
    for copy in stores:
        copy.wait()


def duplicate(*arrays):
    rows, width = arrays[0].shape
    streams = 4
    whole = pl.BlockSpec(memory_space=pl.ANY)
    return pl.pallas_call(
        duplicate_kernel,
        out_shape=[pltpu.HBM(a.shape, a.dtype) for a in arrays],
        in_specs=[whole] * len(arrays),
        out_specs=[whole] * len(arrays),
        scratch_shapes=[
            pltpu.VMEM((len(arrays), streams, rows // streams, width), arrays[0].dtype),
            pltpu.SemaphoreType.DMA((len(arrays), streams)),
            pltpu.SemaphoreType.DMA((len(arrays), streams)),
        ],
        compiler_params=params_of(8),
        cost_estimate=cost(0, sum(8 * a.size for a in arrays)),
        name="duplicate",
    )(*in_hbm(*arrays))


def outer_kernel(replicas, place_ref, *refs):
    share = 1.0 / replicas
    base_refs, sum_refs = refs[3:3 + replicas], refs[3 + replicas:3 + 2 * replicas]
    inner_ref, a_ref, p_ref, m_ref, own_ref, _, *refs = refs[3 + 2 * replicas:]
    w_out, a_out, m_out, mixed, new_a, new_m, sems = refs
    part = a_ref.shape[0]
    scale = share * (1.0 + OUTER_MU) * OUTER_RATE
    columns = pl.ds(pl.multiple_of(place_ref[0] * FRAG_COLS, FRAG_COLS), FRAG_COLS)
    copies = []
    for j in range(replicas):
        fresh = base_refs[j][...] - scale * sum_refs[j][...].astype(jnp.float32)
        mixed[j] = MIX_LOCAL * inner_ref[j] + (1.0 - MIX_LOCAL) * fresh
        rows = pl.ds(pl.multiple_of((place_ref[1] ^ j) * part, 8), part)
        copies.append(pltpu.make_async_copy(mixed.at[j], w_out.at[rows, columns], sems.at[j]))
        copies[-1].start()
    pseudo = p_ref[...] + share * own_ref[...]
    new_moment = OUTER_MU * m_ref[...] + pseudo
    new_m[...] = new_moment
    new_a[...] = a_ref[...] - OUTER_RATE * (OUTER_MU * new_moment + pseudo)
    for i, (src, dst) in enumerate(((new_a, a_out), (new_m, m_out))):
        copies.append(pltpu.make_async_copy(src, dst.at[:, columns], sems.at[replicas + i]))
        copies[-1].start()
    for copy in copies:
        copy.wait()


def outer_step(place, outputs, base, sums, inner, anchor, pseudo, momentum, own_sum, ticket):
    replicas, part = inner.shape[0], inner.shape[1]
    whole = pl.BlockSpec(memory_space=pl.ANY)
    held = pl.BlockSpec(memory_space=pltpu.VMEM)
    return pl.pallas_call(
        functools.partial(outer_kernel, replicas),
        out_shape=[pltpu.HBM(a.shape, a.dtype) for a in outputs],
        in_specs=[pl.BlockSpec(memory_space=pltpu.SMEM)]
        + [whole] * 3
        + [held] * (2 * replicas + 5)
        + [whole],
        out_specs=[whole] * 3,
        scratch_shapes=[
            pltpu.VMEM((replicas, part, FRAG_COLS), jnp.float32),
            pltpu.VMEM((part, FRAG_COLS), jnp.float32),
            pltpu.VMEM((part, FRAG_COLS), jnp.float32),
            pltpu.SemaphoreType.DMA((replicas + 2,)),
        ],
        input_output_aliases={1: 0, 2: 1, 3: 2},
        compiler_params=params_of(12),
        cost_estimate=cost(10 * replicas * part * FRAG_COLS, 20 * replicas * part * FRAG_COLS),
        name="outer_step",
    )(place, *in_hbm(*outputs), *base, *sums, inner, anchor, pseudo, momentum, own_sum, ticket)


def swap(block, axis, offset):
    count = lax.axis_size(axis)
    return lax.ppermute(block, axis, [(i, i ^ offset) for i in range(count)])


def after(value, *others):
    return lax.optimization_barrier((value,) + others)[0]


def body(
    tokens,
    cotangent,
    weights,
    first_moment,
    second_moment,
    anchor,
    momentum,
    due_fragment,
    step_count,
):
    inputs, incoming, params = tokens[0], cotangent[0], weights[0]
    kv_width = incoming.shape[1] // 2
    rows = params.shape[0]
    part = anchor.shape[0]
    replicas = lax.axis_size("rep")
    shards = lax.axis_size("fsdp")
    me = jnp.reshape(lax.axis_index("fsdp"), (1,)).astype(jnp.int32)
    my_rep = lax.axis_index("rep").astype(jnp.int32)
    place = jnp.stack([due_fragment[0], my_rep])
    chips = range(2, shards, 2)
    far = sorted(chips, key=lambda k: (-bin(k).count("1"), k))
    order = [k for k in far[:-2] for k in (k, k + 1)]
    order += far[-2:] + [k + 1 for k in far[-2:]]

    (old,) = due_columns(place, part, params)
    old_sums = [old[0]] + [swap(old[k], "rep", k) for k in range(1, replicas)]

    packed = {}
    for offsets in (order[:1], order[1:4], order[4:], (0, 1)):
        packed |= pack(inputs, me, rows, tuple(offsets))
    blocks = {k: swap(packed[k], "fsdp", k) for k in order}
    blocks[0], blocks[1] = packed[0], swap(packed[1], "fsdp", 1)

    relay = len(far) == 3 and far[0] == far[1] ^ far[2]
    half = inputs.shape[0] // 2
    values = {0: incoming[:, kv_width:]}
    for i, k in enumerate(far[1:] if relay else far):
        values[k] = swap(after(values[0], blocks[order[i]]), "fsdp", k)

    steps_now = step_count[0].astype(jnp.float32)
    plan = jnp.minimum(1.0, steps_now / WARMUP) * (
        0.55 + 0.45 * jnp.cos(jnp.pi * steps_now / STEPS_TOTAL)
    )
    rate = PEAK_RATE * plan
    inv_one = 1.0 / (1.0 - jnp.power(BETA_ONE, steps_now))
    inv_two = 1.0 / (1.0 - jnp.power(BETA_TWO, steps_now))
    scalars = jnp.stack([rate, inv_one, inv_two])
    old_first, old_second = due_columns(place, part, first_moment[0], second_moment[0])
    anchor_cols, moment_cols = (c[0] for c in due_columns(place, part, anchor, momentum))
    pseudo_old = anchor_cols - sum(old_sums[1:], old_sums[0]) / replicas
    base = anchor_cols - OUTER_RATE * (OUTER_MU * (OUTER_MU * moment_cols + pseudo_old) + pseudo_old)
    base = [base] + [swap(base, "rep", k) for k in range(1, replicas)]
    anchor_copy, momentum_copy = duplicate(anchor, momentum)
    key_weights = cast_left(params, kv_width)

    last = far[-1]
    blocks[last + 1] = after(blocks[last + 1], anchor_copy, momentum_copy, scalars, old_first, old_second)
    parts, flipped, relayed = [], {}, {}
    for k in far + [0]:
        theirs, flipped[k + 1] = partial_keys(blocks[k + 1], key_weights)
        theirs = swap(theirs, "fsdp", 1)
        if k == last:
            theirs = after(theirs, *base)
        adds = [(theirs, 0)] + relayed.get(k, [])
        if relay and k == far[0]:
            (upper, lower), flipped[k] = partial_keys(blocks[k], key_weights, adds, 2)
            relayed[far[2]] = [(swap(upper, "fsdp", far[1]), 0)]
            relayed[far[1]] = [(swap(lower, "fsdp", far[2]), half)]
            continue
        part_k, flipped[k] = partial_keys(blocks[k], key_weights, adds)
        if k == last:
            for j in [0] + [j for j in far if j in values]:
                values[j] = after(values[j], part_k)
            if relay:
                upper = swap(values[far[1]][:half], "fsdp", far[2])
                lower = swap(values[far[2]][half:], "fsdp", far[1])
                values[far[0]] = jnp.concatenate([upper, lower], axis=0)
            for j in range(0, shards, 2):
                values[j + 1] = swap(values[j], "fsdp", 1)
        parts.append(swap(part_k, "fsdp", k) if k else part_k)
    spread = [0, 1] + [k + odd for k in far for odd in range(2)]
    near, rest = spread[:shards // 2], spread[shards // 2:]
    pick = lambda table, which: [table[k] for k in which]
    (values_first,) = gradient(place, pick(flipped, near), pick(values, near), last=False)
    keys = {0: key_backward(parts, incoming, 0)}
    for k in far:
        keys[k] = swap(keys[0], "fsdp", k)
    keys[1] = swap(keys[0], "fsdp", 1)

    grad_values, square, due = gradient(
        place, pick(flipped, rest), pick(values, rest), values_first
    )
    for k in near[2::2]:
        keys[k + 1] = swap(after(keys[k], square), "fsdp", 1)
    (keys_first,) = gradient(place, pick(flipped, near), pick(keys, near), last=False)
    for k in rest[::2]:
        keys[k + 1] = swap(after(keys[k], square), "fsdp", 1)
    grad_keys, square, due = gradient(
        place, pick(flipped, rest), pick(keys, rest), keys_first, square, due
    )

    square = square + swap(square, "fsdp", 1)
    squares = [square] + [swap(square, "fsdp", k) for k in chips]

    state = (params, first_moment[0], second_moment[0], grad_keys, grad_values)
    inner, *update = adam_frag(place, scalars, squares, old, old_first, old_second, due)
    steps = rows // ADAM_ROWS
    *results, ticket = adam_rows(scalars, squares, state, 0, steps // 2)
    own_sum = update[0].astype(jnp.float32)
    for k in range(1, replicas):
        own_sum = own_sum + swap(update[k], "rep", k).astype(jnp.float32)
    own_sum, ticket = lax.optimization_barrier((own_sum, ticket))
    sums = [own_sum.astype(jnp.bfloat16)]
    sums += [swap(sums[0], "rep", k) for k in range(1, replicas)]
    results = adam_rows(scalars, squares, state, steps // 2, steps, results)
    weights_out, anchor_out, momentum_out = outer_step(
        place,
        (results[0], anchor_copy, momentum_copy),
        base,
        sums,
        inner,
        anchor_cols,
        pseudo_old,
        moment_cols,
        own_sum,
        ticket,
    )
    plan_out = jnp.reshape(plan, (1,))
    return (
        weights_out[None],
        results[1][None],
        results[2][None],
        anchor_out,
        momentum_out,
        plan_out,
    )


def solution(mesh):
    tokens_spec = P("rep", "fsdp", None)
    outer_spec = P(("fsdp", "rep"), None)
    return jax.shard_map(
        body,
        mesh=mesh,
        in_specs=(tokens_spec,) * 5 + (outer_spec,) * 2 + (P(), P()),
        out_specs=(tokens_spec,) * 3 + (outer_spec,) * 2 + (P(),),
        check_vma=False,
    )
```

```python
import functools

import jax
import jax.numpy as jnp
from jax import lax
from jax.experimental import pallas as pl
from jax.experimental.pallas import tpu as pltpu
from jax.sharding import PartitionSpec as P

HEAD = 128
WARMUP = 2000
STEPS_TOTAL = 100000
FRAG_COLS = 128


BETA_ONE = 0.9
BETA_TWO = 0.95
ADAM_EPS = 1e-08
DECAY = 0.1
PEAK_RATE = 0.0003
CLIP_NORM = 1.0
OUTER_MU = 0.9
OUTER_RATE = 0.7
MIX_LOCAL = 0.5

MIB = 1 << 20
ADAM_ROWS = 128


def in_hbm(*arrays):
    return [pltpu.with_memory_space_constraint(a, pltpu.HBM) for a in arrays]


def params_of(limit):
    return pltpu.CompilerParams(vmem_limit_bytes=limit * MIB)


def cost(flops, moved):
    return pl.CostEstimate(flops=int(flops), bytes_accessed=int(moved), transcendentals=0)


def pack_kernel(offsets, me_ref, src_ref, *refs):
    half = len(offsets)
    out_refs, (held, in_sems, out_sems) = refs[:half], refs[half:]
    streams = in_sems.shape[1]
    count, rows = out_refs[0].shape
    step = count // streams
    fetches, stores = [], []
    for i, offset in enumerate(offsets):
        column = pl.multiple_of((me_ref[0] ^ offset) * rows, HEAD)
        for j in range(streams):
            at = pl.ds(j * step, step)
            block = src_ref.at[at, pl.ds(column, rows)]
            fetches.append(pltpu.make_async_copy(block, held.at[i, at], in_sems.at[i, j]))
            stores.append(pltpu.make_async_copy(held.at[i, at], out_refs[i].at[at], out_sems.at[i, j]))
    for copy in fetches:
        copy.start()
    for fetch, store in zip(fetches, stores):
        fetch.wait()
        store.start()
    for copy in stores:
        copy.wait()


def pack(tokens, me, rows, offsets):
    count = tokens.shape[0]
    streams = 4
    whole = pl.BlockSpec(memory_space=pl.ANY)
    outs = pl.pallas_call(
        functools.partial(pack_kernel, offsets),
        out_shape=[pltpu.HBM((count, rows), tokens.dtype)] * len(offsets),
        in_specs=[pl.BlockSpec(memory_space=pltpu.SMEM), whole],
        out_specs=[whole] * len(offsets),
        scratch_shapes=[
            pltpu.VMEM((len(offsets), count, rows), tokens.dtype),
            pltpu.SemaphoreType.DMA((len(offsets), streams)),
            pltpu.SemaphoreType.DMA((len(offsets), streams)),
        ],
        compiler_params=params_of(12),
        cost_estimate=cost(0, 4 * len(offsets) * count * rows),
        name="pack",
    )(me, *in_hbm(tokens))
    return dict(zip(offsets, outs))


def cast_kernel(src_ref, out_ref):
    out_ref[...] = src_ref[...].astype(out_ref.dtype)


def cast_left(array, width):
    rows = array.shape[0]
    block = pl.BlockSpec((256, width), lambda i: (i, 0))
    return pl.pallas_call(
        cast_kernel,
        out_shape=jax.ShapeDtypeStruct((rows, width), jnp.bfloat16),
        grid=(rows // 256,),
        in_specs=[block],
        out_specs=block,
        compiler_params=params_of(8),
        cost_estimate=cost(0, 6 * rows * width),
        name="cast_left",
    )(*in_hbm(array))


def partial_kernel(pieces, firsts, splits, *refs):
    x_refs, w_ref, refs = refs[:pieces], refs[pieces], refs[pieces + 1:]
    add_refs, out_refs, flip_ref = refs[:len(firsts)], refs[len(firsts):-1], refs[-1]
    x = jnp.concatenate([ref[...] for ref in x_refs], axis=1)
    total = jnp.dot(x, w_ref[...], preferred_element_type=jnp.float32)
    count = total.shape[0]
    for ref, first in zip(add_refs, firsts):
        last = first + ref.shape[0]
        rows = [total[:first], total[first:last] + ref[...].astype(jnp.float32), total[last:]]
        total = jnp.concatenate([r for r in rows if r.shape[0]], axis=0)
    height = count // splits
    for i, ref in enumerate(out_refs):
        ref[...] = total[i * height:(i + 1) * height].astype(ref.dtype)
    step = x_refs[0].shape[1]
    for i, ref in enumerate(x_refs):
        flip_ref[i * step:(i + 1) * step, :] = ref[...].T


def partial_keys(block, key_weights, adds=(), splits=1):
    count, rows = block.shape
    width = key_weights.shape[1]
    pieces = 4 if rows % (4 * HEAD) == 0 else 2
    fixed = lambda a: pl.BlockSpec(a.shape, lambda i: (0, 0))
    *parts, flipped = pl.pallas_call(
        functools.partial(partial_kernel, pieces, [first for _, first in adds], splits),
        out_shape=[jax.ShapeDtypeStruct((count // splits, width), jnp.bfloat16)] * splits
        + [jax.ShapeDtypeStruct((rows, count), jnp.bfloat16)],
        grid=(1,),
        in_specs=[pl.BlockSpec((count, rows // pieces), lambda i, c=c: (0, c)) for c in range(pieces)]
        + [fixed(key_weights)]
        + [fixed(a) for a, _ in adds],
        out_specs=[pl.BlockSpec((count // splits, width), lambda i: (0, 0))] * splits
        + [pl.BlockSpec((rows, count), lambda i: (0, 0))],
        compiler_params=params_of(12),
        cost_estimate=cost(2 * count * rows * width, 4 * count * rows),
        name="partial_keys",
    )(*[block] * pieces, key_weights, *[a for a, _ in adds])
    return parts if splits > 1 else parts[0], flipped


def key_kernel(first, *refs):
    *part_refs, cot_ref, out_ref = refs
    count = out_ref.shape[0]
    raw = sum(ref[...].astype(jnp.float32) for ref in part_refs)
    for h in range(raw.shape[1] // HEAD):
        cols = slice(h * HEAD, (h + 1) * HEAD)
        head = raw[:, cols]
        inverse = lax.rsqrt(jnp.mean(head * head, axis=1, keepdims=True) + 1e-06)
        normed = head * inverse
        upper = cot_ref[first:first + count, cols].astype(jnp.float32)
        back = inverse * (upper - normed * jnp.mean(upper * normed, axis=1, keepdims=True))
        out_ref[:, cols] = back.astype(out_ref.dtype)


def key_backward(parts, incoming, first):
    count, width = parts[0].shape
    block = pl.BlockSpec((count, width), lambda i: (0, 0))
    cot = pl.BlockSpec((incoming.shape[0], width), lambda i: (0, 0))
    return pl.pallas_call(
        functools.partial(key_kernel, first),
        out_shape=jax.ShapeDtypeStruct((count, width), jnp.bfloat16),
        grid=(1,),
        in_specs=[block] * len(parts) + [cot],
        out_specs=block,
        compiler_params=params_of(8),
        cost_estimate=cost(60 * count * width, 12 * count * width),
        name="key_backward",
    )(*parts, incoming)


def grad_kernel(count, has_base, has_more, last, place_ref, *refs):
    refs = list(refs)
    x_refs, u_refs = refs[:count], refs[count:2 * count]
    refs = refs[2 * count:]
    base = refs.pop(0) if has_base else None
    square_in, due_in = (refs.pop(0), refs.pop(0)) if has_more else (None, None)
    out_ref = refs.pop(0)
    x = jnp.concatenate([ref[...] for ref in x_refs], axis=1)
    u = jnp.concatenate([ref[...] for ref in u_refs], axis=0)
    total = jnp.dot(x, u, preferred_element_type=jnp.float32)
    if has_base:
        total = total + base[...]
    out_ref[...] = total
    if last:
        sq_ref, due_ref = refs

        @pl.when(pl.program_id(0) == 0)
        def _():
            sq_ref[...] = square_in[...] if has_more else jnp.zeros_like(sq_ref)

        rows, width = total.shape
        squares = (total * total).reshape(rows // 8, 8, width).sum(axis=0)
        folded = squares[:, :HEAD]
        for h in range(1, width // HEAD):
            folded = folded + squares[:, h * HEAD:(h + 1) * HEAD]
        sq_ref[...] += folded
        heads = width // FRAG_COLS
        mine = place_ref[0] - (0 if has_more else heads)
        mine = jnp.minimum(jnp.maximum(mine, 0), heads - 1) * FRAG_COLS
        column = out_ref[:, pl.ds(pl.multiple_of(mine, FRAG_COLS), FRAG_COLS)]
        if has_more:
            column = jnp.where(place_ref[0] < heads, column, due_in[...])
        due_ref[...] = column


def gradient(place, flipped, upstream, base=None, square=None, due=None, last=True):
    rows, depth = flipped[0].shape
    width = upstream[0].shape[1]
    step = 256
    row_block = lambda cols: pl.BlockSpec((step, cols), lambda i, p: (i, 0))
    fixed = pl.BlockSpec((8, HEAD), lambda i, p: (0, 0))
    args = [*flipped, *upstream]
    specs = [row_block(depth)] * len(flipped)
    specs += [pl.BlockSpec((depth, width), lambda i, p: (0, 0))] * len(upstream)
    if base is not None:
        args.append(base)
        specs.append(row_block(width))
    if square is not None:
        args += [square, due]
        specs += [fixed, row_block(FRAG_COLS)]
    if last:
        shapes = [
            jax.ShapeDtypeStruct((rows, width), jnp.float32),
            jax.ShapeDtypeStruct((8, HEAD), jnp.float32),
            jax.ShapeDtypeStruct((rows, FRAG_COLS), jnp.float32),
        ]
        outs = [row_block(width), fixed, row_block(FRAG_COLS)]
    else:
        shapes = [jax.ShapeDtypeStruct((rows, width), jnp.float32)]
        outs = [row_block(width)]
    depth *= len(flipped)
    return pl.pallas_call(
        functools.partial(grad_kernel, len(flipped), base is not None, square is not None, last),
        out_shape=shapes,
        grid_spec=pltpu.PrefetchScalarGridSpec(
            num_scalar_prefetch=1, grid=(rows // step,), in_specs=specs, out_specs=outs
        ),
        compiler_params=params_of(12),
        cost_estimate=cost(2 * rows * width * depth, 2 * rows * depth + 4 * rows * width),
        name="gradient",
    )(place, *args)


def clip_factor(square_refs):
    square = jnp.sum(sum(ref[...] for ref in square_refs), keepdims=True)
    return jnp.minimum(1.0, CLIP_NORM / (jnp.sqrt(square) + 1e-06))


def adam(old, first, second, grad, factor, scalars):
    rate, inv_one, inv_two = (scalars[i] for i in range(3))
    clipped = grad * factor
    first_new = BETA_ONE * first + (1.0 - BETA_ONE) * clipped
    second_new = BETA_TWO * second + (1.0 - BETA_TWO) * clipped * clipped
    update = rate * (
        first_new * inv_one / (jnp.sqrt(second_new * inv_two) + ADAM_EPS) + DECAY * old
    )
    return update, first_new, second_new


def adam_kernel(squares, extra, sc_ref, w_ref, m_ref, v_ref, gk_ref, gv_ref, *refs):
    factor = clip_factor(refs[:squares])
    w_out, m_out, v_out, *done = refs[squares + extra:]
    width = gk_ref.shape[1]
    for g_ref, cols in ((gk_ref, slice(0, width)), (gv_ref, slice(width, 2 * width))):
        old = w_ref[:, cols]
        update, first_new, second_new = adam(
            old, m_ref[:, cols], v_ref[:, cols], g_ref[...], factor, sc_ref
        )
        w_out[:, cols] = old - update
        m_out[:, cols] = first_new
        v_out[:, cols] = second_new
    for ref in done:
        ref[...] = jnp.zeros_like(ref)


def adam_rows(scalars, squares, state, first, last, into=()):
    rows, width = state[0].shape
    step = ADAM_ROWS
    full = pl.BlockSpec((step, width), lambda i: (i + first, 0))
    half = pl.BlockSpec((step, width // 2), lambda i: (i + first, 0))
    shapes = [pltpu.HBM((rows, width), jnp.float32)] * 3
    outs = [full] * 3
    if not into:
        shapes.append(jax.ShapeDtypeStruct((8, HEAD), jnp.float32))
        outs.append(pl.BlockSpec((8, HEAD), lambda i: (0, 0)))
    count = (last - first) * step
    return pl.pallas_call(
        functools.partial(adam_kernel, len(squares), len(into)),
        out_shape=shapes,
        grid=(last - first,),
        in_specs=[pl.BlockSpec(memory_space=pltpu.SMEM), full, full, full, half, half]
        + [pl.BlockSpec((8, HEAD), lambda i: (0, 0))] * len(squares)
        + [pl.BlockSpec(memory_space=pl.ANY)] * len(into),
        out_specs=outs,
        input_output_aliases={6 + len(squares) + i: i for i in range(len(into))},
        compiler_params=params_of(12),
        cost_estimate=cost(20 * count * width, 28 * count * width),
        name="adam_rows",
    )(scalars, *state, *squares, *in_hbm(*into))


def frag_kernel(squares, place_ref, sc_ref, w_ref, m_ref, v_ref, g_ref, *refs):
    blocks, part, _ = w_ref.shape
    factor = clip_factor(refs[:squares])
    inner_ref, *out_refs = refs[squares:]
    for j in range(blocks):
        at = pl.multiple_of((place_ref[1] ^ j) * part, 8)
        old = w_ref[j]
        update, _, _ = adam(old, m_ref[j], v_ref[j], g_ref[pl.ds(at, part), :], factor, sc_ref)
        inner_ref[j] = old - update
        out_refs[j][...] = update.astype(out_refs[j].dtype)


def adam_frag(place, scalars, squares, old, first, second, grad):
    blocks, part, width = old.shape
    smem = pl.BlockSpec(memory_space=pltpu.SMEM)
    vmem = pl.BlockSpec(memory_space=pltpu.VMEM)
    return pl.pallas_call(
        functools.partial(frag_kernel, len(squares)),
        out_shape=[jax.ShapeDtypeStruct(old.shape, jnp.float32)]
        + [jax.ShapeDtypeStruct((part, width), jnp.bfloat16)] * blocks,
        in_specs=[smem, smem] + [vmem] * (4 + len(squares)),
        out_specs=[vmem] * (1 + blocks),
        compiler_params=params_of(12),
        cost_estimate=cost(20 * old.size, 22 * old.size),
        name="adam_frag",
    )(place, scalars, old, first, second, grad, *squares)


def pick_kernel(blocks, place_ref, *refs):
    outs = refs[len(refs) // (blocks + 1) * blocks:]
    for i, out_ref in enumerate(outs):
        for j in range(blocks):
            out_ref[j] = refs[i * blocks + j][...]


def due_columns(place, part, *arrays):
    blocks = arrays[0].shape[0] // part
    specs = []
    for j in range(blocks):
        at = (lambda i, p, j=j: (p[1] ^ j, p[0])) if blocks > 1 else (lambda i, p: (0, p[0]))
        specs.append(pl.BlockSpec((part, FRAG_COLS), at))
    shape = (blocks, part, FRAG_COLS)
    return pl.pallas_call(
        functools.partial(pick_kernel, blocks),
        out_shape=[jax.ShapeDtypeStruct(shape, a.dtype) for a in arrays],
        grid_spec=pltpu.PrefetchScalarGridSpec(
            num_scalar_prefetch=1,
            grid=(1,),
            in_specs=specs * len(arrays),
            out_specs=[pl.BlockSpec(shape, lambda i, p: (0, 0, 0))] * len(arrays),
        ),
        compiler_params=params_of(12),
        cost_estimate=cost(0, 8 * blocks * part * FRAG_COLS * len(arrays)),
        name="due_columns",
    )(place, *[a for array in in_hbm(*arrays) for a in [array] * blocks])


def duplicate_kernel(*refs):
    half = (len(refs) - 3) // 2
    held, in_sems, out_sems = refs[2 * half:]
    streams = held.shape[1]
    step = held.shape[2]
    places = [(a, i, pl.ds(i * step, step)) for a in range(half) for i in range(streams)]
    fetches = [
        pltpu.make_async_copy(refs[a].at[at], held.at[a, i], in_sems.at[a, i]) for a, i, at in places
    ]
    stores = [
        pltpu.make_async_copy(held.at[a, i], refs[half + a].at[at], out_sems.at[a, i])
        for a, i, at in places
    ]
    for copy in fetches:
        copy.start()
    for fetch, store in zip(fetches, stores):
        fetch.wait()
        store.start()
    for copy in stores:
        copy.wait()


def duplicate(*arrays):
    rows, width = arrays[0].shape
    streams = 4
    whole = pl.BlockSpec(memory_space=pl.ANY)
    return pl.pallas_call(
        duplicate_kernel,
        out_shape=[pltpu.HBM(a.shape, a.dtype) for a in arrays],
        in_specs=[whole] * len(arrays),
        out_specs=[whole] * len(arrays),
        scratch_shapes=[
            pltpu.VMEM((len(arrays), streams, rows // streams, width), arrays[0].dtype),
            pltpu.SemaphoreType.DMA((len(arrays), streams)),
            pltpu.SemaphoreType.DMA((len(arrays), streams)),
        ],
        compiler_params=params_of(8),
        cost_estimate=cost(0, sum(8 * a.size for a in arrays)),
        name="duplicate",
    )(*in_hbm(*arrays))


def outer_kernel(replicas, place_ref, *refs):
    share = 1.0 / replicas
    base_refs, sum_refs = refs[3:3 + replicas], refs[3 + replicas:3 + 2 * replicas]
    inner_ref, a_ref, p_ref, m_ref, own_ref, _, *refs = refs[3 + 2 * replicas:]
    w_out, a_out, m_out, mixed, new_a, new_m, sems = refs
    part = a_ref.shape[0]
    scale = share * (1.0 + OUTER_MU) * OUTER_RATE
    columns = pl.ds(pl.multiple_of(place_ref[0] * FRAG_COLS, FRAG_COLS), FRAG_COLS)
    copies = []
    for j in range(replicas):
        fresh = base_refs[j][...] - scale * sum_refs[j][...].astype(jnp.float32)
        mixed[j] = MIX_LOCAL * inner_ref[j] + (1.0 - MIX_LOCAL) * fresh
        rows = pl.ds(pl.multiple_of((place_ref[1] ^ j) * part, 8), part)
        copies.append(pltpu.make_async_copy(mixed.at[j], w_out.at[rows, columns], sems.at[j]))
        copies[-1].start()
    pseudo = p_ref[...] + share * own_ref[...]
    new_moment = OUTER_MU * m_ref[...] + pseudo
    new_m[...] = new_moment
    new_a[...] = a_ref[...] - OUTER_RATE * (OUTER_MU * new_moment + pseudo)
    for i, (src, dst) in enumerate(((new_a, a_out), (new_m, m_out))):
        copies.append(pltpu.make_async_copy(src, dst.at[:, columns], sems.at[replicas + i]))
        copies[-1].start()
    for copy in copies:
        copy.wait()


def outer_step(place, outputs, base, sums, inner, anchor, pseudo, momentum, own_sum, ticket):
    replicas, part = inner.shape[0], inner.shape[1]
    whole = pl.BlockSpec(memory_space=pl.ANY)
    held = pl.BlockSpec(memory_space=pltpu.VMEM)
    return pl.pallas_call(
        functools.partial(outer_kernel, replicas),
        out_shape=[pltpu.HBM(a.shape, a.dtype) for a in outputs],
        in_specs=[pl.BlockSpec(memory_space=pltpu.SMEM)]
        + [whole] * 3
        + [held] * (2 * replicas + 5)
        + [whole],
        out_specs=[whole] * 3,
        scratch_shapes=[
            pltpu.VMEM((replicas, part, FRAG_COLS), jnp.float32),
            pltpu.VMEM((part, FRAG_COLS), jnp.float32),
            pltpu.VMEM((part, FRAG_COLS), jnp.float32),
            pltpu.SemaphoreType.DMA((replicas + 2,)),
        ],
        input_output_aliases={1: 0, 2: 1, 3: 2},
        compiler_params=params_of(12),
        cost_estimate=cost(10 * replicas * part * FRAG_COLS, 20 * replicas * part * FRAG_COLS),
        name="outer_step",
    )(place, *in_hbm(*outputs), *base, *sums, inner, anchor, pseudo, momentum, own_sum, ticket)


def swap(block, axis, offset):
    count = lax.axis_size(axis)
    return lax.ppermute(block, axis, [(i, i ^ offset) for i in range(count)])


def after(value, *others):
    return lax.optimization_barrier((value,) + others)[0]


def body(
    tokens,
    cotangent,
    weights,
    first_moment,
    second_moment,
    anchor,
    momentum,
    due_fragment,
    step_count,
):
    inputs, incoming, params = tokens[0], cotangent[0], weights[0]
    kv_width = incoming.shape[1] // 2
    rows = params.shape[0]
    part = anchor.shape[0]
    replicas = lax.axis_size("rep")
    shards = lax.axis_size("fsdp")
    me = jnp.reshape(lax.axis_index("fsdp"), (1,)).astype(jnp.int32)
    my_rep = lax.axis_index("rep").astype(jnp.int32)
    place = jnp.stack([due_fragment[0], my_rep])
    chips = range(2, shards, 2)
    far = sorted(chips, key=lambda k: (-bin(k).count("1"), k))
    order = [k for k in far[:-2] for k in (k, k + 1)]
    order += far[-2:] + [k + 1 for k in far[-2:]]

    (old,) = due_columns(place, part, params)
    old_sums = [old[0]] + [swap(old[k], "rep", k) for k in range(1, replicas)]

    packed = {}
    for offsets in (order[:1], order[1:4], order[4:], (0, 1)):
        packed |= pack(inputs, me, rows, tuple(offsets))
    blocks = {k: swap(packed[k], "fsdp", k) for k in order}
    blocks[0], blocks[1] = packed[0], swap(packed[1], "fsdp", 1)

    relay = len(far) == 3 and far[0] == far[1] ^ far[2]
    half = inputs.shape[0] // 2
    values = {0: incoming[:, kv_width:]}

    steps_now = step_count[0].astype(jnp.float32)
    plan = jnp.minimum(1.0, steps_now / WARMUP) * (
        0.55 + 0.45 * jnp.cos(jnp.pi * steps_now / STEPS_TOTAL)
    )
    rate = PEAK_RATE * plan
    inv_one = 1.0 / (1.0 - jnp.power(BETA_ONE, steps_now))
    inv_two = 1.0 / (1.0 - jnp.power(BETA_TWO, steps_now))
    scalars = jnp.stack([rate, inv_one, inv_two])
    old_first, old_second = due_columns(place, part, first_moment[0], second_moment[0])
    anchor_cols, moment_cols = (c[0] for c in due_columns(place, part, anchor, momentum))
    pseudo_old = anchor_cols - sum(old_sums[1:], old_sums[0]) / replicas
    base = anchor_cols - OUTER_RATE * (OUTER_MU * (OUTER_MU * moment_cols + pseudo_old) + pseudo_old)
    base = [base] + [swap(base, "rep", k) for k in range(1, replicas)]
    anchor_copy, momentum_copy = duplicate(anchor, momentum)
    key_weights = cast_left(params, kv_width)

    last = far[-1]
    blocks[last + 1] = after(blocks[last + 1], anchor_copy, momentum_copy, scalars, old_first, old_second)
    parts, flipped, relayed = [], {}, {}
    for k in far + [0]:
        theirs, flipped[k + 1] = partial_keys(blocks[k + 1], key_weights)
        theirs = swap(theirs, "fsdp", 1)
        if k == last:
            theirs = after(theirs, *base)
        adds = [(theirs, 0)] + relayed.get(k, [])
        if k == far[0]:
            blocks[k] = after(blocks[k], blocks[1])
        if relay and k == far[0]:
            (upper, lower), flipped[k] = partial_keys(blocks[k], key_weights, adds, 2)
            for j in far[1:]:
                values[j] = swap(after(values[0], upper), "fsdp", j)
            relayed[far[2]] = [(swap(upper, "fsdp", far[1]), 0)]
            relayed[far[1]] = [(swap(lower, "fsdp", far[2]), half)]
            continue
        part_k, flipped[k] = partial_keys(blocks[k], key_weights, adds)
        if k == far[0]:
            for j in far:
                values[j] = swap(after(values[0], part_k), "fsdp", j)
        if k == last:
            for j in [0] + [j for j in far if j in values]:
                values[j] = after(values[j], part_k)
            if relay:
                upper = swap(values[far[1]][:half], "fsdp", far[2])
                lower = swap(values[far[2]][half:], "fsdp", far[1])
                values[far[0]] = jnp.concatenate([upper, lower], axis=0)
            for j in range(0, shards, 2):
                values[j + 1] = swap(values[j], "fsdp", 1)
        parts.append(swap(part_k, "fsdp", k) if k else part_k)
    spread = [0, 1] + [k + odd for k in far for odd in range(2)]
    near, rest = spread[:shards // 2], spread[shards // 2:]
    pick = lambda table, which: [table[k] for k in which]
    (values_first,) = gradient(place, pick(flipped, near), pick(values, near), last=False)
    keys = {0: key_backward(parts, incoming, 0)}
    for k in far:
        keys[k] = swap(keys[0], "fsdp", k)
    keys[1] = swap(keys[0], "fsdp", 1)

    grad_values, square, due = gradient(
        place, pick(flipped, rest), pick(values, rest), values_first
    )
    for k in near[2::2]:
        keys[k + 1] = swap(after(keys[k], square), "fsdp", 1)
    (keys_first,) = gradient(place, pick(flipped, near), pick(keys, near), last=False)
    for k in rest[::2]:
        keys[k + 1] = swap(after(keys[k], square), "fsdp", 1)
    grad_keys, square, due = gradient(
        place, pick(flipped, rest), pick(keys, rest), keys_first, square, due
    )

    square = square + swap(square, "fsdp", 1)
    squares = [square] + [swap(square, "fsdp", k) for k in chips]

    state = (params, first_moment[0], second_moment[0], grad_keys, grad_values)
    inner, *update = adam_frag(place, scalars, squares, old, old_first, old_second, due)
    steps = rows // ADAM_ROWS
    *results, ticket = adam_rows(scalars, squares, state, 0, steps // 2)
    own_sum = update[0].astype(jnp.float32)
    for k in range(1, replicas):
        own_sum = own_sum + swap(update[k], "rep", k).astype(jnp.float32)
    own_sum, ticket = lax.optimization_barrier((own_sum, ticket))
    sums = [own_sum.astype(jnp.bfloat16)]
    sums += [swap(sums[0], "rep", k) for k in range(1, replicas)]
    results = adam_rows(scalars, squares, state, steps // 2, steps, results)
    weights_out, anchor_out, momentum_out = outer_step(
        place,
        (results[0], anchor_copy, momentum_copy),
        base,
        sums,
        inner,
        anchor_cols,
        pseudo_old,
        moment_cols,
        own_sum,
        ticket,
    )
    plan_out = jnp.reshape(plan, (1,))
    return (
        weights_out[None],
        results[1][None],
        results[2][None],
        anchor_out,
        momentum_out,
        plan_out,
    )


def solution(mesh):
    tokens_spec = P("rep", "fsdp", None)
    outer_spec = P(("fsdp", "rep"), None)
    return jax.shard_map(
        body,
        mesh=mesh,
        in_specs=(tokens_spec,) * 5 + (outer_spec,) * 2 + (P(), P()),
        out_specs=(tokens_spec,) * 3 + (outer_spec,) * 2 + (P(),),
        check_vma=False,
    )
```

```python
import functools

import jax
import jax.numpy as jnp
from jax import lax
from jax.experimental import pallas as pl
from jax.experimental.pallas import tpu as pltpu
from jax.sharding import PartitionSpec as P

HEAD = 128
WARMUP = 2000
STEPS_TOTAL = 100000
FRAG_COLS = 128


BETA_ONE = 0.9
BETA_TWO = 0.95
ADAM_EPS = 1e-08
DECAY = 0.1
PEAK_RATE = 0.0003
CLIP_NORM = 1.0
OUTER_MU = 0.9
OUTER_RATE = 0.7
MIX_LOCAL = 0.5

MIB = 1 << 20
ADAM_ROWS = 128


def in_hbm(*arrays):
    return [pltpu.with_memory_space_constraint(a, pltpu.HBM) for a in arrays]


def params_of(limit):
    return pltpu.CompilerParams(vmem_limit_bytes=limit * MIB)


def cost(flops, moved):
    return pl.CostEstimate(flops=int(flops), bytes_accessed=int(moved), transcendentals=0)


def pack_kernel(offsets, me_ref, src_ref, *refs):
    half = len(offsets)
    out_refs, (held, in_sems, out_sems) = refs[:half], refs[half:]
    streams = in_sems.shape[1]
    count, rows = out_refs[0].shape
    step = count // streams
    fetches, stores = [], []
    for i, offset in enumerate(offsets):
        column = pl.multiple_of((me_ref[0] ^ offset) * rows, HEAD)
        for j in range(streams):
            at = pl.ds(j * step, step)
            block = src_ref.at[at, pl.ds(column, rows)]
            fetches.append(pltpu.make_async_copy(block, held.at[i, at], in_sems.at[i, j]))
            stores.append(pltpu.make_async_copy(held.at[i, at], out_refs[i].at[at], out_sems.at[i, j]))
    for copy in fetches:
        copy.start()
    for fetch, store in zip(fetches, stores):
        fetch.wait()
        store.start()
    for copy in stores:
        copy.wait()


def pack(tokens, me, rows, offsets):
    count = tokens.shape[0]
    streams = 4
    whole = pl.BlockSpec(memory_space=pl.ANY)
    outs = pl.pallas_call(
        functools.partial(pack_kernel, offsets),
        out_shape=[pltpu.HBM((count, rows), tokens.dtype)] * len(offsets),
        in_specs=[pl.BlockSpec(memory_space=pltpu.SMEM), whole],
        out_specs=[whole] * len(offsets),
        scratch_shapes=[
            pltpu.VMEM((len(offsets), count, rows), tokens.dtype),
            pltpu.SemaphoreType.DMA((len(offsets), streams)),
            pltpu.SemaphoreType.DMA((len(offsets), streams)),
        ],
        compiler_params=params_of(12),
        cost_estimate=cost(0, 4 * len(offsets) * count * rows),
        name="pack",
    )(me, *in_hbm(tokens))
    return dict(zip(offsets, outs))


def cast_kernel(src_ref, out_ref):
    out_ref[...] = src_ref[...].astype(out_ref.dtype)


def cast_left(array, width):
    rows = array.shape[0]
    block = pl.BlockSpec((256, width), lambda i: (i, 0))
    return pl.pallas_call(
        cast_kernel,
        out_shape=jax.ShapeDtypeStruct((rows, width), jnp.bfloat16),
        grid=(rows // 256,),
        in_specs=[block],
        out_specs=block,
        compiler_params=params_of(8),
        cost_estimate=cost(0, 6 * rows * width),
        name="cast_left",
    )(*in_hbm(array))


def partial_kernel(pieces, firsts, splits, *refs):
    x_refs, w_ref, refs = refs[:pieces], refs[pieces], refs[pieces + 1:]
    add_refs, out_refs, flip_ref = refs[:len(firsts)], refs[len(firsts):-1], refs[-1]
    x = jnp.concatenate([ref[...] for ref in x_refs], axis=1)
    total = jnp.dot(x, w_ref[...], preferred_element_type=jnp.float32)
    count = total.shape[0]
    for ref, first in zip(add_refs, firsts):
        last = first + ref.shape[0]
        rows = [total[:first], total[first:last] + ref[...].astype(jnp.float32), total[last:]]
        total = jnp.concatenate([r for r in rows if r.shape[0]], axis=0)
    height = count // splits
    for i, ref in enumerate(out_refs):
        ref[...] = total[i * height:(i + 1) * height].astype(ref.dtype)
    step = x_refs[0].shape[1]
    for i, ref in enumerate(x_refs):
        flip_ref[i * step:(i + 1) * step, :] = ref[...].T


def partial_keys(block, key_weights, adds=(), splits=1):
    count, rows = block.shape
    width = key_weights.shape[1]
    pieces = 4 if rows % (4 * HEAD) == 0 else 2
    fixed = lambda a: pl.BlockSpec(a.shape, lambda i: (0, 0))
    *parts, flipped = pl.pallas_call(
        functools.partial(partial_kernel, pieces, [first for _, first in adds], splits),
        out_shape=[jax.ShapeDtypeStruct((count // splits, width), jnp.bfloat16)] * splits
        + [jax.ShapeDtypeStruct((rows, count), jnp.bfloat16)],
        grid=(1,),
        in_specs=[pl.BlockSpec((count, rows // pieces), lambda i, c=c: (0, c)) for c in range(pieces)]
        + [fixed(key_weights)]
        + [fixed(a) for a, _ in adds],
        out_specs=[pl.BlockSpec((count // splits, width), lambda i: (0, 0))] * splits
        + [pl.BlockSpec((rows, count), lambda i: (0, 0))],
        compiler_params=params_of(12),
        cost_estimate=cost(2 * count * rows * width, 4 * count * rows),
        name="partial_keys",
    )(*[block] * pieces, key_weights, *[a for a, _ in adds])
    return parts if splits > 1 else parts[0], flipped


def key_kernel(first, *refs):
    *part_refs, cot_ref, out_ref = refs
    count = out_ref.shape[0]
    raw = sum(ref[...].astype(jnp.float32) for ref in part_refs)
    for h in range(raw.shape[1] // HEAD):
        cols = slice(h * HEAD, (h + 1) * HEAD)
        head = raw[:, cols]
        inverse = lax.rsqrt(jnp.mean(head * head, axis=1, keepdims=True) + 1e-06)
        normed = head * inverse
        upper = cot_ref[first:first + count, cols].astype(jnp.float32)
        back = inverse * (upper - normed * jnp.mean(upper * normed, axis=1, keepdims=True))
        out_ref[:, cols] = back.astype(out_ref.dtype)


def key_backward(parts, incoming, first):
    count, width = parts[0].shape
    block = pl.BlockSpec((count, width), lambda i: (0, 0))
    cot = pl.BlockSpec((incoming.shape[0], width), lambda i: (0, 0))
    return pl.pallas_call(
        functools.partial(key_kernel, first),
        out_shape=jax.ShapeDtypeStruct((count, width), jnp.bfloat16),
        grid=(1,),
        in_specs=[block] * len(parts) + [cot],
        out_specs=block,
        compiler_params=params_of(8),
        cost_estimate=cost(60 * count * width, 12 * count * width),
        name="key_backward",
    )(*parts, incoming)


def grad_kernel(count, has_base, has_more, last, place_ref, *refs):
    refs = list(refs)
    x_refs, u_refs = refs[:count], refs[count:2 * count]
    refs = refs[2 * count:]
    base = refs.pop(0) if has_base else None
    square_in, due_in = (refs.pop(0), refs.pop(0)) if has_more else (None, None)
    out_ref = refs.pop(0)
    x = jnp.concatenate([ref[...] for ref in x_refs], axis=1)
    u = jnp.concatenate([ref[...] for ref in u_refs], axis=0)
    total = jnp.dot(x, u, preferred_element_type=jnp.float32)
    if has_base:
        total = total + base[...]
    out_ref[...] = total
    if last:
        sq_ref, due_ref = refs

        @pl.when(pl.program_id(0) == 0)
        def _():
            sq_ref[...] = square_in[...] if has_more else jnp.zeros_like(sq_ref)

        rows, width = total.shape
        squares = (total * total).reshape(rows // 8, 8, width).sum(axis=0)
        folded = squares[:, :HEAD]
        for h in range(1, width // HEAD):
            folded = folded + squares[:, h * HEAD:(h + 1) * HEAD]
        sq_ref[...] += folded
        heads = width // FRAG_COLS
        mine = place_ref[0] - (0 if has_more else heads)
        mine = jnp.minimum(jnp.maximum(mine, 0), heads - 1) * FRAG_COLS
        column = out_ref[:, pl.ds(pl.multiple_of(mine, FRAG_COLS), FRAG_COLS)]
        if has_more:
            column = jnp.where(place_ref[0] < heads, column, due_in[...])
        due_ref[...] = column


def gradient(place, flipped, upstream, base=None, square=None, due=None, last=True):
    rows, depth = flipped[0].shape
    width = upstream[0].shape[1]
    step = 256
    row_block = lambda cols: pl.BlockSpec((step, cols), lambda i, p: (i, 0))
    fixed = pl.BlockSpec((8, HEAD), lambda i, p: (0, 0))
    args = [*flipped, *upstream]
    specs = [row_block(depth)] * len(flipped)
    specs += [pl.BlockSpec((depth, width), lambda i, p: (0, 0))] * len(upstream)
    if base is not None:
        args.append(base)
        specs.append(row_block(width))
    if square is not None:
        args += [square, due]
        specs += [fixed, row_block(FRAG_COLS)]
    if last:
        shapes = [
            jax.ShapeDtypeStruct((rows, width), jnp.float32),
            jax.ShapeDtypeStruct((8, HEAD), jnp.float32),
            jax.ShapeDtypeStruct((rows, FRAG_COLS), jnp.float32),
        ]
        outs = [row_block(width), fixed, row_block(FRAG_COLS)]
    else:
        shapes = [jax.ShapeDtypeStruct((rows, width), jnp.float32)]
        outs = [row_block(width)]
    depth *= len(flipped)
    return pl.pallas_call(
        functools.partial(grad_kernel, len(flipped), base is not None, square is not None, last),
        out_shape=shapes,
        grid_spec=pltpu.PrefetchScalarGridSpec(
            num_scalar_prefetch=1, grid=(rows // step,), in_specs=specs, out_specs=outs
        ),
        compiler_params=params_of(12),
        cost_estimate=cost(2 * rows * width * depth, 2 * rows * depth + 4 * rows * width),
        name="gradient",
    )(place, *args)


def clip_factor(square_refs):
    square = jnp.sum(sum(ref[...] for ref in square_refs), keepdims=True)
    return jnp.minimum(1.0, CLIP_NORM / (jnp.sqrt(square) + 1e-06))


def adam(old, first, second, grad, factor, scalars):
    rate, inv_one, inv_two = (scalars[i] for i in range(3))
    clipped = grad * factor
    first_new = BETA_ONE * first + (1.0 - BETA_ONE) * clipped
    second_new = BETA_TWO * second + (1.0 - BETA_TWO) * clipped * clipped
    update = rate * (
        first_new * inv_one / (jnp.sqrt(second_new * inv_two) + ADAM_EPS) + DECAY * old
    )
    return update, first_new, second_new


def adam_kernel(squares, extra, sc_ref, w_ref, m_ref, v_ref, gk_ref, gv_ref, *refs):
    factor = clip_factor(refs[:squares])
    w_out, m_out, v_out, *done = refs[squares + extra:]
    width = gk_ref.shape[1]
    for g_ref, cols in ((gk_ref, slice(0, width)), (gv_ref, slice(width, 2 * width))):
        old = w_ref[:, cols]
        update, first_new, second_new = adam(
            old, m_ref[:, cols], v_ref[:, cols], g_ref[...], factor, sc_ref
        )
        w_out[:, cols] = old - update
        m_out[:, cols] = first_new
        v_out[:, cols] = second_new
    for ref in done:
        ref[...] = jnp.zeros_like(ref)


def adam_rows(scalars, squares, state, first, last, into=()):
    rows, width = state[0].shape
    step = ADAM_ROWS
    full = pl.BlockSpec((step, width), lambda i: (i + first, 0))
    half = pl.BlockSpec((step, width // 2), lambda i: (i + first, 0))
    shapes = [pltpu.HBM((rows, width), jnp.float32)] * 3
    outs = [full] * 3
    if not into:
        shapes.append(jax.ShapeDtypeStruct((8, HEAD), jnp.float32))
        outs.append(pl.BlockSpec((8, HEAD), lambda i: (0, 0)))
    count = (last - first) * step
    return pl.pallas_call(
        functools.partial(adam_kernel, len(squares), len(into)),
        out_shape=shapes,
        grid=(last - first,),
        in_specs=[pl.BlockSpec(memory_space=pltpu.SMEM), full, full, full, half, half]
        + [pl.BlockSpec((8, HEAD), lambda i: (0, 0))] * len(squares)
        + [pl.BlockSpec(memory_space=pl.ANY)] * len(into),
        out_specs=outs,
        input_output_aliases={6 + len(squares) + i: i for i in range(len(into))},
        compiler_params=params_of(12),
        cost_estimate=cost(20 * count * width, 28 * count * width),
        name="adam_rows",
    )(scalars, *state, *squares, *in_hbm(*into))


def frag_kernel(squares, place_ref, sc_ref, w_ref, m_ref, v_ref, g_ref, *refs):
    blocks, part, _ = w_ref.shape
    factor = clip_factor(refs[:squares])
    inner_ref, *out_refs = refs[squares:]
    for j in range(blocks):
        at = pl.multiple_of((place_ref[1] ^ j) * part, 8)
        old = w_ref[j]
        update, _, _ = adam(old, m_ref[j], v_ref[j], g_ref[pl.ds(at, part), :], factor, sc_ref)
        inner_ref[j] = old - update
        out_refs[j][...] = update.astype(out_refs[j].dtype)


def adam_frag(place, scalars, squares, old, first, second, grad):
    blocks, part, width = old.shape
    smem = pl.BlockSpec(memory_space=pltpu.SMEM)
    vmem = pl.BlockSpec(memory_space=pltpu.VMEM)
    return pl.pallas_call(
        functools.partial(frag_kernel, len(squares)),
        out_shape=[jax.ShapeDtypeStruct(old.shape, jnp.float32)]
        + [jax.ShapeDtypeStruct((part, width), jnp.bfloat16)] * blocks,
        in_specs=[smem, smem] + [vmem] * (4 + len(squares)),
        out_specs=[vmem] * (1 + blocks),
        compiler_params=params_of(12),
        cost_estimate=cost(20 * old.size, 22 * old.size),
        name="adam_frag",
    )(place, scalars, old, first, second, grad, *squares)


def pick_kernel(blocks, place_ref, *refs):
    outs = refs[len(refs) // (blocks + 1) * blocks:]
    for i, out_ref in enumerate(outs):
        for j in range(blocks):
            out_ref[j] = refs[i * blocks + j][...]


def due_columns(place, part, *arrays):
    blocks = arrays[0].shape[0] // part
    specs = []
    for j in range(blocks):
        at = (lambda i, p, j=j: (p[1] ^ j, p[0])) if blocks > 1 else (lambda i, p: (0, p[0]))
        specs.append(pl.BlockSpec((part, FRAG_COLS), at))
    shape = (blocks, part, FRAG_COLS)
    return pl.pallas_call(
        functools.partial(pick_kernel, blocks),
        out_shape=[jax.ShapeDtypeStruct(shape, a.dtype) for a in arrays],
        grid_spec=pltpu.PrefetchScalarGridSpec(
            num_scalar_prefetch=1,
            grid=(1,),
            in_specs=specs * len(arrays),
            out_specs=[pl.BlockSpec(shape, lambda i, p: (0, 0, 0))] * len(arrays),
        ),
        compiler_params=params_of(12),
        cost_estimate=cost(0, 8 * blocks * part * FRAG_COLS * len(arrays)),
        name="due_columns",
    )(place, *[a for array in in_hbm(*arrays) for a in [array] * blocks])


def duplicate_kernel(*refs):
    half = (len(refs) - 3) // 2
    held, in_sems, out_sems = refs[2 * half:]
    streams = held.shape[1]
    step = held.shape[2]
    places = [(a, i, pl.ds(i * step, step)) for a in range(half) for i in range(streams)]
    fetches = [
        pltpu.make_async_copy(refs[a].at[at], held.at[a, i], in_sems.at[a, i]) for a, i, at in places
    ]
    stores = [
        pltpu.make_async_copy(held.at[a, i], refs[half + a].at[at], out_sems.at[a, i])
        for a, i, at in places
    ]
    for copy in fetches:
        copy.start()
    for fetch, store in zip(fetches, stores):
        fetch.wait()
        store.start()
    for copy in stores:
        copy.wait()


def duplicate(*arrays):
    rows, width = arrays[0].shape
    streams = 4
    whole = pl.BlockSpec(memory_space=pl.ANY)
    return pl.pallas_call(
        duplicate_kernel,
        out_shape=[pltpu.HBM(a.shape, a.dtype) for a in arrays],
        in_specs=[whole] * len(arrays),
        out_specs=[whole] * len(arrays),
        scratch_shapes=[
            pltpu.VMEM((len(arrays), streams, rows // streams, width), arrays[0].dtype),
            pltpu.SemaphoreType.DMA((len(arrays), streams)),
            pltpu.SemaphoreType.DMA((len(arrays), streams)),
        ],
        compiler_params=params_of(8),
        cost_estimate=cost(0, sum(8 * a.size for a in arrays)),
        name="duplicate",
    )(*in_hbm(*arrays))


def outer_kernel(replicas, place_ref, *refs):
    share = 1.0 / replicas
    base_refs, sum_refs = refs[3:3 + replicas], refs[3 + replicas:3 + 2 * replicas]
    inner_ref, a_ref, p_ref, m_ref, own_ref, _, *refs = refs[3 + 2 * replicas:]
    w_out, a_out, m_out, mixed, new_a, new_m, sems = refs
    part = a_ref.shape[0]
    scale = share * (1.0 + OUTER_MU) * OUTER_RATE
    columns = pl.ds(pl.multiple_of(place_ref[0] * FRAG_COLS, FRAG_COLS), FRAG_COLS)
    copies = []
    for j in range(replicas):
        fresh = base_refs[j][...] - scale * sum_refs[j][...].astype(jnp.float32)
        mixed[j] = MIX_LOCAL * inner_ref[j] + (1.0 - MIX_LOCAL) * fresh
        rows = pl.ds(pl.multiple_of((place_ref[1] ^ j) * part, 8), part)
        copies.append(pltpu.make_async_copy(mixed.at[j], w_out.at[rows, columns], sems.at[j]))
        copies[-1].start()
    pseudo = p_ref[...] + share * own_ref[...]
    new_moment = OUTER_MU * m_ref[...] + pseudo
    new_m[...] = new_moment
    new_a[...] = a_ref[...] - OUTER_RATE * (OUTER_MU * new_moment + pseudo)
    for i, (src, dst) in enumerate(((new_a, a_out), (new_m, m_out))):
        copies.append(pltpu.make_async_copy(src, dst.at[:, columns], sems.at[replicas + i]))
        copies[-1].start()
    for copy in copies:
        copy.wait()


def outer_step(place, outputs, base, sums, inner, anchor, pseudo, momentum, own_sum, ticket):
    replicas, part = inner.shape[0], inner.shape[1]
    whole = pl.BlockSpec(memory_space=pl.ANY)
    held = pl.BlockSpec(memory_space=pltpu.VMEM)
    return pl.pallas_call(
        functools.partial(outer_kernel, replicas),
        out_shape=[pltpu.HBM(a.shape, a.dtype) for a in outputs],
        in_specs=[pl.BlockSpec(memory_space=pltpu.SMEM)]
        + [whole] * 3
        + [held] * (2 * replicas + 5)
        + [whole],
        out_specs=[whole] * 3,
        scratch_shapes=[
            pltpu.VMEM((replicas, part, FRAG_COLS), jnp.float32),
            pltpu.VMEM((part, FRAG_COLS), jnp.float32),
            pltpu.VMEM((part, FRAG_COLS), jnp.float32),
            pltpu.SemaphoreType.DMA((replicas + 2,)),
        ],
        input_output_aliases={1: 0, 2: 1, 3: 2},
        compiler_params=params_of(12),
        cost_estimate=cost(10 * replicas * part * FRAG_COLS, 20 * replicas * part * FRAG_COLS),
        name="outer_step",
    )(place, *in_hbm(*outputs), *base, *sums, inner, anchor, pseudo, momentum, own_sum, ticket)


def swap(block, axis, offset):
    count = lax.axis_size(axis)
    return lax.ppermute(block, axis, [(i, i ^ offset) for i in range(count)])


def after(value, *others):
    return lax.optimization_barrier((value,) + others)[0]


def body(
    tokens,
    cotangent,
    weights,
    first_moment,
    second_moment,
    anchor,
    momentum,
    due_fragment,
    step_count,
):
    inputs, incoming, params = tokens[0], cotangent[0], weights[0]
    kv_width = incoming.shape[1] // 2
    rows = params.shape[0]
    part = anchor.shape[0]
    replicas = lax.axis_size("rep")
    shards = lax.axis_size("fsdp")
    me = jnp.reshape(lax.axis_index("fsdp"), (1,)).astype(jnp.int32)
    my_rep = lax.axis_index("rep").astype(jnp.int32)
    place = jnp.stack([due_fragment[0], my_rep])
    chips = range(2, shards, 2)
    far = sorted(chips, key=lambda k: (-bin(k).count("1"), k))
    order = [k for k in far[:-2] for k in (k, k + 1)]
    order += far[-2:] + [k + 1 for k in far[-2:]]

    (old,) = due_columns(place, part, params)
    old_sums = [old[0]] + [swap(old[k], "rep", k) for k in range(1, replicas)]

    packed = {}
    for offsets in (order[:1], order[1:4], order[4:], (0, 1)):
        packed |= pack(inputs, me, rows, tuple(offsets))
    blocks = {k: swap(packed[k], "fsdp", k) for k in order}
    blocks[0], blocks[1] = packed[0], swap(packed[1], "fsdp", 1)

    steps_now = step_count[0].astype(jnp.float32)
    plan = jnp.minimum(1.0, steps_now / WARMUP) * (
        0.55 + 0.45 * jnp.cos(jnp.pi * steps_now / STEPS_TOTAL)
    )
    rate = PEAK_RATE * plan
    inv_one = 1.0 / (1.0 - jnp.power(BETA_ONE, steps_now))
    inv_two = 1.0 / (1.0 - jnp.power(BETA_TWO, steps_now))
    scalars = jnp.stack([rate, inv_one, inv_two])
    old_first, old_second = due_columns(place, part, first_moment[0], second_moment[0])
    anchor_cols, moment_cols = (c[0] for c in due_columns(place, part, anchor, momentum))
    pseudo_old = anchor_cols - sum(old_sums[1:], old_sums[0]) / replicas
    base = anchor_cols - OUTER_RATE * (OUTER_MU * (OUTER_MU * moment_cols + pseudo_old) + pseudo_old)
    base = [base] + [swap(base, "rep", k) for k in range(1, replicas)]
    anchor_copy, momentum_copy = duplicate(anchor, momentum)
    key_weights = cast_left(params, kv_width)

    last = far[-1]
    blocks[last + 1] = after(blocks[last + 1], anchor_copy, momentum_copy, scalars, old_first, old_second)
    relay = len(far) == 3 and far[0] == far[1] ^ far[2]
    half = inputs.shape[0] // 2
    parts, flipped, relayed = [], {}, {}
    for k in far + [0]:
        theirs, flipped[k + 1] = partial_keys(blocks[k + 1], key_weights)
        theirs = swap(theirs, "fsdp", 1)
        if k == last:
            theirs = after(theirs, *base)
        adds = [(theirs, 0)] + relayed.get(k, [])
        if relay and k == far[0]:
            (upper, lower), flipped[k] = partial_keys(blocks[k], key_weights, adds, 2)
            relayed[far[2]] = [(swap(upper, "fsdp", far[1]), 0)]
            relayed[far[1]] = [(swap(lower, "fsdp", far[2]), half)]
            continue
        part_k, flipped[k] = partial_keys(blocks[k], key_weights, adds)
        if k == last:
            values = {0: after(incoming[:, kv_width:], part_k)}
            for j in far[1:] if relay else far:
                values[j] = swap(values[0], "fsdp", j)
            if relay:
                upper = swap(values[far[1]][:half], "fsdp", far[2])
                lower = swap(values[far[2]][half:], "fsdp", far[1])
                values[far[0]] = jnp.concatenate([upper, lower], axis=0)
            for j in range(0, shards, 2):
                values[j + 1] = swap(values[j], "fsdp", 1)
        parts.append(swap(part_k, "fsdp", k) if k else part_k)
    spread = [0, 1] + [k + odd for k in far for odd in range(2)]
    near, rest = spread[:shards // 2], spread[shards // 2:]
    pick = lambda table, which: [table[k] for k in which]
    (values_first,) = gradient(place, pick(flipped, near), pick(values, near), last=False)
    keys = {0: key_backward(parts, incoming, 0)}
    for k in far:
        keys[k] = swap(keys[0], "fsdp", k)
    keys[1] = swap(keys[0], "fsdp", 1)

    grad_values, square, due = gradient(
        place, pick(flipped, rest), pick(values, rest), values_first
    )
    for k in near[2::2]:
        keys[k + 1] = swap(after(keys[k], square), "fsdp", 1)
    (keys_first,) = gradient(place, pick(flipped, near), pick(keys, near), last=False)
    for k in rest[::2]:
        keys[k + 1] = swap(after(keys[k], square), "fsdp", 1)
    grad_keys, square, due = gradient(
        place, pick(flipped, rest), pick(keys, rest), keys_first, square, due
    )

    square = square + swap(square, "fsdp", 1)
    squares = [square] + [swap(square, "fsdp", k) for k in chips]

    state = (params, first_moment[0], second_moment[0], grad_keys, grad_values)
    inner, *update = adam_frag(place, scalars, squares, old, old_first, old_second, due)
    steps = rows // ADAM_ROWS
    *results, ticket = adam_rows(scalars, squares, state, 0, steps // 2)
    own_sum = update[0].astype(jnp.float32)
    for k in range(1, replicas):
        own_sum = own_sum + swap(update[k], "rep", k).astype(jnp.float32)
    own_sum, ticket = lax.optimization_barrier((own_sum, ticket))
    sums = [own_sum.astype(jnp.bfloat16)]
    sums += [swap(sums[0], "rep", k) for k in range(1, replicas)]
    results = adam_rows(scalars, squares, state, steps // 2, steps, results)
    weights_out, anchor_out, momentum_out = outer_step(
        place,
        (results[0], anchor_copy, momentum_copy),
        base,
        sums,
        inner,
        anchor_cols,
        pseudo_old,
        moment_cols,
        own_sum,
        ticket,
    )
    plan_out = jnp.reshape(plan, (1,))
    return (
        weights_out[None],
        results[1][None],
        results[2][None],
        anchor_out,
        momentum_out,
        plan_out,
    )


def solution(mesh):
    tokens_spec = P("rep", "fsdp", None)
    outer_spec = P(("fsdp", "rep"), None)
    return jax.shard_map(
        body,
        mesh=mesh,
        in_specs=(tokens_spec,) * 5 + (outer_spec,) * 2 + (P(), P()),
        out_specs=(tokens_spec,) * 3 + (outer_spec,) * 2 + (P(),),
        check_vma=False,
    )
```

```python
import functools

import jax
import jax.numpy as jnp
from jax import lax
from jax.experimental import pallas as pl
from jax.experimental.pallas import tpu as pltpu
from jax.sharding import PartitionSpec as P

HEAD = 128
WARMUP = 2000
STEPS_TOTAL = 100000
FRAG_COLS = 128


BETA_ONE = 0.9
BETA_TWO = 0.95
ADAM_EPS = 1e-08
DECAY = 0.1
PEAK_RATE = 0.0003
CLIP_NORM = 1.0
OUTER_MU = 0.9
OUTER_RATE = 0.7
MIX_LOCAL = 0.5

MIB = 1 << 20
ADAM_ROWS = 128


def in_hbm(*arrays):
    return [pltpu.with_memory_space_constraint(a, pltpu.HBM) for a in arrays]


def params_of(limit):
    return pltpu.CompilerParams(vmem_limit_bytes=limit * MIB)


def cost(flops, moved):
    return pl.CostEstimate(flops=int(flops), bytes_accessed=int(moved), transcendentals=0)


def pack_kernel(offsets, me_ref, src_ref, *refs):
    half = len(offsets)
    out_refs, (held, in_sems, out_sems) = refs[:half], refs[half:]
    streams = in_sems.shape[1]
    count, rows = out_refs[0].shape
    step = count // streams
    fetches, stores = [], []
    for i, offset in enumerate(offsets):
        column = pl.multiple_of((me_ref[0] ^ offset) * rows, HEAD)
        for j in range(streams):
            at = pl.ds(j * step, step)
            block = src_ref.at[at, pl.ds(column, rows)]
            fetches.append(pltpu.make_async_copy(block, held.at[i, at], in_sems.at[i, j]))
            stores.append(pltpu.make_async_copy(held.at[i, at], out_refs[i].at[at], out_sems.at[i, j]))
    for copy in fetches:
        copy.start()
    for fetch, store in zip(fetches, stores):
        fetch.wait()
        store.start()
    for copy in stores:
        copy.wait()


def pack(tokens, me, rows, offsets):
    count = tokens.shape[0]
    streams = 4
    whole = pl.BlockSpec(memory_space=pl.ANY)
    outs = pl.pallas_call(
        functools.partial(pack_kernel, offsets),
        out_shape=[pltpu.HBM((count, rows), tokens.dtype)] * len(offsets),
        in_specs=[pl.BlockSpec(memory_space=pltpu.SMEM), whole],
        out_specs=[whole] * len(offsets),
        scratch_shapes=[
            pltpu.VMEM((len(offsets), count, rows), tokens.dtype),
            pltpu.SemaphoreType.DMA((len(offsets), streams)),
            pltpu.SemaphoreType.DMA((len(offsets), streams)),
        ],
        compiler_params=params_of(12),
        cost_estimate=cost(0, 4 * len(offsets) * count * rows),
        name="pack",
    )(me, *in_hbm(tokens))
    return dict(zip(offsets, outs))


def cast_kernel(src_ref, out_ref):
    out_ref[...] = src_ref[...].astype(out_ref.dtype)


def cast_left(array, width):
    rows = array.shape[0]
    block = pl.BlockSpec((256, width), lambda i: (i, 0))
    return pl.pallas_call(
        cast_kernel,
        out_shape=jax.ShapeDtypeStruct((rows, width), jnp.bfloat16),
        grid=(rows // 256,),
        in_specs=[block],
        out_specs=block,
        compiler_params=params_of(8),
        cost_estimate=cost(0, 6 * rows * width),
        name="cast_left",
    )(*in_hbm(array))


def partial_kernel(pieces, firsts, splits, *refs):
    x_refs, w_ref, refs = refs[:pieces], refs[pieces], refs[pieces + 1:]
    add_refs, out_refs, flip_ref = refs[:len(firsts)], refs[len(firsts):-1], refs[-1]
    x = jnp.concatenate([ref[...] for ref in x_refs], axis=1)
    total = jnp.dot(x, w_ref[...], preferred_element_type=jnp.float32)
    count = total.shape[0]
    for ref, first in zip(add_refs, firsts):
        last = first + ref.shape[0]
        rows = [total[:first], total[first:last] + ref[...].astype(jnp.float32), total[last:]]
        total = jnp.concatenate([r for r in rows if r.shape[0]], axis=0)
    height = count // splits
    for i, ref in enumerate(out_refs):
        ref[...] = total[i * height:(i + 1) * height].astype(ref.dtype)
    step = x_refs[0].shape[1]
    for i, ref in enumerate(x_refs):
        flip_ref[i * step:(i + 1) * step, :] = ref[...].T


def partial_keys(block, key_weights, adds=(), splits=1):
    count, rows = block.shape
    width = key_weights.shape[1]
    pieces = 4 if rows % (4 * HEAD) == 0 else 2
    fixed = lambda a: pl.BlockSpec(a.shape, lambda i: (0, 0))
    *parts, flipped = pl.pallas_call(
        functools.partial(partial_kernel, pieces, [first for _, first in adds], splits),
        out_shape=[jax.ShapeDtypeStruct((count // splits, width), jnp.bfloat16)] * splits
        + [jax.ShapeDtypeStruct((rows, count), jnp.bfloat16)],
        grid=(1,),
        in_specs=[pl.BlockSpec((count, rows // pieces), lambda i, c=c: (0, c)) for c in range(pieces)]
        + [fixed(key_weights)]
        + [fixed(a) for a, _ in adds],
        out_specs=[pl.BlockSpec((count // splits, width), lambda i: (0, 0))] * splits
        + [pl.BlockSpec((rows, count), lambda i: (0, 0))],
        compiler_params=params_of(12),
        cost_estimate=cost(2 * count * rows * width, 4 * count * rows),
        name="partial_keys",
    )(*[block] * pieces, key_weights, *[a for a, _ in adds])
    return parts if splits > 1 else parts[0], flipped


def key_kernel(first, *refs):
    *part_refs, cot_ref, out_ref = refs
    count = out_ref.shape[0]
    raw = sum(ref[...].astype(jnp.float32) for ref in part_refs)
    for h in range(raw.shape[1] // HEAD):
        cols = slice(h * HEAD, (h + 1) * HEAD)
        head = raw[:, cols]
        inverse = lax.rsqrt(jnp.mean(head * head, axis=1, keepdims=True) + 1e-06)
        normed = head * inverse
        upper = cot_ref[first:first + count, cols].astype(jnp.float32)
        back = inverse * (upper - normed * jnp.mean(upper * normed, axis=1, keepdims=True))
        out_ref[:, cols] = back.astype(out_ref.dtype)


def key_backward(parts, incoming, first):
    count, width = parts[0].shape
    block = pl.BlockSpec((count, width), lambda i: (0, 0))
    cot = pl.BlockSpec((incoming.shape[0], width), lambda i: (0, 0))
    return pl.pallas_call(
        functools.partial(key_kernel, first),
        out_shape=jax.ShapeDtypeStruct((count, width), jnp.bfloat16),
        grid=(1,),
        in_specs=[block] * len(parts) + [cot],
        out_specs=block,
        compiler_params=params_of(8),
        cost_estimate=cost(60 * count * width, 12 * count * width),
        name="key_backward",
    )(*parts, incoming)


def grad_kernel(count, has_base, has_more, last, place_ref, *refs):
    refs = list(refs)
    x_refs, u_refs = refs[:count], refs[count:2 * count]
    refs = refs[2 * count:]
    base = refs.pop(0) if has_base else None
    square_in, due_in = (refs.pop(0), refs.pop(0)) if has_more else (None, None)
    out_ref = refs.pop(0)
    x = jnp.concatenate([ref[...] for ref in x_refs], axis=1)
    u = jnp.concatenate([ref[...] for ref in u_refs], axis=0)
    total = jnp.dot(x, u, preferred_element_type=jnp.float32)
    if has_base:
        total = total + base[...]
    out_ref[...] = total
    if last:
        sq_ref, due_ref = refs

        @pl.when(pl.program_id(0) == 0)
        def _():
            sq_ref[...] = square_in[...] if has_more else jnp.zeros_like(sq_ref)

        rows, width = total.shape
        squares = (total * total).reshape(rows // 8, 8, width).sum(axis=0)
        folded = squares[:, :HEAD]
        for h in range(1, width // HEAD):
            folded = folded + squares[:, h * HEAD:(h + 1) * HEAD]
        sq_ref[...] += folded
        heads = width // FRAG_COLS
        mine = place_ref[0] - (0 if has_more else heads)
        mine = jnp.minimum(jnp.maximum(mine, 0), heads - 1) * FRAG_COLS
        column = out_ref[:, pl.ds(pl.multiple_of(mine, FRAG_COLS), FRAG_COLS)]
        if has_more:
            column = jnp.where(place_ref[0] < heads, column, due_in[...])
        due_ref[...] = column


def gradient(place, flipped, upstream, base=None, square=None, due=None, last=True):
    rows, depth = flipped[0].shape
    width = upstream[0].shape[1]
    step = 256
    row_block = lambda cols: pl.BlockSpec((step, cols), lambda i, p: (i, 0))
    fixed = pl.BlockSpec((8, HEAD), lambda i, p: (0, 0))
    args = [*flipped, *upstream]
    specs = [row_block(depth)] * len(flipped)
    specs += [pl.BlockSpec((depth, width), lambda i, p: (0, 0))] * len(upstream)
    if base is not None:
        args.append(base)
        specs.append(row_block(width))
    if square is not None:
        args += [square, due]
        specs += [fixed, row_block(FRAG_COLS)]
    if last:
        shapes = [
            jax.ShapeDtypeStruct((rows, width), jnp.float32),
            jax.ShapeDtypeStruct((8, HEAD), jnp.float32),
            jax.ShapeDtypeStruct((rows, FRAG_COLS), jnp.float32),
        ]
        outs = [row_block(width), fixed, row_block(FRAG_COLS)]
    else:
        shapes = [jax.ShapeDtypeStruct((rows, width), jnp.float32)]
        outs = [row_block(width)]
    depth *= len(flipped)
    return pl.pallas_call(
        functools.partial(grad_kernel, len(flipped), base is not None, square is not None, last),
        out_shape=shapes,
        grid_spec=pltpu.PrefetchScalarGridSpec(
            num_scalar_prefetch=1, grid=(rows // step,), in_specs=specs, out_specs=outs
        ),
        compiler_params=params_of(12),
        cost_estimate=cost(2 * rows * width * depth, 2 * rows * depth + 4 * rows * width),
        name="gradient",
    )(place, *args)


def clip_factor(square_refs):
    square = jnp.sum(sum(ref[...] for ref in square_refs), keepdims=True)
    return jnp.minimum(1.0, CLIP_NORM / (jnp.sqrt(square) + 1e-06))


def adam(old, first, second, grad, factor, scalars):
    rate, inv_one, inv_two = (scalars[i] for i in range(3))
    clipped = grad * factor
    first_new = BETA_ONE * first + (1.0 - BETA_ONE) * clipped
    second_new = BETA_TWO * second + (1.0 - BETA_TWO) * clipped * clipped
    update = rate * (
        first_new * inv_one / (jnp.sqrt(second_new * inv_two) + ADAM_EPS) + DECAY * old
    )
    return update, first_new, second_new


def adam_kernel(squares, extra, sc_ref, w_ref, m_ref, v_ref, gk_ref, gv_ref, *refs):
    factor = clip_factor(refs[:squares])
    w_out, m_out, v_out, *done = refs[squares + extra:]
    width = gk_ref.shape[1]
    for g_ref, cols in ((gk_ref, slice(0, width)), (gv_ref, slice(width, 2 * width))):
        old = w_ref[:, cols]
        update, first_new, second_new = adam(
            old, m_ref[:, cols], v_ref[:, cols], g_ref[...], factor, sc_ref
        )
        w_out[:, cols] = old - update
        m_out[:, cols] = first_new
        v_out[:, cols] = second_new
    for ref in done:
        ref[...] = jnp.zeros_like(ref)


def adam_rows(scalars, squares, state, first, last, into=()):
    rows, width = state[0].shape
    step = ADAM_ROWS
    full = pl.BlockSpec((step, width), lambda i: (i + first, 0))
    half = pl.BlockSpec((step, width // 2), lambda i: (i + first, 0))
    shapes = [pltpu.HBM((rows, width), jnp.float32)] * 3
    outs = [full] * 3
    if not into:
        shapes.append(jax.ShapeDtypeStruct((8, HEAD), jnp.float32))
        outs.append(pl.BlockSpec((8, HEAD), lambda i: (0, 0)))
    count = (last - first) * step
    return pl.pallas_call(
        functools.partial(adam_kernel, len(squares), len(into)),
        out_shape=shapes,
        grid=(last - first,),
        in_specs=[pl.BlockSpec(memory_space=pltpu.SMEM), full, full, full, half, half]
        + [pl.BlockSpec((8, HEAD), lambda i: (0, 0))] * len(squares)
        + [pl.BlockSpec(memory_space=pl.ANY)] * len(into),
        out_specs=outs,
        input_output_aliases={6 + len(squares) + i: i for i in range(len(into))},
        compiler_params=params_of(12),
        cost_estimate=cost(20 * count * width, 28 * count * width),
        name="adam_rows",
    )(scalars, *state, *squares, *in_hbm(*into))


def frag_kernel(squares, place_ref, sc_ref, w_ref, m_ref, v_ref, g_ref, *refs):
    blocks, part, _ = w_ref.shape
    factor = clip_factor(refs[:squares])
    inner_ref, *out_refs = refs[squares:]
    for j in range(blocks):
        at = pl.multiple_of((place_ref[1] ^ j) * part, 8)
        old = w_ref[j]
        update, _, _ = adam(old, m_ref[j], v_ref[j], g_ref[pl.ds(at, part), :], factor, sc_ref)
        inner_ref[j] = old - update
        out_refs[j][...] = update.astype(out_refs[j].dtype)


def adam_frag(place, scalars, squares, old, first, second, grad):
    blocks, part, width = old.shape
    smem = pl.BlockSpec(memory_space=pltpu.SMEM)
    vmem = pl.BlockSpec(memory_space=pltpu.VMEM)
    return pl.pallas_call(
        functools.partial(frag_kernel, len(squares)),
        out_shape=[jax.ShapeDtypeStruct(old.shape, jnp.float32)]
        + [jax.ShapeDtypeStruct((part, width), jnp.bfloat16)] * blocks,
        in_specs=[smem, smem] + [vmem] * (4 + len(squares)),
        out_specs=[vmem] * (1 + blocks),
        compiler_params=params_of(12),
        cost_estimate=cost(20 * old.size, 22 * old.size),
        name="adam_frag",
    )(place, scalars, old, first, second, grad, *squares)


def pick_kernel(blocks, place_ref, *refs):
    outs = refs[len(refs) // (blocks + 1) * blocks:]
    for i, out_ref in enumerate(outs):
        for j in range(blocks):
            out_ref[j] = refs[i * blocks + j][...]


def due_columns(place, part, *arrays):
    blocks = arrays[0].shape[0] // part
    specs = []
    for j in range(blocks):
        at = (lambda i, p, j=j: (p[1] ^ j, p[0])) if blocks > 1 else (lambda i, p: (0, p[0]))
        specs.append(pl.BlockSpec((part, FRAG_COLS), at))
    shape = (blocks, part, FRAG_COLS)
    return pl.pallas_call(
        functools.partial(pick_kernel, blocks),
        out_shape=[jax.ShapeDtypeStruct(shape, a.dtype) for a in arrays],
        grid_spec=pltpu.PrefetchScalarGridSpec(
            num_scalar_prefetch=1,
            grid=(1,),
            in_specs=specs * len(arrays),
            out_specs=[pl.BlockSpec(shape, lambda i, p: (0, 0, 0))] * len(arrays),
        ),
        compiler_params=params_of(12),
        cost_estimate=cost(0, 8 * blocks * part * FRAG_COLS * len(arrays)),
        name="due_columns",
    )(place, *[a for array in in_hbm(*arrays) for a in [array] * blocks])


def duplicate_kernel(*refs):
    half = (len(refs) - 3) // 2
    held, in_sems, out_sems = refs[2 * half:]
    streams = held.shape[1]
    step = held.shape[2]
    places = [(a, i, pl.ds(i * step, step)) for a in range(half) for i in range(streams)]
    fetches = [
        pltpu.make_async_copy(refs[a].at[at], held.at[a, i], in_sems.at[a, i]) for a, i, at in places
    ]
    stores = [
        pltpu.make_async_copy(held.at[a, i], refs[half + a].at[at], out_sems.at[a, i])
        for a, i, at in places
    ]
    for copy in fetches:
        copy.start()
    for fetch, store in zip(fetches, stores):
        fetch.wait()
        store.start()
    for copy in stores:
        copy.wait()


def duplicate(*arrays):
    rows, width = arrays[0].shape
    streams = 4
    whole = pl.BlockSpec(memory_space=pl.ANY)
    return pl.pallas_call(
        duplicate_kernel,
        out_shape=[pltpu.HBM(a.shape, a.dtype) for a in arrays],
        in_specs=[whole] * len(arrays),
        out_specs=[whole] * len(arrays),
        scratch_shapes=[
            pltpu.VMEM((len(arrays), streams, rows // streams, width), arrays[0].dtype),
            pltpu.SemaphoreType.DMA((len(arrays), streams)),
            pltpu.SemaphoreType.DMA((len(arrays), streams)),
        ],
        compiler_params=params_of(8),
        cost_estimate=cost(0, sum(8 * a.size for a in arrays)),
        name="duplicate",
    )(*in_hbm(*arrays))


def outer_kernel(replicas, place_ref, *refs):
    share = 1.0 / replicas
    base_refs, sum_refs = refs[3:3 + replicas], refs[3 + replicas:3 + 2 * replicas]
    inner_ref, a_ref, p_ref, m_ref, own_ref, _, *refs = refs[3 + 2 * replicas:]
    w_out, a_out, m_out, mixed, new_a, new_m, sems = refs
    part = a_ref.shape[0]
    scale = share * (1.0 + OUTER_MU) * OUTER_RATE
    columns = pl.ds(pl.multiple_of(place_ref[0] * FRAG_COLS, FRAG_COLS), FRAG_COLS)
    copies = []
    for j in range(replicas):
        fresh = base_refs[j][...] - scale * sum_refs[j][...].astype(jnp.float32)
        mixed[j] = MIX_LOCAL * inner_ref[j] + (1.0 - MIX_LOCAL) * fresh
        rows = pl.ds(pl.multiple_of((place_ref[1] ^ j) * part, 8), part)
        copies.append(pltpu.make_async_copy(mixed.at[j], w_out.at[rows, columns], sems.at[j]))
        copies[-1].start()
    pseudo = p_ref[...] + share * own_ref[...]
    new_moment = OUTER_MU * m_ref[...] + pseudo
    new_m[...] = new_moment
    new_a[...] = a_ref[...] - OUTER_RATE * (OUTER_MU * new_moment + pseudo)
    for i, (src, dst) in enumerate(((new_a, a_out), (new_m, m_out))):
        copies.append(pltpu.make_async_copy(src, dst.at[:, columns], sems.at[replicas + i]))
        copies[-1].start()
    for copy in copies:
        copy.wait()


def outer_step(place, outputs, base, sums, inner, anchor, pseudo, momentum, own_sum, ticket):
    replicas, part = inner.shape[0], inner.shape[1]
    whole = pl.BlockSpec(memory_space=pl.ANY)
    held = pl.BlockSpec(memory_space=pltpu.VMEM)
    return pl.pallas_call(
        functools.partial(outer_kernel, replicas),
        out_shape=[pltpu.HBM(a.shape, a.dtype) for a in outputs],
        in_specs=[pl.BlockSpec(memory_space=pltpu.SMEM)]
        + [whole] * 3
        + [held] * (2 * replicas + 5)
        + [whole],
        out_specs=[whole] * 3,
        scratch_shapes=[
            pltpu.VMEM((replicas, part, FRAG_COLS), jnp.float32),
            pltpu.VMEM((part, FRAG_COLS), jnp.float32),
            pltpu.VMEM((part, FRAG_COLS), jnp.float32),
            pltpu.SemaphoreType.DMA((replicas + 2,)),
        ],
        input_output_aliases={1: 0, 2: 1, 3: 2},
        compiler_params=params_of(12),
        cost_estimate=cost(10 * replicas * part * FRAG_COLS, 20 * replicas * part * FRAG_COLS),
        name="outer_step",
    )(place, *in_hbm(*outputs), *base, *sums, inner, anchor, pseudo, momentum, own_sum, ticket)


def swap(block, axis, offset):
    count = lax.axis_size(axis)
    return lax.ppermute(block, axis, [(i, i ^ offset) for i in range(count)])


def after(value, *others):
    return lax.optimization_barrier((value,) + others)[0]


def body(
    tokens,
    cotangent,
    weights,
    first_moment,
    second_moment,
    anchor,
    momentum,
    due_fragment,
    step_count,
):
    inputs, incoming, params = tokens[0], cotangent[0], weights[0]
    kv_width = incoming.shape[1] // 2
    rows = params.shape[0]
    part = anchor.shape[0]
    replicas = lax.axis_size("rep")
    shards = lax.axis_size("fsdp")
    me = jnp.reshape(lax.axis_index("fsdp"), (1,)).astype(jnp.int32)
    my_rep = lax.axis_index("rep").astype(jnp.int32)
    place = jnp.stack([due_fragment[0], my_rep])
    chips = range(2, shards, 2)
    far = sorted(chips, key=lambda k: (-bin(k).count("1"), k))
    order = [k for k in far[:-2] for k in (k, k + 1)]
    order += far[-2:] + [k + 1 for k in far[-2:]]

    packed = {}
    for offsets in (order[:1], order[1:4], order[4:], (0, 1)):
        packed |= pack(inputs, me, rows, tuple(offsets))
    blocks = {}
    for i, k in enumerate(order[:-4]):
        blocks[k] = swap(after(packed[k], *[blocks[j] for j in order[max(i - 2, 0):max(i - 1, 0)]]), "fsdp", k)
    blocks[0], blocks[1] = packed[0], swap(packed[1], "fsdp", 1)

    (old,) = due_columns(place, part, params)
    old_sums = [old[0]] + [swap(old[k], "rep", k) for k in range(1, replicas)]
    anchor_cols, moment_cols = (c[0] for c in due_columns(place, part, anchor, momentum))
    pseudo_old = anchor_cols - sum(old_sums[1:], old_sums[0]) / replicas
    base = anchor_cols - OUTER_RATE * (OUTER_MU * (OUTER_MU * moment_cols + pseudo_old) + pseudo_old)
    base = [base] + [swap(base, "rep", k) for k in range(1, replicas)]

    for ready, i in (((pseudo_old,), len(order) - 4), (tuple(base), len(order) - 2)):
        for k, before in zip(order[i:i + 2], order[i - 2:i]):
            blocks[k] = swap(after(packed[k], blocks[before], *ready), "fsdp", k)

    relay = len(far) == 3 and far[0] == far[1] ^ far[2]
    half = inputs.shape[0] // 2
    values = {0: incoming[:, kv_width:]}
    for i, k in enumerate(far[1:] if relay else far):
        values[k] = swap(after(values[0], blocks[order[i]]), "fsdp", k)
    if relay:
        upper = swap(values[far[1]][:half], "fsdp", far[2])
        lower = swap(values[far[2]][half:], "fsdp", far[1])
        values[far[0]] = jnp.concatenate([upper, lower], axis=0)

    steps_now = step_count[0].astype(jnp.float32)
    plan = jnp.minimum(1.0, steps_now / WARMUP) * (
        0.55 + 0.45 * jnp.cos(jnp.pi * steps_now / STEPS_TOTAL)
    )
    rate = PEAK_RATE * plan
    inv_one = 1.0 / (1.0 - jnp.power(BETA_ONE, steps_now))
    inv_two = 1.0 / (1.0 - jnp.power(BETA_TWO, steps_now))
    scalars = jnp.stack([rate, inv_one, inv_two])
    old_first, old_second = due_columns(place, part, first_moment[0], second_moment[0])
    anchor_copy, momentum_copy = duplicate(anchor, momentum)
    key_weights = cast_left(params, kv_width)

    last = far[-1]
    blocks[last + 1] = after(blocks[last + 1], anchor_copy, momentum_copy, scalars, old_first, old_second)
    parts, flipped, relayed = [], {}, {}
    for k in far + [0]:
        theirs, flipped[k + 1] = partial_keys(blocks[k + 1], key_weights)
        theirs = swap(theirs, "fsdp", 1)
        adds = [(theirs, 0)] + relayed.get(k, [])
        if relay and k == far[0]:
            (upper, lower), flipped[k] = partial_keys(blocks[k], key_weights, adds, 2)
            relayed[far[2]] = [(swap(upper, "fsdp", far[1]), 0)]
            relayed[far[1]] = [(swap(lower, "fsdp", far[2]), half)]
            continue
        part_k, flipped[k] = partial_keys(blocks[k], key_weights, adds)
        if k == last:
            for j in range(0, shards, 2):
                values[j + 1] = swap(after(values[j], part_k), "fsdp", 1)
        parts.append(swap(part_k, "fsdp", k) if k else part_k)
    spread = [0, 1] + [k + odd for k in far for odd in range(2)]
    near, rest = spread[:shards // 2], spread[shards // 2:]
    pick = lambda table, which: [table[k] for k in which]
    (values_first,) = gradient(place, pick(flipped, near), pick(values, near), last=False)
    keys = {0: key_backward(parts, incoming, 0)}
    for k in far:
        keys[k] = swap(keys[0], "fsdp", k)
    keys[1] = swap(keys[0], "fsdp", 1)

    grad_values, square, due = gradient(
        place, pick(flipped, rest), pick(values, rest), values_first
    )
    for k in near[2::2]:
        keys[k + 1] = swap(after(keys[k], square), "fsdp", 1)
    (keys_first,) = gradient(place, pick(flipped, near), pick(keys, near), last=False)
    for k in rest[::2]:
        keys[k + 1] = swap(after(keys[k], square), "fsdp", 1)
    grad_keys, square, due = gradient(
        place, pick(flipped, rest), pick(keys, rest), keys_first, square, due
    )

    square = square + swap(square, "fsdp", 1)
    squares = [square] + [swap(square, "fsdp", k) for k in chips]

    state = (params, first_moment[0], second_moment[0], grad_keys, grad_values)
    inner, *update = adam_frag(place, scalars, squares, old, old_first, old_second, due)
    steps = rows // ADAM_ROWS
    *results, ticket = adam_rows(scalars, squares, state, 0, steps // 2)
    own_sum = update[0].astype(jnp.float32)
    for k in range(1, replicas):
        own_sum = own_sum + swap(update[k], "rep", k).astype(jnp.float32)
    own_sum, ticket = lax.optimization_barrier((own_sum, ticket))
    sums = [own_sum.astype(jnp.bfloat16)]
    sums += [swap(sums[0], "rep", k) for k in range(1, replicas)]
    results = adam_rows(scalars, squares, state, steps // 2, steps, results)
    weights_out, anchor_out, momentum_out = outer_step(
        place,
        (results[0], anchor_copy, momentum_copy),
        base,
        sums,
        inner,
        anchor_cols,
        pseudo_old,
        moment_cols,
        own_sum,
        ticket,
    )
    plan_out = jnp.reshape(plan, (1,))
    return (
        weights_out[None],
        results[1][None],
        results[2][None],
        anchor_out,
        momentum_out,
        plan_out,
    )


def solution(mesh):
    tokens_spec = P("rep", "fsdp", None)
    outer_spec = P(("fsdp", "rep"), None)
    return jax.shard_map(
        body,
        mesh=mesh,
        in_specs=(tokens_spec,) * 5 + (outer_spec,) * 2 + (P(), P()),
        out_specs=(tokens_spec,) * 3 + (outer_spec,) * 2 + (P(),),
        check_vma=False,
    )
```

```python
import functools

import jax
import jax.numpy as jnp
from jax import lax
from jax.experimental import pallas as pl
from jax.experimental.pallas import tpu as pltpu
from jax.sharding import PartitionSpec as P

HEAD = 128
WARMUP = 2000
STEPS_TOTAL = 100000
FRAG_COLS = 128


BETA_ONE = 0.9
BETA_TWO = 0.95
ADAM_EPS = 1e-08
DECAY = 0.1
PEAK_RATE = 0.0003
CLIP_NORM = 1.0
OUTER_MU = 0.9
OUTER_RATE = 0.7
MIX_LOCAL = 0.5

MIB = 1 << 20
ADAM_ROWS = 128


def in_hbm(*arrays):
    return [pltpu.with_memory_space_constraint(a, pltpu.HBM) for a in arrays]


def params_of(limit):
    return pltpu.CompilerParams(vmem_limit_bytes=limit * MIB)


def cost(flops, moved):
    return pl.CostEstimate(flops=int(flops), bytes_accessed=int(moved), transcendentals=0)


def pack_kernel(offsets, me_ref, src_ref, *refs):
    half = len(offsets)
    out_refs, (held, in_sems, out_sems) = refs[:half], refs[half:]
    streams = in_sems.shape[1]
    count, rows = out_refs[0].shape
    step = count // streams
    fetches, stores = [], []
    for i, offset in enumerate(offsets):
        column = pl.multiple_of((me_ref[0] ^ offset) * rows, HEAD)
        for j in range(streams):
            at = pl.ds(j * step, step)
            block = src_ref.at[at, pl.ds(column, rows)]
            fetches.append(pltpu.make_async_copy(block, held.at[i, at], in_sems.at[i, j]))
            stores.append(pltpu.make_async_copy(held.at[i, at], out_refs[i].at[at], out_sems.at[i, j]))
    for copy in fetches:
        copy.start()
    for fetch, store in zip(fetches, stores):
        fetch.wait()
        store.start()
    for copy in stores:
        copy.wait()


def pack(tokens, me, rows, offsets):
    count = tokens.shape[0]
    streams = 4
    whole = pl.BlockSpec(memory_space=pl.ANY)
    outs = pl.pallas_call(
        functools.partial(pack_kernel, offsets),
        out_shape=[pltpu.HBM((count, rows), tokens.dtype)] * len(offsets),
        in_specs=[pl.BlockSpec(memory_space=pltpu.SMEM), whole],
        out_specs=[whole] * len(offsets),
        scratch_shapes=[
            pltpu.VMEM((len(offsets), count, rows), tokens.dtype),
            pltpu.SemaphoreType.DMA((len(offsets), streams)),
            pltpu.SemaphoreType.DMA((len(offsets), streams)),
        ],
        compiler_params=params_of(12),
        cost_estimate=cost(0, 4 * len(offsets) * count * rows),
        name="pack",
    )(me, *in_hbm(tokens))
    return dict(zip(offsets, outs))


def cast_kernel(src_ref, out_ref):
    out_ref[...] = src_ref[...].astype(out_ref.dtype)


def cast_left(array, width):
    rows = array.shape[0]
    block = pl.BlockSpec((256, width), lambda i: (i, 0))
    return pl.pallas_call(
        cast_kernel,
        out_shape=jax.ShapeDtypeStruct((rows, width), jnp.bfloat16),
        grid=(rows // 256,),
        in_specs=[block],
        out_specs=block,
        compiler_params=params_of(8),
        cost_estimate=cost(0, 6 * rows * width),
        name="cast_left",
    )(*in_hbm(array))


def partial_kernel(pieces, firsts, splits, *refs):
    x_refs, w_ref, refs = refs[:pieces], refs[pieces], refs[pieces + 1:]
    add_refs, out_refs, flip_ref = refs[:len(firsts)], refs[len(firsts):-1], refs[-1]
    x = jnp.concatenate([ref[...] for ref in x_refs], axis=1)
    total = jnp.dot(x, w_ref[...], preferred_element_type=jnp.float32)
    count = total.shape[0]
    for ref, first in zip(add_refs, firsts):
        last = first + ref.shape[0]
        rows = [total[:first], total[first:last] + ref[...].astype(jnp.float32), total[last:]]
        total = jnp.concatenate([r for r in rows if r.shape[0]], axis=0)
    height = count // splits
    for i, ref in enumerate(out_refs):
        ref[...] = total[i * height:(i + 1) * height].astype(ref.dtype)
    step = x_refs[0].shape[1]
    for i, ref in enumerate(x_refs):
        flip_ref[i * step:(i + 1) * step, :] = ref[...].T


def partial_keys(block, key_weights, adds=(), splits=1):
    count, rows = block.shape
    width = key_weights.shape[1]
    pieces = 4 if rows % (4 * HEAD) == 0 else 2
    fixed = lambda a: pl.BlockSpec(a.shape, lambda i: (0, 0))
    *parts, flipped = pl.pallas_call(
        functools.partial(partial_kernel, pieces, [first for _, first in adds], splits),
        out_shape=[jax.ShapeDtypeStruct((count // splits, width), jnp.bfloat16)] * splits
        + [jax.ShapeDtypeStruct((rows, count), jnp.bfloat16)],
        grid=(1,),
        in_specs=[pl.BlockSpec((count, rows // pieces), lambda i, c=c: (0, c)) for c in range(pieces)]
        + [fixed(key_weights)]
        + [fixed(a) for a, _ in adds],
        out_specs=[pl.BlockSpec((count // splits, width), lambda i: (0, 0))] * splits
        + [pl.BlockSpec((rows, count), lambda i: (0, 0))],
        compiler_params=params_of(12),
        cost_estimate=cost(2 * count * rows * width, 4 * count * rows),
        name="partial_keys",
    )(*[block] * pieces, key_weights, *[a for a, _ in adds])
    return parts if splits > 1 else parts[0], flipped


def key_kernel(first, *refs):
    *part_refs, cot_ref, out_ref = refs
    count = out_ref.shape[0]
    raw = sum(ref[...].astype(jnp.float32) for ref in part_refs)
    for h in range(raw.shape[1] // HEAD):
        cols = slice(h * HEAD, (h + 1) * HEAD)
        head = raw[:, cols]
        inverse = lax.rsqrt(jnp.mean(head * head, axis=1, keepdims=True) + 1e-06)
        normed = head * inverse
        upper = cot_ref[first:first + count, cols].astype(jnp.float32)
        back = inverse * (upper - normed * jnp.mean(upper * normed, axis=1, keepdims=True))
        out_ref[:, cols] = back.astype(out_ref.dtype)


def key_backward(parts, incoming, first):
    count, width = parts[0].shape
    block = pl.BlockSpec((count, width), lambda i: (0, 0))
    cot = pl.BlockSpec((incoming.shape[0], width), lambda i: (0, 0))
    return pl.pallas_call(
        functools.partial(key_kernel, first),
        out_shape=jax.ShapeDtypeStruct((count, width), jnp.bfloat16),
        grid=(1,),
        in_specs=[block] * len(parts) + [cot],
        out_specs=block,
        compiler_params=params_of(8),
        cost_estimate=cost(60 * count * width, 12 * count * width),
        name="key_backward",
    )(*parts, incoming)


def grad_kernel(count, has_base, has_more, last, place_ref, *refs):
    refs = list(refs)
    x_refs, u_refs = refs[:count], refs[count:2 * count]
    refs = refs[2 * count:]
    base = refs.pop(0) if has_base else None
    square_in, due_in = (refs.pop(0), refs.pop(0)) if has_more else (None, None)
    out_ref = refs.pop(0)
    x = jnp.concatenate([ref[...] for ref in x_refs], axis=1)
    u = jnp.concatenate([ref[...] for ref in u_refs], axis=0)
    total = jnp.dot(x, u, preferred_element_type=jnp.float32)
    if has_base:
        total = total + base[...]
    out_ref[...] = total
    if last:
        sq_ref, due_ref = refs

        @pl.when(pl.program_id(0) == 0)
        def _():
            sq_ref[...] = square_in[...] if has_more else jnp.zeros_like(sq_ref)

        rows, width = total.shape
        squares = (total * total).reshape(rows // 8, 8, width).sum(axis=0)
        folded = squares[:, :HEAD]
        for h in range(1, width // HEAD):
            folded = folded + squares[:, h * HEAD:(h + 1) * HEAD]
        sq_ref[...] += folded
        heads = width // FRAG_COLS
        mine = place_ref[0] - (0 if has_more else heads)
        mine = jnp.minimum(jnp.maximum(mine, 0), heads - 1) * FRAG_COLS
        column = out_ref[:, pl.ds(pl.multiple_of(mine, FRAG_COLS), FRAG_COLS)]
        if has_more:
            column = jnp.where(place_ref[0] < heads, column, due_in[...])
        due_ref[...] = column


def gradient(place, flipped, upstream, base=None, square=None, due=None, last=True):
    rows, depth = flipped[0].shape
    width = upstream[0].shape[1]
    step = 256
    row_block = lambda cols: pl.BlockSpec((step, cols), lambda i, p: (i, 0))
    fixed = pl.BlockSpec((8, HEAD), lambda i, p: (0, 0))
    args = [*flipped, *upstream]
    specs = [row_block(depth)] * len(flipped)
    specs += [pl.BlockSpec((depth, width), lambda i, p: (0, 0))] * len(upstream)
    if base is not None:
        args.append(base)
        specs.append(row_block(width))
    if square is not None:
        args += [square, due]
        specs += [fixed, row_block(FRAG_COLS)]
    if last:
        shapes = [
            jax.ShapeDtypeStruct((rows, width), jnp.float32),
            jax.ShapeDtypeStruct((8, HEAD), jnp.float32),
            jax.ShapeDtypeStruct((rows, FRAG_COLS), jnp.float32),
        ]
        outs = [row_block(width), fixed, row_block(FRAG_COLS)]
    else:
        shapes = [jax.ShapeDtypeStruct((rows, width), jnp.float32)]
        outs = [row_block(width)]
    depth *= len(flipped)
    return pl.pallas_call(
        functools.partial(grad_kernel, len(flipped), base is not None, square is not None, last),
        out_shape=shapes,
        grid_spec=pltpu.PrefetchScalarGridSpec(
            num_scalar_prefetch=1, grid=(rows // step,), in_specs=specs, out_specs=outs
        ),
        compiler_params=params_of(12),
        cost_estimate=cost(2 * rows * width * depth, 2 * rows * depth + 4 * rows * width),
        name="gradient",
    )(place, *args)


def clip_factor(square_refs):
    square = jnp.sum(sum(ref[...] for ref in square_refs), keepdims=True)
    return jnp.minimum(1.0, CLIP_NORM / (jnp.sqrt(square) + 1e-06))


def adam(old, first, second, grad, factor, scalars):
    rate, inv_one, inv_two = (scalars[i] for i in range(3))
    clipped = grad * factor
    first_new = BETA_ONE * first + (1.0 - BETA_ONE) * clipped
    second_new = BETA_TWO * second + (1.0 - BETA_TWO) * clipped * clipped
    update = rate * (
        first_new * inv_one / (jnp.sqrt(second_new * inv_two) + ADAM_EPS) + DECAY * old
    )
    return update, first_new, second_new


def adam_kernel(squares, extra, sc_ref, w_ref, m_ref, v_ref, gk_ref, gv_ref, *refs):
    factor = clip_factor(refs[:squares])
    w_out, m_out, v_out, *done = refs[squares + extra:]
    width = gk_ref.shape[1]
    for g_ref, cols in ((gk_ref, slice(0, width)), (gv_ref, slice(width, 2 * width))):
        old = w_ref[:, cols]
        update, first_new, second_new = adam(
            old, m_ref[:, cols], v_ref[:, cols], g_ref[...], factor, sc_ref
        )
        w_out[:, cols] = old - update
        m_out[:, cols] = first_new
        v_out[:, cols] = second_new
    for ref in done:
        ref[...] = jnp.zeros_like(ref)


def adam_rows(scalars, squares, state, first, last, into=()):
    rows, width = state[0].shape
    step = ADAM_ROWS
    full = pl.BlockSpec((step, width), lambda i: (i + first, 0))
    half = pl.BlockSpec((step, width // 2), lambda i: (i + first, 0))
    shapes = [pltpu.HBM((rows, width), jnp.float32)] * 3
    outs = [full] * 3
    if not into:
        shapes.append(jax.ShapeDtypeStruct((8, HEAD), jnp.float32))
        outs.append(pl.BlockSpec((8, HEAD), lambda i: (0, 0)))
    count = (last - first) * step
    return pl.pallas_call(
        functools.partial(adam_kernel, len(squares), len(into)),
        out_shape=shapes,
        grid=(last - first,),
        in_specs=[pl.BlockSpec(memory_space=pltpu.SMEM), full, full, full, half, half]
        + [pl.BlockSpec((8, HEAD), lambda i: (0, 0))] * len(squares)
        + [pl.BlockSpec(memory_space=pl.ANY)] * len(into),
        out_specs=outs,
        input_output_aliases={6 + len(squares) + i: i for i in range(len(into))},
        compiler_params=params_of(12),
        cost_estimate=cost(20 * count * width, 28 * count * width),
        name="adam_rows",
    )(scalars, *state, *squares, *in_hbm(*into))


def frag_kernel(squares, place_ref, sc_ref, w_ref, m_ref, v_ref, g_ref, *refs):
    blocks, part, _ = w_ref.shape
    factor = clip_factor(refs[:squares])
    inner_ref, *out_refs = refs[squares:]
    for j in range(blocks):
        at = pl.multiple_of((place_ref[1] ^ j) * part, 8)
        old = w_ref[j]
        update, _, _ = adam(old, m_ref[j], v_ref[j], g_ref[pl.ds(at, part), :], factor, sc_ref)
        inner_ref[j] = old - update
        out_refs[j][...] = update.astype(out_refs[j].dtype)


def adam_frag(place, scalars, squares, old, first, second, grad):
    blocks, part, width = old.shape
    smem = pl.BlockSpec(memory_space=pltpu.SMEM)
    vmem = pl.BlockSpec(memory_space=pltpu.VMEM)
    return pl.pallas_call(
        functools.partial(frag_kernel, len(squares)),
        out_shape=[jax.ShapeDtypeStruct(old.shape, jnp.float32)]
        + [jax.ShapeDtypeStruct((part, width), jnp.bfloat16)] * blocks,
        in_specs=[smem, smem] + [vmem] * (4 + len(squares)),
        out_specs=[vmem] * (1 + blocks),
        compiler_params=params_of(12),
        cost_estimate=cost(20 * old.size, 22 * old.size),
        name="adam_frag",
    )(place, scalars, old, first, second, grad, *squares)


def pick_kernel(blocks, place_ref, *refs):
    outs = refs[len(refs) // (blocks + 1) * blocks:]
    for i, out_ref in enumerate(outs):
        for j in range(blocks):
            out_ref[j] = refs[i * blocks + j][...]


def due_columns(place, part, *arrays):
    blocks = arrays[0].shape[0] // part
    specs = []
    for j in range(blocks):
        at = (lambda i, p, j=j: (p[1] ^ j, p[0])) if blocks > 1 else (lambda i, p: (0, p[0]))
        specs.append(pl.BlockSpec((part, FRAG_COLS), at))
    shape = (blocks, part, FRAG_COLS)
    return pl.pallas_call(
        functools.partial(pick_kernel, blocks),
        out_shape=[jax.ShapeDtypeStruct(shape, a.dtype) for a in arrays],
        grid_spec=pltpu.PrefetchScalarGridSpec(
            num_scalar_prefetch=1,
            grid=(1,),
            in_specs=specs * len(arrays),
            out_specs=[pl.BlockSpec(shape, lambda i, p: (0, 0, 0))] * len(arrays),
        ),
        compiler_params=params_of(12),
        cost_estimate=cost(0, 8 * blocks * part * FRAG_COLS * len(arrays)),
        name="due_columns",
    )(place, *[a for array in in_hbm(*arrays) for a in [array] * blocks])


def duplicate_kernel(*refs):
    half = (len(refs) - 3) // 2
    held, in_sems, out_sems = refs[2 * half:]
    streams = held.shape[1]
    step = held.shape[2]
    places = [(a, i, pl.ds(i * step, step)) for a in range(half) for i in range(streams)]
    fetches = [
        pltpu.make_async_copy(refs[a].at[at], held.at[a, i], in_sems.at[a, i]) for a, i, at in places
    ]
    stores = [
        pltpu.make_async_copy(held.at[a, i], refs[half + a].at[at], out_sems.at[a, i])
        for a, i, at in places
    ]
    for copy in fetches:
        copy.start()
    for fetch, store in zip(fetches, stores):
        fetch.wait()
        store.start()
    for copy in stores:
        copy.wait()


def duplicate(*arrays):
    rows, width = arrays[0].shape
    streams = 4
    whole = pl.BlockSpec(memory_space=pl.ANY)
    return pl.pallas_call(
        duplicate_kernel,
        out_shape=[pltpu.HBM(a.shape, a.dtype) for a in arrays],
        in_specs=[whole] * len(arrays),
        out_specs=[whole] * len(arrays),
        scratch_shapes=[
            pltpu.VMEM((len(arrays), streams, rows // streams, width), arrays[0].dtype),
            pltpu.SemaphoreType.DMA((len(arrays), streams)),
            pltpu.SemaphoreType.DMA((len(arrays), streams)),
        ],
        compiler_params=params_of(8),
        cost_estimate=cost(0, sum(8 * a.size for a in arrays)),
        name="duplicate",
    )(*in_hbm(*arrays))


def outer_kernel(replicas, place_ref, *refs):
    share = 1.0 / replicas
    base_refs, sum_refs = refs[3:3 + replicas], refs[3 + replicas:3 + 2 * replicas]
    inner_ref, a_ref, p_ref, m_ref, own_ref, _, *refs = refs[3 + 2 * replicas:]
    w_out, a_out, m_out, mixed, new_a, new_m, sems = refs
    part = a_ref.shape[0]
    scale = share * (1.0 + OUTER_MU) * OUTER_RATE
    columns = pl.ds(pl.multiple_of(place_ref[0] * FRAG_COLS, FRAG_COLS), FRAG_COLS)
    copies = []
    for j in range(replicas):
        fresh = base_refs[j][...] - scale * sum_refs[j][...].astype(jnp.float32)
        mixed[j] = MIX_LOCAL * inner_ref[j] + (1.0 - MIX_LOCAL) * fresh
        rows = pl.ds(pl.multiple_of((place_ref[1] ^ j) * part, 8), part)
        copies.append(pltpu.make_async_copy(mixed.at[j], w_out.at[rows, columns], sems.at[j]))
        copies[-1].start()
    pseudo = p_ref[...] + share * own_ref[...]
    new_moment = OUTER_MU * m_ref[...] + pseudo
    new_m[...] = new_moment
    new_a[...] = a_ref[...] - OUTER_RATE * (OUTER_MU * new_moment + pseudo)
    for i, (src, dst) in enumerate(((new_a, a_out), (new_m, m_out))):
        copies.append(pltpu.make_async_copy(src, dst.at[:, columns], sems.at[replicas + i]))
        copies[-1].start()
    for copy in copies:
        copy.wait()


def outer_step(place, outputs, base, sums, inner, anchor, pseudo, momentum, own_sum, ticket):
    replicas, part = inner.shape[0], inner.shape[1]
    whole = pl.BlockSpec(memory_space=pl.ANY)
    held = pl.BlockSpec(memory_space=pltpu.VMEM)
    return pl.pallas_call(
        functools.partial(outer_kernel, replicas),
        out_shape=[pltpu.HBM(a.shape, a.dtype) for a in outputs],
        in_specs=[pl.BlockSpec(memory_space=pltpu.SMEM)]
        + [whole] * 3
        + [held] * (2 * replicas + 5)
        + [whole],
        out_specs=[whole] * 3,
        scratch_shapes=[
            pltpu.VMEM((replicas, part, FRAG_COLS), jnp.float32),
            pltpu.VMEM((part, FRAG_COLS), jnp.float32),
            pltpu.VMEM((part, FRAG_COLS), jnp.float32),
            pltpu.SemaphoreType.DMA((replicas + 2,)),
        ],
        input_output_aliases={1: 0, 2: 1, 3: 2},
        compiler_params=params_of(12),
        cost_estimate=cost(10 * replicas * part * FRAG_COLS, 20 * replicas * part * FRAG_COLS),
        name="outer_step",
    )(place, *in_hbm(*outputs), *base, *sums, inner, anchor, pseudo, momentum, own_sum, ticket)


def swap(block, axis, offset):
    count = lax.axis_size(axis)
    return lax.ppermute(block, axis, [(i, i ^ offset) for i in range(count)])


def after(value, *others):
    return lax.optimization_barrier((value,) + others)[0]


def body(
    tokens,
    cotangent,
    weights,
    first_moment,
    second_moment,
    anchor,
    momentum,
    due_fragment,
    step_count,
):
    inputs, incoming, params = tokens[0], cotangent[0], weights[0]
    kv_width = incoming.shape[1] // 2
    rows = params.shape[0]
    part = anchor.shape[0]
    replicas = lax.axis_size("rep")
    shards = lax.axis_size("fsdp")
    me = jnp.reshape(lax.axis_index("fsdp"), (1,)).astype(jnp.int32)
    my_rep = lax.axis_index("rep").astype(jnp.int32)
    place = jnp.stack([due_fragment[0], my_rep])
    chips = range(2, shards, 2)
    far = sorted(chips, key=lambda k: (-bin(k).count("1"), k))
    order = [k for k in far[:-2] for k in (k, k + 1)]
    order += far[-2:] + [k + 1 for k in far[-2:]]

    packed = {}
    for offsets in (order[:1], order[1:4], order[4:], (0, 1)):
        packed |= pack(inputs, me, rows, tuple(offsets))
    blocks = {}
    for i, k in enumerate(order[:-4]):
        blocks[k] = swap(after(packed[k], *[blocks[j] for j in order[max(i - 2, 0):max(i - 1, 0)]]), "fsdp", k)
    blocks[0], blocks[1] = packed[0], swap(packed[1], "fsdp", 1)

    (old,) = due_columns(place, part, params)
    old_sums = [old[0]] + [swap(old[k], "rep", k) for k in range(1, replicas)]
    anchor_cols, moment_cols = (c[0] for c in due_columns(place, part, anchor, momentum))
    pseudo_old = anchor_cols - sum(old_sums[1:], old_sums[0]) / replicas
    base = anchor_cols - OUTER_RATE * (OUTER_MU * (OUTER_MU * moment_cols + pseudo_old) + pseudo_old)
    base = [base] + [swap(base, "rep", k) for k in range(1, replicas)]

    for ready, i in (((pseudo_old,), len(order) - 4), (tuple(base), len(order) - 2)):
        for k, before in zip(order[i:i + 2], order[i - 2:i]):
            blocks[k] = swap(after(packed[k], blocks[before], *ready), "fsdp", k)

    steps_now = step_count[0].astype(jnp.float32)
    plan = jnp.minimum(1.0, steps_now / WARMUP) * (
        0.55 + 0.45 * jnp.cos(jnp.pi * steps_now / STEPS_TOTAL)
    )
    rate = PEAK_RATE * plan
    inv_one = 1.0 / (1.0 - jnp.power(BETA_ONE, steps_now))
    inv_two = 1.0 / (1.0 - jnp.power(BETA_TWO, steps_now))
    scalars = jnp.stack([rate, inv_one, inv_two])
    old_first, old_second = due_columns(place, part, first_moment[0], second_moment[0])
    anchor_copy, momentum_copy = duplicate(anchor, momentum)
    key_weights = cast_left(params, kv_width)

    last = far[-1]
    blocks[last + 1] = after(blocks[last + 1], anchor_copy, momentum_copy, scalars, old_first, old_second)
    relay = len(far) == 3 and far[0] == far[1] ^ far[2]
    half = inputs.shape[0] // 2
    parts, flipped, relayed = [], {}, {}
    for k in far + [0]:
        theirs, flipped[k + 1] = partial_keys(blocks[k + 1], key_weights)
        theirs = swap(theirs, "fsdp", 1)
        adds = [(theirs, 0)] + relayed.get(k, [])
        if relay and k == far[0]:
            (upper, lower), flipped[k] = partial_keys(blocks[k], key_weights, adds, 2)
            relayed[far[2]] = [(swap(upper, "fsdp", far[1]), 0)]
            relayed[far[1]] = [(swap(lower, "fsdp", far[2]), half)]
            continue
        part_k, flipped[k] = partial_keys(blocks[k], key_weights, adds)
        if k == last:
            values = {0: after(incoming[:, kv_width:], part_k)}
            for j in far[1:] if relay else far:
                values[j] = swap(values[0], "fsdp", j)
            if relay:
                upper = swap(values[far[1]][:half], "fsdp", far[2])
                lower = swap(values[far[2]][half:], "fsdp", far[1])
                values[far[0]] = jnp.concatenate([upper, lower], axis=0)
            for j in range(0, shards, 2):
                values[j + 1] = swap(values[j], "fsdp", 1)
        parts.append(swap(part_k, "fsdp", k) if k else part_k)
    spread = [0, 1] + [k + odd for k in far for odd in range(2)]
    near, rest = spread[:shards // 2], spread[shards // 2:]
    pick = lambda table, which: [table[k] for k in which]
    (values_first,) = gradient(place, pick(flipped, near), pick(values, near), last=False)
    keys = {0: key_backward(parts, incoming, 0)}
    for k in far:
        keys[k] = swap(keys[0], "fsdp", k)
    keys[1] = swap(keys[0], "fsdp", 1)

    grad_values, square, due = gradient(
        place, pick(flipped, rest), pick(values, rest), values_first
    )
    for k in near[2::2]:
        keys[k + 1] = swap(after(keys[k], square), "fsdp", 1)
    (keys_first,) = gradient(place, pick(flipped, near), pick(keys, near), last=False)
    for k in rest[::2]:
        keys[k + 1] = swap(after(keys[k], square), "fsdp", 1)
    grad_keys, square, due = gradient(
        place, pick(flipped, rest), pick(keys, rest), keys_first, square, due
    )

    square = square + swap(square, "fsdp", 1)
    squares = [square] + [swap(square, "fsdp", k) for k in chips]

    state = (params, first_moment[0], second_moment[0], grad_keys, grad_values)
    inner, *update = adam_frag(place, scalars, squares, old, old_first, old_second, due)
    steps = rows // ADAM_ROWS
    *results, ticket = adam_rows(scalars, squares, state, 0, steps // 2)
    own_sum = update[0].astype(jnp.float32)
    for k in range(1, replicas):
        own_sum = own_sum + swap(update[k], "rep", k).astype(jnp.float32)
    own_sum, ticket = lax.optimization_barrier((own_sum, ticket))
    sums = [own_sum.astype(jnp.bfloat16)]
    sums += [swap(sums[0], "rep", k) for k in range(1, replicas)]
    results = adam_rows(scalars, squares, state, steps // 2, steps, results)
    weights_out, anchor_out, momentum_out = outer_step(
        place,
        (results[0], anchor_copy, momentum_copy),
        base,
        sums,
        inner,
        anchor_cols,
        pseudo_old,
        moment_cols,
        own_sum,
        ticket,
    )
    plan_out = jnp.reshape(plan, (1,))
    return (
        weights_out[None],
        results[1][None],
        results[2][None],
        anchor_out,
        momentum_out,
        plan_out,
    )


def solution(mesh):
    tokens_spec = P("rep", "fsdp", None)
    outer_spec = P(("fsdp", "rep"), None)
    return jax.shard_map(
        body,
        mesh=mesh,
        in_specs=(tokens_spec,) * 5 + (outer_spec,) * 2 + (P(), P()),
        out_specs=(tokens_spec,) * 3 + (outer_spec,) * 2 + (P(),),
        check_vma=False,
    )
```

```python
import functools

import jax
import jax.numpy as jnp
from jax import lax
from jax.experimental import pallas as pl
from jax.experimental.pallas import tpu as pltpu
from jax.sharding import PartitionSpec as P

HEAD = 128
WARMUP = 2000
STEPS_TOTAL = 100000
FRAG_COLS = 128


BETA_ONE = 0.9
BETA_TWO = 0.95
ADAM_EPS = 1e-08
DECAY = 0.1
PEAK_RATE = 0.0003
CLIP_NORM = 1.0
OUTER_MU = 0.9
OUTER_RATE = 0.7
MIX_LOCAL = 0.5

MIB = 1 << 20
ADAM_ROWS = 128


def in_hbm(*arrays):
    return [pltpu.with_memory_space_constraint(a, pltpu.HBM) for a in arrays]


def params_of(limit):
    return pltpu.CompilerParams(vmem_limit_bytes=limit * MIB)


def cost(flops, moved):
    return pl.CostEstimate(flops=int(flops), bytes_accessed=int(moved), transcendentals=0)


def pack_kernel(offsets, me_ref, src_ref, *refs):
    half = len(offsets)
    out_refs, (held, in_sems, out_sems) = refs[:half], refs[half:]
    streams = in_sems.shape[1]
    count, rows = out_refs[0].shape
    step = count // streams
    fetches, stores = [], []
    for i, offset in enumerate(offsets):
        column = pl.multiple_of((me_ref[0] ^ offset) * rows, HEAD)
        for j in range(streams):
            at = pl.ds(j * step, step)
            block = src_ref.at[at, pl.ds(column, rows)]
            fetches.append(pltpu.make_async_copy(block, held.at[i, at], in_sems.at[i, j]))
            stores.append(pltpu.make_async_copy(held.at[i, at], out_refs[i].at[at], out_sems.at[i, j]))
    for copy in fetches:
        copy.start()
    for fetch, store in zip(fetches, stores):
        fetch.wait()
        store.start()
    for copy in stores:
        copy.wait()


def pack(tokens, me, rows, offsets):
    count = tokens.shape[0]
    streams = 4
    whole = pl.BlockSpec(memory_space=pl.ANY)
    outs = pl.pallas_call(
        functools.partial(pack_kernel, offsets),
        out_shape=[pltpu.HBM((count, rows), tokens.dtype)] * len(offsets),
        in_specs=[pl.BlockSpec(memory_space=pltpu.SMEM), whole],
        out_specs=[whole] * len(offsets),
        scratch_shapes=[
            pltpu.VMEM((len(offsets), count, rows), tokens.dtype),
            pltpu.SemaphoreType.DMA((len(offsets), streams)),
            pltpu.SemaphoreType.DMA((len(offsets), streams)),
        ],
        compiler_params=params_of(12),
        cost_estimate=cost(0, 4 * len(offsets) * count * rows),
        name="pack",
    )(me, *in_hbm(tokens))
    return dict(zip(offsets, outs))


def cast_kernel(src_ref, out_ref):
    out_ref[...] = src_ref[...].astype(out_ref.dtype)


def cast_left(array, width):
    rows = array.shape[0]
    block = pl.BlockSpec((256, width), lambda i: (i, 0))
    return pl.pallas_call(
        cast_kernel,
        out_shape=jax.ShapeDtypeStruct((rows, width), jnp.bfloat16),
        grid=(rows // 256,),
        in_specs=[block],
        out_specs=block,
        compiler_params=params_of(8),
        cost_estimate=cost(0, 6 * rows * width),
        name="cast_left",
    )(*in_hbm(array))


def partial_kernel(pieces, firsts, splits, *refs):
    x_refs, w_ref, refs = refs[:pieces], refs[pieces], refs[pieces + 1:]
    add_refs, out_refs, flip_ref = refs[:len(firsts)], refs[len(firsts):-1], refs[-1]
    x = jnp.concatenate([ref[...] for ref in x_refs], axis=1)
    total = jnp.dot(x, w_ref[...], preferred_element_type=jnp.float32)
    count = total.shape[0]
    for ref, first in zip(add_refs, firsts):
        last = first + ref.shape[0]
        rows = [total[:first], total[first:last] + ref[...].astype(jnp.float32), total[last:]]
        total = jnp.concatenate([r for r in rows if r.shape[0]], axis=0)
    height = count // splits
    for i, ref in enumerate(out_refs):
        ref[...] = total[i * height:(i + 1) * height].astype(ref.dtype)
    step = x_refs[0].shape[1]
    for i, ref in enumerate(x_refs):
        flip_ref[i * step:(i + 1) * step, :] = ref[...].T


def partial_keys(block, key_weights, adds=(), splits=1):
    count, rows = block.shape
    width = key_weights.shape[1]
    pieces = 4 if rows % (4 * HEAD) == 0 else 2
    fixed = lambda a: pl.BlockSpec(a.shape, lambda i: (0, 0))
    *parts, flipped = pl.pallas_call(
        functools.partial(partial_kernel, pieces, [first for _, first in adds], splits),
        out_shape=[jax.ShapeDtypeStruct((count // splits, width), jnp.bfloat16)] * splits
        + [jax.ShapeDtypeStruct((rows, count), jnp.bfloat16)],
        grid=(1,),
        in_specs=[pl.BlockSpec((count, rows // pieces), lambda i, c=c: (0, c)) for c in range(pieces)]
        + [fixed(key_weights)]
        + [fixed(a) for a, _ in adds],
        out_specs=[pl.BlockSpec((count // splits, width), lambda i: (0, 0))] * splits
        + [pl.BlockSpec((rows, count), lambda i: (0, 0))],
        compiler_params=params_of(12),
        cost_estimate=cost(2 * count * rows * width, 4 * count * rows),
        name="partial_keys",
    )(*[block] * pieces, key_weights, *[a for a, _ in adds])
    return parts if splits > 1 else parts[0], flipped


def key_kernel(first, *refs):
    *part_refs, cot_ref, out_ref = refs
    count = out_ref.shape[0]
    raw = sum(ref[...].astype(jnp.float32) for ref in part_refs)
    for h in range(raw.shape[1] // HEAD):
        cols = slice(h * HEAD, (h + 1) * HEAD)
        head = raw[:, cols]
        inverse = lax.rsqrt(jnp.mean(head * head, axis=1, keepdims=True) + 1e-06)
        normed = head * inverse
        upper = cot_ref[first:first + count, cols].astype(jnp.float32)
        back = inverse * (upper - normed * jnp.mean(upper * normed, axis=1, keepdims=True))
        out_ref[:, cols] = back.astype(out_ref.dtype)


def key_backward(parts, incoming, first):
    count, width = parts[0].shape
    block = pl.BlockSpec((count, width), lambda i: (0, 0))
    cot = pl.BlockSpec((incoming.shape[0], width), lambda i: (0, 0))
    return pl.pallas_call(
        functools.partial(key_kernel, first),
        out_shape=jax.ShapeDtypeStruct((count, width), jnp.bfloat16),
        grid=(1,),
        in_specs=[block] * len(parts) + [cot],
        out_specs=block,
        compiler_params=params_of(8),
        cost_estimate=cost(60 * count * width, 12 * count * width),
        name="key_backward",
    )(*parts, incoming)


def grad_kernel(count, has_base, has_more, last, place_ref, *refs):
    refs = list(refs)
    x_refs, u_refs = refs[:count], refs[count:2 * count]
    refs = refs[2 * count:]
    base = refs.pop(0) if has_base else None
    square_in, due_in = (refs.pop(0), refs.pop(0)) if has_more else (None, None)
    out_ref = refs.pop(0)
    x = jnp.concatenate([ref[...] for ref in x_refs], axis=1)
    u = jnp.concatenate([ref[...] for ref in u_refs], axis=0)
    total = jnp.dot(x, u, preferred_element_type=jnp.float32)
    if has_base:
        total = total + base[...]
    out_ref[...] = total
    if last:
        sq_ref, due_ref = refs

        @pl.when(pl.program_id(0) == 0)
        def _():
            sq_ref[...] = square_in[...] if has_more else jnp.zeros_like(sq_ref)

        rows, width = total.shape
        squares = (total * total).reshape(rows // 8, 8, width).sum(axis=0)
        folded = squares[:, :HEAD]
        for h in range(1, width // HEAD):
            folded = folded + squares[:, h * HEAD:(h + 1) * HEAD]
        sq_ref[...] += folded
        heads = width // FRAG_COLS
        mine = place_ref[0] - (0 if has_more else heads)
        mine = jnp.minimum(jnp.maximum(mine, 0), heads - 1) * FRAG_COLS
        column = out_ref[:, pl.ds(pl.multiple_of(mine, FRAG_COLS), FRAG_COLS)]
        if has_more:
            column = jnp.where(place_ref[0] < heads, column, due_in[...])
        due_ref[...] = column


def gradient(place, flipped, upstream, base=None, square=None, due=None, last=True):
    rows, depth = flipped[0].shape
    width = upstream[0].shape[1]
    step = 256
    row_block = lambda cols: pl.BlockSpec((step, cols), lambda i, p: (i, 0))
    fixed = pl.BlockSpec((8, HEAD), lambda i, p: (0, 0))
    args = [*flipped, *upstream]
    specs = [row_block(depth)] * len(flipped)
    specs += [pl.BlockSpec((depth, width), lambda i, p: (0, 0))] * len(upstream)
    if base is not None:
        args.append(base)
        specs.append(row_block(width))
    if square is not None:
        args += [square, due]
        specs += [fixed, row_block(FRAG_COLS)]
    if last:
        shapes = [
            jax.ShapeDtypeStruct((rows, width), jnp.float32),
            jax.ShapeDtypeStruct((8, HEAD), jnp.float32),
            jax.ShapeDtypeStruct((rows, FRAG_COLS), jnp.float32),
        ]
        outs = [row_block(width), fixed, row_block(FRAG_COLS)]
    else:
        shapes = [jax.ShapeDtypeStruct((rows, width), jnp.float32)]
        outs = [row_block(width)]
    depth *= len(flipped)
    return pl.pallas_call(
        functools.partial(grad_kernel, len(flipped), base is not None, square is not None, last),
        out_shape=shapes,
        grid_spec=pltpu.PrefetchScalarGridSpec(
            num_scalar_prefetch=1, grid=(rows // step,), in_specs=specs, out_specs=outs
        ),
        compiler_params=params_of(12),
        cost_estimate=cost(2 * rows * width * depth, 2 * rows * depth + 4 * rows * width),
        name="gradient",
    )(place, *args)


def clip_factor(square_refs):
    square = jnp.sum(sum(ref[...] for ref in square_refs), keepdims=True)
    return jnp.minimum(1.0, CLIP_NORM / (jnp.sqrt(square) + 1e-06))


def adam(old, first, second, grad, factor, scalars):
    rate, inv_one, inv_two = (scalars[i] for i in range(3))
    clipped = grad * factor
    first_new = BETA_ONE * first + (1.0 - BETA_ONE) * clipped
    second_new = BETA_TWO * second + (1.0 - BETA_TWO) * clipped * clipped
    update = rate * (
        first_new * inv_one / (jnp.sqrt(second_new * inv_two) + ADAM_EPS) + DECAY * old
    )
    return update, first_new, second_new


def adam_kernel(squares, extra, sc_ref, w_ref, m_ref, v_ref, gk_ref, gv_ref, *refs):
    factor = clip_factor(refs[:squares])
    w_out, m_out, v_out, *done = refs[squares + extra:]
    width = gk_ref.shape[1]
    for g_ref, cols in ((gk_ref, slice(0, width)), (gv_ref, slice(width, 2 * width))):
        old = w_ref[:, cols]
        update, first_new, second_new = adam(
            old, m_ref[:, cols], v_ref[:, cols], g_ref[...], factor, sc_ref
        )
        w_out[:, cols] = old - update
        m_out[:, cols] = first_new
        v_out[:, cols] = second_new
    for ref in done:
        ref[...] = jnp.zeros_like(ref)


def adam_rows(scalars, squares, state, first, last, into=()):
    rows, width = state[0].shape
    step = ADAM_ROWS
    full = pl.BlockSpec((step, width), lambda i: (i + first, 0))
    half = pl.BlockSpec((step, width // 2), lambda i: (i + first, 0))
    shapes = [pltpu.HBM((rows, width), jnp.float32)] * 3
    outs = [full] * 3
    if not into:
        shapes.append(jax.ShapeDtypeStruct((8, HEAD), jnp.float32))
        outs.append(pl.BlockSpec((8, HEAD), lambda i: (0, 0)))
    count = (last - first) * step
    return pl.pallas_call(
        functools.partial(adam_kernel, len(squares), len(into)),
        out_shape=shapes,
        grid=(last - first,),
        in_specs=[pl.BlockSpec(memory_space=pltpu.SMEM), full, full, full, half, half]
        + [pl.BlockSpec((8, HEAD), lambda i: (0, 0))] * len(squares)
        + [pl.BlockSpec(memory_space=pl.ANY)] * len(into),
        out_specs=outs,
        input_output_aliases={6 + len(squares) + i: i for i in range(len(into))},
        compiler_params=params_of(12),
        cost_estimate=cost(20 * count * width, 28 * count * width),
        name="adam_rows",
    )(scalars, *state, *squares, *in_hbm(*into))


def frag_kernel(squares, place_ref, sc_ref, w_ref, m_ref, v_ref, g_ref, *refs):
    blocks, part, _ = w_ref.shape
    factor = clip_factor(refs[:squares])
    inner_ref, *out_refs = refs[squares:]
    for j in range(blocks):
        at = pl.multiple_of((place_ref[1] ^ j) * part, 8)
        old = w_ref[j]
        update, _, _ = adam(old, m_ref[j], v_ref[j], g_ref[pl.ds(at, part), :], factor, sc_ref)
        inner_ref[j] = old - update
        out_refs[j][...] = update.astype(out_refs[j].dtype)


def adam_frag(place, scalars, squares, old, first, second, grad):
    blocks, part, width = old.shape
    smem = pl.BlockSpec(memory_space=pltpu.SMEM)
    vmem = pl.BlockSpec(memory_space=pltpu.VMEM)
    return pl.pallas_call(
        functools.partial(frag_kernel, len(squares)),
        out_shape=[jax.ShapeDtypeStruct(old.shape, jnp.float32)]
        + [jax.ShapeDtypeStruct((part, width), jnp.bfloat16)] * blocks,
        in_specs=[smem, smem] + [vmem] * (4 + len(squares)),
        out_specs=[vmem] * (1 + blocks),
        compiler_params=params_of(12),
        cost_estimate=cost(20 * old.size, 22 * old.size),
        name="adam_frag",
    )(place, scalars, old, first, second, grad, *squares)


def pick_kernel(blocks, place_ref, *refs):
    outs = refs[len(refs) // (blocks + 1) * blocks:]
    for i, out_ref in enumerate(outs):
        for j in range(blocks):
            out_ref[j] = refs[i * blocks + j][...]


def due_columns(place, part, *arrays):
    blocks = arrays[0].shape[0] // part
    specs = []
    for j in range(blocks):
        at = (lambda i, p, j=j: (p[1] ^ j, p[0])) if blocks > 1 else (lambda i, p: (0, p[0]))
        specs.append(pl.BlockSpec((part, FRAG_COLS), at))
    shape = (blocks, part, FRAG_COLS)
    return pl.pallas_call(
        functools.partial(pick_kernel, blocks),
        out_shape=[jax.ShapeDtypeStruct(shape, a.dtype) for a in arrays],
        grid_spec=pltpu.PrefetchScalarGridSpec(
            num_scalar_prefetch=1,
            grid=(1,),
            in_specs=specs * len(arrays),
            out_specs=[pl.BlockSpec(shape, lambda i, p: (0, 0, 0))] * len(arrays),
        ),
        compiler_params=params_of(12),
        cost_estimate=cost(0, 8 * blocks * part * FRAG_COLS * len(arrays)),
        name="due_columns",
    )(place, *[a for array in in_hbm(*arrays) for a in [array] * blocks])


def duplicate_kernel(*refs):
    half = (len(refs) - 3) // 2
    held, in_sems, out_sems = refs[2 * half:]
    streams = held.shape[1]
    step = held.shape[2]
    places = [(a, i, pl.ds(i * step, step)) for a in range(half) for i in range(streams)]
    fetches = [
        pltpu.make_async_copy(refs[a].at[at], held.at[a, i], in_sems.at[a, i]) for a, i, at in places
    ]
    stores = [
        pltpu.make_async_copy(held.at[a, i], refs[half + a].at[at], out_sems.at[a, i])
        for a, i, at in places
    ]
    for copy in fetches:
        copy.start()
    for fetch, store in zip(fetches, stores):
        fetch.wait()
        store.start()
    for copy in stores:
        copy.wait()


def duplicate(*arrays):
    rows, width = arrays[0].shape
    streams = 4
    whole = pl.BlockSpec(memory_space=pl.ANY)
    return pl.pallas_call(
        duplicate_kernel,
        out_shape=[pltpu.HBM(a.shape, a.dtype) for a in arrays],
        in_specs=[whole] * len(arrays),
        out_specs=[whole] * len(arrays),
        scratch_shapes=[
            pltpu.VMEM((len(arrays), streams, rows // streams, width), arrays[0].dtype),
            pltpu.SemaphoreType.DMA((len(arrays), streams)),
            pltpu.SemaphoreType.DMA((len(arrays), streams)),
        ],
        compiler_params=params_of(8),
        cost_estimate=cost(0, sum(8 * a.size for a in arrays)),
        name="duplicate",
    )(*in_hbm(*arrays))


def outer_kernel(replicas, place_ref, *refs):
    share = 1.0 / replicas
    base_refs, sum_refs = refs[3:3 + replicas], refs[3 + replicas:3 + 2 * replicas]
    inner_ref, a_ref, p_ref, m_ref, own_ref, _, *refs = refs[3 + 2 * replicas:]
    w_out, a_out, m_out, mixed, new_a, new_m, sems = refs
    part = a_ref.shape[0]
    scale = share * (1.0 + OUTER_MU) * OUTER_RATE
    columns = pl.ds(pl.multiple_of(place_ref[0] * FRAG_COLS, FRAG_COLS), FRAG_COLS)
    copies = []
    for j in range(replicas):
        fresh = base_refs[j][...] - scale * sum_refs[j][...].astype(jnp.float32)
        mixed[j] = MIX_LOCAL * inner_ref[j] + (1.0 - MIX_LOCAL) * fresh
        rows = pl.ds(pl.multiple_of((place_ref[1] ^ j) * part, 8), part)
        copies.append(pltpu.make_async_copy(mixed.at[j], w_out.at[rows, columns], sems.at[j]))
        copies[-1].start()
    pseudo = p_ref[...] + share * own_ref[...]
    new_moment = OUTER_MU * m_ref[...] + pseudo
    new_m[...] = new_moment
    new_a[...] = a_ref[...] - OUTER_RATE * (OUTER_MU * new_moment + pseudo)
    for i, (src, dst) in enumerate(((new_a, a_out), (new_m, m_out))):
        copies.append(pltpu.make_async_copy(src, dst.at[:, columns], sems.at[replicas + i]))
        copies[-1].start()
    for copy in copies:
        copy.wait()


def outer_step(place, outputs, base, sums, inner, anchor, pseudo, momentum, own_sum, ticket):
    replicas, part = inner.shape[0], inner.shape[1]
    whole = pl.BlockSpec(memory_space=pl.ANY)
    held = pl.BlockSpec(memory_space=pltpu.VMEM)
    return pl.pallas_call(
        functools.partial(outer_kernel, replicas),
        out_shape=[pltpu.HBM(a.shape, a.dtype) for a in outputs],
        in_specs=[pl.BlockSpec(memory_space=pltpu.SMEM)]
        + [whole] * 3
        + [held] * (2 * replicas + 5)
        + [whole],
        out_specs=[whole] * 3,
        scratch_shapes=[
            pltpu.VMEM((replicas, part, FRAG_COLS), jnp.float32),
            pltpu.VMEM((part, FRAG_COLS), jnp.float32),
            pltpu.VMEM((part, FRAG_COLS), jnp.float32),
            pltpu.SemaphoreType.DMA((replicas + 2,)),
        ],
        input_output_aliases={1: 0, 2: 1, 3: 2},
        compiler_params=params_of(12),
        cost_estimate=cost(10 * replicas * part * FRAG_COLS, 20 * replicas * part * FRAG_COLS),
        name="outer_step",
    )(place, *in_hbm(*outputs), *base, *sums, inner, anchor, pseudo, momentum, own_sum, ticket)


def swap(block, axis, offset):
    count = lax.axis_size(axis)
    return lax.ppermute(block, axis, [(i, i ^ offset) for i in range(count)])


def after(value, *others):
    return lax.optimization_barrier((value,) + others)[0]


def body(
    tokens,
    cotangent,
    weights,
    first_moment,
    second_moment,
    anchor,
    momentum,
    due_fragment,
    step_count,
):
    inputs, incoming, params = tokens[0], cotangent[0], weights[0]
    kv_width = incoming.shape[1] // 2
    rows = params.shape[0]
    part = anchor.shape[0]
    replicas = lax.axis_size("rep")
    shards = lax.axis_size("fsdp")
    me = jnp.reshape(lax.axis_index("fsdp"), (1,)).astype(jnp.int32)
    my_rep = lax.axis_index("rep").astype(jnp.int32)
    place = jnp.stack([due_fragment[0], my_rep])
    chips = range(2, shards, 2)
    far = sorted(chips, key=lambda k: (-bin(k).count("1"), k))
    order = [k for k in far[:-2] for k in (k, k + 1)]
    order += far[-2:] + [k + 1 for k in far[-2:]]

    packed = {}
    for offsets in (order[:1], order[1:4], order[4:], (0, 1)):
        packed |= pack(inputs, me, rows, tuple(offsets))
    blocks = {}
    for i, k in enumerate(order[:-4]):
        blocks[k] = swap(after(packed[k], *[blocks[j] for j in order[max(i - 2, 0):max(i - 1, 0)]]), "fsdp", k)
    blocks[0], blocks[1] = packed[0], swap(packed[1], "fsdp", 1)

    (old,) = due_columns(place, part, params)
    old_sums = [old[0]] + [swap(old[k], "rep", k) for k in range(1, replicas)]
    anchor_cols, moment_cols = (c[0] for c in due_columns(place, part, anchor, momentum))
    pseudo_old = anchor_cols - sum(old_sums[1:], old_sums[0]) / replicas
    base = anchor_cols - OUTER_RATE * (OUTER_MU * (OUTER_MU * moment_cols + pseudo_old) + pseudo_old)
    base = [base] + [swap(base, "rep", k) for k in range(1, replicas)]

    for ready, i in (((pseudo_old,), len(order) - 4), (tuple(base), len(order) - 2)):
        for k, before in zip(order[i:i + 2], order[i - 2:i]):
            blocks[k] = swap(after(packed[k], blocks[before], *ready), "fsdp", k)

    steps_now = step_count[0].astype(jnp.float32)
    plan = jnp.minimum(1.0, steps_now / WARMUP) * (
        0.55 + 0.45 * jnp.cos(jnp.pi * steps_now / STEPS_TOTAL)
    )
    rate = PEAK_RATE * plan
    inv_one = 1.0 / (1.0 - jnp.power(BETA_ONE, steps_now))
    inv_two = 1.0 / (1.0 - jnp.power(BETA_TWO, steps_now))
    scalars = jnp.stack([rate, inv_one, inv_two])
    old_first, old_second = due_columns(place, part, first_moment[0], second_moment[0])
    anchor_copy, momentum_copy = duplicate(anchor, momentum)
    key_weights = cast_left(params, kv_width)

    last = far[-1]
    blocks[last + 1] = after(blocks[last + 1], anchor_copy, momentum_copy, scalars, old_first, old_second)
    relay = len(far) == 3 and far[0] == far[1] ^ far[2]
    half = inputs.shape[0] // 2
    parts, flipped, relayed, formed = [], {}, {}, []
    for k in far + [0]:
        theirs, flipped[k + 1] = partial_keys(blocks[k + 1], key_weights)
        theirs = swap(theirs, "fsdp", 1)
        adds = [(theirs, 0)] + relayed.get(k, [])
        if relay and k == far[0]:
            (upper, lower), flipped[k] = partial_keys(blocks[k], key_weights, adds, 2)
            relayed[far[2]] = [(swap(upper, "fsdp", far[1]), 0)]
            relayed[far[1]] = [(swap(lower, "fsdp", far[2]), half)]
            continue
        part_k, flipped[k] = partial_keys(blocks[k], key_weights, adds)
        formed.append(part_k)
        if k == last:
            values = {0: after(incoming[:, kv_width:], *formed)}
            for j in far[1:] if relay else far:
                values[j] = swap(values[0], "fsdp", j)
            if relay:
                upper = swap(values[far[1]][:half], "fsdp", far[2])
                lower = swap(values[far[2]][half:], "fsdp", far[1])
                values[far[0]] = jnp.concatenate([upper, lower], axis=0)
            for j in range(0, shards, 2):
                values[j + 1] = swap(values[j], "fsdp", 1)
        parts.append(swap(part_k, "fsdp", k) if k else part_k)
    spread = [0, 1] + [k + odd for k in far for odd in range(2)]
    near, rest = spread[:shards // 2], spread[shards // 2:]
    pick = lambda table, which: [table[k] for k in which]
    (values_first,) = gradient(place, pick(flipped, near), pick(values, near), last=False)
    keys = {0: key_backward(parts, incoming, 0)}
    for k in far:
        keys[k] = swap(keys[0], "fsdp", k)
    keys[1] = swap(keys[0], "fsdp", 1)

    grad_values, square, due = gradient(
        place, pick(flipped, rest), pick(values, rest), values_first
    )
    for k in near[2::2]:
        keys[k + 1] = swap(after(keys[k], square), "fsdp", 1)
    (keys_first,) = gradient(place, pick(flipped, near), pick(keys, near), last=False)
    for k in rest[::2]:
        keys[k + 1] = swap(after(keys[k], square), "fsdp", 1)
    grad_keys, square, due = gradient(
        place, pick(flipped, rest), pick(keys, rest), keys_first, square, due
    )

    square = square + swap(square, "fsdp", 1)
    squares = [square] + [swap(square, "fsdp", k) for k in chips]

    state = (params, first_moment[0], second_moment[0], grad_keys, grad_values)
    inner, *update = adam_frag(place, scalars, squares, old, old_first, old_second, due)
    steps = rows // ADAM_ROWS
    *results, ticket = adam_rows(scalars, squares, state, 0, steps // 2)
    own_sum = update[0].astype(jnp.float32)
    for k in range(1, replicas):
        own_sum = own_sum + swap(update[k], "rep", k).astype(jnp.float32)
    own_sum, ticket = lax.optimization_barrier((own_sum, ticket))
    sums = [own_sum.astype(jnp.bfloat16)]
    sums += [swap(sums[0], "rep", k) for k in range(1, replicas)]
    results = adam_rows(scalars, squares, state, steps // 2, steps, results)
    weights_out, anchor_out, momentum_out = outer_step(
        place,
        (results[0], anchor_copy, momentum_copy),
        base,
        sums,
        inner,
        anchor_cols,
        pseudo_old,
        moment_cols,
        own_sum,
        ticket,
    )
    plan_out = jnp.reshape(plan, (1,))
    return (
        weights_out[None],
        results[1][None],
        results[2][None],
        anchor_out,
        momentum_out,
        plan_out,
    )


def solution(mesh):
    tokens_spec = P("rep", "fsdp", None)
    outer_spec = P(("fsdp", "rep"), None)
    return jax.shard_map(
        body,
        mesh=mesh,
        in_specs=(tokens_spec,) * 5 + (outer_spec,) * 2 + (P(), P()),
        out_specs=(tokens_spec,) * 3 + (outer_spec,) * 2 + (P(),),
        check_vma=False,
    )
```

```python
import functools

import jax
import jax.numpy as jnp
from jax import lax
from jax.experimental import pallas as pl
from jax.experimental.pallas import tpu as pltpu
from jax.sharding import PartitionSpec as P

HEAD = 128
WARMUP = 2000
STEPS_TOTAL = 100000
FRAG_COLS = 128


BETA_ONE = 0.9
BETA_TWO = 0.95
ADAM_EPS = 1e-08
DECAY = 0.1
PEAK_RATE = 0.0003
CLIP_NORM = 1.0
OUTER_MU = 0.9
OUTER_RATE = 0.7
MIX_LOCAL = 0.5

MIB = 1 << 20
ADAM_ROWS = 128


def in_hbm(*arrays):
    return [pltpu.with_memory_space_constraint(a, pltpu.HBM) for a in arrays]


def params_of(limit):
    return pltpu.CompilerParams(vmem_limit_bytes=limit * MIB)


def cost(flops, moved):
    return pl.CostEstimate(flops=int(flops), bytes_accessed=int(moved), transcendentals=0)


def pack_kernel(offsets, me_ref, src_ref, *refs):
    half = len(offsets)
    out_refs, (held, in_sems, out_sems) = refs[:half], refs[half:]
    streams = in_sems.shape[1]
    count, rows = out_refs[0].shape
    step = count // streams
    fetches, stores = [], []
    for i, offset in enumerate(offsets):
        column = pl.multiple_of((me_ref[0] ^ offset) * rows, HEAD)
        for j in range(streams):
            at = pl.ds(j * step, step)
            block = src_ref.at[at, pl.ds(column, rows)]
            fetches.append(pltpu.make_async_copy(block, held.at[i, at], in_sems.at[i, j]))
            stores.append(pltpu.make_async_copy(held.at[i, at], out_refs[i].at[at], out_sems.at[i, j]))
    for copy in fetches:
        copy.start()
    for fetch, store in zip(fetches, stores):
        fetch.wait()
        store.start()
    for copy in stores:
        copy.wait()


def pack(tokens, me, rows, offsets):
    count = tokens.shape[0]
    streams = 4
    whole = pl.BlockSpec(memory_space=pl.ANY)
    outs = pl.pallas_call(
        functools.partial(pack_kernel, offsets),
        out_shape=[pltpu.HBM((count, rows), tokens.dtype)] * len(offsets),
        in_specs=[pl.BlockSpec(memory_space=pltpu.SMEM), whole],
        out_specs=[whole] * len(offsets),
        scratch_shapes=[
            pltpu.VMEM((len(offsets), count, rows), tokens.dtype),
            pltpu.SemaphoreType.DMA((len(offsets), streams)),
            pltpu.SemaphoreType.DMA((len(offsets), streams)),
        ],
        compiler_params=params_of(12),
        cost_estimate=cost(0, 4 * len(offsets) * count * rows),
        name="pack",
    )(me, *in_hbm(tokens))
    return dict(zip(offsets, outs))


def cast_kernel(src_ref, out_ref):
    out_ref[...] = src_ref[...].astype(out_ref.dtype)


def cast_left(array, width):
    rows = array.shape[0]
    block = pl.BlockSpec((256, width), lambda i: (i, 0))
    return pl.pallas_call(
        cast_kernel,
        out_shape=jax.ShapeDtypeStruct((rows, width), jnp.bfloat16),
        grid=(rows // 256,),
        in_specs=[block],
        out_specs=block,
        compiler_params=params_of(8),
        cost_estimate=cost(0, 6 * rows * width),
        name="cast_left",
    )(*in_hbm(array))


def partial_kernel(pieces, firsts, splits, *refs):
    x_refs, w_ref, refs = refs[:pieces], refs[pieces], refs[pieces + 1:]
    add_refs, out_refs, flip_ref = refs[:len(firsts)], refs[len(firsts):-1], refs[-1]
    x = jnp.concatenate([ref[...] for ref in x_refs], axis=1)
    total = jnp.dot(x, w_ref[...], preferred_element_type=jnp.float32)
    count = total.shape[0]
    for ref, first in zip(add_refs, firsts):
        last = first + ref.shape[0]
        rows = [total[:first], total[first:last] + ref[...].astype(jnp.float32), total[last:]]
        total = jnp.concatenate([r for r in rows if r.shape[0]], axis=0)
    height = count // splits
    for i, ref in enumerate(out_refs):
        ref[...] = total[i * height:(i + 1) * height].astype(ref.dtype)
    step = x_refs[0].shape[1]
    for i, ref in enumerate(x_refs):
        flip_ref[i * step:(i + 1) * step, :] = ref[...].T


def partial_keys(block, key_weights, adds=(), splits=1):
    count, rows = block.shape
    width = key_weights.shape[1]
    pieces = 4 if rows % (4 * HEAD) == 0 else 2
    fixed = lambda a: pl.BlockSpec(a.shape, lambda i: (0, 0))
    *parts, flipped = pl.pallas_call(
        functools.partial(partial_kernel, pieces, [first for _, first in adds], splits),
        out_shape=[jax.ShapeDtypeStruct((count // splits, width), jnp.bfloat16)] * splits
        + [jax.ShapeDtypeStruct((rows, count), jnp.bfloat16)],
        grid=(1,),
        in_specs=[pl.BlockSpec((count, rows // pieces), lambda i, c=c: (0, c)) for c in range(pieces)]
        + [fixed(key_weights)]
        + [fixed(a) for a, _ in adds],
        out_specs=[pl.BlockSpec((count // splits, width), lambda i: (0, 0))] * splits
        + [pl.BlockSpec((rows, count), lambda i: (0, 0))],
        compiler_params=params_of(12),
        cost_estimate=cost(2 * count * rows * width, 4 * count * rows),
        name="partial_keys",
    )(*[block] * pieces, key_weights, *[a for a, _ in adds])
    return parts if splits > 1 else parts[0], flipped


def key_kernel(first, *refs):
    *part_refs, cot_ref, out_ref = refs
    count = out_ref.shape[0]
    raw = sum(ref[...].astype(jnp.float32) for ref in part_refs)
    for h in range(raw.shape[1] // HEAD):
        cols = slice(h * HEAD, (h + 1) * HEAD)
        head = raw[:, cols]
        inverse = lax.rsqrt(jnp.mean(head * head, axis=1, keepdims=True) + 1e-06)
        normed = head * inverse
        upper = cot_ref[first:first + count, cols].astype(jnp.float32)
        back = inverse * (upper - normed * jnp.mean(upper * normed, axis=1, keepdims=True))
        out_ref[:, cols] = back.astype(out_ref.dtype)


def key_backward(parts, incoming, first):
    count, width = parts[0].shape
    block = pl.BlockSpec((count, width), lambda i: (0, 0))
    cot = pl.BlockSpec((incoming.shape[0], width), lambda i: (0, 0))
    return pl.pallas_call(
        functools.partial(key_kernel, first),
        out_shape=jax.ShapeDtypeStruct((count, width), jnp.bfloat16),
        grid=(1,),
        in_specs=[block] * len(parts) + [cot],
        out_specs=block,
        compiler_params=params_of(8),
        cost_estimate=cost(60 * count * width, 12 * count * width),
        name="key_backward",
    )(*parts, incoming)


def grad_kernel(count, has_base, has_more, last, place_ref, *refs):
    refs = list(refs)
    x_refs, u_refs = refs[:count], refs[count:2 * count]
    refs = refs[2 * count:]
    base = refs.pop(0) if has_base else None
    square_in, due_in = (refs.pop(0), refs.pop(0)) if has_more else (None, None)
    out_ref = refs.pop(0)
    x = jnp.concatenate([ref[...] for ref in x_refs], axis=1)
    u = jnp.concatenate([ref[...] for ref in u_refs], axis=0)
    total = jnp.dot(x, u, preferred_element_type=jnp.float32)
    if has_base:
        total = total + base[...]
    out_ref[...] = total
    if last:
        sq_ref, due_ref = refs

        @pl.when(pl.program_id(0) == 0)
        def _():
            sq_ref[...] = square_in[...] if has_more else jnp.zeros_like(sq_ref)

        rows, width = total.shape
        squares = (total * total).reshape(rows // 8, 8, width).sum(axis=0)
        folded = squares[:, :HEAD]
        for h in range(1, width // HEAD):
            folded = folded + squares[:, h * HEAD:(h + 1) * HEAD]
        sq_ref[...] += folded
        heads = width // FRAG_COLS
        mine = place_ref[0] - (0 if has_more else heads)
        mine = jnp.minimum(jnp.maximum(mine, 0), heads - 1) * FRAG_COLS
        column = out_ref[:, pl.ds(pl.multiple_of(mine, FRAG_COLS), FRAG_COLS)]
        if has_more:
            column = jnp.where(place_ref[0] < heads, column, due_in[...])
        due_ref[...] = column


def gradient(place, flipped, upstream, base=None, square=None, due=None, last=True):
    rows, depth = flipped[0].shape
    width = upstream[0].shape[1]
    step = 256
    row_block = lambda cols: pl.BlockSpec((step, cols), lambda i, p: (i, 0))
    fixed = pl.BlockSpec((8, HEAD), lambda i, p: (0, 0))
    args = [*flipped, *upstream]
    specs = [row_block(depth)] * len(flipped)
    specs += [pl.BlockSpec((depth, width), lambda i, p: (0, 0))] * len(upstream)
    if base is not None:
        args.append(base)
        specs.append(row_block(width))
    if square is not None:
        args += [square, due]
        specs += [fixed, row_block(FRAG_COLS)]
    if last:
        shapes = [
            jax.ShapeDtypeStruct((rows, width), jnp.float32),
            jax.ShapeDtypeStruct((8, HEAD), jnp.float32),
            jax.ShapeDtypeStruct((rows, FRAG_COLS), jnp.float32),
        ]
        outs = [row_block(width), fixed, row_block(FRAG_COLS)]
    else:
        shapes = [jax.ShapeDtypeStruct((rows, width), jnp.float32)]
        outs = [row_block(width)]
    depth *= len(flipped)
    return pl.pallas_call(
        functools.partial(grad_kernel, len(flipped), base is not None, square is not None, last),
        out_shape=shapes,
        grid_spec=pltpu.PrefetchScalarGridSpec(
            num_scalar_prefetch=1, grid=(rows // step,), in_specs=specs, out_specs=outs
        ),
        compiler_params=params_of(12),
        cost_estimate=cost(2 * rows * width * depth, 2 * rows * depth + 4 * rows * width),
        name="gradient",
    )(place, *args)


def clip_factor(square_refs):
    square = jnp.sum(sum(ref[...] for ref in square_refs), keepdims=True)
    return jnp.minimum(1.0, CLIP_NORM / (jnp.sqrt(square) + 1e-06))


def adam(old, first, second, grad, factor, scalars):
    rate, inv_one, inv_two = (scalars[i] for i in range(3))
    clipped = grad * factor
    first_new = BETA_ONE * first + (1.0 - BETA_ONE) * clipped
    second_new = BETA_TWO * second + (1.0 - BETA_TWO) * clipped * clipped
    update = rate * (
        first_new * inv_one / (jnp.sqrt(second_new * inv_two) + ADAM_EPS) + DECAY * old
    )
    return update, first_new, second_new


def adam_kernel(squares, extra, sc_ref, w_ref, m_ref, v_ref, gk_ref, gv_ref, *refs):
    factor = clip_factor(refs[:squares])
    w_out, m_out, v_out, *done = refs[squares + extra:]
    width = gk_ref.shape[1]
    for g_ref, cols in ((gk_ref, slice(0, width)), (gv_ref, slice(width, 2 * width))):
        old = w_ref[:, cols]
        update, first_new, second_new = adam(
            old, m_ref[:, cols], v_ref[:, cols], g_ref[...], factor, sc_ref
        )
        w_out[:, cols] = old - update
        m_out[:, cols] = first_new
        v_out[:, cols] = second_new
    for ref in done:
        ref[...] = jnp.zeros_like(ref)


def adam_rows(scalars, squares, state, first, last, into=()):
    rows, width = state[0].shape
    step = ADAM_ROWS
    full = pl.BlockSpec((step, width), lambda i: (i + first, 0))
    half = pl.BlockSpec((step, width // 2), lambda i: (i + first, 0))
    shapes = [pltpu.HBM((rows, width), jnp.float32)] * 3
    outs = [full] * 3
    if not into:
        shapes.append(jax.ShapeDtypeStruct((8, HEAD), jnp.float32))
        outs.append(pl.BlockSpec((8, HEAD), lambda i: (0, 0)))
    count = (last - first) * step
    return pl.pallas_call(
        functools.partial(adam_kernel, len(squares), len(into)),
        out_shape=shapes,
        grid=(last - first,),
        in_specs=[pl.BlockSpec(memory_space=pltpu.SMEM), full, full, full, half, half]
        + [pl.BlockSpec((8, HEAD), lambda i: (0, 0))] * len(squares)
        + [pl.BlockSpec(memory_space=pl.ANY)] * len(into),
        out_specs=outs,
        input_output_aliases={6 + len(squares) + i: i for i in range(len(into))},
        compiler_params=params_of(12),
        cost_estimate=cost(20 * count * width, 28 * count * width),
        name="adam_rows",
    )(scalars, *state, *squares, *in_hbm(*into))


def frag_kernel(squares, place_ref, sc_ref, w_ref, m_ref, v_ref, g_ref, *refs):
    blocks, part, _ = w_ref.shape
    factor = clip_factor(refs[:squares])
    inner_ref, *out_refs = refs[squares:]
    for j in range(blocks):
        at = pl.multiple_of((place_ref[1] ^ j) * part, 8)
        old = w_ref[j]
        update, _, _ = adam(old, m_ref[j], v_ref[j], g_ref[pl.ds(at, part), :], factor, sc_ref)
        inner_ref[j] = old - update
        out_refs[j][...] = update.astype(out_refs[j].dtype)


def adam_frag(place, scalars, squares, old, first, second, grad):
    blocks, part, width = old.shape
    smem = pl.BlockSpec(memory_space=pltpu.SMEM)
    vmem = pl.BlockSpec(memory_space=pltpu.VMEM)
    return pl.pallas_call(
        functools.partial(frag_kernel, len(squares)),
        out_shape=[jax.ShapeDtypeStruct(old.shape, jnp.float32)]
        + [jax.ShapeDtypeStruct((part, width), jnp.bfloat16)] * blocks,
        in_specs=[smem, smem] + [vmem] * (4 + len(squares)),
        out_specs=[vmem] * (1 + blocks),
        compiler_params=params_of(12),
        cost_estimate=cost(20 * old.size, 22 * old.size),
        name="adam_frag",
    )(place, scalars, old, first, second, grad, *squares)


def pick_kernel(blocks, place_ref, *refs):
    outs = refs[len(refs) // (blocks + 1) * blocks:]
    for i, out_ref in enumerate(outs):
        for j in range(blocks):
            out_ref[j] = refs[i * blocks + j][...]


def due_columns(place, part, *arrays):
    blocks = arrays[0].shape[0] // part
    specs = []
    for j in range(blocks):
        at = (lambda i, p, j=j: (p[1] ^ j, p[0])) if blocks > 1 else (lambda i, p: (0, p[0]))
        specs.append(pl.BlockSpec((part, FRAG_COLS), at))
    shape = (blocks, part, FRAG_COLS)
    return pl.pallas_call(
        functools.partial(pick_kernel, blocks),
        out_shape=[jax.ShapeDtypeStruct(shape, a.dtype) for a in arrays],
        grid_spec=pltpu.PrefetchScalarGridSpec(
            num_scalar_prefetch=1,
            grid=(1,),
            in_specs=specs * len(arrays),
            out_specs=[pl.BlockSpec(shape, lambda i, p: (0, 0, 0))] * len(arrays),
        ),
        compiler_params=params_of(12),
        cost_estimate=cost(0, 8 * blocks * part * FRAG_COLS * len(arrays)),
        name="due_columns",
    )(place, *[a for array in in_hbm(*arrays) for a in [array] * blocks])


def duplicate_kernel(*refs):
    half = (len(refs) - 3) // 2
    held, in_sems, out_sems = refs[2 * half:]
    streams = held.shape[1]
    step = held.shape[2]
    places = [(a, i, pl.ds(i * step, step)) for a in range(half) for i in range(streams)]
    fetches = [
        pltpu.make_async_copy(refs[a].at[at], held.at[a, i], in_sems.at[a, i]) for a, i, at in places
    ]
    stores = [
        pltpu.make_async_copy(held.at[a, i], refs[half + a].at[at], out_sems.at[a, i])
        for a, i, at in places
    ]
    for copy in fetches:
        copy.start()
    for fetch, store in zip(fetches, stores):
        fetch.wait()
        store.start()
    for copy in stores:
        copy.wait()


def duplicate(*arrays):
    rows, width = arrays[0].shape
    streams = 4
    whole = pl.BlockSpec(memory_space=pl.ANY)
    return pl.pallas_call(
        duplicate_kernel,
        out_shape=[pltpu.HBM(a.shape, a.dtype) for a in arrays],
        in_specs=[whole] * len(arrays),
        out_specs=[whole] * len(arrays),
        scratch_shapes=[
            pltpu.VMEM((len(arrays), streams, rows // streams, width), arrays[0].dtype),
            pltpu.SemaphoreType.DMA((len(arrays), streams)),
            pltpu.SemaphoreType.DMA((len(arrays), streams)),
        ],
        compiler_params=params_of(8),
        cost_estimate=cost(0, sum(8 * a.size for a in arrays)),
        name="duplicate",
    )(*in_hbm(*arrays))


def outer_kernel(replicas, place_ref, *refs):
    share = 1.0 / replicas
    base_refs, sum_refs = refs[3:3 + replicas], refs[3 + replicas:3 + 2 * replicas]
    inner_ref, a_ref, p_ref, m_ref, own_ref, _, *refs = refs[3 + 2 * replicas:]
    w_out, a_out, m_out, mixed, new_a, new_m, sems = refs
    part = a_ref.shape[0]
    scale = share * (1.0 + OUTER_MU) * OUTER_RATE
    columns = pl.ds(pl.multiple_of(place_ref[0] * FRAG_COLS, FRAG_COLS), FRAG_COLS)
    copies = []
    for j in range(replicas):
        fresh = base_refs[j][...] - scale * sum_refs[j][...].astype(jnp.float32)
        mixed[j] = MIX_LOCAL * inner_ref[j] + (1.0 - MIX_LOCAL) * fresh
        rows = pl.ds(pl.multiple_of((place_ref[1] ^ j) * part, 8), part)
        copies.append(pltpu.make_async_copy(mixed.at[j], w_out.at[rows, columns], sems.at[j]))
        copies[-1].start()
    pseudo = p_ref[...] + share * own_ref[...]
    new_moment = OUTER_MU * m_ref[...] + pseudo
    new_m[...] = new_moment
    new_a[...] = a_ref[...] - OUTER_RATE * (OUTER_MU * new_moment + pseudo)
    for i, (src, dst) in enumerate(((new_a, a_out), (new_m, m_out))):
        copies.append(pltpu.make_async_copy(src, dst.at[:, columns], sems.at[replicas + i]))
        copies[-1].start()
    for copy in copies:
        copy.wait()


def outer_step(place, outputs, base, sums, inner, anchor, pseudo, momentum, own_sum, ticket):
    replicas, part = inner.shape[0], inner.shape[1]
    whole = pl.BlockSpec(memory_space=pl.ANY)
    held = pl.BlockSpec(memory_space=pltpu.VMEM)
    return pl.pallas_call(
        functools.partial(outer_kernel, replicas),
        out_shape=[pltpu.HBM(a.shape, a.dtype) for a in outputs],
        in_specs=[pl.BlockSpec(memory_space=pltpu.SMEM)]
        + [whole] * 3
        + [held] * (2 * replicas + 5)
        + [whole],
        out_specs=[whole] * 3,
        scratch_shapes=[
            pltpu.VMEM((replicas, part, FRAG_COLS), jnp.float32),
            pltpu.VMEM((part, FRAG_COLS), jnp.float32),
            pltpu.VMEM((part, FRAG_COLS), jnp.float32),
            pltpu.SemaphoreType.DMA((replicas + 2,)),
        ],
        input_output_aliases={1: 0, 2: 1, 3: 2},
        compiler_params=params_of(12),
        cost_estimate=cost(10 * replicas * part * FRAG_COLS, 20 * replicas * part * FRAG_COLS),
        name="outer_step",
    )(place, *in_hbm(*outputs), *base, *sums, inner, anchor, pseudo, momentum, own_sum, ticket)


def swap(block, axis, offset):
    count = lax.axis_size(axis)
    return lax.ppermute(block, axis, [(i, i ^ offset) for i in range(count)])


def after(value, *others):
    return lax.optimization_barrier((value,) + others)[0]


def body(
    tokens,
    cotangent,
    weights,
    first_moment,
    second_moment,
    anchor,
    momentum,
    due_fragment,
    step_count,
):
    inputs, incoming, params = tokens[0], cotangent[0], weights[0]
    kv_width = incoming.shape[1] // 2
    rows = params.shape[0]
    part = anchor.shape[0]
    replicas = lax.axis_size("rep")
    shards = lax.axis_size("fsdp")
    me = jnp.reshape(lax.axis_index("fsdp"), (1,)).astype(jnp.int32)
    my_rep = lax.axis_index("rep").astype(jnp.int32)
    place = jnp.stack([due_fragment[0], my_rep])
    chips = range(2, shards, 2)
    far = sorted(chips, key=lambda k: (-bin(k).count("1"), k))
    order = [k for k in far[:-2] for k in (k, k + 1)]
    order += far[-2:] + [k + 1 for k in far[-2:]]

    (old,) = due_columns(place, part, params)
    old_sums = [old[0]] + [swap(old[k], "rep", k) for k in range(1, replicas)]

    packed = {}
    for offsets in (order[:1], order[1:4], order[4:], (0, 1)):
        packed |= pack(inputs, me, rows, tuple(offsets))
    blocks = {k: swap(packed[k], "fsdp", k) for k in order}
    blocks[0], blocks[1] = packed[0], swap(packed[1], "fsdp", 1)

    relay = len(far) == 3 and far[0] == far[1] ^ far[2]
    half = inputs.shape[0] // 2
    values = {0: incoming[:, kv_width:]}
    for i, k in enumerate(far[1:] if relay else far):
        values[k] = swap(after(values[0], blocks[order[i]]), "fsdp", k)
    if relay:
        upper = swap(values[far[1]][:half], "fsdp", far[2])
        lower = swap(values[far[2]][half:], "fsdp", far[1])
        values[far[0]] = jnp.concatenate([upper, lower], axis=0)

    steps_now = step_count[0].astype(jnp.float32)
    plan = jnp.minimum(1.0, steps_now / WARMUP) * (
        0.55 + 0.45 * jnp.cos(jnp.pi * steps_now / STEPS_TOTAL)
    )
    rate = PEAK_RATE * plan
    inv_one = 1.0 / (1.0 - jnp.power(BETA_ONE, steps_now))
    inv_two = 1.0 / (1.0 - jnp.power(BETA_TWO, steps_now))
    scalars = jnp.stack([rate, inv_one, inv_two])
    old_first, old_second = due_columns(place, part, first_moment[0], second_moment[0])
    anchor_cols, moment_cols = (c[0] for c in due_columns(place, part, anchor, momentum))
    pseudo_old = anchor_cols - sum(old_sums[1:], old_sums[0]) / replicas
    base = anchor_cols - OUTER_RATE * (OUTER_MU * (OUTER_MU * moment_cols + pseudo_old) + pseudo_old)
    base = [base] + [swap(base, "rep", k) for k in range(1, replicas)]
    anchor_copy, momentum_copy = duplicate(anchor, momentum)
    key_weights = cast_left(params, kv_width)

    last = far[-1]
    blocks[last + 1] = after(blocks[last + 1], anchor_copy, momentum_copy, scalars, old_first, old_second)
    parts, flipped, relayed = [], {}, {}
    for k in far + [0]:
        theirs, flipped[k + 1] = partial_keys(blocks[k + 1], key_weights)
        theirs = swap(theirs, "fsdp", 1)
        if k == last:
            theirs = after(theirs, *base)
        adds = [(theirs, 0)] + relayed.get(k, [])
        if relay and k == far[0]:
            (upper, lower), flipped[k] = partial_keys(blocks[k], key_weights, adds, 2)
            relayed[far[2]] = [(swap(upper, "fsdp", far[1]), 0)]
            relayed[far[1]] = [(swap(lower, "fsdp", far[2]), half)]
            continue
        part_k, flipped[k] = partial_keys(blocks[k], key_weights, adds)
        if k == last:
            for j in range(0, shards, 2):
                values[j + 1] = swap(after(values[j], part_k), "fsdp", 1)
        parts.append(swap(part_k, "fsdp", k) if k else part_k)
    spread = [0, 1] + [k + odd for k in far for odd in range(2)]
    near, rest = spread[:shards // 2], spread[shards // 2:]
    pick = lambda table, which: [table[k] for k in which]
    (values_first,) = gradient(place, pick(flipped, near), pick(values, near), last=False)
    keys = {0: key_backward(parts, incoming, 0)}
    for k in far:
        keys[k] = swap(keys[0], "fsdp", k)
    keys[1] = swap(keys[0], "fsdp", 1)

    grad_values, square, due = gradient(
        place, pick(flipped, rest), pick(values, rest), values_first
    )
    for k in near[2::2]:
        keys[k + 1] = swap(after(keys[k], square), "fsdp", 1)
    (keys_first,) = gradient(place, pick(flipped, near), pick(keys, near), last=False)
    for k in rest[::2]:
        keys[k + 1] = swap(after(keys[k], square), "fsdp", 1)
    grad_keys, square, due = gradient(
        place, pick(flipped, rest), pick(keys, rest), keys_first, square, due
    )

    square = square + swap(square, "fsdp", 1)
    squares = [square] + [swap(square, "fsdp", k) for k in chips]

    state = (params, first_moment[0], second_moment[0], grad_keys, grad_values)
    inner, *update = adam_frag(place, scalars, squares, old, old_first, old_second, due)
    steps = rows // ADAM_ROWS
    *results, ticket = adam_rows(scalars, squares, state, 0, steps // 2)
    own_sum = update[0].astype(jnp.float32)
    for k in range(1, replicas):
        own_sum = own_sum + swap(update[k], "rep", k).astype(jnp.float32)
    own_sum, ticket = lax.optimization_barrier((own_sum, ticket))
    sums = [own_sum.astype(jnp.bfloat16)]
    sums += [swap(sums[0], "rep", k) for k in range(1, replicas)]
    results = adam_rows(scalars, squares, state, steps // 2, steps, results)
    weights_out, anchor_out, momentum_out = outer_step(
        place,
        (results[0], anchor_copy, momentum_copy),
        base,
        sums,
        inner,
        anchor_cols,
        pseudo_old,
        moment_cols,
        own_sum,
        ticket,
    )
    plan_out = jnp.reshape(plan, (1,))
    return (
        weights_out[None],
        results[1][None],
        results[2][None],
        anchor_out,
        momentum_out,
        plan_out,
    )


def solution(mesh):
    tokens_spec = P("rep", "fsdp", None)
    outer_spec = P(("fsdp", "rep"), None)
    return jax.shard_map(
        body,
        mesh=mesh,
        in_specs=(tokens_spec,) * 5 + (outer_spec,) * 2 + (P(), P()),
        out_specs=(tokens_spec,) * 3 + (outer_spec,) * 2 + (P(),),
        check_vma=False,
    )
```
